32 devices in a mesh: section: 4 (over y, x), dp: 8 (over z, core).
Axes of the slice: x: 2, y: 2, z: 4, core: 2. Of those that a mesh axis runs over, the one named last changes fastest.
Arguments:
- hidden_in: bfloat16 [2, 2048, 1024], P(None, 'dp'), may hold values from -6 to 6
- cotangent: bfloat16 [2, 2048, 1024], P(None, 'dp'), may hold values from -6 to 6
- bucket_len: int32 [2, 8, 4], P(None, 'dp'), may hold values from 1 to 192, 256 in all within a row
- live_mask: int32 [2, 2048], P(None, 'dp'), may hold values 0 or 1
- routes: int32 [2, 2048, 1], P(None, 'dp'), may hold values from 0 to 7; in each aligned block of 256 rows (0 to 255, 256 to 511, ..., all dimensions but the last counted through in order) at most 48 rows name the same one
- ln1_gain: bfloat16 [1024], P(('section', 'dp')), may hold values from 0.5 to 1.5
- ln1_bias: bfloat16 [1024], P(('section', 'dp')), may hold values from -4 to 4
- w_qkv: bfloat16 [1024, 3072], P(('section', 'dp')), may hold values from -0.1875 to 0.1875
- w_attn_out: bfloat16 [1024, 1024], P(('section', 'dp')), may hold values from -0.75 to 0.75
- ln2_gain: bfloat16 [1024], P(('section', 'dp')), may hold values from 0.5 to 1.5
- ln2_bias: bfloat16 [1024], P(('section', 'dp')), may hold values from -4 to 4
- w_up: bfloat16 [1024, 4096], P(('section', 'dp')), may hold values from -0.1875 to 0.1875
- w_down: bfloat16 [4096, 1024], P(('section', 'dp')), may hold values from -0.09375 to 0.09375
- expert_in: bfloat16 [8, 1024, 4096], P('dp', None, 'section'), may hold values from -0.1875 to 0.1875
- expert_out: bfloat16 [8, 4096, 1024], P('dp', 'section'), may hold values from -0.09375 to 0.09375
- expert_gain: bfloat16 [8, 1024], P('dp', 'section'), may hold values from 0.5 to 1.5
- expert_bias: bfloat16 [8, 1024], P('dp', 'section'), may hold values from -4 to 4
- centroids: bfloat16 [8, 1024], P('dp', 'section'), may hold values from -0.09375 to 0.09375
Outputs:
- block_out: bfloat16 [2, 2048, 1024], P(None, 'dp', 'section')
- input_grad: float32 [2, 2048, 1024], P(None, 'dp', 'section')
- grad_ln1_gain: float32 [1024], P(('section', 'dp'))
- grad_ln1_bias: float32 [1024], P(('section', 'dp'))
- grad_w_qkv: float32 [1024, 3072], P(('section', 'dp'))
- grad_w_attn_out: float32 [1024, 1024], P(('section', 'dp'))
- grad_ln2_gain: float32 [1024], P(('section', 'dp'))
- grad_ln2_bias: float32 [1024], P(('section', 'dp'))
- grad_w_up: float32 [1024, 4096], P(('section', 'dp'))
- grad_w_down: float32 [4096, 1024], P(('section', 'dp'))
- grad_expert_in: float32 [8, 1024, 4096], P('dp', None, 'section')
- grad_expert_out: float32 [8, 4096, 1024], P('dp', 'section')
- grad_expert_gain: float32 [8, 1024], P('dp', 'section')
- grad_expert_bias: float32 [8, 1024], P('dp', 'section')
- grad_centroids: float32 [8, 1024], P('dp', 'section')
The draws below stay inside these ranges and needn't reach their ends.
Inputs may be any that keep to these rules, and one draw needn't show every extreme that they name: `routes`: in each block of 256 slots of a micro-batch (the slots of one index of dp), at most 48 slots name one expert. `bucket_len`: each block's 4 lengths sum to 256.
All inputs are finite; a program needn't handle non-finite values. No bound on the sum of `live_mask` on one device may be relied on, other than what follows from the above.
Results may differ from the reference program's by a relative error of at most 0.013.
Values may be sent and summed in bfloat16 or wider, within the bound.
A program may use at most 448 MiB of HBM per device.

```python
import math
import jax
import jax.numpy as jnp
import numpy as np
from jax import lax

D = 1024
HEADS = 16
FF = 4096
TOK_DEV = 256
MB = 2
NSEQ = 4
EXPERTS = 8
CAP = 48
TOKENS = 2048
N_DP = 8


def touch_ends(entries, own_key, smallest, top_value):
    spot = [jax.random.randint(jax.random.fold_in(own_key, axis), (), 0, length) for axis, length in enumerate(entries.shape)]
    widest = entries.shape.index(max(entries.shape))
    beside = spot[:widest] + [(spot[widest] + 1) % entries.shape[widest]] + spot[widest + 1:]
    return entries.at[tuple(spot)].set(smallest).at[tuple(beside)].set(top_value)


def steps_of(stream_key, shape, cuts, least, top_value):
    def one(axis_at, shards_of):
        draws = jax.random.uniform(jax.random.fold_in(jax.random.fold_in(stream_key, 6), axis_at), (shards_of,), jnp.float32, least / len(cuts), top_value / len(cuts))
        return jnp.repeat(jnp.exp(draws), shape[axis_at] // shards_of).reshape((-1,) + (1,) * (len(shape) - axis_at - 1))

    level = one(*cuts[0])
    for cut in cuts[1:]:
        level = level * one(*cut)
    return level


def profile(amount, total, reach, slope):
    portions = [(1 << 20) // math.isqrt(grade ** slope) + 1 for grade in range(2, amount + 1)]
    spare, given = total - reach - (amount - 1), [1] * (amount - 1)
    while spare > 0:
        candidates = [i for i in range(amount - 1) if given[i] < reach]
        pool, left = sum([portions[i] for i in candidates]), spare
        for i in candidates:
            more = min(reach - given[i], max(1, left * portions[i] // pool), spare)
            given[i] = given[i] + more
            spare = spare - more
    return np.array([reach] + given)


def uneven(key, count, total, most, slope):
    if count == 2:
        one = jax.random.randint(key, (), max(1, total - most), min(most, total - 1) + 1)
        return jnp.stack([one, total - one])
    tallies = jnp.asarray(profile(count, total, most, slope), jnp.int32)
    pairs = (count - 1) // 2
    giver, taker = tallies[1:1 + 2 * pairs:2], tallies[2:2 + 2 * pairs:2]
    slack = jnp.minimum(giver - 1, most - taker)
    shifted = jax.random.randint(jax.random.fold_in(key, 1), (pairs,), 0, 1 << 20) % (slack + 1)
    tallies = tallies.at[1:1 + 2 * pairs:2].set(giver - shifted).at[2:2 + 2 * pairs:2].set(taker + shifted)
    return tallies[jax.random.permutation(jax.random.fold_in(key, 2), count)]


def shared_out(rng, own, number, rows, number_of, top, reach, lean):
    ranking = jax.random.permutation(rng, number_of)
    heavy_load, ordinary = portions_of(number_of, rows * top, reach, lean, True), portions_of(number_of, rows * top, reach, lean, False)
    places = jnp.arange(number_of)

    def named(tallies, turn):
        used = int((tallies > 0).sum())
        fixed = max(1, used // 4)
        shifted = fixed + (places - fixed + turn * (used - fixed)) % max(1, number_of - fixed)
        return jnp.zeros((number_of,), jnp.int32).at[ranking[jnp.where(places < fixed, places, shifted)]].set(jnp.asarray(tallies, jnp.int32))

    tallies = jnp.where(number % 4 == 0, named(heavy_load, number // 4), named(ordinary, number - number // 4 - 1))
    mixed = jax.random.permutation(jax.random.fold_in(own, 3), number_of)
    donor, receiver = mixed[0:number_of // 2 * 2:2], mixed[1:number_of // 2 * 2:2]
    slack = jnp.minimum(tallies[donor] - 1, reach - tallies[receiver]) // 2
    slack = jnp.where((donor == ranking[0]) | (receiver == ranking[0]) | (tallies[receiver] == 0), 0, jnp.maximum(slack, 0))
    shifted = jax.random.randint(jax.random.fold_in(own, 4), (number_of // 2,), 0, 1 << 20) % (slack + 1)
    tallies = tallies.at[donor].add(-shifted).at[receiver].add(shifted)
    members = jnp.searchsorted(jnp.cumsum(tallies), jnp.arange(rows * top), side="right").astype(jnp.int32)
    table = members.reshape(top, rows).T
    table = table[jax.random.permutation(jax.random.fold_in(own, 1), rows)]
    turn = jax.random.randint(jax.random.fold_in(own, 2), (rows, 1), 0, top)
    return jnp.take_along_axis(table, (jnp.arange(top)[None, :] + turn) % top, axis=1)


def portions_of(number_of, total, reach, slope, full):
    portions = [(1 << 20) // math.isqrt(rank ** slope) + 1 for rank in range(1, number_of + 1)]
    largest = reach if full else min(reach, max(-(-total // number_of), total * portions[0] // sum(portions)))
    least = 1 if total - largest >= number_of - 1 else 0
    holding, rest = [largest] + [least] * (number_of - 1), total - largest - least * (number_of - 1)
    while rest > 0:
        movable = [i for i in range(1, number_of) if holding[i] < largest] or [i for i in range(1, number_of) if holding[i] < reach]
        mass, budget = sum([portions[i] for i in movable]), rest
        for i in movable:
            extra = min(reach - holding[i], max(1, budget * portions[i] // mass), rest)
            holding[i] = holding[i] + extra
            rest = rest - extra
    return np.array(holding)


def normal_values(key, dims, deviation, most, shards=(), kind=jnp.bfloat16):
    values = deviation * jax.random.normal(key, dims, jnp.float32)
    if shards:
        values = values * steps_of(key, dims, shards, -0.22, 0.18)
    return jnp.clip(values, -most, most).astype(kind)


def setup_inputs(seed: int = 0) -> dict:
    key_of = jax.random.split(jax.random.key(seed), 19)
    hidden_in = normal_values(key_of[0], (MB, TOKENS, D), 1.0, 6.0, ((1, 8),))
    cotangent = normal_values(key_of[1], (MB, TOKENS, D), 1.0, 6.0, ((1, 8),))
    bucket_len = jax.vmap(lambda own: uneven(own, NSEQ, TOK_DEV, 3 * TOK_DEV // 4, 2))(jax.random.split(key_of[2], MB * N_DP)).reshape((MB, N_DP, NSEQ)).astype(jnp.int32)
    live_mask = touch_ends((jax.random.randint(key_of[3], (MB, TOKENS), 0, 8) < 7).astype(jnp.int32), jax.random.fold_in(key_of[3], 1), 0, 1)
    routes_keys = jax.random.split(jax.random.fold_in(key_of[4], 1), MB * TOKENS // TOK_DEV)
    routes_turns = jax.random.permutation(jax.random.fold_in(key_of[4], 3), MB * TOKENS // TOK_DEV)
    routes = jax.vmap(lambda own, number: shared_out(jax.random.fold_in(key_of[4], 2), own, number, TOK_DEV, EXPERTS, 1, CAP, 0))(routes_keys, routes_turns).reshape((MB, TOKENS, 1))
    ln1_gain = jnp.clip(1.0 + 0.1 * jax.random.normal(key_of[5], (D,), jnp.float32), 0.5, 1.5).astype(jnp.bfloat16)
    ln1_bias = normal_values(key_of[6], (D,), 0.3, 4.0, ((0, 32),))
    w_qkv = normal_values(key_of[7], (D, 3 * D), D ** -0.5, 0.1875, ((0, 32),))
    w_attn_out = normal_values(key_of[8], (D, D), (D // 16) ** -0.5, 0.75, ((0, 32),))
    ln2_gain = jnp.clip(1.0 + 0.1 * jax.random.normal(key_of[9], (D,), jnp.float32), 0.5, 1.5).astype(jnp.bfloat16)
    ln2_bias = normal_values(key_of[10], (D,), 0.3, 4.0, ((0, 32),))
    w_up = normal_values(key_of[11], (D, FF), D ** -0.5, 0.1875, ((0, 32),))
    w_down = normal_values(key_of[12], (FF, D), FF ** -0.5, 0.09375, ((0, 32),))
    expert_in = normal_values(key_of[13], (EXPERTS, D, FF), D ** -0.5, 0.1875, ((0, 8), (2, 4)))
    expert_out = normal_values(key_of[14], (EXPERTS, FF, D), FF ** -0.5, 0.09375, ((0, 8), (1, 4)))
    expert_gain = jnp.clip(1.0 + 0.1 * jax.random.normal(key_of[15], (EXPERTS, D), jnp.float32), 0.5, 1.5).astype(jnp.bfloat16)
    expert_bias = normal_values(key_of[16], (EXPERTS, D), 0.3, 4.0, ((0, 8), (1, 4)))
    centroids = normal_values(key_of[17], (EXPERTS, D), (4 * D) ** -0.5, 0.09375, ((0, 8), (1, 4)))
    return {"hidden_in": hidden_in, "cotangent": cotangent, "bucket_len": bucket_len, "live_mask": live_mask, "routes": routes, "ln1_gain": ln1_gain, "ln1_bias": ln1_bias, "w_qkv": w_qkv, "w_attn_out": w_attn_out, "ln2_gain": ln2_gain, "ln2_bias": ln2_bias, "w_up": w_up, "w_down": w_down, "expert_in": expert_in, "expert_out": expert_out, "expert_gain": expert_gain, "expert_bias": expert_bias, "centroids": centroids}


@jax.custom_vjp
def low(v):
    return lax.optimization_barrier(v.astype(jnp.bfloat16)).astype(jnp.float32)

@jax.custom_vjp
def low_back(v):
    return v

def low_keep(v):
    return (low(v), None)

def low_pass(kept, grad):
    return (grad,)

def back_keep(v):
    return (v, None)

def back_low(kept, grad):
    return (low(grad),)
low.defvjp(low_keep, low_pass)
low_back.defvjp(back_keep, back_low)
epsilon = 1e-05
masked_value = -1e+30
highest = lax.Precision.HIGHEST

def rounded_both(values):
    return low_back(low(values))

def layer_norm(values, gain, bias):
    center = values - lax.optimization_barrier(jnp.mean(values, axis=-1, keepdims=True))
    spread = lax.optimization_barrier(jnp.mean(center * center, axis=-1, keepdims=True))
    return center * lax.rsqrt(spread + epsilon) * gain + bias

def allowed_pairs(segment, live):
    places = jnp.arange(segment.shape[0], dtype=jnp.int32)
    same = segment[:, None] == segment[None, :]
    causal = places[None, :] <= places[:, None]
    opened = (live[None, :] == 1) | (places[None, :] == places[:, None])
    return same & causal & opened

def attend_block(normed, segment, live, w_qkv):
    row_count = normed.shape[0]
    size = D // HEADS
    mixed_qkv = rounded_both(jnp.dot(normed, w_qkv, precision=highest))
    queries = mixed_qkv[:, :D].reshape(row_count, HEADS, size)
    key_rows = mixed_qkv[:, D:2 * D].reshape(row_count, HEADS, size)
    value_rows = mixed_qkv[:, 2 * D:].reshape(row_count, HEADS, size)
    raw = jnp.einsum('qhd,khd->hqk', queries, key_rows, precision=highest) * size ** (-0.5)
    scores = jnp.where(allowed_pairs(segment, live)[None], low_back(raw), masked_value)
    top = lax.optimization_barrier(jnp.max(scores, axis=-1, keepdims=True))
    weights = jnp.exp(scores - top)
    probs = low(weights / lax.optimization_barrier(jnp.sum(weights, axis=-1, keepdims=True)))
    mixed = jnp.einsum('hqk,khd->qhd', probs, value_rows, precision=highest)
    return rounded_both(mixed.reshape(row_count, D))

def expert_apply(rows, w_in, w_out, gain, bias, centroid):
    normed = low(layer_norm(rows, gain, bias))
    pre = low_back(jnp.dot(normed, w_in, precision=highest))
    result = low_back(jnp.dot(low(jax.nn.gelu(pre)), w_out, precision=highest))
    alpha = jax.nn.sigmoid(lax.optimization_barrier(jnp.sum(rows * centroid, axis=-1, keepdims=True)))
    return rounded_both(alpha * result)

def forward(hidden, params, segments, live, dest, table):
    ln1_gain, ln1_bias, w_qkv, w_attn_out, ln2_gain, ln2_bias, w_up, w_down, expert_in, expert_out, expert_gain, expert_bias, centroids = params
    attend_saved = jax.checkpoint(attend_block)
    expert_saved = jax.checkpoint(expert_apply)
    results = []
    for batch_now in range(MB):
        start = hidden[batch_now]
        normed = low(layer_norm(start, ln1_gain, ln1_bias)).reshape(N_DP, TOK_DEV, D)
        attended = lax.map(lambda item: attend_saved(item[0], item[1], item[2], w_qkv), (normed, segments[batch_now], live[batch_now]))
        first = rounded_both(start + jnp.dot(attended.reshape(TOKENS, D), w_attn_out, precision=highest))
        normed_two = low(layer_norm(first, ln2_gain, ln2_bias))
        pre = low_back(jnp.dot(normed_two, w_up, precision=highest))
        second = rounded_both(first + jnp.dot(low(jax.nn.gelu(pre)), w_down, precision=highest))
        gathered = low_back(jnp.take(second, table[batch_now], axis=0, mode='fill', fill_value=0.0))
        gated = lax.map(lambda item: expert_saved(item[0], item[1], item[2], item[3], item[4], item[5]), (gathered.reshape(EXPERTS, N_DP * CAP, D), expert_in, expert_out, expert_gain, expert_bias, centroids))
        results.append(second + jnp.take(gated.reshape(EXPERTS * N_DP * CAP, D), dest[batch_now], axis=0))
    return jnp.stack(results)

def reference(hidden_in, cotangent, bucket_len, live_mask, routes, ln1_gain, ln1_bias, w_qkv, w_attn_out, ln2_gain, ln2_bias, w_up, w_down, expert_in, expert_out, expert_gain, expert_bias, centroids):
    ends = jnp.cumsum(bucket_len, axis=-1)
    slots = jnp.arange(TOK_DEV, dtype=jnp.int32)
    segments = lax.optimization_barrier(jnp.sum((slots[None, None, :, None] >= ends[:, :, None, :]).astype(jnp.int32), axis=-1))
    live = live_mask.reshape(MB, N_DP, TOK_DEV)
    chosen = routes[:, :, 0].reshape(MB, N_DP, TOK_DEV)
    picks = (chosen[..., None] == jnp.arange(EXPERTS, dtype=jnp.int32)).astype(jnp.int32)
    ranks = lax.optimization_barrier(jnp.sum((jnp.cumsum(picks, axis=2) - picks) * picks, axis=-1)).astype(jnp.int32)
    sources = jnp.arange(N_DP, dtype=jnp.int32)[None, :, None]
    dest = (chosen * (N_DP * CAP) + sources * CAP + ranks).reshape(MB, TOKENS).astype(jnp.int32)
    token_ids = jnp.arange(TOKENS, dtype=jnp.int32)
    table = jnp.stack([jnp.full((EXPERTS * N_DP * CAP,), TOKENS, jnp.int32).at[dest[batch_now]].set(token_ids) for batch_now in range(MB)])
    params = tuple((weight.astype(jnp.float32) for weight in (ln1_gain, ln1_bias, w_qkv, w_attn_out, ln2_gain, ln2_bias, w_up, w_down, expert_in, expert_out, expert_gain, expert_bias, centroids)))

    def whole(hidden, weights):
        return forward(hidden, weights, segments, live, dest, table)
    block_out, pullback = jax.vjp(whole, hidden_in.astype(jnp.float32), params)
    input_grad, grads = pullback(cotangent.astype(jnp.float32))
    return (block_out.astype(jnp.bfloat16), input_grad, grads[0], grads[1], grads[2], grads[3], grads[4], grads[5], grads[6], grads[7], grads[8], grads[9], grads[10], grads[11], grads[12])
```

```python
import jax
import jax.numpy as jnp
from jax import lax
from jax.sharding import PartitionSpec as P

HEADS = 16
epsilon = 1e-05
masked_value = -1e30
f32 = jnp.float32
bf16 = jnp.bfloat16


def norm_parts(values):
    center = values - jnp.mean(values, axis=-1, keepdims=True)
    spread = jnp.mean(center * center, axis=-1, keepdims=True)
    rs = lax.rsqrt(spread + epsilon)
    return center * rs, rs


def gelu_back(pre, grad):
    outputs, pullback = jax.vjp(jax.nn.gelu, pre)
    return pullback(grad)[0]


def dot(a, b):
    return jnp.dot(a, b, preferred_element_type=f32)


def dot_tn(a, b):
    return jnp.einsum("rd,re->de", a, b, preferred_element_type=f32)


def dot_nt(a, b):
    return jnp.einsum("re,de->rd", a, b, preferred_element_type=f32)


def sum_scatter(part):
    return lax.psum_scatter(
        part.astype(bf16), "section", scatter_dimension=part.ndim - 1, tiled=True
    ).astype(f32)


def gather_features(part):
    return lax.all_gather(part, "section", axis=part.ndim - 1, tiled=True)


def on_device(
    hidden_in,
    cotangent,
    bucket_len,
    live_mask,
    routes,
    ln1_gain,
    ln1_bias,
    w_qkv,
    w_attn_out,
    ln2_gain,
    ln2_bias,
    w_up,
    w_down,
    expert_in,
    expert_out,
    expert_gain,
    expert_bias,
    centroids,
):
    sections = lax.axis_size("section")
    groups = lax.axis_size("dp")
    section = lax.axis_index("section")
    micro, rows, width = hidden_in.shape
    quarter = width // sections
    heads = HEADS // sections
    size = width // HEADS
    ff = w_up.shape[1] // sections
    capacity = 3 * rows // (2 * groups)
    shard = w_up.shape[0]
    own_cols = section * quarter

    def mine(values):
        return lax.dynamic_slice_in_dim(values, own_cols, quarter, values.ndim - 1)

    def column_group(weight, pieces):
        cols = weight.shape[1] // (pieces * sections)
        parts = weight.reshape(shard, pieces, sections, cols).transpose(2, 0, 1, 3)
        parts = parts.reshape(sections, shard, pieces * cols)
        parts = lax.all_to_all(parts, "section", split_axis=0, concat_axis=0, tiled=True)
        full = lax.all_gather(parts, "dp", axis=1, tiled=True)
        return full.reshape(width, pieces * cols)

    def column_group_back(grad, pieces):
        cols = grad.shape[1] // pieces
        parts = grad.astype(bf16).reshape(sections, groups * shard, pieces * cols)
        parts = lax.psum_scatter(parts, "dp", scatter_dimension=1, tiled=True)
        parts = lax.all_to_all(parts, "section", split_axis=0, concat_axis=0, tiled=True)
        parts = parts.reshape(sections, shard, pieces, cols).transpose(1, 2, 0, 3)
        return parts.reshape(shard, pieces * sections * cols).astype(f32)

    def row_group_back(grad):
        return lax.psum_scatter(
            grad.astype(bf16), "dp", scatter_dimension=0, tiled=True
        ).astype(f32)

    vectors = lax.all_gather(
        jnp.stack([ln1_gain, ln1_bias, ln2_gain, ln2_bias]), ("section", "dp"), axis=1, tiled=True
    ).astype(f32)
    gain_one, bias_one, gain_two, bias_two = vectors
    expert_vectors = lax.all_gather(
        jnp.concatenate([expert_gain, expert_bias, centroids]), "section", axis=1, tiled=True
    ).astype(f32)
    expert_g, expert_b, centroid = expert_vectors
    wqkv = column_group(w_qkv, 3)
    wo = lax.all_gather(w_attn_out, "dp", axis=0, tiled=True)
    wup = column_group(w_up, 1)
    wdown = lax.all_gather(w_down, "dp", axis=0, tiled=True)
    win = expert_in[0]
    wout = expert_out[0]

    ends = jnp.cumsum(bucket_len[:, 0, :], axis=-1)
    slot_ids = jnp.arange(rows, dtype=jnp.int32)
    segments = jnp.sum((slot_ids[None, :, None] >= ends[:, None, :]).astype(jnp.int32), axis=-1)
    same = segments[:, :, None] == segments[:, None, :]
    causal = slot_ids[None, None, :] <= slot_ids[None, :, None]
    opened = (live_mask[:, None, :] == 1) | (slot_ids[None, None, :] == slot_ids[None, :, None])
    allowed = (same & causal & opened)[:, None]
    chosen = routes[:, :, 0]
    picks = (chosen[:, :, None] == jnp.arange(groups, dtype=jnp.int32)).astype(jnp.int32)
    ranks = jnp.sum((jnp.cumsum(picks, axis=1) - picks) * picks, axis=2)
    places = chosen * capacity + ranks
    place_ids = jnp.arange(groups * capacity, dtype=jnp.int32)
    picked = (places[:, None, :] == place_ids[None, :, None]).astype(bf16)

    def dispatch(values):
        out = jnp.einsum("mpt,mtf->pmf", picked, values, preferred_element_type=f32).astype(bf16)
        out = out.reshape(groups, capacity * micro, quarter)
        return lax.all_to_all(out, "dp", split_axis=0, concat_axis=0, tiled=True)

    def give_back(values):
        out = lax.all_to_all(values, "dp", split_axis=0, concat_axis=0, tiled=True)
        out = out.reshape(groups * capacity, micro, quarter)
        return jnp.einsum("mpt,pmf->mtf", picked, out, preferred_element_type=f32)

    dge = gather_features(dispatch(mine(cotangent))).reshape(-1, width).astype(f32)

    x = hidden_in.reshape(micro * rows, width).astype(f32)
    n1, rs1 = norm_parts(x)
    a1 = (n1 * gain_one + bias_one).astype(bf16)
    qkv = dot(a1, wqkv).astype(bf16)
    q, k, v = (
        qkv[:, i * quarter : (i + 1) * quarter].reshape(micro, rows, heads, size) for i in range(3)
    )
    scale = size ** (-0.5)
    raw = jnp.einsum("mqhd,mkhd->mhqk", q, k, preferred_element_type=f32) * scale
    scores = jnp.where(allowed, raw, masked_value)
    weights = jnp.exp(scores - jnp.max(scores, axis=-1, keepdims=True))
    probs = weights / jnp.sum(weights, axis=-1, keepdims=True)
    probs_low = probs.astype(bf16)
    mixed = jnp.einsum("mhqk,mkhd->mqhd", probs_low, v, preferred_element_type=f32)
    o = mixed.reshape(micro * rows, quarter).astype(bf16)
    y1q = (mine(x) + sum_scatter(dot(o, wo))).astype(bf16)
    y1 = gather_features(y1q).astype(f32)
    n2, rs2 = norm_parts(y1)
    a2 = (n2 * gain_two + bias_two).astype(bf16)
    h = dot(a2, wup)
    u = jax.nn.gelu(h).astype(bf16)
    y2q = (y1q.astype(f32) + sum_scatter(dot(u, wdown))).astype(bf16)

    xe = gather_features(dispatch(y2q.reshape(micro, rows, quarter))).reshape(-1, width)
    xe = xe.astype(f32)
    ne, rse = norm_parts(xe)
    en = (ne * expert_g + expert_b).astype(bf16)
    he = dot(en, win)
    ue = jax.nn.gelu(he).astype(bf16)
    fe_part = dot(ue, wout)
    alpha = jax.nn.sigmoid(jnp.sum(xe * centroid, axis=-1, keepdims=True))
    fe = sum_scatter(fe_part)
    ge = (alpha * fe).astype(bf16).reshape(groups, capacity * micro, quarter)
    block_out = (
        y2q.reshape(micro, rows, quarter).astype(f32) + give_back(ge)
    ).astype(bf16)

    dfe = (alpha * dge).astype(bf16)
    due = dot_nt(dfe, wout)
    grad_out = dot_tn(ue, dfe)
    dhe = gelu_back(he, due).astype(bf16)
    grad_in = dot_tn(en, dhe)
    den_part = dot_nt(dhe, win)
    gden = den_part * expert_g
    stats = lax.psum(
        jnp.stack(
            [
                jnp.mean(gden, axis=-1),
                jnp.mean(gden * ne, axis=-1),
                jnp.sum(dge * fe_part, axis=-1),
            ]
        ),
        "section",
    )[..., None]
    den = sum_scatter(den_part)
    neq = mine(ne)
    dlogit = stats[2] * alpha * (1.0 - alpha)
    dxe_ln = rse * (mine(expert_g) * den - stats[0] - neq * stats[1])
    dxe = (dxe_ln + dlogit * mine(centroid)).astype(bf16)
    grad_expert_gain = jnp.sum(den * neq, axis=0)
    grad_expert_bias = jnp.sum(den, axis=0)
    grad_centroid = jnp.sum(dlogit * mine(xe), axis=0)
    back = give_back(dxe.reshape(groups, capacity * micro, quarter))
    dy2q = (mine(cotangent).astype(f32) + back).astype(bf16).reshape(micro * rows, quarter)

    dy2 = gather_features(dy2q)
    grad_down = dot_tn(u, dy2)
    dh = gelu_back(h, dot_nt(dy2, wdown)).astype(bf16)
    grad_up = dot_tn(a2, dh)
    da2_part = dot_nt(dh, wup)
    gda2 = da2_part * gain_two
    stats = lax.psum(
        jnp.stack([jnp.mean(gda2, axis=-1), jnp.mean(gda2 * n2, axis=-1)]), "section"
    )[..., None]
    da2 = sum_scatter(da2_part)
    n2q = mine(n2)
    dy1q = dy2q.astype(f32) + rs2 * (mine(gain_two) * da2 - stats[0] - n2q * stats[1])
    dy1q = dy1q.astype(bf16)
    dy1 = gather_features(dy1q)
    grad_wo = dot_tn(o, dy1)
    do = dot_nt(dy1, wo).astype(bf16).reshape(micro, rows, heads, size)
    dp = jnp.einsum("mqhd,mkhd->mhqk", do, v, preferred_element_type=f32)
    dv = jnp.einsum("mhqk,mqhd->mkhd", probs_low, do, preferred_element_type=f32)
    delta = jnp.sum(probs * dp, axis=-1, keepdims=True)
    ds = (probs * (dp - delta)).astype(bf16)
    dq = jnp.einsum("mhqk,mkhd->mqhd", ds, k, preferred_element_type=f32) * scale
    dk = jnp.einsum("mhqk,mqhd->mkhd", ds, q, preferred_element_type=f32) * scale
    dqkv = jnp.concatenate(
        [part.reshape(micro * rows, quarter) for part in (dq, dk, dv)], axis=1
    ).astype(bf16)
    grad_qkv = dot_tn(a1, dqkv)
    da1_part = dot_nt(dqkv, wqkv)
    gda1 = da1_part * gain_one
    stats = lax.psum(
        jnp.stack([jnp.mean(gda1, axis=-1), jnp.mean(gda1 * n1, axis=-1)]), "section"
    )[..., None]
    da1 = sum_scatter(da1_part)
    n1q = mine(n1)
    dx = dy1q.astype(f32) + rs1 * (mine(gain_one) * da1 - stats[0] - n1q * stats[1])

    vector_grads = lax.psum_scatter(
        jnp.stack(
            [
                jnp.sum(da1 * n1q, axis=0),
                jnp.sum(da1, axis=0),
                jnp.sum(da2 * n2q, axis=0),
                jnp.sum(da2, axis=0),
            ]
        ),
        "dp",
        scatter_dimension=1,
        tiled=True,
    )
    return (
        block_out,
        dx.reshape(micro, rows, quarter),
        vector_grads[0],
        vector_grads[1],
        column_group_back(grad_qkv, 3),
        row_group_back(grad_wo),
        vector_grads[2],
        vector_grads[3],
        column_group_back(grad_up, 1),
        row_group_back(grad_down),
        grad_in[None],
        grad_out[None],
        grad_expert_gain[None],
        grad_expert_bias[None],
        grad_centroid[None],
    )


def solution(mesh):
    everywhere = ("section", "dp")
    tokens = P(None, "dp", None)
    outs = P(None, "dp", "section")
    per_expert = P("dp", "section")
    return jax.shard_map(
        on_device,
        mesh=mesh,
        in_specs=(
            tokens,
            tokens,
            tokens,
            P(None, "dp"),
            tokens,
            P(everywhere),
            P(everywhere),
            P(everywhere, None),
            P(everywhere, None),
            P(everywhere),
            P(everywhere),
            P(everywhere, None),
            P(everywhere, None),
            P("dp", None, "section"),
            P("dp", "section", None),
            per_expert,
            per_expert,
            per_expert,
        ),
        out_specs=(
            outs,
            outs,
            P(everywhere),
            P(everywhere),
            P(everywhere, None),
            P(everywhere, None),
            P(everywhere),
            P(everywhere),
            P(everywhere, None),
            P(everywhere, None),
            P("dp", None, "section"),
            P("dp", "section", None),
            per_expert,
            per_expert,
            per_expert,
        ),
        check_vma=False,
    )
```

```python
import functools
import types

import jax
import jax.numpy as jnp
from jax import lax
from jax.experimental import pallas as pl
from jax.experimental.pallas import tpu as pltpu
from jax.sharding import PartitionSpec as P

HEADS = 16
epsilon = 1e-05
masked_value = -1e30
f32 = jnp.float32
bf16 = jnp.bfloat16


def norm_parts(values):
    center = values - jnp.mean(values, axis=-1, keepdims=True)
    spread = jnp.mean(center * center, axis=-1, keepdims=True)
    rs = lax.rsqrt(spread + epsilon)
    return center * rs, rs


def gelu_back(pre, grad):
    outputs, pullback = jax.vjp(jax.nn.gelu, pre)
    return pullback(grad)[0]


def dot(a, b):
    return jnp.dot(a, b, preferred_element_type=f32)


def dot_tn(a, b):
    return jnp.einsum("rd,re->de", a, b, preferred_element_type=f32)


def dot_nt(a, b):
    return jnp.einsum("re,de->rd", a, b, preferred_element_type=f32)


def sum_scatter(part):
    return lax.psum_scatter(
        part.astype(bf16), "section", scatter_dimension=part.ndim - 1, tiled=True
    ).astype(f32)


def gather_features(part):
    return lax.all_gather(part, "section", axis=part.ndim - 1, tiled=True)


def with_collectives(
    hidden_in,
    cotangent,
    bucket_len,
    live_mask,
    routes,
    ln1_gain,
    ln1_bias,
    w_qkv,
    w_attn_out,
    ln2_gain,
    ln2_bias,
    w_up,
    w_down,
    expert_in,
    expert_out,
    expert_gain,
    expert_bias,
    centroids,
):
    sections = lax.axis_size("section")
    groups = lax.axis_size("dp")
    section = lax.axis_index("section")
    micro, rows, width = hidden_in.shape
    quarter = width // sections
    heads = HEADS // sections
    size = width // HEADS
    ff = w_up.shape[1] // sections
    capacity = 3 * rows // (2 * groups)
    shard = w_up.shape[0]
    own_cols = section * quarter

    def mine(values):
        return lax.dynamic_slice_in_dim(values, own_cols, quarter, values.ndim - 1)

    def column_group(weight, pieces):
        cols = weight.shape[1] // (pieces * sections)
        parts = weight.reshape(shard, pieces, sections, cols).transpose(2, 0, 1, 3)
        parts = parts.reshape(sections, shard, pieces * cols)
        parts = lax.all_to_all(parts, "section", split_axis=0, concat_axis=0, tiled=True)
        full = lax.all_gather(parts, "dp", axis=1, tiled=True)
        return full.reshape(width, pieces * cols)

    def column_group_back(grad, pieces):
        cols = grad.shape[1] // pieces
        parts = grad.astype(bf16).reshape(sections, groups * shard, pieces * cols)
        parts = lax.psum_scatter(parts, "dp", scatter_dimension=1, tiled=True)
        parts = lax.all_to_all(parts, "section", split_axis=0, concat_axis=0, tiled=True)
        parts = parts.reshape(sections, shard, pieces, cols).transpose(1, 2, 0, 3)
        return parts.reshape(shard, pieces * sections * cols).astype(f32)

    def row_group_back(grad):
        return lax.psum_scatter(
            grad.astype(bf16), "dp", scatter_dimension=0, tiled=True
        ).astype(f32)

    vectors = lax.all_gather(
        jnp.stack([ln1_gain, ln1_bias, ln2_gain, ln2_bias]), ("section", "dp"), axis=1, tiled=True
    ).astype(f32)
    gain_one, bias_one, gain_two, bias_two = vectors
    expert_vectors = lax.all_gather(
        jnp.concatenate([expert_gain, expert_bias, centroids]), "section", axis=1, tiled=True
    ).astype(f32)
    expert_g, expert_b, centroid = expert_vectors
    wqkv = column_group(w_qkv, 3)
    wo = lax.all_gather(w_attn_out, "dp", axis=0, tiled=True)
    wup = column_group(w_up, 1)
    wdown = lax.all_gather(w_down, "dp", axis=0, tiled=True)
    win = expert_in[0]
    wout = expert_out[0]

    ends = jnp.cumsum(bucket_len[:, 0, :], axis=-1)
    slot_ids = jnp.arange(rows, dtype=jnp.int32)
    segments = jnp.sum((slot_ids[None, :, None] >= ends[:, None, :]).astype(jnp.int32), axis=-1)
    same = segments[:, :, None] == segments[:, None, :]
    causal = slot_ids[None, None, :] <= slot_ids[None, :, None]
    opened = (live_mask[:, None, :] == 1) | (slot_ids[None, None, :] == slot_ids[None, :, None])
    allowed = (same & causal & opened)[:, None]
    chosen = routes[:, :, 0]
    picks = (chosen[:, :, None] == jnp.arange(groups, dtype=jnp.int32)).astype(jnp.int32)
    ranks = jnp.sum((jnp.cumsum(picks, axis=1) - picks) * picks, axis=2)
    places = chosen * capacity + ranks
    place_ids = jnp.arange(groups * capacity, dtype=jnp.int32)
    picked = (places[:, None, :] == place_ids[None, :, None]).astype(bf16)

    def dispatch(values):
        out = jnp.einsum("mpt,mtf->pmf", picked, values, preferred_element_type=f32).astype(bf16)
        out = out.reshape(groups, capacity * micro, quarter)
        return lax.all_to_all(out, "dp", split_axis=0, concat_axis=0, tiled=True)

    def give_back(values):
        out = lax.all_to_all(values, "dp", split_axis=0, concat_axis=0, tiled=True)
        out = out.reshape(groups * capacity, micro, quarter)
        return jnp.einsum("mpt,pmf->mtf", picked, out, preferred_element_type=f32)

    dge = gather_features(dispatch(mine(cotangent))).reshape(-1, width).astype(f32)

    x = hidden_in.reshape(micro * rows, width).astype(f32)
    n1, rs1 = norm_parts(x)
    a1 = (n1 * gain_one + bias_one).astype(bf16)
    qkv = dot(a1, wqkv).astype(bf16)
    q, k, v = (
        qkv[:, i * quarter : (i + 1) * quarter].reshape(micro, rows, heads, size) for i in range(3)
    )
    scale = size ** (-0.5)
    raw = jnp.einsum("mqhd,mkhd->mhqk", q, k, preferred_element_type=f32) * scale
    scores = jnp.where(allowed, raw, masked_value)
    weights = jnp.exp(scores - jnp.max(scores, axis=-1, keepdims=True))
    probs = weights / jnp.sum(weights, axis=-1, keepdims=True)
    probs_low = probs.astype(bf16)
    mixed = jnp.einsum("mhqk,mkhd->mqhd", probs_low, v, preferred_element_type=f32)
    o = mixed.reshape(micro * rows, quarter).astype(bf16)
    y1q = (mine(x) + sum_scatter(dot(o, wo))).astype(bf16)
    y1 = gather_features(y1q).astype(f32)
    n2, rs2 = norm_parts(y1)
    a2 = (n2 * gain_two + bias_two).astype(bf16)
    h = dot(a2, wup)
    u = jax.nn.gelu(h).astype(bf16)
    y2q = (y1q.astype(f32) + sum_scatter(dot(u, wdown))).astype(bf16)

    xe = gather_features(dispatch(y2q.reshape(micro, rows, quarter))).reshape(-1, width)
    xe = xe.astype(f32)
    ne, rse = norm_parts(xe)
    en = (ne * expert_g + expert_b).astype(bf16)
    he = dot(en, win)
    ue = jax.nn.gelu(he).astype(bf16)
    fe_part = dot(ue, wout)
    alpha = jax.nn.sigmoid(jnp.sum(xe * centroid, axis=-1, keepdims=True))
    fe = sum_scatter(fe_part)
    ge = (alpha * fe).astype(bf16).reshape(groups, capacity * micro, quarter)
    block_out = (
        y2q.reshape(micro, rows, quarter).astype(f32) + give_back(ge)
    ).astype(bf16)

    dfe = (alpha * dge).astype(bf16)
    due = dot_nt(dfe, wout)
    grad_out = dot_tn(ue, dfe)
    dhe = gelu_back(he, due).astype(bf16)
    grad_in = dot_tn(en, dhe)
    den_part = dot_nt(dhe, win)
    gden = den_part * expert_g
    stats = lax.psum(
        jnp.stack(
            [
                jnp.mean(gden, axis=-1),
                jnp.mean(gden * ne, axis=-1),
                jnp.sum(dge * fe_part, axis=-1),
            ]
        ),
        "section",
    )[..., None]
    den = sum_scatter(den_part)
    neq = mine(ne)
    dlogit = stats[2] * alpha * (1.0 - alpha)
    dxe_ln = rse * (mine(expert_g) * den - stats[0] - neq * stats[1])
    dxe = (dxe_ln + dlogit * mine(centroid)).astype(bf16)
    grad_expert_gain = jnp.sum(den * neq, axis=0)
    grad_expert_bias = jnp.sum(den, axis=0)
    grad_centroid = jnp.sum(dlogit * mine(xe), axis=0)
    back = give_back(dxe.reshape(groups, capacity * micro, quarter))
    dy2q = (mine(cotangent).astype(f32) + back).astype(bf16).reshape(micro * rows, quarter)

    dy2 = gather_features(dy2q)
    grad_down = dot_tn(u, dy2)
    dh = gelu_back(h, dot_nt(dy2, wdown)).astype(bf16)
    grad_up = dot_tn(a2, dh)
    da2_part = dot_nt(dh, wup)
    gda2 = da2_part * gain_two
    stats = lax.psum(
        jnp.stack([jnp.mean(gda2, axis=-1), jnp.mean(gda2 * n2, axis=-1)]), "section"
    )[..., None]
    da2 = sum_scatter(da2_part)
    n2q = mine(n2)
    dy1q = dy2q.astype(f32) + rs2 * (mine(gain_two) * da2 - stats[0] - n2q * stats[1])
    dy1q = dy1q.astype(bf16)
    dy1 = gather_features(dy1q)
    grad_wo = dot_tn(o, dy1)
    do = dot_nt(dy1, wo).astype(bf16).reshape(micro, rows, heads, size)
    dp = jnp.einsum("mqhd,mkhd->mhqk", do, v, preferred_element_type=f32)
    dv = jnp.einsum("mhqk,mqhd->mkhd", probs_low, do, preferred_element_type=f32)
    delta = jnp.sum(probs * dp, axis=-1, keepdims=True)
    ds = (probs * (dp - delta)).astype(bf16)
    dq = jnp.einsum("mhqk,mkhd->mqhd", ds, k, preferred_element_type=f32) * scale
    dk = jnp.einsum("mhqk,mqhd->mkhd", ds, q, preferred_element_type=f32) * scale
    dqkv = jnp.concatenate(
        [part.reshape(micro * rows, quarter) for part in (dq, dk, dv)], axis=1
    ).astype(bf16)
    grad_qkv = dot_tn(a1, dqkv)
    da1_part = dot_nt(dqkv, wqkv)
    gda1 = da1_part * gain_one
    stats = lax.psum(
        jnp.stack([jnp.mean(gda1, axis=-1), jnp.mean(gda1 * n1, axis=-1)]), "section"
    )[..., None]
    da1 = sum_scatter(da1_part)
    n1q = mine(n1)
    dx = dy1q.astype(f32) + rs1 * (mine(gain_one) * da1 - stats[0] - n1q * stats[1])

    vector_grads = lax.psum_scatter(
        jnp.stack(
            [
                jnp.sum(da1 * n1q, axis=0),
                jnp.sum(da1, axis=0),
                jnp.sum(da2 * n2q, axis=0),
                jnp.sum(da2, axis=0),
            ]
        ),
        "dp",
        scatter_dimension=1,
        tiled=True,
    )
    return (
        block_out,
        dx.reshape(micro, rows, quarter),
        vector_grads[0],
        vector_grads[1],
        column_group_back(grad_qkv, 3),
        row_group_back(grad_wo),
        vector_grads[2],
        vector_grads[3],
        column_group_back(grad_up, 1),
        row_group_back(grad_down),
        grad_in[None],
        grad_out[None],
        grad_expert_gain[None],
        grad_expert_bias[None],
        grad_centroid[None],
    )


MESH = pl.DeviceIdType.MESH
KEYS = 320
CHUNK = 32


def tn(a, b):
    return lax.dot_general(a, b, (((0,), (0,)), ((), ())), preferred_element_type=f32)


def nt(a, b):
    return lax.dot_general(a, b, (((1,), (1,)), ((), ())), preferred_element_type=f32)


def tanh_parts(v):
    root = 0.7978845608028654
    t = jnp.tanh(root * (v + 0.044715 * (v * v * v)))
    return t, root


def gelu_of(v):
    t, _ = tanh_parts(v)
    return v * (0.5 * (1.0 + t))


def gelu_slope(v):
    t, root = tanh_parts(v)
    return 0.5 * (1.0 + t) + 0.5 * v * (1.0 - t * t) * root * (1.0 + 0.134145 * (v * v))


def to_rows(columns):
    lane = lax.broadcasted_iota(jnp.int32, (columns[0].shape[0], 128), 1)
    wide = jnp.zeros(lane.shape, f32)
    for i, column in enumerate(columns):
        wide = jnp.where(lane == i, column, wide)
    return wide.T[:8]


def to_columns(rows):
    return jnp.concatenate([rows, jnp.zeros((120, rows.shape[1]), f32)], axis=0).T


def layout(dims):
    S, G, M, T, D, Q, FQ, C, sh, shd = dims
    nz = G // 2
    R = G * C
    heads = HEADS // S
    return dict(
        wqkv=((S, nz, 2, sh, 3 * Q), bf16),
        wo=((nz, 2, sh, D), bf16),
        wup=((S, nz, 2, sh, FQ), bf16),
        wdn=((nz, 2, shd, D), bf16),
        win=((S, nz, 2, sh, FQ), bf16),
        wout=((nz, 2, shd, D), bf16),
        vg=((S, G, 8, 128), f32),
        vecs=((8, D), f32),
        evec=((8, D), f32),
        mask=((M, T, T), f32),
        perm=((M, R, T), bf16),
        cots=((M, R, Q), bf16),
        y2s=((M, R, Q), bf16),
        ges=((M, R, Q), bf16),
        dxs=((M, R, Q), bf16),
        ger=((M, R, Q), bf16),
        dxr=((M, R, Q), bf16),
        tst=((M, T, 128), f32),
        est=((M, R, 128), f32),
        a=((M, T, D), bf16),
        qkv=((M, T, 3 * Q), bf16),
        probs=((M, heads, T, T), f32),
        o=((M, T, Q), bf16),
        y1=((M, T, D), bf16),
        h=((M, T, FQ), f32),
        u=((M, T, FQ), bf16),
        y2q=((M, T, Q), bf16),
        xe=((M, R, D), bf16),
        dge=((M, R, D), bf16),
        en=((M, R, D), bf16),
        ue=((M, R, FQ), bf16),
        dhe=((M, R, FQ), bf16),
        dfe=((M, R, D), bf16),
        he=((R, FQ), f32),
        fes=((M, S - 1, R, Q), bf16),
        fer=((M, S - 1, R, Q), bf16),
        feo=((M, R, Q), f32),
        dns=((M, S - 1, R, Q), bf16),
        dnr=((M, S - 1, R, Q), bf16),
        dno=((M, R, Q), f32),
        ess=((M, 8, R), f32),
        esr=((M, S - 1, 8, R), f32),
        ts=((M, S - 1, T, Q), bf16),
        r1=((M, S - 1, T, Q), bf16),
        r2=((M, S - 1, T, Q), bf16),
        own=((M, T, Q), f32),
        tss=((2, M, 8, T), f32),
        tsr=((2, M, S - 1, 8, T), f32),
        dy2=((M, T, D), bf16),
        dh=((M, T, FQ), bf16),
        dqkv=((M, T, 3 * Q), bf16),
        gwo=((nz, 2, sh, D), bf16),
        gqk=((S, nz, 2, sh, 3 * Q), bf16),
        bdn=((nz, shd, D), bf16),
        bup=((S, nz, sh, FQ), bf16),
        bwo=((nz, sh, D), bf16),
        bqk=((S, nz, sh, 3 * Q), bf16),
        zdn=((nz - 1, shd, D), bf16),
        zup=((nz - 1, S, sh, FQ), bf16),
        zwo=((nz - 1, sh, D), bf16),
        zqk=((nz - 1, S, sh, 3 * Q), bf16),
        ups=((S, sh, FQ), bf16),
        upr=((S - 1, sh, FQ), bf16),
        qks=((S, sh, 3 * Q), bf16),
        qkr=((S - 1, sh, 3 * Q), bf16),
        stage=((2, 256, D), f32),
        vsum=((8, Q), f32),
        vsr=((G - 1, 8, Q), f32),
    )


INPUTS = [
    "hidden",
    "cot",
    "bucket",
    "live",
    "routes",
    "vin",
    "ein",
    "wqkv_in",
    "wo_in",
    "wup_in",
    "wdn_in",
    "win_in",
    "wout_in",
]
OUTPUTS = [
    "out",
    "dx",
    "vgo",
    "gqk_out",
    "gwo_out",
    "gup_out",
    "gdn_out",
    "gin_out",
    "gout_out",
    "evo",
]


def block_kernel(dims, names, *args):
    r = types.SimpleNamespace(**dict(zip(names, args)))
    S, G, M, T, D, Q, FQ, C, sh, shd = dims
    nz = G // 2
    R = G * C
    heads = HEADS // S
    size = D // HEADS
    scale = size ** (-0.5)
    s = lax.axis_index("section")
    d = lax.axis_index("dp")
    z = lax.div(d, 2)
    c = lax.rem(d, 2)
    beside = (s, d + 1 - 2 * c)

    def sec(i):
        return lax.rem(s + i, S)

    def dpi(j):
        return lax.rem(d + j, G)

    def zi(j):
        return lax.rem(z + j, nz)

    def to_sec(i):
        return (sec(i), d)

    def to_dp(j):
        return (s, dpi(j))

    def to_z(j):
        return (s, zi(j) * 2 + c)

    def col(q, n=Q):
        return pl.ds(pl.multiple_of(q * n, n), n)

    def seats(e):
        return pl.ds(pl.multiple_of(e * C, C), C)

    mine = col(s)
    places = {}
    pending = {}

    def copy(src, dst, k, device):
        i = places.setdefault(k, len(places))
        return pltpu.make_async_remote_copy(
            src_ref=src,
            dst_ref=dst,
            send_sem=r.ssem.at[i],
            recv_sem=r.rsem.at[i],
            device_id=device,
            device_id_type=MESH,
        )

    def send(src, dst, k, device):
        pending[k] = copy(src, dst, k, device)
        pending[k].start()

    def sent(k):
        pending.pop(k).wait_send()

    def recv(dst, k):
        copy(dst, dst, k, beside).wait_recv()

    def each(rows, step, body):
        @pl.loop(0, rows // step)
        def _(i):
            body(pl.ds(pl.multiple_of(i * step, step), step))

    others = range(1, S)

    def gather_send(ref, m, k):
        for i in others:
            send(ref.at[m, :, mine], ref.at[m, :, mine], (k, m, i), to_sec(i))

    def gather_recv(ref, m, k):
        for i in others:
            recv(ref.at[m, :, col(sec(S - i))], (k, m, i))

    def sum_send(tile, out, arrive, own, m, k, before=None, hold=False):
        for i in others:
            if before is not None:
                sent((before, m, i))
            out[m, i - 1] = tile(sec(i)).astype(bf16)
            if not hold:
                send(out.at[m, i - 1], arrive.at[m, i - 1], (k, m, i), to_sec(i))
        own[m] = tile(s)

    def sum_start(out, arrive, m, k):
        for i in others:
            send(out.at[m, i - 1], arrive.at[m, i - 1], (k, m, i), to_sec(i))

    def sum_recv(arrive, m, k):
        for i in others:
            recv(arrive.at[m, i - 1], (k, m, i))

    def summed(own, arrive, m, rows):
        total = own[m, rows]
        for i in others:
            total += arrive[m, i - 1, rows].astype(f32)
        return total

    def dispatch_send(src, dst, m, k):
        dst[m, seats(d), mine] = src[m, seats(d)]
        for j in range(1, G):
            send(src.at[m, seats(dpi(j))], dst.at[m, seats(d), mine], (k, m, j), to_dp(j))

    def dispatch_recv(dst, m, k):
        for j in range(1, G):
            recv(dst.at[m, seats(dpi(G - j)), mine], (k, m, j))

    def return_send(src, dst, m, k):
        dst[m, seats(d)] = src[m, seats(d)]
        for j in range(1, G):
            send(src.at[m, seats(dpi(j))], dst.at[m, seats(d)], (k, m, j), to_dp(j))

    def return_recv(dst, m, k):
        for j in range(1, G):
            recv(dst.at[m, seats(dpi(G - j))], (k, m, j))

    def part(ref, zz, cc):
        return ref.at[:, zz, cc] if len(ref.shape) == 5 else ref.at[zz, cc]

    def weight_start(ref, k):
        for j in range(1, nz):
            send(part(ref, z, c), part(ref, z, c), (k, "z", j), to_z(j))
        send(part(ref, z, c), part(ref, z, c), (k, "c", 0), beside)

    def weight_wait(ref, k):
        for j in range(1, nz):
            zz = zi(nz - j)
            recv(part(ref, zz, c), (k, "z", j))
            send(part(ref, zz, c), part(ref, zz, c), (k, "c", j), beside)
        for j in range(nz):
            recv(part(ref, zi(nz - j) if j else z, 1 - c), (k, "c", j))

    barrier = pltpu.get_barrier_semaphore()
    for i in others:
        pl.semaphore_signal(barrier, inc=1, device_id=to_sec(i), device_id_type=MESH)
    for j in range(1, G):
        pl.semaphore_signal(barrier, inc=1, device_id=to_dp(j), device_id_type=MESH)
    pl.semaphore_wait(barrier, S + G - 2)

    load_in = pltpu.make_async_copy(r.win_in, r.win, r.lsem.at[0])
    load_out = pltpu.make_async_copy(r.wout_in, r.wout, r.lsem.at[1])
    for i in others:
        for piece in range(3):
            src = r.wqkv_in.at[:, pl.ds(pl.multiple_of(piece * D + sec(i) * Q, Q), Q)]
            dst = r.wqkv.at[s, z, c, :, piece * Q : (piece + 1) * Q]
            send(src, dst, ("q1", piece, i), to_sec(i))
        send(r.vin, r.vg.at[s, d], ("v1", i), to_sec(i))
        send(r.ein, r.evec.at[:, mine], ("e1", i), to_sec(i))
    for i in others:
        send(r.wup_in.at[:, col(sec(i), FQ)], r.wup.at[s, z, c], ("u1", i), to_sec(i))
    load_in.start()
    load_out.start()
    for piece in range(3):
        r.wqkv[s, z, c, :, piece * Q : (piece + 1) * Q] = r.wqkv_in[
            :, pl.ds(pl.multiple_of(piece * D + s * Q, Q), Q)
        ]
    r.wup[s, z, c] = r.wup_in[:, col(s, FQ)]
    r.wo[z, c] = r.wo_in[...]
    r.wdn[z, c] = r.wdn_in[...]
    r.vg[s, d] = r.vin[...]
    r.evec[:, mine] = r.ein[...]

    early = lax.broadcasted_iota(jnp.int32, (T, T), 0)
    late = lax.broadcasted_iota(jnp.int32, (T, T), 1)
    for m in range(M):
        route = r.routes[m : m + 1, :]
        expert_ids = lax.broadcasted_iota(jnp.int32, (G, T), 0)
        picks = jnp.where(expert_ids == route, 1.0, 0.0)
        before = jnp.where(early < late, 1.0, 0.0).astype(bf16)
        counts = jnp.dot(picks.astype(bf16), before, preferred_element_type=f32)
        rank = jnp.sum(counts * picks, axis=0, keepdims=True)
        place = route.astype(f32) * float(C) + rank
        seat_ids = lax.broadcasted_iota(jnp.int32, (R, T), 0).astype(f32)
        r.perm[m] = jnp.where(seat_ids == place, 1.0, 0.0).astype(bf16)
        r.cots[m] = jnp.dot(r.perm[m], r.cot[m, :, mine], preferred_element_type=f32).astype(bf16)

    for i in others:
        for piece in range(3):
            recv(r.wqkv.at[sec(S - i), z, c, :, piece * Q : (piece + 1) * Q], ("q1", piece, i))
    weight_start(r.wqkv, "wqkv")
    for i in others:
        recv(r.vg.at[sec(S - i), d], ("v1", i))
        recv(r.evec.at[:, col(sec(S - i))], ("e1", i))
    for j in range(1, G):
        send(r.vg.at[:, d], r.vg.at[:, d], ("v2", j), to_dp(j))
    for m in range(M):
        dispatch_send(r.cots, r.dge, m, "cot")
    weight_start(r.wo, "wo")

    for m in range(M):
        end = r.bucket[m, 0]
        seg_q = (early >= end).astype(jnp.int32)
        seg_k = (late >= end).astype(jnp.int32)
        for b in range(1, r.bucket.shape[1]):
            end = end + r.bucket[m, b]
            seg_q += (early >= end).astype(jnp.int32)
            seg_k += (late >= end).astype(jnp.int32)
        live = jnp.broadcast_to(r.live[m : m + 1, :], (T, T))
        allowed = (seg_q == seg_k) & (late <= early) & ((live == 1) | (late == early))
        r.mask[m] = jnp.where(allowed, 1.0, 0.0)

    for j in range(1, G):
        recv(r.vg.at[:, dpi(G - j)], ("v2", j))
    spread_row = lax.broadcasted_iota(jnp.int32, (128, D), 0)
    spread_lane = lax.broadcasted_iota(jnp.int32, (128, D), 1)
    spread = jnp.where(lax.rem(spread_lane, sh) == spread_row, 1.0, 0.0).astype(bf16)
    stacked = r.vg[...].reshape(S * G * 8, 128).astype(bf16)
    wide = jnp.dot(stacked, spread, preferred_element_type=f32)
    row_id = lax.broadcasted_iota(jnp.int32, (S * G * 8, D), 0)
    lane_id = lax.broadcasted_iota(jnp.int32, (S * G * 8, D), 1)
    low = lax.shift_right_logical(row_id, 3) * sh
    wide = jnp.where((lane_id >= low) & (lane_id < low + sh), wide, 0.0)
    r.vecs[...] = jnp.sum(wide.reshape(S * G, 8, D), axis=0)

    def normed(values):
        mean = jnp.mean(values, axis=1, keepdims=True)
        center = values - mean
        rs = lax.rsqrt(jnp.mean(center * center, axis=1, keepdims=True) + epsilon)
        return center * rs, mean, rs

    def norm_tokens(src, m, at, keep):
        gain = r.vecs[2 * at : 2 * at + 1, :]
        bias = r.vecs[2 * at + 1 : 2 * at + 2, :]

        def body(rows):
            n, mean, rs = normed(src[m, rows].astype(f32))
            if keep:
                r.tst[m, rows, 2 * at : 2 * at + 1] = mean
                r.tst[m, rows, 2 * at + 1 : 2 * at + 2] = rs
            r.a[m, rows] = (n * gain + bias).astype(bf16)

        each(T, CHUNK, body)

    for m in range(M):
        norm_tokens(r.hidden, m, 0, True)
    for i in others:
        recv(r.wup.at[sec(S - i), z, c], ("u1", i))
    weight_start(r.wup, "wup")
    weight_wait(r.wqkv, "wqkv")
    weight_start(r.wdn, "wdn")

    def attend(m):
        @pl.loop(0, 3)
        def _(t):
            w = r.wqkv[:, :, :, :, col(t)].reshape(D, Q)
            r.qkv[m, :, col(t)] = jnp.dot(r.a[m], w, preferred_element_type=f32).astype(bf16)

        for hh in range(heads):
            at = hh * size
            q = r.qkv[m, :, at : at + size]
            k = r.qkv[m, :, Q + at : Q + at + size]
            v = r.qkv[m, :, 2 * Q + at : 2 * Q + at + size]
            scores = jnp.where(r.mask[m] > 0.0, nt(q, k) * scale, masked_value)
            weights = jnp.exp(scores - jnp.max(scores, axis=1, keepdims=True))
            p = weights / jnp.sum(weights, axis=1, keepdims=True)
            r.probs[m, hh] = p
            mixed = jnp.dot(p.astype(bf16), v, preferred_element_type=f32)
            r.o[m, :, at : at + size] = mixed.astype(bf16)

    def y1_tile(m):
        return lambda q: jnp.dot(
            r.o[m], r.wo[:, :, :, col(q)].reshape(Q, Q), preferred_element_type=f32
        )

    attend(0)
    weight_wait(r.wo, "wo")
    sum_send(y1_tile(0), r.ts, r.r1, r.own, 0, "y1")
    attend(1)
    sum_send(y1_tile(1), r.ts, r.r1, r.own, 1, "y1")
    weight_wait(r.wup, "wup")

    def finish_y1(m):
        sum_recv(r.r1, m, "y1")

        def body(rows):
            total = r.hidden[m, rows, mine].astype(f32) + summed(r.own, r.r1, m, rows)
            r.y1[m, rows, mine] = total.astype(bf16)

        each(T, 64, body)
        gather_send(r.y1, m, "y1g")

    finish_y1(0)
    finish_y1(1)
    for m in range(M):
        dispatch_recv(r.dge, m, "cot")
        gather_send(r.dge, m, "dge")

    def up(m):
        gather_recv(r.y1, m, "y1g")
        norm_tokens(r.y1, m, 1, True)

        @pl.loop(0, FQ // Q)
        def _(t):
            w = r.wup[:, :, :, :, col(t)].reshape(D, Q)
            pre = jnp.dot(r.a[m], w, preferred_element_type=f32)
            r.h[m, :, col(t)] = pre
            r.u[m, :, col(t)] = gelu_of(pre).astype(bf16)

    def y2_tile(m):
        return lambda q: jnp.dot(
            r.u[m], r.wdn[:, :, :, col(q)].reshape(FQ, Q), preferred_element_type=f32
        )

    up(0)
    weight_wait(r.wdn, "wdn")
    sum_send(y2_tile(0), r.ts, r.r2, r.own, 0, "y2", "y1")
    up(1)
    sum_send(y2_tile(1), r.ts, r.r2, r.own, 1, "y2", "y1")

    def finish_y2(m):
        sum_recv(r.r2, m, "y2")

        def body(rows):
            total = r.y1[m, rows, mine].astype(f32) + summed(r.own, r.r2, m, rows)
            r.y2q[m, rows] = total.astype(bf16)

        each(T, 64, body)
        r.y2s[m] = jnp.dot(r.perm[m], r.y2q[m], preferred_element_type=f32).astype(bf16)
        dispatch_send(r.y2s, r.xe, m, "y2d")

    finish_y2(0)
    finish_y2(1)
    for m in range(M):
        dispatch_recv(r.xe, m, "y2d")
        gather_send(r.xe, m, "xe")
    load_in.wait()
    load_out.wait()

    def expert(m):
        gather_recv(r.dge, m, "dge")
        gather_recv(r.xe, m, "xe")
        gain, bias, centroid = r.evec[0:1, :], r.evec[1:2, :], r.evec[2:3, :]

        def body(rows):
            v = r.xe[m, rows].astype(f32)
            n, mean, rs = normed(v)
            alpha = jax.nn.sigmoid(jnp.sum(v * centroid, axis=1, keepdims=True))
            r.est[m, rows, 0:1] = mean
            r.est[m, rows, 1:2] = rs
            r.est[m, rows, 2:3] = alpha
            r.en[m, rows] = (n * gain + bias).astype(bf16)
            r.dfe[m, rows] = (alpha * r.dge[m, rows].astype(f32)).astype(bf16)

        each(R, CHUNK, body)

        @pl.loop(0, FQ // Q)
        def _(t):
            w = r.win[:, :, :, :, col(t)].reshape(D, Q)
            pre = jnp.dot(r.en[m], w, preferred_element_type=f32)
            r.ue[m, :, col(t)] = gelu_of(pre).astype(bf16)
            due = nt(r.dfe[m], r.wout[t].reshape(Q, D))
            r.dhe[m, :, col(t)] = (due * gelu_slope(pre)).astype(bf16)

        stats = [jnp.zeros((R, 1), f32) for _ in range(3)]

        def fe_tile(q):
            tile = jnp.dot(
                r.ue[m], r.wout[:, :, :, col(q)].reshape(FQ, Q), preferred_element_type=f32
            )
            stats[2] += jnp.sum(tile * r.dge[m, :, col(q)].astype(f32), axis=1, keepdims=True)
            return tile

        def den_tile(q):
            tile = nt(r.dhe[m], r.win[q].reshape(Q, FQ))
            scaled = tile * r.evec[0:1, col(q)]
            n = (r.xe[m, :, col(q)].astype(f32) - r.est[m, :, 0:1]) * r.est[m, :, 1:2]
            stats[0] += jnp.sum(scaled, axis=1, keepdims=True)
            stats[1] += jnp.sum(scaled * n, axis=1, keepdims=True)
            return tile

        sum_send(fe_tile, r.fes, r.fer, r.feo, m, "fe", hold=True)
        sum_send(den_tile, r.dns, r.dnr, r.dno, m, "den")
        r.ess[m] = to_rows(stats)
        for i in others:
            send(r.ess.at[m], r.esr.at[m, i - 1], ("est", m, i), to_sec(i))

    expert(0)
    expert(1)

    def finish_den(m):
        sum_recv(r.dnr, m, "den")
        total = r.ess[m]
        for i in others:
            recv(r.esr.at[m, i - 1], ("est", m, i))
            total += r.esr[m, i - 1]
        r.est[m, :, 8:16] = to_columns(total)[:, 0:8]
        gain, centroid = r.evec[0:1, mine], r.evec[2:3, mine]
        if m == 0:
            r.evo[...] = jnp.zeros_like(r.evo)

        def body(rows):
            den = summed(r.dno, r.dnr, m, rows)
            xq = r.xe[m, rows, mine].astype(f32)
            rs, alpha = r.est[m, rows, 1:2], r.est[m, rows, 2:3]
            n = (xq - r.est[m, rows, 0:1]) * rs
            m1, m2 = r.est[m, rows, 8:9] * (1.0 / D), r.est[m, rows, 9:10] * (1.0 / D)
            dlogit = r.est[m, rows, 10:11] * alpha * (1.0 - alpha)
            grad = rs * (gain * den - m1 - n * m2) + dlogit * centroid
            r.dxs[m, rows] = grad.astype(bf16)
            r.evo[0:1, :] += jnp.sum(den * n, axis=0, keepdims=True)
            r.evo[1:2, :] += jnp.sum(den, axis=0, keepdims=True)
            r.evo[2:3, :] += jnp.sum(dlogit * xq, axis=0, keepdims=True)

        each(R, 64 if R % 64 == 0 else CHUNK, body)
        return_send(r.dxs, r.dxr, m, "dxb")

    finish_den(0)
    finish_den(1)
    for m in range(M):
        sum_start(r.fes, r.fer, m, "fe")

    writes = []
    for left, right, out in ((r.en, r.dhe, r.gin_out), (r.ue, r.dfe, r.gout_out)):
        for t in range(D // 256):
            slot = len(writes) % 2
            if len(writes) >= 2:
                writes[-2].wait()
            rows = slice(t * 256, (t + 1) * 256)
            lhs = left[:, :, rows].reshape(M * R, 256)
            r.stage[slot] = tn(lhs, right[...].reshape(M * R, D))
            writes.append(pltpu.make_async_copy(r.stage.at[slot], out.at[rows], r.lsem.at[2 + slot]))
            writes[-1].start()

    def finish_dxe(m):
        return_recv(r.dxr, m, "dxb")
        back = tn(r.perm[m], r.dxr[m])
        r.dy2[m, :, mine] = (r.cot[m, :, mine].astype(f32) + back).astype(bf16)
        gather_send(r.dy2, m, "dy2")

    finish_dxe(0)
    finish_dxe(1)

    def token_stats(m, at, src):
        stats = [jnp.zeros((T, 1), f32) for _ in range(2)]

        def add(q, tile):
            scaled = tile * r.vecs[2 * at : 2 * at + 1, col(q)]
            mean, rs = r.tst[m, :, 2 * at : 2 * at + 1], r.tst[m, :, 2 * at + 1 : 2 * at + 2]
            n = (src[m, :, col(q)].astype(f32) - mean) * rs
            stats[0] += jnp.sum(scaled, axis=1, keepdims=True)
            stats[1] += jnp.sum(scaled * n, axis=1, keepdims=True)
            return tile

        return stats, add

    def stats_send(m, at, stats):
        r.tss[at, m] = to_rows(stats)
        for i in others:
            send(r.tss.at[at, m], r.tsr.at[at, m, i - 1], ("tst", at, m, i), to_sec(i))

    def stats_recv(m, at):
        total = r.tss[at, m]
        for i in others:
            recv(r.tsr.at[at, m, i - 1], ("tst", at, m, i))
            total += r.tsr[at, m, i - 1]
        r.tst[m, :, 8:16] = to_columns(total)[:, 0:8]

    def dense_back(m):
        gather_recv(r.dy2, m, "dy2")

        @pl.loop(0, FQ // Q)
        def _(t):
            du = nt(r.dy2[m], r.wdn[t].reshape(Q, D))
            r.dh[m, :, col(t)] = (du * gelu_slope(r.h[m, :, col(t)])).astype(bf16)

        stats, add = token_stats(m, 1, r.y1)
        sum_send(
            lambda q: add(q, nt(r.dh[m], r.wup[q].reshape(Q, FQ))),
            r.ts,
            r.r1,
            r.own,
            m,
            "da2",
            "y2",
        )
        stats_send(m, 1, stats)

    def norm_back(m, at, src, grad_in, own, arrive, emit):
        gain = r.vecs[2 * at : 2 * at + 1, mine]

        def body(rows):
            grad = summed(own, arrive, m, rows)
            mean, rs = r.tst[m, rows, 2 * at : 2 * at + 1], r.tst[m, rows, 2 * at + 1 : 2 * at + 2]
            n = (src[m, rows, mine].astype(f32) - mean) * rs
            m1, m2 = r.tst[m, rows, 8:9] * (1.0 / D), r.tst[m, rows, 9:10] * (1.0 / D)
            emit(rows, grad_in[m, rows, mine].astype(f32) + rs * (gain * grad - m1 - n * m2))
            r.vsum[2 * at : 2 * at + 1, :] += jnp.sum(grad * n, axis=0, keepdims=True)
            r.vsum[2 * at + 1 : 2 * at + 2, :] += jnp.sum(grad, axis=0, keepdims=True)

        each(T, 64, body)

    def finish_da2(m):
        sum_recv(r.r1, m, "da2")
        stats_recv(m, 1)
        for i in others:
            sent(("y1g", m, i))

        def emit(rows, value):
            r.y1[m, rows, mine] = value.astype(bf16)

        norm_back(m, 1, r.y1, r.dy2, r.own, r.r1, emit)
        gather_send(r.y1, m, "dy1")

    def grads_pair(g, b, k):
        src = g.at[:, :, 1 - c] if len(g.shape) == 5 else g.at[:, 1 - c]
        send(src, b, (k, "p"), beside)

    def grads_spread(g, b, arrive, k):
        recv(b, (k, "p"))
        if len(g.shape) == 5:

            @pl.loop(0, nz)
            def _(zz):
                for q in range(S):
                    g[q, zz, c] = (g[q, zz, c].astype(f32) + b[q, zz].astype(f32)).astype(bf16)
        else:

            @pl.loop(0, nz)
            def _(zz):
                g[zz, c] = (g[zz, c].astype(f32) + b[zz].astype(f32)).astype(bf16)

        for j in range(1, nz):
            send(part(g, zi(j), c), arrive.at[j - 1], (k, "g", j), to_z(j))

    def grads_recv(arrive, k):
        for j in range(1, nz):
            recv(arrive.at[j - 1], (k, "g", j))

    dense_back(0)
    dense_back(1)

    @pl.loop(0, nz)
    def _(t):
        lhs = r.u[:, :, col(t)].reshape(M * T, Q)
        grad = tn(lhs, r.dy2[...].reshape(M * T, D))
        r.wout[t] = grad.astype(bf16).reshape(2, shd, D)

    grads_pair(r.wout, r.bdn, "gdn")

    r.vsum[...] = jnp.zeros_like(r.vsum)
    finish_da2(0)
    finish_da2(1)

    @pl.loop(0, S)
    def _(t):
        lhs = r.a[:, :, col(t)].reshape(M * T, Q)
        grad = tn(lhs, r.dh[...].reshape(M * T, FQ))
        r.win[t] = grad.astype(bf16).reshape(nz, 2, sh, FQ)

    grads_pair(r.win, r.bup, "gup")
    grads_spread(r.wout, r.bdn, r.zdn, "gdn")

    def finish_fe(m):
        sum_recv(r.fer, m, "fe")

        def body(rows):
            fe = summed(r.feo, r.fer, m, rows)
            r.ges[m, rows] = (r.est[m, rows, 2:3] * fe).astype(bf16)

        each(R, 64 if R % 64 == 0 else CHUNK, body)
        return_send(r.ges, r.ger, m, "geb")

    for m in range(M):
        norm_tokens(r.hidden, m, 0, False)
        finish_fe(m)

    def attend_back(m):
        gather_recv(r.y1, m, "dy1")
        out_grad = nt(r.y1[m], r.wo[...].reshape(Q, D)).astype(bf16)
        for hh in range(heads):
            at = hh * size
            q = r.qkv[m, :, at : at + size]
            k = r.qkv[m, :, Q + at : Q + at + size]
            v = r.qkv[m, :, 2 * Q + at : 2 * Q + at + size]
            go = out_grad[:, at : at + size]
            p = r.probs[m, hh]
            dp = nt(go, v)
            dv = tn(p.astype(bf16), go)
            ds = (p * (dp - jnp.sum(p * dp, axis=1, keepdims=True))).astype(bf16)
            dq = jnp.dot(ds, k, preferred_element_type=f32) * scale
            dk = tn(ds, q) * scale
            r.dqkv[m, :, at : at + size] = dq.astype(bf16)
            r.dqkv[m, :, Q + at : Q + at + size] = dk.astype(bf16)
            r.dqkv[m, :, 2 * Q + at : 2 * Q + at + size] = dv.astype(bf16)
        stats, add = token_stats(m, 0, r.hidden)
        sum_send(
            lambda q: add(q, nt(r.dqkv[m], r.wqkv[q].reshape(Q, 3 * Q))),
            r.ts,
            r.r2,
            r.own,
            m,
            "da1",
            "da2",
        )
        stats_send(m, 0, stats)

    attend_back(0)
    attend_back(1)

    @pl.loop(0, S)
    def _(t):
        lhs = r.a[:, :, col(t)].reshape(M * T, Q)
        grad = tn(lhs, r.dqkv[...].reshape(M * T, 3 * Q))
        r.gqk[t] = grad.astype(bf16).reshape(nz, 2, sh, 3 * Q)

    grads_pair(r.gqk, r.bqk, "gqk")
    grad = tn(r.o[...].reshape(M * T, Q), r.y1[...].reshape(M * T, D))
    r.gwo[...] = grad.astype(bf16).reshape(nz, 2, sh, D)
    grads_pair(r.gwo, r.bwo, "gwo")
    grads_spread(r.win, r.bup, r.zup, "gup")
    grads_spread(r.gqk, r.bqk, r.zqk, "gqk")
    grads_spread(r.gwo, r.bwo, r.zwo, "gwo")

    def finish_da1(m):
        sum_recv(r.r2, m, "da1")
        stats_recv(m, 0)

        def emit(rows, value):
            r.dx[m, rows] = value

        norm_back(m, 0, r.hidden, r.y1, r.own, r.r2, emit)

    finish_da1(0)
    finish_da1(1)
    for j in range(1, G):
        send(r.vsum, r.vsr.at[j - 1], ("vs", j), to_dp(j))

    for m in range(M):
        return_recv(r.ger, m, "geb")
        back = tn(r.perm[m], r.ger[m])
        r.out[m] = (r.y2q[m].astype(f32) + back).astype(bf16)

    def row_result(g, arrive, out, k, rows):
        grads_recv(arrive, k)
        mine_part = part(g, z, c)

        def body(at):
            total = mine_part[at].astype(f32)
            for j in range(1, nz):
                total += arrive[j - 1, at].astype(f32)
            out[at] = total

        each(rows, CHUNK, body)

    def column_send(g, arrive, out, back, k):
        grads_recv(arrive, k)

        @pl.loop(0, S)
        def _(q):
            total = g[q, z, c].astype(f32)
            for j in range(1, nz):
                total += arrive[j - 1, q].astype(f32)
            out[q] = total.astype(bf16)

        for i in others:
            send(out.at[sec(i)], back.at[i - 1], (k, "s", i), to_sec(i))

    def column_result(sums, back, out, pieces, k):
        width = sums.shape[2] // pieces
        for i in range(S):
            if i:
                recv(back.at[i - 1], (k, "s", i))
            q = sec(S - i) if i else s
            value = (back[i - 1] if i else sums[s]).astype(f32)
            for piece in range(pieces):
                at = pl.ds(pl.multiple_of(piece * S * width + q * width, width), width)
                out[:, at] = value[:, piece * width : (piece + 1) * width]

    row_result(r.wout, r.zdn, r.gdn_out, "gdn", shd)
    column_send(r.win, r.zup, r.ups, r.upr, "gup")
    column_send(r.gqk, r.zqk, r.qks, r.qkr, "gqk")
    row_result(r.gwo, r.zwo, r.gwo_out, "gwo", sh)
    total = r.vsum[...]
    for j in range(1, G):
        recv(r.vsr.at[j - 1], ("vs", j))
        total += r.vsr[j - 1]
    r.vgo[...] = total
    column_result(r.ups, r.upr, r.gup_out, 1, "gup")
    column_result(r.qks, r.qkr, r.gqk_out, 3, "gqk")
    for write in writes[-2:]:
        write.wait()
    for k in list(pending):
        sent(k)
    assert len(places) <= KEYS, len(places)


def with_kernel(
    hidden_in,
    cotangent,
    bucket_len,
    live_mask,
    routes,
    ln1_gain,
    ln1_bias,
    w_qkv,
    w_attn_out,
    ln2_gain,
    ln2_bias,
    w_up,
    w_down,
    expert_in,
    expert_out,
    expert_gain,
    expert_bias,
    centroids,
):
    S = lax.axis_size("section")
    G = lax.axis_size("dp")
    M, T, D = hidden_in.shape
    Q = D // S
    FQ = w_up.shape[1] // S
    C = 3 * T // (2 * G)
    sh, shd = w_up.shape[0], w_down.shape[0]
    dims = (S, G, M, T, D, Q, FQ, C, sh, shd)
    vin = jnp.stack([ln1_gain, ln1_bias, ln2_gain, ln2_bias]).astype(f32)
    vin = jnp.pad(vin, ((0, 4), (0, 128 - sh)))
    ein = jnp.concatenate([expert_gain, expert_bias, centroids]).astype(f32)
    ein = jnp.pad(ein, ((0, 5), (0, 0)))
    scratch = layout(dims)
    names = INPUTS + OUTPUTS + list(scratch) + ["ssem", "rsem", "lsem"]
    vmem = pl.BlockSpec(memory_space=pltpu.VMEM)
    smem = pl.BlockSpec(memory_space=pltpu.SMEM)
    anywhere = pl.BlockSpec(memory_space=pl.ANY)
    shapes = (
        ((M, T, Q), bf16),
        ((M, T, Q), f32),
        ((8, Q), f32),
        ((sh, 3 * D), f32),
        ((sh, D), f32),
        ((sh, S * FQ), f32),
        ((shd, D), f32),
        ((D, FQ), f32),
        ((FQ, D), f32),
        ((8, Q), f32),
    )
    outs = pl.pallas_call(
        functools.partial(block_kernel, dims, names),
        name="block",
        out_shape=[jax.ShapeDtypeStruct(*shape) for shape in shapes],
        in_specs=[vmem, vmem, smem] + [vmem] * 8 + [anywhere] * 2,
        out_specs=[vmem] * 7 + [anywhere] * 2 + [vmem],
        scratch_shapes=[pltpu.VMEM(*shape) for shape in scratch.values()]
        + [pltpu.SemaphoreType.DMA((KEYS,))] * 2
        + [pltpu.SemaphoreType.DMA((4,))],
        compiler_params=pltpu.CompilerParams(
            collective_id=0, has_side_effects=True, vmem_limit_bytes=63 << 20
        ),
    )(
        hidden_in,
        cotangent,
        bucket_len[:, 0, :],
        live_mask,
        routes[:, :, 0],
        vin,
        ein,
        w_qkv,
        w_attn_out,
        w_up,
        w_down,
        expert_in.reshape(S, G // 2, 2, sh, FQ),
        expert_out.reshape(G // 2, 2, shd, D),
    )
    out, dx, vectors, gqkv, gwo, gup, gdn, gin, gout, evectors = outs
    vectors = lax.dynamic_slice_in_dim(vectors, lax.axis_index("dp") * sh, sh, 1)
    return (
        out,
        dx,
        vectors[0],
        vectors[1],
        gqkv,
        gwo,
        vectors[2],
        vectors[3],
        gup,
        gdn,
        gin[None],
        gout[None],
        evectors[0:1],
        evectors[1:2],
        evectors[2:3],
    )


def on_device(*args):
    groups = lax.axis_size("dp")
    rows, shard = args[0].shape[1], args[11].shape[0]
    capacity = 3 * rows // (2 * groups)
    if capacity % 16 or shard % 16:
        return with_collectives(*args)
    return with_kernel(*args)


def solution(mesh):
    everywhere = ("section", "dp")
    tokens = P(None, "dp", None)
    outs = P(None, "dp", "section")
    per_expert = P("dp", "section")
    return jax.shard_map(
        on_device,
        mesh=mesh,
        in_specs=(
            tokens,
            tokens,
            tokens,
            P(None, "dp"),
            tokens,
            P(everywhere),
            P(everywhere),
            P(everywhere, None),
            P(everywhere, None),
            P(everywhere),
            P(everywhere),
            P(everywhere, None),
            P(everywhere, None),
            P("dp", None, "section"),
            P("dp", "section", None),
            per_expert,
            per_expert,
            per_expert,
        ),
        out_specs=(
            outs,
            outs,
            P(everywhere),
            P(everywhere),
            P(everywhere, None),
            P(everywhere, None),
            P(everywhere),
            P(everywhere),
            P(everywhere, None),
            P(everywhere, None),
            P("dp", None, "section"),
            P("dp", "section", None),
            per_expert,
            per_expert,
            per_expert,
        ),
        check_vma=False,
    )
```

```python
import functools
import types

import jax
import jax.numpy as jnp
from jax import lax
from jax.experimental import pallas as pl
from jax.experimental.pallas import tpu as pltpu
from jax.sharding import PartitionSpec as P

HEADS = 16
epsilon = 1e-05
masked_value = -1e30
f32 = jnp.float32
bf16 = jnp.bfloat16


def norm_parts(values):
    center = values - jnp.mean(values, axis=-1, keepdims=True)
    spread = jnp.mean(center * center, axis=-1, keepdims=True)
    rs = lax.rsqrt(spread + epsilon)
    return center * rs, rs


def gelu_back(pre, grad):
    outputs, pullback = jax.vjp(jax.nn.gelu, pre)
    return pullback(grad)[0]


def dot(a, b):
    return jnp.dot(a, b, preferred_element_type=f32)


def dot_tn(a, b):
    return jnp.einsum("rd,re->de", a, b, preferred_element_type=f32)


def dot_nt(a, b):
    return jnp.einsum("re,de->rd", a, b, preferred_element_type=f32)


def sum_scatter(part):
    return lax.psum_scatter(
        part.astype(bf16), "section", scatter_dimension=part.ndim - 1, tiled=True
    ).astype(f32)


def gather_features(part):
    return lax.all_gather(part, "section", axis=part.ndim - 1, tiled=True)


def with_collectives(
    hidden_in,
    cotangent,
    bucket_len,
    live_mask,
    routes,
    ln1_gain,
    ln1_bias,
    w_qkv,
    w_attn_out,
    ln2_gain,
    ln2_bias,
    w_up,
    w_down,
    expert_in,
    expert_out,
    expert_gain,
    expert_bias,
    centroids,
):
    sections = lax.axis_size("section")
    groups = lax.axis_size("dp")
    section = lax.axis_index("section")
    micro, rows, width = hidden_in.shape
    quarter = width // sections
    heads = HEADS // sections
    size = width // HEADS
    ff = w_up.shape[1] // sections
    capacity = 3 * rows // (2 * groups)
    shard = w_up.shape[0]
    own_cols = section * quarter

    def mine(values):
        return lax.dynamic_slice_in_dim(values, own_cols, quarter, values.ndim - 1)

    def column_group(weight, pieces):
        cols = weight.shape[1] // (pieces * sections)
        parts = weight.reshape(shard, pieces, sections, cols).transpose(2, 0, 1, 3)
        parts = parts.reshape(sections, shard, pieces * cols)
        parts = lax.all_to_all(parts, "section", split_axis=0, concat_axis=0, tiled=True)
        full = lax.all_gather(parts, "dp", axis=1, tiled=True)
        return full.reshape(width, pieces * cols)

    def column_group_back(grad, pieces):
        cols = grad.shape[1] // pieces
        parts = grad.astype(bf16).reshape(sections, groups * shard, pieces * cols)
        parts = lax.psum_scatter(parts, "dp", scatter_dimension=1, tiled=True)
        parts = lax.all_to_all(parts, "section", split_axis=0, concat_axis=0, tiled=True)
        parts = parts.reshape(sections, shard, pieces, cols).transpose(1, 2, 0, 3)
        return parts.reshape(shard, pieces * sections * cols).astype(f32)

    def row_group_back(grad):
        return lax.psum_scatter(
            grad.astype(bf16), "dp", scatter_dimension=0, tiled=True
        ).astype(f32)

    vectors = lax.all_gather(
        jnp.stack([ln1_gain, ln1_bias, ln2_gain, ln2_bias]), ("section", "dp"), axis=1, tiled=True
    ).astype(f32)
    gain_one, bias_one, gain_two, bias_two = vectors
    expert_vectors = lax.all_gather(
        jnp.concatenate([expert_gain, expert_bias, centroids]), "section", axis=1, tiled=True
    ).astype(f32)
    expert_g, expert_b, centroid = expert_vectors
    wqkv = column_group(w_qkv, 3)
    wo = lax.all_gather(w_attn_out, "dp", axis=0, tiled=True)
    wup = column_group(w_up, 1)
    wdown = lax.all_gather(w_down, "dp", axis=0, tiled=True)
    win = expert_in[0]
    wout = expert_out[0]

    ends = jnp.cumsum(bucket_len[:, 0, :], axis=-1)
    slot_ids = jnp.arange(rows, dtype=jnp.int32)
    segments = jnp.sum((slot_ids[None, :, None] >= ends[:, None, :]).astype(jnp.int32), axis=-1)
    same = segments[:, :, None] == segments[:, None, :]
    causal = slot_ids[None, None, :] <= slot_ids[None, :, None]
    opened = (live_mask[:, None, :] == 1) | (slot_ids[None, None, :] == slot_ids[None, :, None])
    allowed = (same & causal & opened)[:, None]
    chosen = routes[:, :, 0]
    picks = (chosen[:, :, None] == jnp.arange(groups, dtype=jnp.int32)).astype(jnp.int32)
    ranks = jnp.sum((jnp.cumsum(picks, axis=1) - picks) * picks, axis=2)
    places = chosen * capacity + ranks
    place_ids = jnp.arange(groups * capacity, dtype=jnp.int32)
    picked = (places[:, None, :] == place_ids[None, :, None]).astype(bf16)

    def dispatch(values):
        out = jnp.einsum("mpt,mtf->pmf", picked, values, preferred_element_type=f32).astype(bf16)
        out = out.reshape(groups, capacity * micro, quarter)
        return lax.all_to_all(out, "dp", split_axis=0, concat_axis=0, tiled=True)

    def give_back(values):
        out = lax.all_to_all(values, "dp", split_axis=0, concat_axis=0, tiled=True)
        out = out.reshape(groups * capacity, micro, quarter)
        return jnp.einsum("mpt,pmf->mtf", picked, out, preferred_element_type=f32)

    dge = gather_features(dispatch(mine(cotangent))).reshape(-1, width).astype(f32)

    x = hidden_in.reshape(micro * rows, width).astype(f32)
    n1, rs1 = norm_parts(x)
    a1 = (n1 * gain_one + bias_one).astype(bf16)
    qkv = dot(a1, wqkv).astype(bf16)
    q, k, v = (
        qkv[:, i * quarter : (i + 1) * quarter].reshape(micro, rows, heads, size) for i in range(3)
    )
    scale = size ** (-0.5)
    raw = jnp.einsum("mqhd,mkhd->mhqk", q, k, preferred_element_type=f32) * scale
    scores = jnp.where(allowed, raw, masked_value)
    weights = jnp.exp(scores - jnp.max(scores, axis=-1, keepdims=True))
    probs = weights / jnp.sum(weights, axis=-1, keepdims=True)
    probs_low = probs.astype(bf16)
    mixed = jnp.einsum("mhqk,mkhd->mqhd", probs_low, v, preferred_element_type=f32)
    o = mixed.reshape(micro * rows, quarter).astype(bf16)
    y1q = (mine(x) + sum_scatter(dot(o, wo))).astype(bf16)
    y1 = gather_features(y1q).astype(f32)
    n2, rs2 = norm_parts(y1)
    a2 = (n2 * gain_two + bias_two).astype(bf16)
    h = dot(a2, wup)
    u = jax.nn.gelu(h).astype(bf16)
    y2q = (y1q.astype(f32) + sum_scatter(dot(u, wdown))).astype(bf16)

    xe = gather_features(dispatch(y2q.reshape(micro, rows, quarter))).reshape(-1, width)
    xe = xe.astype(f32)
    ne, rse = norm_parts(xe)
    en = (ne * expert_g + expert_b).astype(bf16)
    he = dot(en, win)
    ue = jax.nn.gelu(he).astype(bf16)
    fe_part = dot(ue, wout)
    alpha = jax.nn.sigmoid(jnp.sum(xe * centroid, axis=-1, keepdims=True))
    fe = sum_scatter(fe_part)
    ge = (alpha * fe).astype(bf16).reshape(groups, capacity * micro, quarter)
    block_out = (
        y2q.reshape(micro, rows, quarter).astype(f32) + give_back(ge)
    ).astype(bf16)

    dfe = (alpha * dge).astype(bf16)
    due = dot_nt(dfe, wout)
    grad_out = dot_tn(ue, dfe)
    dhe = gelu_back(he, due).astype(bf16)
    grad_in = dot_tn(en, dhe)
    den_part = dot_nt(dhe, win)
    gden = den_part * expert_g
    stats = lax.psum(
        jnp.stack(
            [
                jnp.mean(gden, axis=-1),
                jnp.mean(gden * ne, axis=-1),
                jnp.sum(dge * fe_part, axis=-1),
            ]
        ),
        "section",
    )[..., None]
    den = sum_scatter(den_part)
    neq = mine(ne)
    dlogit = stats[2] * alpha * (1.0 - alpha)
    dxe_ln = rse * (mine(expert_g) * den - stats[0] - neq * stats[1])
    dxe = (dxe_ln + dlogit * mine(centroid)).astype(bf16)
    grad_expert_gain = jnp.sum(den * neq, axis=0)
    grad_expert_bias = jnp.sum(den, axis=0)
    grad_centroid = jnp.sum(dlogit * mine(xe), axis=0)
    back = give_back(dxe.reshape(groups, capacity * micro, quarter))
    dy2q = (mine(cotangent).astype(f32) + back).astype(bf16).reshape(micro * rows, quarter)

    dy2 = gather_features(dy2q)
    grad_down = dot_tn(u, dy2)
    dh = gelu_back(h, dot_nt(dy2, wdown)).astype(bf16)
    grad_up = dot_tn(a2, dh)
    da2_part = dot_nt(dh, wup)
    gda2 = da2_part * gain_two
    stats = lax.psum(
        jnp.stack([jnp.mean(gda2, axis=-1), jnp.mean(gda2 * n2, axis=-1)]), "section"
    )[..., None]
    da2 = sum_scatter(da2_part)
    n2q = mine(n2)
    dy1q = dy2q.astype(f32) + rs2 * (mine(gain_two) * da2 - stats[0] - n2q * stats[1])
    dy1q = dy1q.astype(bf16)
    dy1 = gather_features(dy1q)
    grad_wo = dot_tn(o, dy1)
    do = dot_nt(dy1, wo).astype(bf16).reshape(micro, rows, heads, size)
    dp = jnp.einsum("mqhd,mkhd->mhqk", do, v, preferred_element_type=f32)
    dv = jnp.einsum("mhqk,mqhd->mkhd", probs_low, do, preferred_element_type=f32)
    delta = jnp.sum(probs * dp, axis=-1, keepdims=True)
    ds = (probs * (dp - delta)).astype(bf16)
    dq = jnp.einsum("mhqk,mkhd->mqhd", ds, k, preferred_element_type=f32) * scale
    dk = jnp.einsum("mhqk,mqhd->mkhd", ds, q, preferred_element_type=f32) * scale
    dqkv = jnp.concatenate(
        [part.reshape(micro * rows, quarter) for part in (dq, dk, dv)], axis=1
    ).astype(bf16)
    grad_qkv = dot_tn(a1, dqkv)
    da1_part = dot_nt(dqkv, wqkv)
    gda1 = da1_part * gain_one
    stats = lax.psum(
        jnp.stack([jnp.mean(gda1, axis=-1), jnp.mean(gda1 * n1, axis=-1)]), "section"
    )[..., None]
    da1 = sum_scatter(da1_part)
    n1q = mine(n1)
    dx = dy1q.astype(f32) + rs1 * (mine(gain_one) * da1 - stats[0] - n1q * stats[1])

    vector_grads = lax.psum_scatter(
        jnp.stack(
            [
                jnp.sum(da1 * n1q, axis=0),
                jnp.sum(da1, axis=0),
                jnp.sum(da2 * n2q, axis=0),
                jnp.sum(da2, axis=0),
            ]
        ),
        "dp",
        scatter_dimension=1,
        tiled=True,
    )
    return (
        block_out,
        dx.reshape(micro, rows, quarter),
        vector_grads[0],
        vector_grads[1],
        column_group_back(grad_qkv, 3),
        row_group_back(grad_wo),
        vector_grads[2],
        vector_grads[3],
        column_group_back(grad_up, 1),
        row_group_back(grad_down),
        grad_in[None],
        grad_out[None],
        grad_expert_gain[None],
        grad_expert_bias[None],
        grad_centroid[None],
    )


MESH = pl.DeviceIdType.MESH
KEYS = 320
CHUNK = 32


def tn(a, b):
    return lax.dot_general(a, b, (((0,), (0,)), ((), ())), preferred_element_type=f32)


def nt(a, b):
    return lax.dot_general(a, b, (((1,), (1,)), ((), ())), preferred_element_type=f32)


def tanh_parts(v):
    root = 0.7978845608028654
    t = jnp.tanh(root * (v + 0.044715 * (v * v * v)))
    return t, root


def gelu_both(v):
    t, root = tanh_parts(v)
    half = 0.5 * (1.0 + t)
    return v * half, half + 0.5 * v * (1.0 - t * t) * root * (1.0 + 0.134145 * (v * v))


def to_rows(columns):
    lane = lax.broadcasted_iota(jnp.int32, (columns[0].shape[0], 128), 1)
    wide = jnp.zeros(lane.shape, f32)
    for i, column in enumerate(columns):
        wide = jnp.where(lane == i, column, wide)
    return wide.T[:8]


def to_columns(rows):
    return jnp.concatenate([rows, jnp.zeros((120, rows.shape[1]), f32)], axis=0).T


def layout(dims):
    S, G, M, T, D, Q, FQ, C, sh, shd = dims
    nz = G // 2
    R = G * C
    heads = HEADS // S
    return dict(
        wqkv=((S, nz, 2, sh, 3 * Q), bf16),
        wo=((nz, 2, sh, D), bf16),
        wup=((S, nz, 2, sh, FQ), bf16),
        wdn=((nz, 2, shd, D), bf16),
        win=((S, nz, 2, sh, FQ), bf16),
        wout=((nz, 2, shd, D), bf16),
        vg=((S, G, 8, 128), f32),
        vecs=((8, D), f32),
        evec=((8, D), f32),
        mask=((M, T, T), f32),
        perm=((M, R, T), bf16),
        cots=((M, R, Q), bf16),
        y2s=((M, R, Q), bf16),
        ges=((M, R, Q), bf16),
        dxs=((M, R, Q), bf16),
        ger=((M, R, Q), bf16),
        dxr=((M, R, Q), bf16),
        tst=((M, T, 128), f32),
        est=((M, R, 128), f32),
        a=((M, T, D), bf16),
        qkv=((M, T, 3 * Q), bf16),
        probs=((M, heads, T, T), f32),
        o=((M, T, Q), bf16),
        y1=((M, T, D), bf16),
        h=((M, T, FQ), f32),
        u=((M, T, FQ), bf16),
        y2q=((M, T, Q), bf16),
        xe=((M, R, D), bf16),
        dge=((M, R, D), bf16),
        en=((M, R, D), bf16),
        ue=((M, R, FQ), bf16),
        dhe=((M, R, FQ), bf16),
        dfe=((M, R, D), bf16),
        slope=((R, FQ), f32),
        fes=((M, S - 1, R, Q), bf16),
        fer=((M, S - 1, R, Q), bf16),
        feo=((M, R, Q), f32),
        dns=((M, S - 1, R, Q), bf16),
        dnr=((M, S - 1, R, Q), bf16),
        dno=((M, R, Q), f32),
        ess=((M, 8, R), f32),
        esr=((M, S - 1, 8, R), f32),
        ts=((M, S - 1, T, Q), bf16),
        r1=((M, S - 1, T, Q), bf16),
        r2=((M, S - 1, T, Q), bf16),
        own=((M, T, Q), f32),
        tss=((2, M, 8, T), f32),
        tsr=((2, M, S - 1, 8, T), f32),
        dy2=((M, T, D), bf16),
        dh=((M, T, FQ), bf16),
        dqkv=((M, T, 3 * Q), bf16),
        gwo=((nz, 2, sh, D), bf16),
        gqk=((S, nz, 2, sh, 3 * Q), bf16),
        bdn=((nz, shd, D), bf16),
        bup=((S, nz, sh, FQ), bf16),
        bwo=((nz, sh, D), bf16),
        bqk=((S, nz, sh, 3 * Q), bf16),
        zdn=((nz - 1, shd, D), bf16),
        zup=((nz - 1, S, sh, FQ), bf16),
        zwo=((nz - 1, sh, D), bf16),
        zqk=((nz - 1, S, sh, 3 * Q), bf16),
        ups=((S, sh, FQ), bf16),
        upr=((S - 1, sh, FQ), bf16),
        qks=((S, sh, 3 * Q), bf16),
        qkr=((S - 1, sh, 3 * Q), bf16),
        stage=((2, 256, D), f32),
        vsum=((8, Q), f32),
        vsr=((G - 1, 8, Q), f32),
    )


INPUTS = [
    "hidden",
    "cot",
    "bucket",
    "live",
    "routes",
    "vin",
    "ein",
    "wqkv_in",
    "wo_in",
    "wup_in",
    "wdn_in",
    "win_in",
    "wout_in",
]
OUTPUTS = [
    "out",
    "dx",
    "vgo",
    "gqk_out",
    "gwo_out",
    "gup_out",
    "gdn_out",
    "gin_out",
    "gout_out",
    "evo",
]


def block_kernel(dims, names, *args):
    r = types.SimpleNamespace(**dict(zip(names, args)))
    S, G, M, T, D, Q, FQ, C, sh, shd = dims
    nz = G // 2
    R = G * C
    heads = HEADS // S
    size = D // HEADS
    scale = size ** (-0.5)
    s = lax.axis_index("section")
    d = lax.axis_index("dp")
    z = lax.div(d, 2)
    c = lax.rem(d, 2)
    beside = (s, d + 1 - 2 * c)
    near = z + 1 - 2 * lax.rem(z, 2)
    far = lax.rem(z + 2, nz)
    near_far = lax.rem(near + 2, nz)

    def sec(i):
        return lax.rem(s + i, S)

    def dpi(j):
        return lax.rem(d + j, G)

    def zi(j):
        return lax.rem(z + j, nz)

    def to_sec(i):
        return (sec(i), d)

    def to_dp(j):
        return (s, dpi(j))

    def to_z(j):
        return (s, zi(j) * 2 + c)

    def col(q, n=Q):
        return pl.ds(pl.multiple_of(q * n, n), n)

    def seats(e):
        return pl.ds(pl.multiple_of(e * C, C), C)

    mine = col(s)
    places = {}
    pending = {}

    def copy(src, dst, k, device):
        i = places.setdefault(k, len(places))
        return pltpu.make_async_remote_copy(
            src_ref=src,
            dst_ref=dst,
            send_sem=r.ssem.at[i],
            recv_sem=r.rsem.at[i],
            device_id=device,
            device_id_type=MESH,
        )

    def send(src, dst, k, device):
        pending[k] = copy(src, dst, k, device)
        pending[k].start()

    def sent(k):
        pending.pop(k).wait_send()

    def recv(dst, k):
        copy(dst, dst, k, beside).wait_recv()

    def each(rows, step, body):
        @pl.loop(0, rows // step)
        def _(i):
            body(pl.ds(pl.multiple_of(i * step, step), step))

    others = range(1, S)

    def gather_send(ref, m, k):
        for i in others:
            send(ref.at[m, :, mine], ref.at[m, :, mine], (k, m, i), to_sec(i))

    def gather_recv(ref, m, k):
        for i in others:
            recv(ref.at[m, :, col(sec(S - i))], (k, m, i))

    def sum_send(tile, out, arrive, own, m, k, before=None, hold=False):
        for i in others:
            if before is not None:
                sent((before, m, i))
            out[m, i - 1] = tile(sec(i)).astype(bf16)
            if not hold:
                send(out.at[m, i - 1], arrive.at[m, i - 1], (k, m, i), to_sec(i))
        own[m] = tile(s)

    def sum_start(out, arrive, m, k):
        for i in others:
            send(out.at[m, i - 1], arrive.at[m, i - 1], (k, m, i), to_sec(i))

    def sum_recv(arrive, m, k):
        for i in others:
            recv(arrive.at[m, i - 1], (k, m, i))

    def summed(own, arrive, m, rows):
        total = own[m, rows]
        for i in others:
            total += arrive[m, i - 1, rows].astype(f32)
        return total

    def dispatch_send(src, dst, m, k):
        dst[m, seats(d), mine] = src[m, seats(d)]
        for j in range(1, G):
            send(src.at[m, seats(dpi(j))], dst.at[m, seats(d), mine], (k, m, j), to_dp(j))

    def dispatch_recv(dst, m, k):
        for j in range(1, G):
            recv(dst.at[m, seats(dpi(G - j)), mine], (k, m, j))

    def return_send(src, dst, m, k):
        dst[m, seats(d)] = src[m, seats(d)]
        for j in range(1, G):
            send(src.at[m, seats(dpi(j))], dst.at[m, seats(d)], (k, m, j), to_dp(j))

    def return_recv(dst, m, k):
        for j in range(1, G):
            recv(dst.at[m, seats(dpi(G - j))], (k, m, j))

    def part(ref, zz, cc):
        return ref.at[:, zz, cc] if len(ref.shape) == 5 else ref.at[zz, cc]

    def weight_start(ref, k):
        send(part(ref, z, c), part(ref, z, c), (k, "far"), (s, far * 2 + c))
        send(part(ref, z, c), part(ref, z, c), (k, "near"), (s, near * 2 + c))
        send(part(ref, z, c), part(ref, z, c), (k, "c", 0), beside)

    def weight_far(ref, k):
        recv(part(ref, far, c), (k, "far"))
        send(part(ref, far, c), part(ref, far, c), (k, "near far"), (s, near * 2 + c))
        send(part(ref, far, c), part(ref, far, c), (k, "c", 1), beside)

    def weight_near(ref, k):
        recv(part(ref, near, c), (k, "near"))
        send(part(ref, near, c), part(ref, near, c), (k, "c", 2), beside)
        recv(part(ref, near_far, c), (k, "near far"))
        send(part(ref, near_far, c), part(ref, near_far, c), (k, "c", 3), beside)

    def weight_wait(ref, k):
        for i, zz in enumerate((z, far, near, near_far)):
            recv(part(ref, zz, 1 - c), (k, "c", i))

    barrier = pltpu.get_barrier_semaphore()
    for i in others:
        pl.semaphore_signal(barrier, inc=1, device_id=to_sec(i), device_id_type=MESH)
    for j in range(1, G):
        pl.semaphore_signal(barrier, inc=1, device_id=to_dp(j), device_id_type=MESH)
    pl.semaphore_wait(barrier, S + G - 2)

    load_in = pltpu.make_async_copy(r.win_in, r.win, r.lsem.at[0])
    load_out = pltpu.make_async_copy(r.wout_in, r.wout, r.lsem.at[1])
    for i in others:
        for piece in range(3):
            src = r.wqkv_in.at[:, pl.ds(pl.multiple_of(piece * D + sec(i) * Q, Q), Q)]
            dst = r.wqkv.at[s, z, c, :, piece * Q : (piece + 1) * Q]
            send(src, dst, ("q1", piece, i), to_sec(i))
        send(r.vin, r.vg.at[s, d], ("v1", i), to_sec(i))
        send(r.ein, r.evec.at[:, mine], ("e1", i), to_sec(i))
    for i in others:
        send(r.wup_in.at[:, col(sec(i), FQ)], r.wup.at[s, z, c], ("u1", i), to_sec(i))
    load_in.start()
    load_out.start()
    for piece in range(3):
        r.wqkv[s, z, c, :, piece * Q : (piece + 1) * Q] = r.wqkv_in[
            :, pl.ds(pl.multiple_of(piece * D + s * Q, Q), Q)
        ]
    r.wup[s, z, c] = r.wup_in[:, col(s, FQ)]
    r.wo[z, c] = r.wo_in[...]
    r.wdn[z, c] = r.wdn_in[...]
    r.vg[s, d] = r.vin[...]
    r.evec[:, mine] = r.ein[...]

    early = lax.broadcasted_iota(jnp.int32, (T, T), 0)
    late = lax.broadcasted_iota(jnp.int32, (T, T), 1)
    for m in range(M):
        route = r.routes[m : m + 1, :]
        expert_ids = lax.broadcasted_iota(jnp.int32, (G, T), 0)
        picks = jnp.where(expert_ids == route, 1.0, 0.0)
        before = jnp.where(early < late, 1.0, 0.0).astype(bf16)
        counts = jnp.dot(picks.astype(bf16), before, preferred_element_type=f32)
        rank = jnp.sum(counts * picks, axis=0, keepdims=True)
        place = route.astype(f32) * float(C) + rank
        seat_ids = lax.broadcasted_iota(jnp.int32, (R, T), 0).astype(f32)
        r.perm[m] = jnp.where(seat_ids == place, 1.0, 0.0).astype(bf16)
        r.cots[m] = jnp.dot(r.perm[m], r.cot[m, :, mine], preferred_element_type=f32).astype(bf16)

        dispatch_send(r.cots, r.dge, m, "cot")

    for i in others:
        recv(r.vg.at[sec(S - i), d], ("v1", i))
        recv(r.evec.at[:, col(sec(S - i))], ("e1", i))
    for j in range(1, G):
        send(r.vg.at[:, d], r.vg.at[:, d], ("v2", j), to_dp(j))
    for i in others:
        for piece in range(3):
            recv(r.wqkv.at[sec(S - i), z, c, :, piece * Q : (piece + 1) * Q], ("q1", piece, i))
    weight_start(r.wqkv, "wqkv")

    for m in range(M):
        end = r.bucket[m, 0]
        seg_q = (early >= end).astype(jnp.int32)
        seg_k = (late >= end).astype(jnp.int32)
        for b in range(1, r.bucket.shape[1]):
            end = end + r.bucket[m, b]
            seg_q += (early >= end).astype(jnp.int32)
            seg_k += (late >= end).astype(jnp.int32)
        live = jnp.broadcast_to(r.live[m : m + 1, :], (T, T))
        allowed = (seg_q == seg_k) & (late <= early) & ((live == 1) | (late == early))
        r.mask[m] = jnp.where(allowed, 1.0, 0.0)

    for j in range(1, G):
        recv(r.vg.at[:, dpi(G - j)], ("v2", j))
    spread_row = lax.broadcasted_iota(jnp.int32, (128, D), 0)
    spread_lane = lax.broadcasted_iota(jnp.int32, (128, D), 1)
    spread = jnp.where(lax.rem(spread_lane, sh) == spread_row, 1.0, 0.0).astype(bf16)
    stacked = r.vg[...].reshape(S * G * 8, 128).astype(bf16)
    wide = jnp.dot(stacked, spread, preferred_element_type=f32)
    row_id = lax.broadcasted_iota(jnp.int32, (S * G * 8, D), 0)
    lane_id = lax.broadcasted_iota(jnp.int32, (S * G * 8, D), 1)
    low = lax.shift_right_logical(row_id, 3) * sh
    wide = jnp.where((lane_id >= low) & (lane_id < low + sh), wide, 0.0)
    r.vecs[...] = jnp.sum(wide.reshape(S * G, 8, D), axis=0)

    def normed(values):
        mean = jnp.mean(values, axis=1, keepdims=True)
        center = values - mean
        rs = lax.rsqrt(jnp.mean(center * center, axis=1, keepdims=True) + epsilon)
        return center * rs, mean, rs

    def norm_tokens(src, m, at, keep):
        gain = r.vecs[2 * at : 2 * at + 1, :]
        bias = r.vecs[2 * at + 1 : 2 * at + 2, :]

        def body(rows):
            n, mean, rs = normed(src[m, rows].astype(f32))
            if keep:
                r.tst[m, rows, 2 * at : 2 * at + 1] = mean
                r.tst[m, rows, 2 * at + 1 : 2 * at + 2] = rs
            r.a[m, rows] = (n * gain + bias).astype(bf16)

        each(T, CHUNK, body)

    for m in range(M):
        norm_tokens(r.hidden, m, 0, True)
    weight_far(r.wqkv, "wqkv")
    weight_start(r.wo, "wo")
    for m in range(M):
        dispatch_recv(r.dge, m, "cot")
        gather_send(r.dge, m, "dge")
    for i in others:
        recv(r.wup.at[sec(S - i), z, c], ("u1", i))
    weight_start(r.wup, "wup")
    weight_near(r.wqkv, "wqkv")
    weight_far(r.wo, "wo")
    weight_wait(r.wqkv, "wqkv")

    def attend(m):
        @pl.loop(0, 3)
        def _(t):
            w = r.wqkv[:, :, :, :, col(t)].reshape(D, Q)
            r.qkv[m, :, col(t)] = jnp.dot(r.a[m], w, preferred_element_type=f32).astype(bf16)

        for hh in range(heads):
            at = hh * size
            q = r.qkv[m, :, at : at + size]
            k = r.qkv[m, :, Q + at : Q + at + size]
            v = r.qkv[m, :, 2 * Q + at : 2 * Q + at + size]
            scores = jnp.where(r.mask[m] > 0.0, nt(q, k) * scale, masked_value)
            weights = jnp.exp(scores - jnp.max(scores, axis=1, keepdims=True))
            p = weights / jnp.sum(weights, axis=1, keepdims=True)
            r.probs[m, hh] = p
            mixed = jnp.dot(p.astype(bf16), v, preferred_element_type=f32)
            r.o[m, :, at : at + size] = mixed.astype(bf16)

    def y1_tile(m):
        return lambda q: jnp.dot(
            r.o[m], r.wo[:, :, :, col(q)].reshape(Q, Q), preferred_element_type=f32
        )

    attend(0)
    weight_near(r.wo, "wo")
    weight_far(r.wup, "wup")
    weight_start(r.wdn, "wdn")
    weight_wait(r.wo, "wo")
    sum_send(y1_tile(0), r.ts, r.r1, r.own, 0, "y1")
    attend(1)
    sum_send(y1_tile(1), r.ts, r.r1, r.own, 1, "y1")
    weight_near(r.wup, "wup")

    def finish_y1(m):
        sum_recv(r.r1, m, "y1")

        def body(rows):
            total = r.hidden[m, rows, mine].astype(f32) + summed(r.own, r.r1, m, rows)
            r.y1[m, rows, mine] = total.astype(bf16)

        each(T, 64, body)
        gather_send(r.y1, m, "y1g")

    finish_y1(0)
    finish_y1(1)
    weight_wait(r.wup, "wup")
    weight_far(r.wdn, "wdn")

    def up(m):
        gather_recv(r.y1, m, "y1g")
        norm_tokens(r.y1, m, 1, True)

        @pl.loop(0, FQ // Q)
        def _(t):
            w = r.wup[:, :, :, :, col(t)].reshape(D, Q)
            pre = jnp.dot(r.a[m], w, preferred_element_type=f32)
            value, slope = gelu_both(pre)
            r.u[m, :, col(t)] = value.astype(bf16)
            r.h[m, :, col(t)] = slope

    def y2_tile(m):
        return lambda q: jnp.dot(
            r.u[m], r.wdn[:, :, :, col(q)].reshape(FQ, Q), preferred_element_type=f32
        )

    up(0)
    up(1)
    weight_near(r.wdn, "wdn")
    weight_wait(r.wdn, "wdn")
    sum_send(y2_tile(0), r.ts, r.r2, r.own, 0, "y2", "y1")
    sum_send(y2_tile(1), r.ts, r.r2, r.own, 1, "y2", "y1")

    def finish_y2(m):
        sum_recv(r.r2, m, "y2")

        def body(rows):
            total = r.y1[m, rows, mine].astype(f32) + summed(r.own, r.r2, m, rows)
            r.y2q[m, rows] = total.astype(bf16)

        each(T, 64, body)
        r.y2s[m] = jnp.dot(r.perm[m], r.y2q[m], preferred_element_type=f32).astype(bf16)
        dispatch_send(r.y2s, r.xe, m, "y2d")

    finish_y2(0)
    finish_y2(1)
    for m in range(M):
        dispatch_recv(r.xe, m, "y2d")
        gather_send(r.xe, m, "xe")
    load_in.wait()
    load_out.wait()

    def expert(m):
        gather_recv(r.dge, m, "dge")
        gather_recv(r.xe, m, "xe")
        gain, bias, centroid = r.evec[0:1, :], r.evec[1:2, :], r.evec[2:3, :]

        def body(rows):
            v = r.xe[m, rows].astype(f32)
            n, mean, rs = normed(v)
            alpha = jax.nn.sigmoid(jnp.sum(v * centroid, axis=1, keepdims=True))
            r.est[m, rows, 0:1] = mean
            r.est[m, rows, 1:2] = rs
            r.est[m, rows, 2:3] = alpha
            r.en[m, rows] = (n * gain + bias).astype(bf16)
            r.dfe[m, rows] = (alpha * r.dge[m, rows].astype(f32)).astype(bf16)

        each(R, CHUNK, body)

        @pl.loop(0, FQ // Q)
        def _(t):
            w = r.win[:, :, :, :, col(t)].reshape(D, Q)
            pre = jnp.dot(r.en[m], w, preferred_element_type=f32)
            value, slope = gelu_both(pre)
            r.ue[m, :, col(t)] = value.astype(bf16)
            r.slope[:, col(t)] = slope

        stats = [jnp.zeros((R, 1), f32) for _ in range(3)]

        def fe_tile(q):
            tile = jnp.dot(
                r.ue[m], r.wout[:, :, :, col(q)].reshape(FQ, Q), preferred_element_type=f32
            )
            stats[2] += jnp.sum(tile * r.dge[m, :, col(q)].astype(f32), axis=1, keepdims=True)
            return tile

        def den_tile(q):
            tile = nt(r.dhe[m], r.win[q].reshape(Q, FQ))
            scaled = tile * r.evec[0:1, col(q)]
            n = (r.xe[m, :, col(q)].astype(f32) - r.est[m, :, 0:1]) * r.est[m, :, 1:2]
            stats[0] += jnp.sum(scaled, axis=1, keepdims=True)
            stats[1] += jnp.sum(scaled * n, axis=1, keepdims=True)
            return tile

        sum_send(fe_tile, r.fes, r.fer, r.feo, m, "fe", hold=m > 0)

        @pl.loop(0, FQ // Q)
        def _(t):
            due = nt(r.dfe[m], r.wout[t].reshape(Q, D))
            r.dhe[m, :, col(t)] = (due * r.slope[:, col(t)]).astype(bf16)

        sum_send(den_tile, r.dns, r.dnr, r.dno, m, "den")
        r.ess[m] = to_rows(stats)
        for i in others:
            send(r.ess.at[m], r.esr.at[m, i - 1], ("est", m, i), to_sec(i))

    expert(0)
    expert(1)

    def finish_den(m):
        sum_recv(r.dnr, m, "den")
        total = r.ess[m]
        for i in others:
            recv(r.esr.at[m, i - 1], ("est", m, i))
            total += r.esr[m, i - 1]
        r.est[m, :, 8:16] = to_columns(total)[:, 0:8]
        gain, centroid = r.evec[0:1, mine], r.evec[2:3, mine]
        if m == 0:
            r.evo[...] = jnp.zeros_like(r.evo)

        def body(rows):
            den = summed(r.dno, r.dnr, m, rows)
            xq = r.xe[m, rows, mine].astype(f32)
            rs, alpha = r.est[m, rows, 1:2], r.est[m, rows, 2:3]
            n = (xq - r.est[m, rows, 0:1]) * rs
            m1, m2 = r.est[m, rows, 8:9] * (1.0 / D), r.est[m, rows, 9:10] * (1.0 / D)
            dlogit = r.est[m, rows, 10:11] * alpha * (1.0 - alpha)
            grad = rs * (gain * den - m1 - n * m2) + dlogit * centroid
            r.dxs[m, rows] = grad.astype(bf16)
            r.evo[0:1, :] += jnp.sum(den * n, axis=0, keepdims=True)
            r.evo[1:2, :] += jnp.sum(den, axis=0, keepdims=True)
            r.evo[2:3, :] += jnp.sum(dlogit * xq, axis=0, keepdims=True)

        each(R, 64 if R % 64 == 0 else CHUNK, body)
        return_send(r.dxs, r.dxr, m, "dxb")

    def finish_fe(m):
        sum_recv(r.fer, m, "fe")

        def body(rows):
            fe = summed(r.feo, r.fer, m, rows)
            r.ges[m, rows] = (r.est[m, rows, 2:3] * fe).astype(bf16)

        each(R, 64 if R % 64 == 0 else CHUNK, body)
        return_send(r.ges, r.ger, m, "geb")

    finish_den(0)
    finish_den(1)
    sum_start(r.fes, r.fer, 1, "fe")
    finish_fe(0)

    writes = []
    for left, right, out in ((r.en, r.dhe, r.gin_out), (r.ue, r.dfe, r.gout_out)):
        for t in range(D // 256):
            slot = len(writes) % 2
            if len(writes) >= 2:
                writes[-2].wait()
            rows = slice(t * 256, (t + 1) * 256)
            lhs = left[:, :, rows].reshape(M * R, 256)
            r.stage[slot] = tn(lhs, right[...].reshape(M * R, D))
            writes.append(pltpu.make_async_copy(r.stage.at[slot], out.at[rows], r.lsem.at[2 + slot]))
            writes[-1].start()

    def finish_dxe(m):
        return_recv(r.dxr, m, "dxb")
        back = tn(r.perm[m], r.dxr[m])
        r.dy2[m, :, mine] = (r.cot[m, :, mine].astype(f32) + back).astype(bf16)
        gather_send(r.dy2, m, "dy2")

    finish_dxe(0)
    finish_dxe(1)
    finish_fe(1)

    def token_stats(m, at, src):
        stats = [jnp.zeros((T, 1), f32) for _ in range(2)]

        def add(q, tile):
            scaled = tile * r.vecs[2 * at : 2 * at + 1, col(q)]
            mean, rs = r.tst[m, :, 2 * at : 2 * at + 1], r.tst[m, :, 2 * at + 1 : 2 * at + 2]
            n = (src[m, :, col(q)].astype(f32) - mean) * rs
            stats[0] += jnp.sum(scaled, axis=1, keepdims=True)
            stats[1] += jnp.sum(scaled * n, axis=1, keepdims=True)
            return tile

        return stats, add

    def stats_send(m, at, stats):
        r.tss[at, m] = to_rows(stats)
        for i in others:
            send(r.tss.at[at, m], r.tsr.at[at, m, i - 1], ("tst", at, m, i), to_sec(i))

    def stats_recv(m, at):
        total = r.tss[at, m]
        for i in others:
            recv(r.tsr.at[at, m, i - 1], ("tst", at, m, i))
            total += r.tsr[at, m, i - 1]
        r.tst[m, :, 8:16] = to_columns(total)[:, 0:8]

    def dense_back(m):
        gather_recv(r.dy2, m, "dy2")

        @pl.loop(0, FQ // Q)
        def _(t):
            du = nt(r.dy2[m], r.wdn[t].reshape(Q, D))
            r.dh[m, :, col(t)] = (du * r.h[m, :, col(t)]).astype(bf16)

        stats, add = token_stats(m, 1, r.y1)
        sum_send(
            lambda q: add(q, nt(r.dh[m], r.wup[q].reshape(Q, FQ))),
            r.ts,
            r.r1,
            r.own,
            m,
            "da2",
            "y2",
        )
        stats_send(m, 1, stats)

    def norm_back(m, at, src, grad_in, own, arrive, emit):
        gain = r.vecs[2 * at : 2 * at + 1, mine]

        def body(rows):
            grad = summed(own, arrive, m, rows)
            mean, rs = r.tst[m, rows, 2 * at : 2 * at + 1], r.tst[m, rows, 2 * at + 1 : 2 * at + 2]
            n = (src[m, rows, mine].astype(f32) - mean) * rs
            m1, m2 = r.tst[m, rows, 8:9] * (1.0 / D), r.tst[m, rows, 9:10] * (1.0 / D)
            emit(rows, grad_in[m, rows, mine].astype(f32) + rs * (gain * grad - m1 - n * m2))
            r.vsum[2 * at : 2 * at + 1, :] += jnp.sum(grad * n, axis=0, keepdims=True)
            r.vsum[2 * at + 1 : 2 * at + 2, :] += jnp.sum(grad, axis=0, keepdims=True)

        each(T, 64, body)

    def finish_da2(m):
        sum_recv(r.r1, m, "da2")
        stats_recv(m, 1)
        for i in others:
            sent(("y1g", m, i))

        def emit(rows, value):
            r.y1[m, rows, mine] = value.astype(bf16)

        norm_back(m, 1, r.y1, r.dy2, r.own, r.r1, emit)
        gather_send(r.y1, m, "dy1")

    def grads_pair(g, b, k):
        src = g.at[:, :, 1 - c] if len(g.shape) == 5 else g.at[:, 1 - c]
        send(src, b, (k, "p"), beside)

    def grads_add(g, zz, arrive):
        if len(g.shape) == 5:

            @pl.loop(0, S)
            def _(q):
                g[q, zz, c] = (g[q, zz, c].astype(f32) + arrive[q].astype(f32)).astype(bf16)
        else:
            g[zz, c] = (g[zz, c].astype(f32) + arrive[...].astype(f32)).astype(bf16)

    def grads_paired(g, b, k):
        recv(b, (k, "p"))
        for zz in range(nz):
            grads_add(g, zz, b.at[:, zz] if len(g.shape) == 5 else b.at[zz])

    def grads_near(g, b, arrive, k):
        grads_paired(g, b, k)
        send(part(g, near_far, c), arrive.at[1], (k, "nf"), (s, near * 2 + c))
        send(part(g, near, c), arrive.at[0], (k, "n"), (s, near * 2 + c))

    def grads_far(g, arrive, k):
        recv(arrive.at[1], (k, "nf"))
        grads_add(g, far, arrive.at[1])
        send(part(g, far, c), arrive.at[2], (k, "f"), (s, far * 2 + c))

    def grads_near_recv(arrive, k):
        recv(arrive.at[0], (k, "n"))
        recv(arrive.at[2], (k, "f"))
        return 0, 2

    def grads_spread(g, b, arrive, k):
        grads_paired(g, b, k)
        for j in range(1, nz):
            send(part(g, zi(j), c), arrive.at[j - 1], (k, "g", j), to_z(j))

    def grads_recv(arrive, k):
        for j in range(1, nz):
            recv(arrive.at[j - 1], (k, "g", j))
        return range(nz - 1)

    dense_back(0)
    dense_back(1)

    @pl.loop(0, nz)
    def _(t):
        lhs = r.u[:, :, col(t)].reshape(M * T, Q)
        grad = tn(lhs, r.dy2[...].reshape(M * T, D))
        r.wout[t] = grad.astype(bf16).reshape(2, shd, D)

    grads_pair(r.wout, r.bdn, "gdn")

    r.vsum[...] = jnp.zeros_like(r.vsum)
    finish_da2(0)
    finish_da2(1)

    @pl.loop(0, S)
    def _(t):
        lhs = r.a[:, :, col(t)].reshape(M * T, Q)
        grad = tn(lhs, r.dh[...].reshape(M * T, FQ))
        r.win[t] = grad.astype(bf16).reshape(nz, 2, sh, FQ)

    grads_pair(r.win, r.bup, "gup")
    grads_near(r.wout, r.bdn, r.zdn, "gdn")

    for m in range(M):
        norm_tokens(r.hidden, m, 0, False)

    def attend_back(m):
        gather_recv(r.y1, m, "dy1")
        out_grad = nt(r.y1[m], r.wo[...].reshape(Q, D)).astype(bf16)
        for hh in range(heads):
            at = hh * size
            q = r.qkv[m, :, at : at + size]
            k = r.qkv[m, :, Q + at : Q + at + size]
            v = r.qkv[m, :, 2 * Q + at : 2 * Q + at + size]
            go = out_grad[:, at : at + size]
            p = r.probs[m, hh]
            dp = nt(go, v)
            dv = tn(p.astype(bf16), go)
            ds = (p * (dp - jnp.sum(p * dp, axis=1, keepdims=True))).astype(bf16)
            dq = jnp.dot(ds, k, preferred_element_type=f32) * scale
            dk = tn(ds, q) * scale
            r.dqkv[m, :, at : at + size] = dq.astype(bf16)
            r.dqkv[m, :, Q + at : Q + at + size] = dk.astype(bf16)
            r.dqkv[m, :, 2 * Q + at : 2 * Q + at + size] = dv.astype(bf16)
        stats, add = token_stats(m, 0, r.hidden)
        sum_send(
            lambda q: add(q, nt(r.dqkv[m], r.wqkv[q].reshape(Q, 3 * Q))),
            r.ts,
            r.r2,
            r.own,
            m,
            "da1",
            "da2",
        )
        stats_send(m, 0, stats)

    attend_back(0)
    grads_near(r.win, r.bup, r.zup, "gup")
    attend_back(1)
    grads_far(r.wout, r.zdn, "gdn")

    @pl.loop(0, S)
    def _(t):
        lhs = r.a[:, :, col(t)].reshape(M * T, Q)
        grad = tn(lhs, r.dqkv[...].reshape(M * T, 3 * Q))
        r.gqk[t] = grad.astype(bf16).reshape(nz, 2, sh, 3 * Q)

    grads_pair(r.gqk, r.bqk, "gqk")
    grad = tn(r.o[...].reshape(M * T, Q), r.y1[...].reshape(M * T, D))
    r.gwo[...] = grad.astype(bf16).reshape(nz, 2, sh, D)
    grads_pair(r.gwo, r.bwo, "gwo")
    grads_far(r.win, r.zup, "gup")
    grads_spread(r.gqk, r.bqk, r.zqk, "gqk")
    grads_spread(r.gwo, r.bwo, r.zwo, "gwo")

    def finish_da1(m):
        sum_recv(r.r2, m, "da1")
        stats_recv(m, 0)

        def emit(rows, value):
            r.dx[m, rows] = value

        norm_back(m, 0, r.hidden, r.y1, r.own, r.r2, emit)

    finish_da1(0)
    finish_da1(1)
    for j in range(1, G):
        send(r.vsum, r.vsr.at[j - 1], ("vs", j), to_dp(j))

    for m in range(M):
        return_recv(r.ger, m, "geb")
        back = tn(r.perm[m], r.ger[m])
        r.out[m] = (r.y2q[m].astype(f32) + back).astype(bf16)

    def row_result(g, arrive, out, k, rows, wait):
        slots = wait(arrive, k)
        mine_part = part(g, z, c)

        def body(at):
            total = mine_part[at].astype(f32)
            for slot in slots:
                total += arrive[slot, at].astype(f32)
            out[at] = total

        each(rows, CHUNK, body)

    def column_send(g, arrive, out, back, k, wait):
        slots = wait(arrive, k)

        @pl.loop(0, S)
        def _(q):
            total = g[q, z, c].astype(f32)
            for slot in slots:
                total += arrive[slot, q].astype(f32)
            out[q] = total.astype(bf16)

        for i in others:
            send(out.at[sec(i)], back.at[i - 1], (k, "s", i), to_sec(i))

    def column_result(sums, back, out, pieces, k):
        width = sums.shape[2] // pieces
        for i in range(S):
            if i:
                recv(back.at[i - 1], (k, "s", i))
            q = sec(S - i) if i else s
            value = (back[i - 1] if i else sums[s]).astype(f32)
            for piece in range(pieces):
                at = pl.ds(pl.multiple_of(piece * S * width + q * width, width), width)
                out[:, at] = value[:, piece * width : (piece + 1) * width]

    row_result(r.wout, r.zdn, r.gdn_out, "gdn", shd, grads_near_recv)
    column_send(r.win, r.zup, r.ups, r.upr, "gup", grads_near_recv)
    column_send(r.gqk, r.zqk, r.qks, r.qkr, "gqk", grads_recv)
    row_result(r.gwo, r.zwo, r.gwo_out, "gwo", sh, grads_recv)
    total = r.vsum[...]
    for j in range(1, G):
        recv(r.vsr.at[j - 1], ("vs", j))
        total += r.vsr[j - 1]
    r.vgo[...] = total
    column_result(r.ups, r.upr, r.gup_out, 1, "gup")
    column_result(r.qks, r.qkr, r.gqk_out, 3, "gqk")
    for write in writes[-2:]:
        write.wait()
    for k in list(pending):
        sent(k)
    assert len(places) <= KEYS, len(places)


def hand_over(*refs):
    count = len(refs) // 2
    first = pl.program_id(0) == 0
    for src, dst in zip(refs[:count], refs[count:]):
        if src.shape[0] == 256 and src.shape[1] == 1024:
            dst[...] = src[...]
        else:

            @pl.when(first)
            def _(src=src, dst=dst):
                dst[...] = src[...]


def with_kernel(
    hidden_in,
    cotangent,
    bucket_len,
    live_mask,
    routes,
    ln1_gain,
    ln1_bias,
    w_qkv,
    w_attn_out,
    ln2_gain,
    ln2_bias,
    w_up,
    w_down,
    expert_in,
    expert_out,
    expert_gain,
    expert_bias,
    centroids,
):
    S = lax.axis_size("section")
    G = lax.axis_size("dp")
    M, T, D = hidden_in.shape
    Q = D // S
    FQ = w_up.shape[1] // S
    C = 3 * T // (2 * G)
    sh, shd = w_up.shape[0], w_down.shape[0]
    dims = (S, G, M, T, D, Q, FQ, C, sh, shd)
    vin = jnp.stack([ln1_gain, ln1_bias, ln2_gain, ln2_bias]).astype(f32)
    vin = jnp.pad(vin, ((0, 4), (0, 128 - sh)))
    ein = jnp.concatenate([expert_gain, expert_bias, centroids]).astype(f32)
    ein = jnp.pad(ein, ((0, 5), (0, 0)))
    scratch = layout(dims)
    names = INPUTS + OUTPUTS + list(scratch) + ["ssem", "rsem", "lsem"]
    vmem = pl.BlockSpec(memory_space=pltpu.VMEM)
    smem = pl.BlockSpec(memory_space=pltpu.SMEM)
    anywhere = pl.BlockSpec(memory_space=pl.ANY)
    shapes = (
        ((M, T, Q), bf16),
        ((M, T, Q), f32),
        ((8, Q), f32),
        ((sh, 3 * D), f32),
        ((sh, D), f32),
        ((sh, S * FQ), f32),
        ((shd, D), f32),
        ((D, FQ), f32),
        ((FQ, D), f32),
        ((8, Q), f32),
    )
    outs = pl.pallas_call(
        functools.partial(block_kernel, dims, names),
        name="block",
        out_shape=[jax.ShapeDtypeStruct(*shape) for shape in shapes],
        in_specs=[vmem, vmem, smem] + [vmem] * 8 + [anywhere] * 2,
        out_specs=[vmem] * 7 + [anywhere] * 2 + [vmem],
        scratch_shapes=[pltpu.VMEM(*shape) for shape in scratch.values()]
        + [pltpu.SemaphoreType.DMA((KEYS,))] * 2
        + [pltpu.SemaphoreType.DMA((4,))],
        compiler_params=pltpu.CompilerParams(
            collective_id=0, has_side_effects=True, vmem_limit_bytes=63 << 20
        ),
    )(
        hidden_in,
        cotangent,
        bucket_len[:, 0, :],
        live_mask,
        routes[:, :, 0],
        vin,
        ein,
        w_qkv,
        w_attn_out,
        w_up,
        w_down,
        expert_in.reshape(S, G // 2, 2, sh, FQ),
        expert_out.reshape(G // 2, 2, shd, D),
    )
    specs = [
        pl.BlockSpec((256, shape[1]), lambda i: (i, 0))
        if shape == (D, FQ) or shape == (FQ, D)
        else pl.BlockSpec(shape, lambda i, n=len(shape): (0,) * n)
        for shape, _ in shapes
    ]
    outs = pl.pallas_call(
        hand_over,
        name="hand_over",
        grid=(D // 256,),
        out_shape=[jax.ShapeDtypeStruct(*shape) for shape in shapes],
        in_specs=specs,
        out_specs=specs,
        compiler_params=pltpu.CompilerParams(vmem_limit_bytes=32 << 20),
    )(*outs)
    out, dx, vectors, gqkv, gwo, gup, gdn, gin, gout, evectors = outs
    vectors = lax.dynamic_slice_in_dim(vectors, lax.axis_index("dp") * sh, sh, 1)
    return (
        out,
        dx,
        vectors[0],
        vectors[1],
        gqkv,
        gwo,
        vectors[2],
        vectors[3],
        gup,
        gdn,
        gin[None],
        gout[None],
        evectors[0:1],
        evectors[1:2],
        evectors[2:3],
    )


def on_device(*args):
    groups = lax.axis_size("dp")
    rows, shard = args[0].shape[1], args[11].shape[0]
    capacity = 3 * rows // (2 * groups)
    if capacity % 16 or shard % 16 or groups != 8:
        return with_collectives(*args)
    return with_kernel(*args)


def solution(mesh):
    everywhere = ("section", "dp")
    tokens = P(None, "dp", None)
    outs = P(None, "dp", "section")
    per_expert = P("dp", "section")
    return jax.shard_map(
        on_device,
        mesh=mesh,
        in_specs=(
            tokens,
            tokens,
            tokens,
            P(None, "dp"),
            tokens,
            P(everywhere),
            P(everywhere),
            P(everywhere, None),
            P(everywhere, None),
            P(everywhere),
            P(everywhere),
            P(everywhere, None),
            P(everywhere, None),
            P("dp", None, "section"),
            P("dp", "section", None),
            per_expert,
            per_expert,
            per_expert,
        ),
        out_specs=(
            outs,
            outs,
            P(everywhere),
            P(everywhere),
            P(everywhere, None),
            P(everywhere, None),
            P(everywhere),
            P(everywhere),
            P(everywhere, None),
            P(everywhere, None),
            P("dp", None, "section"),
            P("dp", "section", None),
            per_expert,
            per_expert,
            per_expert,
        ),
        check_vma=False,
    )
```

```python
import functools
import math
import types

import jax
import jax.numpy as jnp
from jax import lax
from jax.experimental import pallas as pl
from jax.experimental.pallas import tpu as pltpu
from jax.sharding import PartitionSpec as P

HEADS = 16
epsilon = 1e-05
masked_value = -1e30
f32 = jnp.float32
bf16 = jnp.bfloat16


def norm_parts(values):
    center = values - jnp.mean(values, axis=-1, keepdims=True)
    spread = jnp.mean(center * center, axis=-1, keepdims=True)
    rs = lax.rsqrt(spread + epsilon)
    return center * rs, rs


def gelu_back(pre, grad):
    outputs, pullback = jax.vjp(jax.nn.gelu, pre)
    return pullback(grad)[0]


def dot(a, b):
    return jnp.dot(a, b, preferred_element_type=f32)


def dot_tn(a, b):
    return jnp.einsum("rd,re->de", a, b, preferred_element_type=f32)


def dot_nt(a, b):
    return jnp.einsum("re,de->rd", a, b, preferred_element_type=f32)


def sum_scatter(part):
    return lax.psum_scatter(
        part.astype(bf16), "section", scatter_dimension=part.ndim - 1, tiled=True
    ).astype(f32)


def gather_features(part):
    return lax.all_gather(part, "section", axis=part.ndim - 1, tiled=True)


def with_collectives(
    hidden_in,
    cotangent,
    bucket_len,
    live_mask,
    routes,
    ln1_gain,
    ln1_bias,
    w_qkv,
    w_attn_out,
    ln2_gain,
    ln2_bias,
    w_up,
    w_down,
    expert_in,
    expert_out,
    expert_gain,
    expert_bias,
    centroids,
):
    sections = lax.axis_size("section")
    groups = lax.axis_size("dp")
    section = lax.axis_index("section")
    micro, rows, width = hidden_in.shape
    quarter = width // sections
    heads = HEADS // sections
    size = width // HEADS
    ff = w_up.shape[1] // sections
    capacity = 3 * rows // (2 * groups)
    shard = w_up.shape[0]
    own_cols = section * quarter

    def mine(values):
        return lax.dynamic_slice_in_dim(values, own_cols, quarter, values.ndim - 1)

    def column_group(weight, pieces):
        cols = weight.shape[1] // (pieces * sections)
        parts = weight.reshape(shard, pieces, sections, cols).transpose(2, 0, 1, 3)
        parts = parts.reshape(sections, shard, pieces * cols)
        parts = lax.all_to_all(parts, "section", split_axis=0, concat_axis=0, tiled=True)
        full = lax.all_gather(parts, "dp", axis=1, tiled=True)
        return full.reshape(width, pieces * cols)

    def column_group_back(grad, pieces):
        cols = grad.shape[1] // pieces
        parts = grad.astype(bf16).reshape(sections, groups * shard, pieces * cols)
        parts = lax.psum_scatter(parts, "dp", scatter_dimension=1, tiled=True)
        parts = lax.all_to_all(parts, "section", split_axis=0, concat_axis=0, tiled=True)
        parts = parts.reshape(sections, shard, pieces, cols).transpose(1, 2, 0, 3)
        return parts.reshape(shard, pieces * sections * cols).astype(f32)

    def row_group_back(grad):
        return lax.psum_scatter(
            grad.astype(bf16), "dp", scatter_dimension=0, tiled=True
        ).astype(f32)

    vectors = lax.all_gather(
        jnp.stack([ln1_gain, ln1_bias, ln2_gain, ln2_bias]), ("section", "dp"), axis=1, tiled=True
    ).astype(f32)
    gain_one, bias_one, gain_two, bias_two = vectors
    expert_vectors = lax.all_gather(
        jnp.concatenate([expert_gain, expert_bias, centroids]), "section", axis=1, tiled=True
    ).astype(f32)
    expert_g, expert_b, centroid = expert_vectors
    wqkv = column_group(w_qkv, 3)
    wo = lax.all_gather(w_attn_out, "dp", axis=0, tiled=True)
    wup = column_group(w_up, 1)
    wdown = lax.all_gather(w_down, "dp", axis=0, tiled=True)
    win = expert_in[0]
    wout = expert_out[0]

    ends = jnp.cumsum(bucket_len[:, 0, :], axis=-1)
    slot_ids = jnp.arange(rows, dtype=jnp.int32)
    segments = jnp.sum((slot_ids[None, :, None] >= ends[:, None, :]).astype(jnp.int32), axis=-1)
    same = segments[:, :, None] == segments[:, None, :]
    causal = slot_ids[None, None, :] <= slot_ids[None, :, None]
    opened = (live_mask[:, None, :] == 1) | (slot_ids[None, None, :] == slot_ids[None, :, None])
    allowed = (same & causal & opened)[:, None]
    chosen = routes[:, :, 0]
    picks = (chosen[:, :, None] == jnp.arange(groups, dtype=jnp.int32)).astype(jnp.int32)
    ranks = jnp.sum((jnp.cumsum(picks, axis=1) - picks) * picks, axis=2)
    places = chosen * capacity + ranks
    place_ids = jnp.arange(groups * capacity, dtype=jnp.int32)
    picked = (places[:, None, :] == place_ids[None, :, None]).astype(bf16)

    def dispatch(values):
        out = jnp.einsum("mpt,mtf->pmf", picked, values, preferred_element_type=f32).astype(bf16)
        out = out.reshape(groups, capacity * micro, quarter)
        return lax.all_to_all(out, "dp", split_axis=0, concat_axis=0, tiled=True)

    def give_back(values):
        out = lax.all_to_all(values, "dp", split_axis=0, concat_axis=0, tiled=True)
        out = out.reshape(groups * capacity, micro, quarter)
        return jnp.einsum("mpt,pmf->mtf", picked, out, preferred_element_type=f32)

    dge = gather_features(dispatch(mine(cotangent))).reshape(-1, width).astype(f32)

    x = hidden_in.reshape(micro * rows, width).astype(f32)
    n1, rs1 = norm_parts(x)
    a1 = (n1 * gain_one + bias_one).astype(bf16)
    qkv = dot(a1, wqkv).astype(bf16)
    q, k, v = (
        qkv[:, i * quarter : (i + 1) * quarter].reshape(micro, rows, heads, size) for i in range(3)
    )
    scale = size ** (-0.5)
    raw = jnp.einsum("mqhd,mkhd->mhqk", q, k, preferred_element_type=f32) * scale
    scores = jnp.where(allowed, raw, masked_value)
    weights = jnp.exp(scores - jnp.max(scores, axis=-1, keepdims=True))
    probs = weights / jnp.sum(weights, axis=-1, keepdims=True)
    probs_low = probs.astype(bf16)
    mixed = jnp.einsum("mhqk,mkhd->mqhd", probs_low, v, preferred_element_type=f32)
    o = mixed.reshape(micro * rows, quarter).astype(bf16)
    y1q = (mine(x) + sum_scatter(dot(o, wo))).astype(bf16)
    y1 = gather_features(y1q).astype(f32)
    n2, rs2 = norm_parts(y1)
    a2 = (n2 * gain_two + bias_two).astype(bf16)
    h = dot(a2, wup)
    u = jax.nn.gelu(h).astype(bf16)
    y2q = (y1q.astype(f32) + sum_scatter(dot(u, wdown))).astype(bf16)

    xe = gather_features(dispatch(y2q.reshape(micro, rows, quarter))).reshape(-1, width)
    xe = xe.astype(f32)
    ne, rse = norm_parts(xe)
    en = (ne * expert_g + expert_b).astype(bf16)
    he = dot(en, win)
    ue = jax.nn.gelu(he).astype(bf16)
    fe_part = dot(ue, wout)
    alpha = jax.nn.sigmoid(jnp.sum(xe * centroid, axis=-1, keepdims=True))
    fe = sum_scatter(fe_part)
    ge = (alpha * fe).astype(bf16).reshape(groups, capacity * micro, quarter)
    block_out = (
        y2q.reshape(micro, rows, quarter).astype(f32) + give_back(ge)
    ).astype(bf16)

    dfe = (alpha * dge).astype(bf16)
    due = dot_nt(dfe, wout)
    grad_out = dot_tn(ue, dfe)
    dhe = gelu_back(he, due).astype(bf16)
    grad_in = dot_tn(en, dhe)
    den_part = dot_nt(dhe, win)
    gden = den_part * expert_g
    stats = lax.psum(
        jnp.stack(
            [
                jnp.mean(gden, axis=-1),
                jnp.mean(gden * ne, axis=-1),
                jnp.sum(dge * fe_part, axis=-1),
            ]
        ),
        "section",
    )[..., None]
    den = sum_scatter(den_part)
    neq = mine(ne)
    dlogit = stats[2] * alpha * (1.0 - alpha)
    dxe_ln = rse * (mine(expert_g) * den - stats[0] - neq * stats[1])
    dxe = (dxe_ln + dlogit * mine(centroid)).astype(bf16)
    grad_expert_gain = jnp.sum(den * neq, axis=0)
    grad_expert_bias = jnp.sum(den, axis=0)
    grad_centroid = jnp.sum(dlogit * mine(xe), axis=0)
    back = give_back(dxe.reshape(groups, capacity * micro, quarter))
    dy2q = (mine(cotangent).astype(f32) + back).astype(bf16).reshape(micro * rows, quarter)

    dy2 = gather_features(dy2q)
    grad_down = dot_tn(u, dy2)
    dh = gelu_back(h, dot_nt(dy2, wdown)).astype(bf16)
    grad_up = dot_tn(a2, dh)
    da2_part = dot_nt(dh, wup)
    gda2 = da2_part * gain_two
    stats = lax.psum(
        jnp.stack([jnp.mean(gda2, axis=-1), jnp.mean(gda2 * n2, axis=-1)]), "section"
    )[..., None]
    da2 = sum_scatter(da2_part)
    n2q = mine(n2)
    dy1q = dy2q.astype(f32) + rs2 * (mine(gain_two) * da2 - stats[0] - n2q * stats[1])
    dy1q = dy1q.astype(bf16)
    dy1 = gather_features(dy1q)
    grad_wo = dot_tn(o, dy1)
    do = dot_nt(dy1, wo).astype(bf16).reshape(micro, rows, heads, size)
    dp = jnp.einsum("mqhd,mkhd->mhqk", do, v, preferred_element_type=f32)
    dv = jnp.einsum("mhqk,mqhd->mkhd", probs_low, do, preferred_element_type=f32)
    delta = jnp.sum(probs * dp, axis=-1, keepdims=True)
    ds = (probs * (dp - delta)).astype(bf16)
    dq = jnp.einsum("mhqk,mkhd->mqhd", ds, k, preferred_element_type=f32) * scale
    dk = jnp.einsum("mhqk,mqhd->mkhd", ds, q, preferred_element_type=f32) * scale
    dqkv = jnp.concatenate(
        [part.reshape(micro * rows, quarter) for part in (dq, dk, dv)], axis=1
    ).astype(bf16)
    grad_qkv = dot_tn(a1, dqkv)
    da1_part = dot_nt(dqkv, wqkv)
    gda1 = da1_part * gain_one
    stats = lax.psum(
        jnp.stack([jnp.mean(gda1, axis=-1), jnp.mean(gda1 * n1, axis=-1)]), "section"
    )[..., None]
    da1 = sum_scatter(da1_part)
    n1q = mine(n1)
    dx = dy1q.astype(f32) + rs1 * (mine(gain_one) * da1 - stats[0] - n1q * stats[1])

    vector_grads = lax.psum_scatter(
        jnp.stack(
            [
                jnp.sum(da1 * n1q, axis=0),
                jnp.sum(da1, axis=0),
                jnp.sum(da2 * n2q, axis=0),
                jnp.sum(da2, axis=0),
            ]
        ),
        "dp",
        scatter_dimension=1,
        tiled=True,
    )
    return (
        block_out,
        dx.reshape(micro, rows, quarter),
        vector_grads[0],
        vector_grads[1],
        column_group_back(grad_qkv, 3),
        row_group_back(grad_wo),
        vector_grads[2],
        vector_grads[3],
        column_group_back(grad_up, 1),
        row_group_back(grad_down),
        grad_in[None],
        grad_out[None],
        grad_expert_gain[None],
        grad_expert_bias[None],
        grad_centroid[None],
    )


MESH = pl.DeviceIdType.MESH
KEYS = 320
CHUNK = 128


def tn(a, b):
    return lax.dot_general(a, b, (((0,), (0,)), ((), ())), preferred_element_type=f32)


def nt(a, b):
    return lax.dot_general(a, b, (((1,), (1,)), ((), ())), preferred_element_type=f32)


def tanh_parts(v):
    root = 0.7978845608028654
    t = jnp.tanh(root * (v + 0.044715 * (v * v * v)))
    return t, root


def gelu_both(v):
    t, root = tanh_parts(v)
    half = 0.5 * (1.0 + t)
    return v * half, half + 0.5 * v * (1.0 - t * t) * root * (1.0 + 0.134145 * (v * v))


def to_rows(columns):
    lane = lax.broadcasted_iota(jnp.int32, (columns[0].shape[0], 128), 1)
    wide = jnp.zeros(lane.shape, f32)
    for i, column in enumerate(columns):
        wide = jnp.where(lane == i, column, wide)
    return wide.T[:8]


def to_columns(rows):
    return jnp.concatenate([rows, jnp.zeros((120, rows.shape[1]), f32)], axis=0).T


def layout(dims):
    S, G, M, T, D, Q, FQ, C, sh, shd = dims
    nz = G // 2
    R = G * C
    heads = HEADS // S
    return dict(
        wqkv=((S, nz, 2, sh, 3 * Q), bf16),
        wo=((nz, 2, sh, D), bf16),
        wup=((S, nz, 2, sh, FQ), bf16),
        wdn=((nz, 2, shd, D), bf16),
        win=((S, nz, 2, sh, FQ), bf16),
        wout=((nz, 2, shd, D), bf16),
        vg=((S, G, 8, 128), f32),
        vecs=((8, D), f32),
        evec=((8, D), f32),
        mask=((M, T, T), f32),
        perm=((M, R, T), bf16),
        cots=((M, R, Q), bf16),
        y2s=((M, R, Q), bf16),
        ges=((M, R, Q), bf16),
        dxs=((M, R, Q), bf16),
        ger=((M, R, Q), bf16),
        dxr=((M, R, Q), bf16),
        tst=((M, T, 128), f32),
        est=((M, R, 128), f32),
        a1=((M, T, D), bf16),
        a2=((M, T, D), bf16),
        qkv=((M, T, 3 * Q), bf16),
        probs=((M, heads, T, T), f32),
        o=((M, T, Q), bf16),
        y1=((M, T, D), bf16),
        h=((M, T, FQ), f32),
        u=((M, T, FQ), bf16),
        y2q=((M, T, Q), bf16),
        xe=((M, R, D), bf16),
        dge=((M, R, D), bf16),
        en=((M, R, D), bf16),
        ue=((M, R, FQ), bf16),
        dhe=((M, R, FQ), bf16),
        dfe=((M, R, D), bf16),
        slope=((R, FQ), f32),
        fes=((M, S - 1, R, Q), bf16),
        fer=((M, S - 1, R, Q), bf16),
        feo=((M, R, Q), f32),
        dns=((M, S - 1, R, Q), bf16),
        dnr=((M, S - 1, R, Q), bf16),
        dno=((M, R, Q), f32),
        ess=((M, 8, R), f32),
        esr=((M, S - 1, 8, R), f32),
        ts=((M, S - 1, T, Q), bf16),
        r1=((M, S - 1, T, Q), bf16),
        r2=((M, S - 1, T, Q), bf16),
        own=((M, T, Q), f32),
        tss=((2, M, 8, T), f32),
        tsr=((2, M, S - 1, 8, T), f32),
        dy2=((M, T, D), bf16),
        dh=((M, T, FQ), bf16),
        dqkv=((M, T, 3 * Q), bf16),
        gwo=((nz, 2, sh, D), bf16),
        gqk=((S, nz, 2, sh, 3 * Q), bf16),
        bdn=((nz, shd, D), bf16),
        bup=((S, nz, sh, FQ), bf16),
        bwo=((nz, sh, D), bf16),
        bqk=((S, nz, sh, 3 * Q), bf16),
        zdn=((nz - 1, shd, D), bf16),
        zup=((nz - 1, S, sh, FQ), bf16),
        zwo=((nz - 1, sh, D), bf16),
        zqk=((nz - 1, S, sh, 3 * Q), bf16),
        ups=((S, sh, FQ), bf16),
        upr=((S - 1, sh, FQ), bf16),
        qks=((S, sh, 3 * Q), bf16),
        qkr=((S - 1, sh, 3 * Q), bf16),
        stage=((2, 256, D), f32),
        vsum=((8, Q), f32),
        vsr=((G - 1, 8, Q), f32),
    )


INPUTS = [
    "hidden",
    "cot",
    "bucket",
    "live",
    "routes",
    "vin",
    "ein",
    "wqkv_in",
    "wo_in",
    "wup_in",
    "wdn_in",
    "win_in",
    "wout_in",
]
OUTPUTS = [
    "out",
    "dx",
    "vgo",
    "gqk_out",
    "gwo_out",
    "gup_out",
    "gdn_out",
    "gin_out",
    "gout_out",
    "evo",
]


def block_kernel(dims, names, *args):
    r = types.SimpleNamespace(**dict(zip(names, args)))
    S, G, M, T, D, Q, FQ, C, sh, shd = dims
    nz = G // 2
    R = G * C
    heads = HEADS // S
    size = D // HEADS
    scale = size ** (-0.5)
    s = lax.axis_index("section")
    d = lax.axis_index("dp")
    z = lax.div(d, 2)
    c = lax.rem(d, 2)
    beside = (s, d + 1 - 2 * c)
    near = z + 1 - 2 * lax.rem(z, 2)
    far = lax.rem(z + 2, nz)
    near_far = lax.rem(near + 2, nz)

    def sec(i):
        return lax.rem(s + i, S)

    def dpi(j):
        return lax.rem(d + j, G)

    def zi(j):
        return lax.rem(z + j, nz)

    def to_sec(i):
        return (sec(i), d)

    def to_dp(j):
        return (s, dpi(j))

    def to_z(j):
        return (s, zi(j) * 2 + c)

    def col(q, n=Q):
        return pl.ds(pl.multiple_of(q * n, n), n)

    def seats(e):
        return pl.ds(pl.multiple_of(e * C, C), C)

    mine = col(s)
    places = {}
    pending = {}

    def copy(src, dst, k, device):
        i = places.setdefault(k, len(places))
        return pltpu.make_async_remote_copy(
            src_ref=src,
            dst_ref=dst,
            send_sem=r.ssem.at[i],
            recv_sem=r.rsem.at[i],
            device_id=device,
            device_id_type=MESH,
        )

    def send(src, dst, k, device):
        pending[k] = copy(src, dst, k, device)
        pending[k].start()

    def sent(k):
        pending.pop(k).wait_send()

    def recv(dst, k):
        copy(dst, dst, k, beside).wait_recv()

    def each(rows, body):
        step = math.gcd(rows, CHUNK)

        @pl.loop(0, rows // step)
        def _(i):
            body(pl.ds(pl.multiple_of(i * step, step), step))

    others = range(1, S)

    def gather_send(ref, m, k):
        for i in others:
            send(ref.at[m, :, mine], ref.at[m, :, mine], (k, m, i), to_sec(i))

    def gather_recv(ref, m, k):
        for i in others:
            recv(ref.at[m, :, col(sec(S - i))], (k, m, i))

    def sum_send(tile, out, arrive, own, m, k, before=None, hold=False):
        for i in others:
            if before is not None:
                sent((before, m, i))
            out[m, i - 1] = tile(sec(i)).astype(bf16)
            if not hold:
                send(out.at[m, i - 1], arrive.at[m, i - 1], (k, m, i), to_sec(i))
        own[m] = tile(s)

    def sum_start(out, arrive, m, k):
        for i in others:
            send(out.at[m, i - 1], arrive.at[m, i - 1], (k, m, i), to_sec(i))

    def sum_recv(arrive, m, k):
        for i in others:
            recv(arrive.at[m, i - 1], (k, m, i))

    def summed(own, arrive, m, rows):
        total = own[m, rows]
        for i in others:
            total += arrive[m, i - 1, rows].astype(f32)
        return total

    def dispatch_send(src, dst, m, k):
        dst[m, seats(d), mine] = src[m, seats(d)]
        for j in range(1, G):
            send(src.at[m, seats(dpi(j))], dst.at[m, seats(d), mine], (k, m, j), to_dp(j))

    def dispatch_recv(dst, m, k):
        for j in range(1, G):
            recv(dst.at[m, seats(dpi(G - j)), mine], (k, m, j))

    def return_send(src, dst, m, k):
        dst[m, seats(d)] = src[m, seats(d)]
        for j in range(1, G):
            send(src.at[m, seats(dpi(j))], dst.at[m, seats(d)], (k, m, j), to_dp(j))

    def return_recv(dst, m, k):
        for j in range(1, G):
            recv(dst.at[m, seats(dpi(G - j))], (k, m, j))

    def part(ref, zz, cc):
        return ref.at[:, zz, cc] if len(ref.shape) == 5 else ref.at[zz, cc]

    def weight_start(ref, k):
        send(part(ref, z, c), part(ref, z, c), (k, "far"), (s, far * 2 + c))
        send(part(ref, z, c), part(ref, z, c), (k, "c", 0), beside)

    def weight_next(ref, k):
        send(part(ref, z, c), part(ref, z, c), (k, "near"), (s, near * 2 + c))

    def weight_far(ref, k):
        recv(part(ref, far, c), (k, "far"))
        send(part(ref, far, c), part(ref, far, c), (k, "near far"), (s, near * 2 + c))
        send(part(ref, far, c), part(ref, far, c), (k, "c", 1), beside)

    def weight_near(ref, k):
        recv(part(ref, near, c), (k, "near"))
        send(part(ref, near, c), part(ref, near, c), (k, "c", 2), beside)
        recv(part(ref, near_far, c), (k, "near far"))
        send(part(ref, near_far, c), part(ref, near_far, c), (k, "c", 3), beside)

    def weight_wait(ref, k):
        for i, zz in enumerate((z, far, near, near_far)):
            recv(part(ref, zz, 1 - c), (k, "c", i))

    load_in = pltpu.make_async_copy(r.win_in, r.win, r.lsem.at[0])
    load_out = pltpu.make_async_copy(r.wout_in, r.wout, r.lsem.at[1])

    early = lax.broadcasted_iota(jnp.int32, (T, T), 0)
    late = lax.broadcasted_iota(jnp.int32, (T, T), 1)

    def seat_tokens(m):
        route = r.routes[m : m + 1, :]
        expert_ids = lax.broadcasted_iota(jnp.int32, (G, T), 0)
        picks = jnp.where(expert_ids == route, 1.0, 0.0)
        before = jnp.where(early < late, 1.0, 0.0).astype(bf16)
        counts = jnp.dot(picks.astype(bf16), before, preferred_element_type=f32)
        rank = jnp.sum(counts * picks, axis=0, keepdims=True)
        place = route.astype(f32) * float(C) + rank
        seat_ids = lax.broadcasted_iota(jnp.int32, (R, T), 0).astype(f32)
        r.perm[m] = jnp.where(seat_ids == place, 1.0, 0.0).astype(bf16)
        r.cots[m] = jnp.dot(r.perm[m], r.cot[m, :, mine], preferred_element_type=f32).astype(bf16)

    def entry():
        barrier = pltpu.get_barrier_semaphore()
        for i in others:
            pl.semaphore_signal(barrier, inc=1, device_id=to_sec(i), device_id_type=MESH)
        for j in range(1, G):
            pl.semaphore_signal(barrier, inc=1, device_id=to_dp(j), device_id_type=MESH)
        r.vg[s, d] = r.vin[...]
        r.evec[:, mine] = r.ein[...]
        for piece in range(3):
            r.wqkv[s, z, c, :, piece * Q : (piece + 1) * Q] = r.wqkv_in[
                :, pl.ds(pl.multiple_of(piece * D + s * Q, Q), Q)
            ]
        r.wo[z, c] = r.wo_in[...]
        seat_tokens(0)
        seat_tokens(1)
        pl.semaphore_wait(barrier, S + G - 2)
        for i in others:
            send(r.vin, r.vg.at[s, d], ("v1", i), to_sec(i))
        for i in others:
            for piece in range(3):
                src = r.wqkv_in.at[:, pl.ds(pl.multiple_of(piece * D + sec(i) * Q, Q), Q)]
                dst = r.wqkv.at[s, z, c, :, piece * Q : (piece + 1) * Q]
                send(src, dst, ("q1", piece, i), to_sec(i))
        dispatch_send(r.cots, r.dge, 0, "cot")
        dispatch_send(r.cots, r.dge, 1, "cot")
        for i in others:
            send(r.wup_in.at[:, col(sec(i), FQ)], r.wup.at[s, z, c], ("u1", i), to_sec(i))
            send(r.ein, r.evec.at[:, mine], ("e1", i), to_sec(i))
        for i in others:
            recv(r.vg.at[sec(S - i), d], ("v1", i))
        for j in range(1, G):
            send(r.vg.at[:, d], r.vg.at[:, d], ("v2", j), to_dp(j))
        for i in others:
            for piece in range(3):
                recv(r.wqkv.at[sec(S - i), z, c, :, piece * Q : (piece + 1) * Q], ("q1", piece, i))
        weight_start(r.wqkv, "wqkv")
        weight_next(r.wqkv, "wqkv")
        load_in.start()
        load_out.start()

    def mask_tokens(m):
        end = r.bucket[m, 0]
        seg_q = (early >= end).astype(jnp.int32)
        seg_k = (late >= end).astype(jnp.int32)
        for b in range(1, r.bucket.shape[1]):
            end = end + r.bucket[m, b]
            seg_q += (early >= end).astype(jnp.int32)
            seg_k += (late >= end).astype(jnp.int32)
        live = jnp.broadcast_to(r.live[m : m + 1, :], (T, T))
        allowed = (seg_q == seg_k) & (late <= early) & ((live == 1) | (late == early))
        r.mask[m] = jnp.where(allowed, 1.0, 0.0)

    def spread_vectors():
        for j in range(1, G):
            recv(r.vg.at[:, dpi(G - j)], ("v2", j))
        spread_row = lax.broadcasted_iota(jnp.int32, (128, D), 0)
        spread_lane = lax.broadcasted_iota(jnp.int32, (128, D), 1)
        spread = jnp.where(lax.rem(spread_lane, sh) == spread_row, 1.0, 0.0).astype(bf16)
        stacked = r.vg[...].reshape(S * G * 8, 128).astype(bf16)
        wide = jnp.dot(stacked, spread, preferred_element_type=f32)
        row_id = lax.broadcasted_iota(jnp.int32, (S * G * 8, D), 0)
        lane_id = lax.broadcasted_iota(jnp.int32, (S * G * 8, D), 1)
        low = lax.shift_right_logical(row_id, 3) * sh
        wide = jnp.where((lane_id >= low) & (lane_id < low + sh), wide, 0.0)
        r.vecs[...] = jnp.sum(wide.reshape(S * G, 8, D), axis=0)

    def normed(values):
        mean = jnp.mean(values, axis=1, keepdims=True)
        center = values - mean
        rs = lax.rsqrt(jnp.mean(center * center, axis=1, keepdims=True) + epsilon)
        return center * rs, mean, rs

    def norm_tokens(src, dst, m, at):
        gain = r.vecs[2 * at : 2 * at + 1, :]
        bias = r.vecs[2 * at + 1 : 2 * at + 2, :]

        def body(rows):
            n, mean, rs = normed(src[m, rows].astype(f32))
            r.tst[m, rows, 2 * at : 2 * at + 1] = mean
            r.tst[m, rows, 2 * at + 1 : 2 * at + 2] = rs
            dst[m, rows] = (n * gain + bias).astype(bf16)

        each(T, body)

    entry()
    r.wup[s, z, c] = r.wup_in[:, col(s, FQ)]
    r.wdn[z, c] = r.wdn_in[...]
    mask_tokens(0)
    mask_tokens(1)
    for m in range(M):
        dispatch_recv(r.dge, m, "cot")
        gather_send(r.dge, m, "dge")
    weight_far(r.wqkv, "wqkv")
    weight_start(r.wo, "wo")
    weight_next(r.wo, "wo")
    for i in others:
        recv(r.evec.at[:, col(sec(S - i))], ("e1", i))
        recv(r.wup.at[sec(S - i), z, c], ("u1", i))
    weight_start(r.wup, "wup")
    spread_vectors()
    norm_tokens(r.hidden, r.a1, 0, 0)
    norm_tokens(r.hidden, r.a1, 1, 0)
    weight_near(r.wqkv, "wqkv")
    weight_far(r.wo, "wo")
    weight_next(r.wup, "wup")
    weight_wait(r.wqkv, "wqkv")

    def attend(m):
        @pl.loop(0, 3)
        def _(t):
            w = r.wqkv[:, :, :, :, col(t)].reshape(D, Q)
            r.qkv[m, :, col(t)] = jnp.dot(r.a1[m], w, preferred_element_type=f32).astype(bf16)

        for hh in range(heads):
            at = hh * size
            q = r.qkv[m, :, at : at + size]
            k = r.qkv[m, :, Q + at : Q + at + size]
            v = r.qkv[m, :, 2 * Q + at : 2 * Q + at + size]
            scores = jnp.where(r.mask[m] > 0.0, nt(q, k) * scale, masked_value)
            weights = jnp.exp(scores - jnp.max(scores, axis=1, keepdims=True))
            p = weights / jnp.sum(weights, axis=1, keepdims=True)
            r.probs[m, hh] = p
            mixed = jnp.dot(p.astype(bf16), v, preferred_element_type=f32)
            r.o[m, :, at : at + size] = mixed.astype(bf16)

    def y1_tile(m):
        return lambda q: jnp.dot(
            r.o[m], r.wo[:, :, :, col(q)].reshape(Q, Q), preferred_element_type=f32
        )

    def finish_y1(m):
        sum_recv(r.r1, m, "y1")

        def body(rows):
            total = r.hidden[m, rows, mine].astype(f32) + summed(r.own, r.r1, m, rows)
            r.y1[m, rows, mine] = total.astype(bf16)

        each(T, body)
        gather_send(r.y1, m, "y1g")

    attend(0)
    weight_near(r.wo, "wo")
    weight_wait(r.wo, "wo")
    sum_send(y1_tile(0), r.ts, r.r1, r.own, 0, "y1")
    attend(1)
    sum_send(y1_tile(1), r.ts, r.r1, r.own, 1, "y1")
    weight_far(r.wup, "wup")
    weight_start(r.wdn, "wdn")
    weight_next(r.wdn, "wdn")
    finish_y1(0)
    finish_y1(1)
    weight_near(r.wup, "wup")
    weight_wait(r.wup, "wup")

    def up(m):
        gather_recv(r.y1, m, "y1g")
        norm_tokens(r.y1, r.a2, m, 1)

        @pl.loop(0, FQ // Q)
        def _(t):
            w = r.wup[:, :, :, :, col(t)].reshape(D, Q)
            pre = jnp.dot(r.a2[m], w, preferred_element_type=f32)
            value, slope = gelu_both(pre)
            r.u[m, :, col(t)] = value.astype(bf16)
            r.h[m, :, col(t)] = slope

    def y2_tile(m):
        return lambda q: jnp.dot(
            r.u[m], r.wdn[:, :, :, col(q)].reshape(FQ, Q), preferred_element_type=f32
        )

    weight_far(r.wdn, "wdn")
    up(0)
    up(1)
    weight_near(r.wdn, "wdn")
    weight_wait(r.wdn, "wdn")
    sum_send(y2_tile(0), r.ts, r.r2, r.own, 0, "y2", "y1")
    sum_send(y2_tile(1), r.ts, r.r2, r.own, 1, "y2", "y1")

    def finish_y2(m):
        sum_recv(r.r2, m, "y2")

        def body(rows):
            total = r.y1[m, rows, mine].astype(f32) + summed(r.own, r.r2, m, rows)
            r.y2q[m, rows] = total.astype(bf16)

        each(T, body)
        r.y2s[m] = jnp.dot(r.perm[m], r.y2q[m], preferred_element_type=f32).astype(bf16)
        dispatch_send(r.y2s, r.xe, m, "y2d")

    finish_y2(0)
    finish_y2(1)
    for m in range(M):
        dispatch_recv(r.xe, m, "y2d")
        gather_send(r.xe, m, "xe")
    load_in.wait()
    load_out.wait()

    def expert(m):
        gather_recv(r.dge, m, "dge")
        gather_recv(r.xe, m, "xe")
        gain, bias, centroid = r.evec[0:1, :], r.evec[1:2, :], r.evec[2:3, :]

        def body(rows):
            v = r.xe[m, rows].astype(f32)
            n, mean, rs = normed(v)
            alpha = jax.nn.sigmoid(jnp.sum(v * centroid, axis=1, keepdims=True))
            r.est[m, rows, 0:1] = mean
            r.est[m, rows, 1:2] = rs
            r.est[m, rows, 2:3] = alpha
            r.en[m, rows] = (n * gain + bias).astype(bf16)
            r.dfe[m, rows] = (alpha * r.dge[m, rows].astype(f32)).astype(bf16)

        each(R, body)

        @pl.loop(0, FQ // Q)
        def _(t):
            w = r.win[:, :, :, :, col(t)].reshape(D, Q)
            pre = jnp.dot(r.en[m], w, preferred_element_type=f32)
            value, slope = gelu_both(pre)
            r.ue[m, :, col(t)] = value.astype(bf16)
            r.slope[:, col(t)] = slope

        stats = [jnp.zeros((R, 1), f32) for _ in range(3)]

        def fe_tile(q):
            tile = jnp.dot(
                r.ue[m], r.wout[:, :, :, col(q)].reshape(FQ, Q), preferred_element_type=f32
            )
            stats[2] += jnp.sum(tile * r.dge[m, :, col(q)].astype(f32), axis=1, keepdims=True)
            return tile

        def den_tile(q):
            tile = nt(r.dhe[m], r.win[q].reshape(Q, FQ))
            scaled = tile * r.evec[0:1, col(q)]
            n = (r.xe[m, :, col(q)].astype(f32) - r.est[m, :, 0:1]) * r.est[m, :, 1:2]
            stats[0] += jnp.sum(scaled, axis=1, keepdims=True)
            stats[1] += jnp.sum(scaled * n, axis=1, keepdims=True)
            return tile

        @pl.loop(0, FQ // Q)
        def _(t):
            due = nt(r.dfe[m], r.wout[t].reshape(Q, D))
            r.dhe[m, :, col(t)] = (due * r.slope[:, col(t)]).astype(bf16)

        sum_send(den_tile, r.dns, r.dnr, r.dno, m, "den")
        sum_send(fe_tile, r.fes, r.fer, r.feo, m, "fe", hold=True)
        r.ess[m] = to_rows(stats)
        for i in others:
            send(r.ess.at[m], r.esr.at[m, i - 1], ("est", m, i), to_sec(i))

    expert(0)
    expert(1)

    def finish_den(m):
        sum_recv(r.dnr, m, "den")
        total = r.ess[m]
        for i in others:
            recv(r.esr.at[m, i - 1], ("est", m, i))
            total += r.esr[m, i - 1]
        r.est[m, :, 8:16] = to_columns(total)[:, 0:8]
        gain, centroid = r.evec[0:1, mine], r.evec[2:3, mine]
        if m == 0:
            r.evo[...] = jnp.zeros_like(r.evo)

        def body(rows):
            den = summed(r.dno, r.dnr, m, rows)
            xq = r.xe[m, rows, mine].astype(f32)
            rs, alpha = r.est[m, rows, 1:2], r.est[m, rows, 2:3]
            n = (xq - r.est[m, rows, 0:1]) * rs
            m1, m2 = r.est[m, rows, 8:9] * (1.0 / D), r.est[m, rows, 9:10] * (1.0 / D)
            dlogit = r.est[m, rows, 10:11] * alpha * (1.0 - alpha)
            grad = rs * (gain * den - m1 - n * m2) + dlogit * centroid
            r.dxs[m, rows] = grad.astype(bf16)
            r.evo[0:1, :] += jnp.sum(den * n, axis=0, keepdims=True)
            r.evo[1:2, :] += jnp.sum(den, axis=0, keepdims=True)
            r.evo[2:3, :] += jnp.sum(dlogit * xq, axis=0, keepdims=True)

        each(R, body)
        return_send(r.dxs, r.dxr, m, "dxb")

    def finish_fe(m):
        sum_recv(r.fer, m, "fe")

        def body(rows):
            fe = summed(r.feo, r.fer, m, rows)
            r.ges[m, rows] = (r.est[m, rows, 2:3] * fe).astype(bf16)

        each(R, body)
        return_send(r.ges, r.ger, m, "geb")

    finish_den(0)
    finish_den(1)

    writes = []

    def expert_weights(left, right, out):
        for t in range(D // 256):
            slot = len(writes) % 2
            if len(writes) >= 2:
                writes[-2].wait()
            rows = slice(t * 256, (t + 1) * 256)
            lhs = left[:, :, rows].reshape(M * R, 256)
            r.stage[slot] = tn(lhs, right[...].reshape(M * R, D))
            writes.append(pltpu.make_async_copy(r.stage.at[slot], out.at[rows], r.lsem.at[2 + slot]))
            writes[-1].start()

    expert_weights(r.en, r.dhe, r.gin_out)

    def finish_dxe(m):
        return_recv(r.dxr, m, "dxb")
        back = tn(r.perm[m], r.dxr[m])
        r.dy2[m, :, mine] = (r.cot[m, :, mine].astype(f32) + back).astype(bf16)
        gather_send(r.dy2, m, "dy2")

    finish_dxe(0)
    finish_dxe(1)
    expert_weights(r.ue, r.dfe, r.gout_out)

    def token_stats(m, at, src):
        stats = [jnp.zeros((T, 1), f32) for _ in range(2)]

        def add(q, tile):
            scaled = tile * r.vecs[2 * at : 2 * at + 1, col(q)]
            mean, rs = r.tst[m, :, 2 * at : 2 * at + 1], r.tst[m, :, 2 * at + 1 : 2 * at + 2]
            n = (src[m, :, col(q)].astype(f32) - mean) * rs
            stats[0] += jnp.sum(scaled, axis=1, keepdims=True)
            stats[1] += jnp.sum(scaled * n, axis=1, keepdims=True)
            return tile

        return stats, add

    def stats_send(m, at, stats):
        r.tss[at, m] = to_rows(stats)
        for i in others:
            send(r.tss.at[at, m], r.tsr.at[at, m, i - 1], ("tst", at, m, i), to_sec(i))

    def stats_recv(m, at):
        total = r.tss[at, m]
        for i in others:
            recv(r.tsr.at[at, m, i - 1], ("tst", at, m, i))
            total += r.tsr[at, m, i - 1]
        r.tst[m, :, 8:16] = to_columns(total)[:, 0:8]

    def dense_back(m):
        if m == 0:
            gather_recv(r.dy2, m, "dy2")

        @pl.loop(0, FQ // Q)
        def _(t):
            du = nt(r.dy2[m], r.wdn[t].reshape(Q, D))
            r.dh[m, :, col(t)] = (du * r.h[m, :, col(t)]).astype(bf16)

        stats, add = token_stats(m, 1, r.y1)
        sum_send(
            lambda q: add(q, nt(r.dh[m], r.wup[q].reshape(Q, FQ))),
            r.ts,
            r.r1,
            r.own,
            m,
            "da2",
            "y2",
        )
        stats_send(m, 1, stats)

    def norm_back(m, at, src, grad_in, own, arrive, emit):
        gain = r.vecs[2 * at : 2 * at + 1, mine]

        def body(rows):
            grad = summed(own, arrive, m, rows)
            mean, rs = r.tst[m, rows, 2 * at : 2 * at + 1], r.tst[m, rows, 2 * at + 1 : 2 * at + 2]
            n = (src[m, rows, mine].astype(f32) - mean) * rs
            m1, m2 = r.tst[m, rows, 8:9] * (1.0 / D), r.tst[m, rows, 9:10] * (1.0 / D)
            emit(rows, grad_in[m, rows, mine].astype(f32) + rs * (gain * grad - m1 - n * m2))
            r.vsum[2 * at : 2 * at + 1, :] += jnp.sum(grad * n, axis=0, keepdims=True)
            r.vsum[2 * at + 1 : 2 * at + 2, :] += jnp.sum(grad, axis=0, keepdims=True)

        each(T, body)

    def finish_da2(m):
        sum_recv(r.r1, m, "da2")
        stats_recv(m, 1)
        for i in others:
            sent(("y1g", m, i))

        def emit(rows, value):
            r.y1[m, rows, mine] = value.astype(bf16)

        norm_back(m, 1, r.y1, r.dy2, r.own, r.r1, emit)
        gather_send(r.y1, m, "dy1")

    def grads_pair(g, b, k):
        src = g.at[:, :, 1 - c] if len(g.shape) == 5 else g.at[:, 1 - c]
        send(src, b, (k, "p"), beside)

    def grads_add(g, zz, arrive):
        if len(g.shape) == 5:

            @pl.loop(0, S)
            def _(q):
                g[q, zz, c] = (g[q, zz, c].astype(f32) + arrive[q].astype(f32)).astype(bf16)
        else:
            g[zz, c] = (g[zz, c].astype(f32) + arrive[...].astype(f32)).astype(bf16)

    def grads_paired(g, b, k):
        recv(b, (k, "p"))
        for zz in range(nz):
            grads_add(g, zz, b.at[:, zz] if len(g.shape) == 5 else b.at[zz])

    def grads_near(g, b, arrive, k):
        grads_paired(g, b, k)
        send(part(g, near_far, c), arrive.at[1], (k, "nf"), (s, near * 2 + c))
        send(part(g, near, c), arrive.at[0], (k, "n"), (s, near * 2 + c))

    def grads_far(g, arrive, k):
        recv(arrive.at[1], (k, "nf"))
        grads_add(g, far, arrive.at[1])
        send(part(g, far, c), arrive.at[2], (k, "f"), (s, far * 2 + c))

    def grads_near_recv(arrive, k):
        recv(arrive.at[0], (k, "n"))
        recv(arrive.at[2], (k, "f"))
        return 0, 2

    def down_weights():
        @pl.loop(0, nz)
        def _(t):
            lhs = r.u[:, :, col(t)].reshape(M * T, Q)
            grad = tn(lhs, r.dy2[...].reshape(M * T, D))
            r.wout[t] = grad.astype(bf16).reshape(2, shd, D)

        grads_pair(r.wout, r.bdn, "gdn")

    def up_weights():
        @pl.loop(0, S)
        def _(t):
            lhs = r.a2[:, :, col(t)].reshape(M * T, Q)
            grad = tn(lhs, r.dh[...].reshape(M * T, FQ))
            r.win[t] = grad.astype(bf16).reshape(nz, 2, sh, FQ)

        grads_pair(r.win, r.bup, "gup")

    def attention_weights():
        @pl.loop(0, S)
        def _(t):
            lhs = r.a1[:, :, col(t)].reshape(M * T, Q)
            grad = tn(lhs, r.dqkv[...].reshape(M * T, 3 * Q))
            r.gqk[t] = grad.astype(bf16).reshape(nz, 2, sh, 3 * Q)

        grads_pair(r.gqk, r.bqk, "gqk")
        grad = tn(r.o[...].reshape(M * T, Q), r.y1[...].reshape(M * T, D))
        r.gwo[...] = grad.astype(bf16).reshape(nz, 2, sh, D)
        grads_pair(r.gwo, r.bwo, "gwo")

    r.vsum[...] = jnp.zeros_like(r.vsum)
    dense_back(0)
    gather_recv(r.dy2, 1, "dy2")
    down_weights()
    dense_back(1)
    finish_da2(0)
    grads_near(r.wout, r.bdn, r.zdn, "gdn")
    up_weights()
    finish_da2(1)
    grads_near(r.win, r.bup, r.zup, "gup")

    def attend_back(m):
        gather_recv(r.y1, m, "dy1")
        sum_start(r.fes, r.fer, m, "fe")
        out_grad = nt(r.y1[m], r.wo[...].reshape(Q, D)).astype(bf16)
        for hh in range(heads):
            at = hh * size
            q = r.qkv[m, :, at : at + size]
            k = r.qkv[m, :, Q + at : Q + at + size]
            v = r.qkv[m, :, 2 * Q + at : 2 * Q + at + size]
            go = out_grad[:, at : at + size]
            p = r.probs[m, hh]
            dp = nt(go, v)
            dv = tn(p.astype(bf16), go)
            ds = (p * (dp - jnp.sum(p * dp, axis=1, keepdims=True))).astype(bf16)
            dq = jnp.dot(ds, k, preferred_element_type=f32) * scale
            dk = tn(ds, q) * scale
            r.dqkv[m, :, at : at + size] = dq.astype(bf16)
            r.dqkv[m, :, Q + at : Q + at + size] = dk.astype(bf16)
            r.dqkv[m, :, 2 * Q + at : 2 * Q + at + size] = dv.astype(bf16)
        stats, add = token_stats(m, 0, r.hidden)
        sum_send(
            lambda q: add(q, nt(r.dqkv[m], r.wqkv[q].reshape(Q, 3 * Q))),
            r.ts,
            r.r2,
            r.own,
            m,
            "da1",
            "da2",
        )
        stats_send(m, 0, stats)

    def finish_da1(m):
        sum_recv(r.r2, m, "da1")
        stats_recv(m, 0)

        def emit(rows, value):
            r.dx[m, rows] = value

        norm_back(m, 0, r.hidden, r.y1, r.own, r.r2, emit)

    attend_back(0)
    grads_far(r.wout, r.zdn, "gdn")
    attend_back(1)
    grads_far(r.win, r.zup, "gup")
    attention_weights()
    finish_da1(0)
    grads_near(r.gqk, r.bqk, r.zqk, "gqk")
    grads_near(r.gwo, r.bwo, r.zwo, "gwo")
    finish_fe(0)
    finish_da1(1)
    for j in range(1, G):
        send(r.vsum, r.vsr.at[j - 1], ("vs", j), to_dp(j))
    finish_fe(1)
    grads_far(r.gqk, r.zqk, "gqk")
    grads_far(r.gwo, r.zwo, "gwo")

    def finish_out(m):
        return_recv(r.ger, m, "geb")
        back = tn(r.perm[m], r.ger[m])
        r.out[m] = (r.y2q[m].astype(f32) + back).astype(bf16)

    finish_out(0)
    finish_out(1)

    def row_result(g, arrive, out, k, rows, wait):
        slots = wait(arrive, k)
        mine_part = part(g, z, c)

        def body(at):
            total = mine_part[at].astype(f32)
            for slot in slots:
                total += arrive[slot, at].astype(f32)
            out[at] = total

        each(rows, body)

    def column_send(g, arrive, out, back, k, wait):
        slots = wait(arrive, k)

        @pl.loop(0, S)
        def _(q):
            total = g[q, z, c].astype(f32)
            for slot in slots:
                total += arrive[slot, q].astype(f32)
            out[q] = total.astype(bf16)

        for i in others:
            send(out.at[sec(i)], back.at[i - 1], (k, "s", i), to_sec(i))

    def column_result(sums, back, out, pieces, k):
        width = sums.shape[2] // pieces
        for i in range(S):
            if i:
                recv(back.at[i - 1], (k, "s", i))
            q = sec(S - i) if i else s
            value = (back[i - 1] if i else sums[s]).astype(f32)
            for piece in range(pieces):
                at = pl.ds(pl.multiple_of(piece * S * width + q * width, width), width)
                out[:, at] = value[:, piece * width : (piece + 1) * width]

    row_result(r.wout, r.zdn, r.gdn_out, "gdn", shd, grads_near_recv)
    column_send(r.win, r.zup, r.ups, r.upr, "gup", grads_near_recv)
    column_send(r.gqk, r.zqk, r.qks, r.qkr, "gqk", grads_near_recv)
    row_result(r.gwo, r.zwo, r.gwo_out, "gwo", sh, grads_near_recv)
    total = r.vsum[...]
    for j in range(1, G):
        recv(r.vsr.at[j - 1], ("vs", j))
        total += r.vsr[j - 1]
    r.vgo[...] = total
    column_result(r.ups, r.upr, r.gup_out, 1, "gup")
    column_result(r.qks, r.qkr, r.gqk_out, 3, "gqk")
    for write in writes[-2:]:
        write.wait()
    for k in list(pending):
        sent(k)
    assert len(places) <= KEYS, len(places)


def hand_over(*refs):
    count = len(refs) // 2
    first = pl.program_id(0) == 0
    for src, dst in zip(refs[:count], refs[count:]):
        if src.shape[0] == 256 and src.shape[1] == 1024:
            dst[...] = src[...]
        else:

            @pl.when(first)
            def _(src=src, dst=dst):
                dst[...] = src[...]


def with_kernel(
    hidden_in,
    cotangent,
    bucket_len,
    live_mask,
    routes,
    ln1_gain,
    ln1_bias,
    w_qkv,
    w_attn_out,
    ln2_gain,
    ln2_bias,
    w_up,
    w_down,
    expert_in,
    expert_out,
    expert_gain,
    expert_bias,
    centroids,
):
    S = lax.axis_size("section")
    G = lax.axis_size("dp")
    M, T, D = hidden_in.shape
    Q = D // S
    FQ = w_up.shape[1] // S
    C = 3 * T // (2 * G)
    sh, shd = w_up.shape[0], w_down.shape[0]
    dims = (S, G, M, T, D, Q, FQ, C, sh, shd)
    vin = jnp.stack([ln1_gain, ln1_bias, ln2_gain, ln2_bias]).astype(f32)
    vin = jnp.pad(vin, ((0, 4), (0, 128 - sh)))
    ein = jnp.concatenate([expert_gain, expert_bias, centroids]).astype(f32)
    ein = jnp.pad(ein, ((0, 5), (0, 0)))
    scratch = layout(dims)
    names = INPUTS + OUTPUTS + list(scratch) + ["ssem", "rsem", "lsem"]
    vmem = pl.BlockSpec(memory_space=pltpu.VMEM)
    smem = pl.BlockSpec(memory_space=pltpu.SMEM)
    anywhere = pl.BlockSpec(memory_space=pl.ANY)
    shapes = (
        ((M, T, Q), bf16),
        ((M, T, Q), f32),
        ((8, Q), f32),
        ((sh, 3 * D), f32),
        ((sh, D), f32),
        ((sh, S * FQ), f32),
        ((shd, D), f32),
        ((D, FQ), f32),
        ((FQ, D), f32),
        ((8, Q), f32),
    )
    outs = pl.pallas_call(
        functools.partial(block_kernel, dims, names),
        name="block",
        out_shape=[jax.ShapeDtypeStruct(*shape) for shape in shapes],
        in_specs=[vmem, vmem, smem] + [vmem] * 8 + [anywhere] * 2,
        out_specs=[vmem] * 7 + [anywhere] * 2 + [vmem],
        scratch_shapes=[pltpu.VMEM(*shape) for shape in scratch.values()]
        + [pltpu.SemaphoreType.DMA((KEYS,))] * 2
        + [pltpu.SemaphoreType.DMA((4,))],
        compiler_params=pltpu.CompilerParams(
            collective_id=0, has_side_effects=True, vmem_limit_bytes=63 << 20
        ),
    )(
        hidden_in,
        cotangent,
        bucket_len[:, 0, :],
        live_mask,
        routes[:, :, 0],
        vin,
        ein,
        w_qkv,
        w_attn_out,
        w_up,
        w_down,
        expert_in.reshape(S, G // 2, 2, sh, FQ),
        expert_out.reshape(G // 2, 2, shd, D),
    )
    specs = [
        pl.BlockSpec((256, shape[1]), lambda i: (i, 0))
        if shape == (D, FQ) or shape == (FQ, D)
        else pl.BlockSpec(shape, lambda i, n=len(shape): (0,) * n)
        for shape, _ in shapes
    ]
    outs = pl.pallas_call(
        hand_over,
        name="hand_over",
        grid=(D // 256,),
        out_shape=[jax.ShapeDtypeStruct(*shape) for shape in shapes],
        in_specs=specs,
        out_specs=specs,
        compiler_params=pltpu.CompilerParams(vmem_limit_bytes=63 << 20),
    )(*outs)
    out, dx, vectors, gqkv, gwo, gup, gdn, gin, gout, evectors = outs
    vectors = lax.dynamic_slice_in_dim(vectors, lax.axis_index("dp") * sh, sh, 1)
    return (
        out,
        dx,
        vectors[0],
        vectors[1],
        gqkv,
        gwo,
        vectors[2],
        vectors[3],
        gup,
        gdn,
        gin[None],
        gout[None],
        evectors[0:1],
        evectors[1:2],
        evectors[2:3],
    )


def on_device(*args):
    groups = lax.axis_size("dp")
    rows, shard = args[0].shape[1], args[11].shape[0]
    capacity = 3 * rows // (2 * groups)
    if capacity % 16 or shard % 16 or groups != 8:
        return with_collectives(*args)
    return with_kernel(*args)


def solution(mesh):
    everywhere = ("section", "dp")
    tokens = P(None, "dp", None)
    outs = P(None, "dp", "section")
    per_expert = P("dp", "section")
    return jax.shard_map(
        on_device,
        mesh=mesh,
        in_specs=(
            tokens,
            tokens,
            tokens,
            P(None, "dp"),
            tokens,
            P(everywhere),
            P(everywhere),
            P(everywhere, None),
            P(everywhere, None),
            P(everywhere),
            P(everywhere),
            P(everywhere, None),
            P(everywhere, None),
            P("dp", None, "section"),
            P("dp", "section", None),
            per_expert,
            per_expert,
            per_expert,
        ),
        out_specs=(
            outs,
            outs,
            P(everywhere),
            P(everywhere),
            P(everywhere, None),
            P(everywhere, None),
            P(everywhere),
            P(everywhere),
            P(everywhere, None),
            P(everywhere, None),
            P("dp", None, "section"),
            P("dp", "section", None),
            per_expert,
            per_expert,
            per_expert,
        ),
        check_vma=False,
    )
```

```python
import functools
import math
import types

import jax
import jax.numpy as jnp
from jax import lax
from jax.experimental import pallas as pl
from jax.experimental.pallas import tpu as pltpu
from jax.sharding import PartitionSpec as P

HEADS = 16
epsilon = 1e-05
masked_value = -1e30
f32 = jnp.float32
bf16 = jnp.bfloat16


def norm_parts(values):
    center = values - jnp.mean(values, axis=-1, keepdims=True)
    spread = jnp.mean(center * center, axis=-1, keepdims=True)
    rs = lax.rsqrt(spread + epsilon)
    return center * rs, rs


def gelu_back(pre, grad):
    outputs, pullback = jax.vjp(jax.nn.gelu, pre)
    return pullback(grad)[0]


def dot(a, b):
    return jnp.dot(a, b, preferred_element_type=f32)


def dot_tn(a, b):
    return jnp.einsum("rd,re->de", a, b, preferred_element_type=f32)


def dot_nt(a, b):
    return jnp.einsum("re,de->rd", a, b, preferred_element_type=f32)


def sum_scatter(part):
    return lax.psum_scatter(
        part.astype(bf16), "section", scatter_dimension=part.ndim - 1, tiled=True
    ).astype(f32)


def gather_features(part):
    return lax.all_gather(part, "section", axis=part.ndim - 1, tiled=True)


def with_collectives(
    hidden_in,
    cotangent,
    bucket_len,
    live_mask,
    routes,
    ln1_gain,
    ln1_bias,
    w_qkv,
    w_attn_out,
    ln2_gain,
    ln2_bias,
    w_up,
    w_down,
    expert_in,
    expert_out,
    expert_gain,
    expert_bias,
    centroids,
):
    sections = lax.axis_size("section")
    groups = lax.axis_size("dp")
    section = lax.axis_index("section")
    micro, rows, width = hidden_in.shape
    quarter = width // sections
    heads = HEADS // sections
    size = width // HEADS
    ff = w_up.shape[1] // sections
    capacity = 3 * rows // (2 * groups)
    shard = w_up.shape[0]
    own_cols = section * quarter

    def mine(values):
        return lax.dynamic_slice_in_dim(values, own_cols, quarter, values.ndim - 1)

    def column_group(weight, pieces):
        cols = weight.shape[1] // (pieces * sections)
        parts = weight.reshape(shard, pieces, sections, cols).transpose(2, 0, 1, 3)
        parts = parts.reshape(sections, shard, pieces * cols)
        parts = lax.all_to_all(parts, "section", split_axis=0, concat_axis=0, tiled=True)
        full = lax.all_gather(parts, "dp", axis=1, tiled=True)
        return full.reshape(width, pieces * cols)

    def column_group_back(grad, pieces):
        cols = grad.shape[1] // pieces
        parts = grad.astype(bf16).reshape(sections, groups * shard, pieces * cols)
        parts = lax.psum_scatter(parts, "dp", scatter_dimension=1, tiled=True)
        parts = lax.all_to_all(parts, "section", split_axis=0, concat_axis=0, tiled=True)
        parts = parts.reshape(sections, shard, pieces, cols).transpose(1, 2, 0, 3)
        return parts.reshape(shard, pieces * sections * cols).astype(f32)

    def row_group_back(grad):
        return lax.psum_scatter(
            grad.astype(bf16), "dp", scatter_dimension=0, tiled=True
        ).astype(f32)

    vectors = lax.all_gather(
        jnp.stack([ln1_gain, ln1_bias, ln2_gain, ln2_bias]), ("section", "dp"), axis=1, tiled=True
    ).astype(f32)
    gain_one, bias_one, gain_two, bias_two = vectors
    expert_vectors = lax.all_gather(
        jnp.concatenate([expert_gain, expert_bias, centroids]), "section", axis=1, tiled=True
    ).astype(f32)
    expert_g, expert_b, centroid = expert_vectors
    wqkv = column_group(w_qkv, 3)
    wo = lax.all_gather(w_attn_out, "dp", axis=0, tiled=True)
    wup = column_group(w_up, 1)
    wdown = lax.all_gather(w_down, "dp", axis=0, tiled=True)
    win = expert_in[0]
    wout = expert_out[0]

    ends = jnp.cumsum(bucket_len[:, 0, :], axis=-1)
    slot_ids = jnp.arange(rows, dtype=jnp.int32)
    segments = jnp.sum((slot_ids[None, :, None] >= ends[:, None, :]).astype(jnp.int32), axis=-1)
    same = segments[:, :, None] == segments[:, None, :]
    causal = slot_ids[None, None, :] <= slot_ids[None, :, None]
    opened = (live_mask[:, None, :] == 1) | (slot_ids[None, None, :] == slot_ids[None, :, None])
    allowed = (same & causal & opened)[:, None]
    chosen = routes[:, :, 0]
    picks = (chosen[:, :, None] == jnp.arange(groups, dtype=jnp.int32)).astype(jnp.int32)
    ranks = jnp.sum((jnp.cumsum(picks, axis=1) - picks) * picks, axis=2)
    places = chosen * capacity + ranks
    place_ids = jnp.arange(groups * capacity, dtype=jnp.int32)
    picked = (places[:, None, :] == place_ids[None, :, None]).astype(bf16)

    def dispatch(values):
        out = jnp.einsum("mpt,mtf->pmf", picked, values, preferred_element_type=f32).astype(bf16)
        out = out.reshape(groups, capacity * micro, quarter)
        return lax.all_to_all(out, "dp", split_axis=0, concat_axis=0, tiled=True)

    def give_back(values):
        out = lax.all_to_all(values, "dp", split_axis=0, concat_axis=0, tiled=True)
        out = out.reshape(groups * capacity, micro, quarter)
        return jnp.einsum("mpt,pmf->mtf", picked, out, preferred_element_type=f32)

    dge = gather_features(dispatch(mine(cotangent))).reshape(-1, width).astype(f32)

    x = hidden_in.reshape(micro * rows, width).astype(f32)
    n1, rs1 = norm_parts(x)
    a1 = (n1 * gain_one + bias_one).astype(bf16)
    qkv = dot(a1, wqkv).astype(bf16)
    q, k, v = (
        qkv[:, i * quarter : (i + 1) * quarter].reshape(micro, rows, heads, size) for i in range(3)
    )
    scale = size ** (-0.5)
    raw = jnp.einsum("mqhd,mkhd->mhqk", q, k, preferred_element_type=f32) * scale
    scores = jnp.where(allowed, raw, masked_value)
    weights = jnp.exp(scores - jnp.max(scores, axis=-1, keepdims=True))
    probs = weights / jnp.sum(weights, axis=-1, keepdims=True)
    probs_low = probs.astype(bf16)
    mixed = jnp.einsum("mhqk,mkhd->mqhd", probs_low, v, preferred_element_type=f32)
    o = mixed.reshape(micro * rows, quarter).astype(bf16)
    y1q = (mine(x) + sum_scatter(dot(o, wo))).astype(bf16)
    y1 = gather_features(y1q).astype(f32)
    n2, rs2 = norm_parts(y1)
    a2 = (n2 * gain_two + bias_two).astype(bf16)
    h = dot(a2, wup)
    u = jax.nn.gelu(h).astype(bf16)
    y2q = (y1q.astype(f32) + sum_scatter(dot(u, wdown))).astype(bf16)

    xe = gather_features(dispatch(y2q.reshape(micro, rows, quarter))).reshape(-1, width)
    xe = xe.astype(f32)
    ne, rse = norm_parts(xe)
    en = (ne * expert_g + expert_b).astype(bf16)
    he = dot(en, win)
    ue = jax.nn.gelu(he).astype(bf16)
    fe_part = dot(ue, wout)
    alpha = jax.nn.sigmoid(jnp.sum(xe * centroid, axis=-1, keepdims=True))
    fe = sum_scatter(fe_part)
    ge = (alpha * fe).astype(bf16).reshape(groups, capacity * micro, quarter)
    block_out = (
        y2q.reshape(micro, rows, quarter).astype(f32) + give_back(ge)
    ).astype(bf16)

    dfe = (alpha * dge).astype(bf16)
    due = dot_nt(dfe, wout)
    grad_out = dot_tn(ue, dfe)
    dhe = gelu_back(he, due).astype(bf16)
    grad_in = dot_tn(en, dhe)
    den_part = dot_nt(dhe, win)
    gden = den_part * expert_g
    stats = lax.psum(
        jnp.stack(
            [
                jnp.mean(gden, axis=-1),
                jnp.mean(gden * ne, axis=-1),
                jnp.sum(dge * fe_part, axis=-1),
            ]
        ),
        "section",
    )[..., None]
    den = sum_scatter(den_part)
    neq = mine(ne)
    dlogit = stats[2] * alpha * (1.0 - alpha)
    dxe_ln = rse * (mine(expert_g) * den - stats[0] - neq * stats[1])
    dxe = (dxe_ln + dlogit * mine(centroid)).astype(bf16)
    grad_expert_gain = jnp.sum(den * neq, axis=0)
    grad_expert_bias = jnp.sum(den, axis=0)
    grad_centroid = jnp.sum(dlogit * mine(xe), axis=0)
    back = give_back(dxe.reshape(groups, capacity * micro, quarter))
    dy2q = (mine(cotangent).astype(f32) + back).astype(bf16).reshape(micro * rows, quarter)

    dy2 = gather_features(dy2q)
    grad_down = dot_tn(u, dy2)
    dh = gelu_back(h, dot_nt(dy2, wdown)).astype(bf16)
    grad_up = dot_tn(a2, dh)
    da2_part = dot_nt(dh, wup)
    gda2 = da2_part * gain_two
    stats = lax.psum(
        jnp.stack([jnp.mean(gda2, axis=-1), jnp.mean(gda2 * n2, axis=-1)]), "section"
    )[..., None]
    da2 = sum_scatter(da2_part)
    n2q = mine(n2)
    dy1q = dy2q.astype(f32) + rs2 * (mine(gain_two) * da2 - stats[0] - n2q * stats[1])
    dy1q = dy1q.astype(bf16)
    dy1 = gather_features(dy1q)
    grad_wo = dot_tn(o, dy1)
    do = dot_nt(dy1, wo).astype(bf16).reshape(micro, rows, heads, size)
    dp = jnp.einsum("mqhd,mkhd->mhqk", do, v, preferred_element_type=f32)
    dv = jnp.einsum("mhqk,mqhd->mkhd", probs_low, do, preferred_element_type=f32)
    delta = jnp.sum(probs * dp, axis=-1, keepdims=True)
    ds = (probs * (dp - delta)).astype(bf16)
    dq = jnp.einsum("mhqk,mkhd->mqhd", ds, k, preferred_element_type=f32) * scale
    dk = jnp.einsum("mhqk,mqhd->mkhd", ds, q, preferred_element_type=f32) * scale
    dqkv = jnp.concatenate(
        [part.reshape(micro * rows, quarter) for part in (dq, dk, dv)], axis=1
    ).astype(bf16)
    grad_qkv = dot_tn(a1, dqkv)
    da1_part = dot_nt(dqkv, wqkv)
    gda1 = da1_part * gain_one
    stats = lax.psum(
        jnp.stack([jnp.mean(gda1, axis=-1), jnp.mean(gda1 * n1, axis=-1)]), "section"
    )[..., None]
    da1 = sum_scatter(da1_part)
    n1q = mine(n1)
    dx = dy1q.astype(f32) + rs1 * (mine(gain_one) * da1 - stats[0] - n1q * stats[1])

    vector_grads = lax.psum_scatter(
        jnp.stack(
            [
                jnp.sum(da1 * n1q, axis=0),
                jnp.sum(da1, axis=0),
                jnp.sum(da2 * n2q, axis=0),
                jnp.sum(da2, axis=0),
            ]
        ),
        "dp",
        scatter_dimension=1,
        tiled=True,
    )
    return (
        block_out,
        dx.reshape(micro, rows, quarter),
        vector_grads[0],
        vector_grads[1],
        column_group_back(grad_qkv, 3),
        row_group_back(grad_wo),
        vector_grads[2],
        vector_grads[3],
        column_group_back(grad_up, 1),
        row_group_back(grad_down),
        grad_in[None],
        grad_out[None],
        grad_expert_gain[None],
        grad_expert_bias[None],
        grad_centroid[None],
    )


MESH = pl.DeviceIdType.MESH
KEYS = 93
CHAIN = {
    "y1": 0,
    "y1g": 1,
    "y2": 0,
    "xe": 1,
    "den": 0,
    "dy2": 1,
    "da2": 0,
    "dy1": 1,
    "da1": 0,
}
SHARED = {
    "geb": "y2d",
    "dxb": "cot",
    "fe": "dge",
    "est": "stats",
    "tst": "stats",
    "vs": "v2",
    "gdn": "wdn",
    "gup": "wup",
    "gwo": "wo",
    "gqk": "wqkv",
    "p": "c",
    "n": "near",
    "nf": "near far",
    "f": "far",
}


def semaphore_of(k):
    if k[0] in CHAIN:
        return ("chain", CHAIN[k[0]]) + k[1:]
    if k[0] == "q1":
        return ("stats", k[1], k[2]) if k[1] < 2 else ("chain", 1, 0, k[2])
    if k[0] == "v1":
        return "chain", 1, 1, k[1]
    if k[1] == "s":
        return "u1" if k[0] == "gup" else "e1", k[2]
    if k[0] == "tst":
        return ("stats",) + k[2:]
    return tuple(SHARED.get(part, part) for part in k)
CHUNK = 128


def tn(a, b):
    return lax.dot_general(a, b, (((0,), (0,)), ((), ())), preferred_element_type=f32)


def nt(a, b):
    return lax.dot_general(a, b, (((1,), (1,)), ((), ())), preferred_element_type=f32)


def tanh_parts(v):
    root = 0.7978845608028654
    t = jnp.tanh(root * (v + 0.044715 * (v * v * v)))
    return t, root


def gelu_both(v):
    t, root = tanh_parts(v)
    half = 0.5 * (1.0 + t)
    return v * half, half + 0.5 * v * (1.0 - t * t) * root * (1.0 + 0.134145 * (v * v))


def to_rows(columns):
    lane = lax.broadcasted_iota(jnp.int32, (columns[0].shape[0], 128), 1)
    wide = jnp.zeros(lane.shape, f32)
    for i, column in enumerate(columns):
        wide = jnp.where(lane == i, column, wide)
    return wide.T[:8]


def to_columns(rows):
    return jnp.concatenate([rows, jnp.zeros((120, rows.shape[1]), f32)], axis=0).T


def layout(dims):
    S, G, M, T, D, Q, FQ, C, sh, shd = dims
    nz = G // 2
    R = G * C
    heads = HEADS // S
    return dict(
        wqkv=((S, nz, 2, sh, 3 * Q), bf16),
        wo=((nz, 2, sh, D), bf16),
        wup=((S, nz, 2, sh, FQ), bf16),
        wdn=((nz, 2, shd, D), bf16),
        win=((S, nz, 2, sh, FQ), bf16),
        wout=((nz, 2, shd, D), bf16),
        vin=((8, 128), f32),
        ein=((8, Q), f32),
        vg=((S, G, 8, 128), f32),
        vecs=((8, D), f32),
        evec=((8, D), f32),
        mask=((M, T, T), f32),
        perm=((M, R, T), bf16),
        cots=((M, R, Q), bf16),
        y2s=((M, R, Q), bf16),
        ges=((M, R, Q), bf16),
        dxs=((M, R, Q), bf16),
        ger=((M, R, Q), bf16),
        dxr=((M, R, Q), bf16),
        tst=((M, T, 128), f32),
        est=((M, R, 128), f32),
        a1=((M, T, D), bf16),
        a2=((M, T, D), bf16),
        qkv=((M, T, 3 * Q), bf16),
        probs=((M, heads, T, T), f32),
        o=((M, T, Q), bf16),
        y1=((M, T, D), bf16),
        h=((M, T, FQ), f32),
        u=((M, T, FQ), bf16),
        y2q=((M, T, Q), bf16),
        xe=((M, R, D), bf16),
        dge=((M, R, D), bf16),
        en=((M, R, D), bf16),
        ue=((M, R, FQ), bf16),
        dhe=((M, R, FQ), bf16),
        dfe=((M, R, D), bf16),
        slope=((R, FQ), f32),
        fes=((M, S - 1, R, Q), bf16),
        fer=((M, S - 1, R, Q), bf16),
        feo=((M, R, Q), f32),
        dns=((M, S - 1, R, Q), bf16),
        dnr=((M, S - 1, R, Q), bf16),
        dno=((M, R, Q), f32),
        ess=((M, 8, R), f32),
        esr=((M, S - 1, 8, R), f32),
        ts=((M, S - 1, T, Q), bf16),
        r1=((M, S - 1, T, Q), bf16),
        r2=((M, S - 1, T, Q), bf16),
        own=((M, T, Q), f32),
        tss=((2, M, 8, T), f32),
        tsr=((2, M, S - 1, 8, T), f32),
        dy2=((M, T, D), bf16),
        dh=((M, T, FQ), bf16),
        dqkv=((M, T, 3 * Q), bf16),
        gwo=((nz, 2, sh, D), bf16),
        gqk=((S, nz, 2, sh, 3 * Q), bf16),
        bdn=((nz, shd, D), bf16),
        bup=((S, nz, sh, FQ), bf16),
        bwo=((nz, sh, D), bf16),
        bqk=((S, nz, sh, 3 * Q), bf16),
        zdn=((nz - 1, shd, D), bf16),
        zup=((nz - 1, S, sh, FQ), bf16),
        zwo=((nz - 1, sh, D), bf16),
        zqk=((nz - 1, S, sh, 3 * Q), bf16),
        ups=((S, sh, FQ), bf16),
        upr=((S - 1, sh, FQ), bf16),
        qks=((S, sh, 3 * Q), bf16),
        qkr=((S - 1, sh, 3 * Q), bf16),
        stage=((2, 256, D), bf16),
        out=((M, T, Q), bf16),
        dx=((M, T, Q), f32),
        vgo=((8, 128), f32),
        gqk_out=((sh, 3 * D), f32),
        gwo_out=((sh, D), f32),
        gup_out=((sh, S * FQ), f32),
        gdn_out=((shd, D), f32),
        evo=((8, Q), f32),
        vsum=((8, Q), f32),
        vsr=((G - 1, 8, Q), f32),
    )


INPUTS = [
    "hidden",
    "cot",
    "bucket",
    "live",
    "routes",
    "gain_one",
    "bias_one",
    "gain_two",
    "bias_two",
    "gain_e",
    "bias_e",
    "centroid",
    "wqkv_in",
    "wo_in",
    "wup_in",
    "wdn_in",
    "win_in",
    "wout_in",
]
RESULTS = [
    "out",
    "dx",
    "vgo",
    "gqk_out",
    "gwo_out",
    "gup_out",
    "gdn_out",
    "evo",
]
OUTPUTS = ["to_" + name for name in RESULTS] + ["gin_out", "gout_out"]


def block_kernel(dims, names, *args):
    r = types.SimpleNamespace(**dict(zip(names, args)))
    S, G, M, T, D, Q, FQ, C, sh, shd = dims
    nz = G // 2
    R = G * C
    heads = HEADS // S
    size = D // HEADS
    scale = size ** (-0.5)
    s = lax.axis_index("section")
    d = lax.axis_index("dp")
    z = lax.div(d, 2)
    c = lax.rem(d, 2)
    beside = (s, d + 1 - 2 * c)
    near = z + 1 - 2 * lax.rem(z, 2)
    far = lax.rem(z + 2, nz)
    near_far = lax.rem(near + 2, nz)

    def sec(i):
        return lax.rem(s + i, S)

    def dpi(j):
        return lax.rem(d + j, G)

    def zi(j):
        return lax.rem(z + j, nz)

    def to_sec(i):
        return (sec(i), d)

    def to_dp(j):
        return (s, dpi(j))

    def to_z(j):
        return (s, zi(j) * 2 + c)

    def col(q, n=Q):
        return pl.ds(pl.multiple_of(q * n, n), n)

    def seats(e):
        return pl.ds(pl.multiple_of(e * C, C), C)

    mine = col(s)
    places = {}
    pending = {}

    def copy(src, dst, k, device):
        i = places.setdefault(semaphore_of(k), len(places))
        return pltpu.make_async_remote_copy(
            src_ref=src,
            dst_ref=dst,
            send_sem=r.ssem.at[i],
            recv_sem=r.rsem.at[i],
            device_id=device,
            device_id_type=MESH,
        )

    def send(src, dst, k, device):
        sent(k)
        pending[semaphore_of(k)] = copy(src, dst, k, device)
        pending[semaphore_of(k)].start()

    def sent(k):
        last = pending.pop(semaphore_of(k), None)
        if last is not None:
            last.wait_send()

    def recv(dst, k):
        copy(dst, dst, k, beside).wait_recv()

    def each(rows, body):
        step = math.gcd(rows, CHUNK)

        @pl.loop(0, rows // step)
        def _(i):
            body(pl.ds(pl.multiple_of(i * step, step), step))

    others = range(1, S)

    def gather_send(ref, m, k):
        for i in others:
            send(ref.at[m, :, mine], ref.at[m, :, mine], (k, m, i), to_sec(i))

    def gather_recv(ref, m, k):
        for i in others:
            recv(ref.at[m, :, col(sec(S - i))], (k, m, i))

    def sum_send(tile, out, arrive, own, m, k, before=None, hold=False):
        for i in others:
            if before is not None:
                sent((before, m, i))
            out[m, i - 1] = tile(sec(i)).astype(bf16)
            if not hold:
                send(out.at[m, i - 1], arrive.at[m, i - 1], (k, m, i), to_sec(i))
        own[m] = tile(s)

    def sum_start(out, arrive, m, k):
        for i in others:
            send(out.at[m, i - 1], arrive.at[m, i - 1], (k, m, i), to_sec(i))

    def sum_recv(arrive, m, k, then=None):
        for i in others:
            recv(arrive.at[m, i - 1], (k, m, i))
            if then is not None and i == S - 2:
                then()

    def summed(own, arrive, m, rows):
        total = own[m, rows]
        for i in others:
            total += arrive[m, i - 1, rows].astype(f32)
        return total

    def dispatch_send(src, dst, m, k):
        dst[m, seats(d), mine] = src[m, seats(d)]
        for j in range(1, G):
            send(src.at[m, seats(dpi(j))], dst.at[m, seats(d), mine], (k, m, j), to_dp(j))

    def dispatch_recv(dst, m, k):
        for j in range(1, G):
            recv(dst.at[m, seats(dpi(G - j)), mine], (k, m, j))

    def return_send(src, dst, m, k):
        dst[m, seats(d)] = src[m, seats(d)]
        for j in range(1, G):
            send(src.at[m, seats(dpi(j))], dst.at[m, seats(d)], (k, m, j), to_dp(j))

    def return_recv(dst, m, k):
        for j in range(1, G):
            recv(dst.at[m, seats(dpi(G - j))], (k, m, j))

    def part(ref, zz, cc):
        return ref.at[:, zz, cc] if len(ref.shape) == 5 else ref.at[zz, cc]

    def weight_start(ref, k):
        send(part(ref, z, c), part(ref, z, c), (k, "far"), (s, far * 2 + c))
        send(part(ref, z, c), part(ref, z, c), (k, "c", 0), beside)

    def weight_next(ref, k):
        send(part(ref, z, c), part(ref, z, c), (k, "near"), (s, near * 2 + c))

    def weight_far(ref, k):
        recv(part(ref, far, c), (k, "far"))
        send(part(ref, far, c), part(ref, far, c), (k, "near far"), (s, near * 2 + c))
        send(part(ref, far, c), part(ref, far, c), (k, "c", 1), beside)

    def weight_near(ref, k):
        recv(part(ref, near, c), (k, "near"))
        send(part(ref, near, c), part(ref, near, c), (k, "c", 2), beside)
        recv(part(ref, near_far, c), (k, "near far"))
        send(part(ref, near_far, c), part(ref, near_far, c), (k, "c", 3), beside)

    def weight_wait(ref, k):
        for i, zz in enumerate((z, far, near, near_far)):
            recv(part(ref, zz, 1 - c), (k, "c", i))

    load_in = pltpu.make_async_copy(r.win_in, r.win, r.lsem.at[0])
    load_out = pltpu.make_async_copy(r.wout_in, r.wout, r.lsem.at[1])

    early = lax.broadcasted_iota(jnp.int32, (T, T), 0)
    late = lax.broadcasted_iota(jnp.int32, (T, T), 1)

    def seat_tokens(m):
        route = r.routes[m]
        expert_ids = lax.broadcasted_iota(jnp.int32, (G, T), 0)
        picks = jnp.where(expert_ids == route, 1.0, 0.0)
        before = jnp.where(early < late, 1.0, 0.0).astype(bf16)
        counts = jnp.dot(picks.astype(bf16), before, preferred_element_type=f32)
        rank = jnp.sum(counts * picks, axis=0, keepdims=True)
        place = route.astype(f32) * float(C) + rank
        seat_ids = lax.broadcasted_iota(jnp.int32, (R, T), 0).astype(f32)
        r.perm[m] = jnp.where(seat_ids == place, 1.0, 0.0).astype(bf16)
        r.cots[m] = jnp.dot(r.perm[m], r.cot[m, :, mine], preferred_element_type=f32).astype(bf16)

    def entry():
        barrier = pltpu.get_barrier_semaphore()
        for i in others:
            pl.semaphore_signal(barrier, inc=1, device_id=to_sec(i), device_id_type=MESH)
        for j in range(1, G):
            pl.semaphore_signal(barrier, inc=1, device_id=to_dp(j), device_id_type=MESH)
        r.vin[...] = jnp.zeros_like(r.vin)
        for i, ref in enumerate((r.gain_one, r.bias_one, r.gain_two, r.bias_two)):
            r.vin[i : i + 1, 0:sh] = ref[...].astype(f32)
        r.ein[...] = jnp.zeros_like(r.ein)
        for i, ref in enumerate((r.gain_e, r.bias_e, r.centroid)):
            r.ein[i : i + 1, :] = ref[...].astype(f32)
        r.vg[s, d] = r.vin[...]
        r.evec[:, mine] = r.ein[...]
        for piece in range(3):
            r.wqkv[s, z, c, :, piece * Q : (piece + 1) * Q] = r.wqkv_in[
                :, pl.ds(pl.multiple_of(piece * D + s * Q, Q), Q)
            ]
        r.wo[z, c] = r.wo_in[...]
        seat_tokens(0)
        seat_tokens(1)
        pl.semaphore_wait(barrier, S + G - 2)
        for i in others:
            send(r.vin, r.vg.at[s, d], ("v1", i), to_sec(i))
        for i in others:
            for piece in range(3):
                src = r.wqkv_in.at[:, pl.ds(pl.multiple_of(piece * D + sec(i) * Q, Q), Q)]
                dst = r.wqkv.at[s, z, c, :, piece * Q : (piece + 1) * Q]
                send(src, dst, ("q1", piece, i), to_sec(i))
        dispatch_send(r.cots, r.dge, 0, "cot")
        dispatch_send(r.cots, r.dge, 1, "cot")
        for i in others:
            send(r.wup_in.at[:, col(sec(i), FQ)], r.wup.at[s, z, c], ("u1", i), to_sec(i))
            send(r.ein, r.evec.at[:, mine], ("e1", i), to_sec(i))
        for i in others:
            recv(r.vg.at[sec(S - i), d], ("v1", i))
        for j in range(1, G):
            send(r.vg.at[:, d], r.vg.at[:, d], ("v2", j), to_dp(j))
        for i in others:
            for piece in range(3):
                recv(r.wqkv.at[sec(S - i), z, c, :, piece * Q : (piece + 1) * Q], ("q1", piece, i))
        weight_start(r.wqkv, "wqkv")
        weight_next(r.wqkv, "wqkv")
        load_in.start()
        load_out.start()

    def mask_tokens(m):
        end = r.bucket[m, 0, 0]
        seg_q = (early >= end).astype(jnp.int32)
        seg_k = (late >= end).astype(jnp.int32)
        for b in range(1, r.bucket.shape[2]):
            end = end + r.bucket[m, 0, b]
            seg_q += (early >= end).astype(jnp.int32)
            seg_k += (late >= end).astype(jnp.int32)
        live = jnp.broadcast_to(r.live[m : m + 1, :], (T, T))
        allowed = (seg_q == seg_k) & (late <= early) & ((live == 1) | (late == early))
        r.mask[m] = jnp.where(allowed, 1.0, 0.0)

    def spread_vectors():
        for j in range(1, G):
            recv(r.vg.at[:, dpi(G - j)], ("v2", j))
        spread_row = lax.broadcasted_iota(jnp.int32, (128, D), 0)
        spread_lane = lax.broadcasted_iota(jnp.int32, (128, D), 1)
        spread = jnp.where(lax.rem(spread_lane, sh) == spread_row, 1.0, 0.0).astype(bf16)
        stacked = r.vg[...].reshape(S * G * 8, 128).astype(bf16)
        wide = jnp.dot(stacked, spread, preferred_element_type=f32)
        row_id = lax.broadcasted_iota(jnp.int32, (S * G * 8, D), 0)
        lane_id = lax.broadcasted_iota(jnp.int32, (S * G * 8, D), 1)
        low = lax.shift_right_logical(row_id, 3) * sh
        wide = jnp.where((lane_id >= low) & (lane_id < low + sh), wide, 0.0)
        r.vecs[...] = jnp.sum(wide.reshape(S * G, 8, D), axis=0)

    def normed(values):
        mean = jnp.mean(values, axis=1, keepdims=True)
        center = values - mean
        rs = lax.rsqrt(jnp.mean(center * center, axis=1, keepdims=True) + epsilon)
        return center * rs, mean, rs

    def norm_tokens(src, dst, m, at):
        gain = r.vecs[2 * at : 2 * at + 1, :]
        bias = r.vecs[2 * at + 1 : 2 * at + 2, :]

        def body(rows):
            n, mean, rs = normed(src[m, rows].astype(f32))
            r.tst[m, rows, 2 * at : 2 * at + 1] = mean
            r.tst[m, rows, 2 * at + 1 : 2 * at + 2] = rs
            dst[m, rows] = (n * gain + bias).astype(bf16)

        each(T, body)

    entry()
    r.wup[s, z, c] = r.wup_in[:, col(s, FQ)]
    r.wdn[z, c] = r.wdn_in[...]
    mask_tokens(0)
    mask_tokens(1)
    for m in range(M):
        dispatch_recv(r.dge, m, "cot")
        gather_send(r.dge, m, "dge")
    weight_far(r.wqkv, "wqkv")
    weight_start(r.wo, "wo")
    weight_next(r.wo, "wo")
    for i in others:
        recv(r.evec.at[:, col(sec(S - i))], ("e1", i))
        recv(r.wup.at[sec(S - i), z, c], ("u1", i))
    weight_start(r.wup, "wup")
    spread_vectors()
    norm_tokens(r.hidden, r.a1, 0, 0)
    norm_tokens(r.hidden, r.a1, 1, 0)
    weight_near(r.wqkv, "wqkv")
    weight_far(r.wo, "wo")
    weight_next(r.wup, "wup")
    weight_wait(r.wqkv, "wqkv")

    def attend(m):
        @pl.loop(0, 3)
        def _(t):
            w = r.wqkv[:, :, :, :, col(t)].reshape(D, Q)
            r.qkv[m, :, col(t)] = jnp.dot(r.a1[m], w, preferred_element_type=f32).astype(bf16)

        for hh in range(heads):
            at = hh * size
            q = r.qkv[m, :, at : at + size]
            k = r.qkv[m, :, Q + at : Q + at + size]
            v = r.qkv[m, :, 2 * Q + at : 2 * Q + at + size]
            scores = jnp.where(r.mask[m] > 0.0, nt(q, k) * scale, masked_value)
            weights = jnp.exp(scores - jnp.max(scores, axis=1, keepdims=True))
            p = weights / jnp.sum(weights, axis=1, keepdims=True)
            r.probs[m, hh] = p
            mixed = jnp.dot(p.astype(bf16), v, preferred_element_type=f32)
            r.o[m, :, at : at + size] = mixed.astype(bf16)

    def y1_tile(m):
        return lambda q: jnp.dot(
            r.o[m], r.wo[:, :, :, col(q)].reshape(Q, Q), preferred_element_type=f32
        )

    def finish_y1(m):
        sum_recv(r.r1, m, "y1")

        def body(rows):
            total = r.hidden[m, rows, mine].astype(f32) + summed(r.own, r.r1, m, rows)
            r.y1[m, rows, mine] = total.astype(bf16)

        each(T, body)
        gather_send(r.y1, m, "y1g")

    attend(0)
    weight_near(r.wo, "wo")
    weight_wait(r.wo, "wo")
    sum_send(y1_tile(0), r.ts, r.r1, r.own, 0, "y1")
    attend(1)
    sum_send(y1_tile(1), r.ts, r.r1, r.own, 1, "y1")
    weight_far(r.wup, "wup")
    weight_start(r.wdn, "wdn")
    weight_next(r.wdn, "wdn")
    finish_y1(0)
    finish_y1(1)
    weight_near(r.wup, "wup")
    weight_wait(r.wup, "wup")

    def up(m):
        gather_recv(r.y1, m, "y1g")
        norm_tokens(r.y1, r.a2, m, 1)

        @pl.loop(0, FQ // Q)
        def _(t):
            w = r.wup[:, :, :, :, col(t)].reshape(D, Q)
            pre = jnp.dot(r.a2[m], w, preferred_element_type=f32)
            value, slope = gelu_both(pre)
            r.u[m, :, col(t)] = value.astype(bf16)
            r.h[m, :, col(t)] = slope

    def y2_tile(m):
        return lambda q: jnp.dot(
            r.u[m], r.wdn[:, :, :, col(q)].reshape(FQ, Q), preferred_element_type=f32
        )

    weight_far(r.wdn, "wdn")
    up(0)
    up(1)
    weight_near(r.wdn, "wdn")
    weight_wait(r.wdn, "wdn")
    sum_send(y2_tile(0), r.ts, r.r2, r.own, 0, "y2", "y1")
    sum_send(y2_tile(1), r.ts, r.r2, r.own, 1, "y2", "y1", hold=True)

    def finish_y2(m):
        sum_recv(r.r2, m, "y2", None if m else lambda: sum_start(r.ts, r.r2, 1, "y2"))

        def body(rows):
            total = r.y1[m, rows, mine].astype(f32) + summed(r.own, r.r2, m, rows)
            r.y2q[m, rows] = total.astype(bf16)

        each(T, body)
        r.y2s[m] = jnp.dot(r.perm[m], r.y2q[m], preferred_element_type=f32).astype(bf16)
        dispatch_send(r.y2s, r.xe, m, "y2d")

    finish_y2(0)
    dispatch_recv(r.xe, 0, "y2d")
    gather_send(r.xe, 0, "xe")
    finish_y2(1)
    load_in.wait()
    load_out.wait()

    def expert(m):
        gather_recv(r.dge, m, "dge")
        gather_recv(r.xe, m, "xe")
        if m == 0:
            dispatch_recv(r.xe, 1, "y2d")
            gather_send(r.xe, 1, "xe")
        gain, bias, centroid = r.evec[0:1, :], r.evec[1:2, :], r.evec[2:3, :]

        def body(rows):
            v = r.xe[m, rows].astype(f32)
            n, mean, rs = normed(v)
            alpha = jax.nn.sigmoid(jnp.sum(v * centroid, axis=1, keepdims=True))
            r.est[m, rows, 0:1] = mean
            r.est[m, rows, 1:2] = rs
            r.est[m, rows, 2:3] = alpha
            r.en[m, rows] = (n * gain + bias).astype(bf16)
            r.dfe[m, rows] = (alpha * r.dge[m, rows].astype(f32)).astype(bf16)

        each(R, body)

        @pl.loop(0, FQ // Q)
        def _(t):
            w = r.win[:, :, :, :, col(t)].reshape(D, Q)
            pre = jnp.dot(r.en[m], w, preferred_element_type=f32)
            value, slope = gelu_both(pre)
            r.ue[m, :, col(t)] = value.astype(bf16)
            r.slope[:, col(t)] = slope

        stats = [jnp.zeros((R, 1), f32) for _ in range(3)]

        def fe_tile(q):
            tile = jnp.dot(
                r.ue[m], r.wout[:, :, :, col(q)].reshape(FQ, Q), preferred_element_type=f32
            )
            stats[2] += jnp.sum(tile * r.dge[m, :, col(q)].astype(f32), axis=1, keepdims=True)
            return tile

        def den_tile(q):
            tile = nt(r.dhe[m], r.win[q].reshape(Q, FQ))
            scaled = tile * r.evec[0:1, col(q)]
            n = (r.xe[m, :, col(q)].astype(f32) - r.est[m, :, 0:1]) * r.est[m, :, 1:2]
            stats[0] += jnp.sum(scaled, axis=1, keepdims=True)
            stats[1] += jnp.sum(scaled * n, axis=1, keepdims=True)
            return tile

        @pl.loop(0, FQ // Q)
        def _(t):
            due = nt(r.dfe[m], r.wout[t].reshape(Q, D))
            r.dhe[m, :, col(t)] = (due * r.slope[:, col(t)]).astype(bf16)

        sum_send(den_tile, r.dns, r.dnr, r.dno, m, "den")
        sum_send(fe_tile, r.fes, r.fer, r.feo, m, "fe", hold=True)
        r.ess[m] = to_rows(stats)
        for i in others:
            send(r.ess.at[m], r.esr.at[m, i - 1], ("est", m, i), to_sec(i))

    expert(0)
    expert(1)

    def finish_den(m):
        sum_recv(r.dnr, m, "den")
        total = r.ess[m]
        for i in others:
            recv(r.esr.at[m, i - 1], ("est", m, i))
            total += r.esr[m, i - 1]
        r.est[m, :, 8:16] = to_columns(total)[:, 0:8]
        gain, centroid = r.evec[0:1, mine], r.evec[2:3, mine]
        if m == 0:
            r.evo[...] = jnp.zeros_like(r.evo)

        def body(rows):
            den = summed(r.dno, r.dnr, m, rows)
            xq = r.xe[m, rows, mine].astype(f32)
            rs, alpha = r.est[m, rows, 1:2], r.est[m, rows, 2:3]
            n = (xq - r.est[m, rows, 0:1]) * rs
            m1, m2 = r.est[m, rows, 8:9] * (1.0 / D), r.est[m, rows, 9:10] * (1.0 / D)
            dlogit = r.est[m, rows, 10:11] * alpha * (1.0 - alpha)
            grad = rs * (gain * den - m1 - n * m2) + dlogit * centroid
            r.dxs[m, rows] = grad.astype(bf16)
            r.evo[0:1, :] += jnp.sum(den * n, axis=0, keepdims=True)
            r.evo[1:2, :] += jnp.sum(den, axis=0, keepdims=True)
            r.evo[2:3, :] += jnp.sum(dlogit * xq, axis=0, keepdims=True)

        each(R, body)
        return_send(r.dxs, r.dxr, m, "dxb")

    def finish_fe(m):
        sum_recv(r.fer, m, "fe")

        def body(rows):
            fe = summed(r.feo, r.fer, m, rows)
            r.ges[m, rows] = (r.est[m, rows, 2:3] * fe).astype(bf16)

        each(R, body)
        return_send(r.ges, r.ger, m, "geb")

    def finish_dxe(m):
        return_recv(r.dxr, m, "dxb")
        back = tn(r.perm[m], r.dxr[m])
        r.dy2[m, :, mine] = (r.cot[m, :, mine].astype(f32) + back).astype(bf16)
        gather_send(r.dy2, m, "dy2")

    finish_den(0)
    finish_dxe(0)
    finish_den(1)

    writes = []
    results = []

    def give(name):
        i = RESULTS.index(name)
        one = pltpu.make_async_copy(getattr(r, name), getattr(r, "to_" + name), r.lsem.at[4 + i])
        one.start()
        results.append(one)

    def expert_weights(left, right, out):
        for t in range(D // 256):
            slot = len(writes) % 2
            if len(writes) >= 2:
                writes[-2].wait()
            rows = slice(t * 256, (t + 1) * 256)
            lhs = left[:, :, rows].reshape(M * R, 256)
            r.stage[slot] = tn(lhs, right[...].reshape(M * R, D)).astype(bf16)
            writes.append(pltpu.make_async_copy(r.stage.at[slot], out.at[rows], r.lsem.at[2 + slot]))
            writes[-1].start()

    give("evo")
    expert_weights(r.en, r.dhe, r.gin_out)

    finish_dxe(1)
    expert_weights(r.ue, r.dfe, r.gout_out)

    def token_stats(m, at, src):
        stats = [jnp.zeros((T, 1), f32) for _ in range(2)]

        def add(q, tile):
            scaled = tile * r.vecs[2 * at : 2 * at + 1, col(q)]
            mean, rs = r.tst[m, :, 2 * at : 2 * at + 1], r.tst[m, :, 2 * at + 1 : 2 * at + 2]
            n = (src[m, :, col(q)].astype(f32) - mean) * rs
            stats[0] += jnp.sum(scaled, axis=1, keepdims=True)
            stats[1] += jnp.sum(scaled * n, axis=1, keepdims=True)
            return tile

        return stats, add

    def stats_send(m, at, stats):
        r.tss[at, m] = to_rows(stats)
        for i in others:
            send(r.tss.at[at, m], r.tsr.at[at, m, i - 1], ("tst", at, m, i), to_sec(i))

    def stats_recv(m, at):
        total = r.tss[at, m]
        for i in others:
            recv(r.tsr.at[at, m, i - 1], ("tst", at, m, i))
            total += r.tsr[at, m, i - 1]
        r.tst[m, :, 8:16] = to_columns(total)[:, 0:8]

    def dense_back(m):
        if m == 0:
            gather_recv(r.dy2, m, "dy2")

        @pl.loop(0, FQ // Q)
        def _(t):
            du = nt(r.dy2[m], r.wdn[t].reshape(Q, D))
            r.dh[m, :, col(t)] = (du * r.h[m, :, col(t)]).astype(bf16)

        stats, add = token_stats(m, 1, r.y1)
        sum_send(
            lambda q: add(q, nt(r.dh[m], r.wup[q].reshape(Q, FQ))),
            r.ts,
            r.r1,
            r.own,
            m,
            "da2",
            "y2",
        )
        stats_send(m, 1, stats)

    def norm_back(m, at, src, grad_in, own, arrive, emit):
        gain = r.vecs[2 * at : 2 * at + 1, mine]

        def body(rows):
            grad = summed(own, arrive, m, rows)
            mean, rs = r.tst[m, rows, 2 * at : 2 * at + 1], r.tst[m, rows, 2 * at + 1 : 2 * at + 2]
            n = (src[m, rows, mine].astype(f32) - mean) * rs
            m1, m2 = r.tst[m, rows, 8:9] * (1.0 / D), r.tst[m, rows, 9:10] * (1.0 / D)
            emit(rows, grad_in[m, rows, mine].astype(f32) + rs * (gain * grad - m1 - n * m2))
            r.vsum[2 * at : 2 * at + 1, :] += jnp.sum(grad * n, axis=0, keepdims=True)
            r.vsum[2 * at + 1 : 2 * at + 2, :] += jnp.sum(grad, axis=0, keepdims=True)

        each(T, body)

    def finish_da2(m):
        sum_recv(r.r1, m, "da2")
        stats_recv(m, 1)
        for i in others:
            sent(("y1g", m, i))

        def emit(rows, value):
            r.y1[m, rows, mine] = value.astype(bf16)

        norm_back(m, 1, r.y1, r.dy2, r.own, r.r1, emit)
        gather_send(r.y1, m, "dy1")

    blocks = (near_far, near, far, z)

    def grads_pair(g, b, k):
        for i, zz in enumerate(blocks):
            src = g.at[:, zz, 1 - c] if len(g.shape) == 5 else g.at[zz, 1 - c]
            dst = b.at[:, zz] if len(g.shape) == 5 else b.at[zz]
            send(src, dst, (k, "p", i), beside)

    def grads_add(g, zz, arrive):
        if len(g.shape) == 5:

            @pl.loop(0, S)
            def _(q):
                g[q, zz, c] = (g[q, zz, c].astype(f32) + arrive[q].astype(f32)).astype(bf16)
        else:
            g[zz, c] = (g[zz, c].astype(f32) + arrive[...].astype(f32)).astype(bf16)

    def grads_paired(g, b, k, i):
        zz = blocks[i]
        piece = b.at[:, zz] if len(g.shape) == 5 else b.at[zz]
        recv(piece, (k, "p", i))
        grads_add(g, zz, piece)

    def grads_near(g, b, arrive, k):
        grads_paired(g, b, k, 0)
        send(part(g, near_far, c), arrive.at[1], (k, "nf"), (s, near * 2 + c))
        grads_paired(g, b, k, 1)
        send(part(g, near, c), arrive.at[0], (k, "n"), (s, near * 2 + c))
        grads_paired(g, b, k, 2)
        grads_paired(g, b, k, 3)

    def grads_far(g, arrive, k):
        recv(arrive.at[1], (k, "nf"))
        grads_add(g, far, arrive.at[1])
        send(part(g, far, c), arrive.at[2], (k, "f"), (s, far * 2 + c))

    def grads_near_recv(arrive, k):
        recv(arrive.at[0], (k, "n"))
        recv(arrive.at[2], (k, "f"))
        return 0, 2

    def down_weights():
        for i, t in enumerate(blocks):
            lhs = r.u[:, :, col(t)].reshape(M * T, Q)
            grad = tn(lhs, r.dy2[...].reshape(M * T, D))
            r.wout[t] = grad.astype(bf16).reshape(2, shd, D)
            send(r.wout.at[t, 1 - c], r.bdn.at[t], ("gdn", "p", i), beside)

    def up_weights():
        @pl.loop(0, S)
        def _(t):
            lhs = r.a2[:, :, col(t)].reshape(M * T, Q)
            grad = tn(lhs, r.dh[...].reshape(M * T, FQ))
            r.win[t] = grad.astype(bf16).reshape(nz, 2, sh, FQ)

        grads_pair(r.win, r.bup, "gup")

    def qkv_weights():
        @pl.loop(0, S)
        def _(t):
            lhs = r.a1[:, :, col(t)].reshape(M * T, Q)
            grad = tn(lhs, r.dqkv[...].reshape(M * T, 3 * Q))
            r.gqk[t] = grad.astype(bf16).reshape(nz, 2, sh, 3 * Q)

        grads_pair(r.gqk, r.bqk, "gqk")

    def out_weights():
        grad = tn(r.o[...].reshape(M * T, Q), r.y1[...].reshape(M * T, D))
        r.gwo[...] = grad.astype(bf16).reshape(nz, 2, sh, D)
        grads_pair(r.gwo, r.bwo, "gwo")

    r.vsum[...] = jnp.zeros_like(r.vsum)
    dense_back(0)
    gather_recv(r.dy2, 1, "dy2")
    down_weights()
    grads_near(r.wout, r.bdn, r.zdn, "gdn")
    dense_back(1)
    finish_da2(0)
    up_weights()
    finish_da2(1)
    grads_near(r.win, r.bup, r.zup, "gup")

    def attend_back(m):
        if m == 0:
            gather_recv(r.y1, m, "dy1")
        sum_start(r.fes, r.fer, m, "fe")
        out_grad = nt(r.y1[m], r.wo[...].reshape(Q, D)).astype(bf16)
        for hh in range(heads):
            at = hh * size
            q = r.qkv[m, :, at : at + size]
            k = r.qkv[m, :, Q + at : Q + at + size]
            v = r.qkv[m, :, 2 * Q + at : 2 * Q + at + size]
            go = out_grad[:, at : at + size]
            p = r.probs[m, hh]
            dp = nt(go, v)
            dv = tn(p.astype(bf16), go)
            ds = (p * (dp - jnp.sum(p * dp, axis=1, keepdims=True))).astype(bf16)
            dq = jnp.dot(ds, k, preferred_element_type=f32) * scale
            dk = tn(ds, q) * scale
            r.dqkv[m, :, at : at + size] = dq.astype(bf16)
            r.dqkv[m, :, Q + at : Q + at + size] = dk.astype(bf16)
            r.dqkv[m, :, 2 * Q + at : 2 * Q + at + size] = dv.astype(bf16)
        stats, add = token_stats(m, 0, r.hidden)
        sum_send(
            lambda q: add(q, nt(r.dqkv[m], r.wqkv[q].reshape(Q, 3 * Q))),
            r.ts,
            r.r2,
            r.own,
            m,
            "da1",
            "da2",
        )
        stats_send(m, 0, stats)

    def finish_da1(m):
        sum_recv(r.r2, m, "da1")
        stats_recv(m, 0)

        def emit(rows, value):
            r.dx[m, rows] = value

        norm_back(m, 0, r.hidden, r.y1, r.own, r.r2, emit)

    attend_back(0)
    grads_far(r.wout, r.zdn, "gdn")
    gather_recv(r.y1, 1, "dy1")
    out_weights()
    attend_back(1)
    qkv_weights()
    grads_near(r.gwo, r.bwo, r.zwo, "gwo")
    grads_far(r.win, r.zup, "gup")
    grads_near(r.gqk, r.bqk, r.zqk, "gqk")
    finish_da1(0)
    grads_far(r.gwo, r.zwo, "gwo")
    grads_far(r.gqk, r.zqk, "gqk")
    finish_fe(0)
    finish_fe(1)
    finish_da1(1)
    give("dx")
    for j in range(1, G):
        send(r.vsum, r.vsr.at[j - 1], ("vs", j), to_dp(j))

    def finish_out(m):
        return_recv(r.ger, m, "geb")
        back = tn(r.perm[m], r.ger[m])
        r.out[m] = (r.y2q[m].astype(f32) + back).astype(bf16)


    def row_result(g, arrive, out, k, rows, wait):
        slots = wait(arrive, k)
        mine_part = part(g, z, c)

        def body(at):
            total = mine_part[at].astype(f32)
            for slot in slots:
                total += arrive[slot, at].astype(f32)
            out[at] = total

        each(rows, body)

    def column_send(g, arrive, out, back, k, wait):
        slots = wait(arrive, k)

        @pl.loop(0, S)
        def _(q):
            total = g[q, z, c].astype(f32)
            for slot in slots:
                total += arrive[slot, q].astype(f32)
            out[q] = total.astype(bf16)

        for i in others:
            send(out.at[sec(i)], back.at[i - 1], (k, "s", i), to_sec(i))

    def column_result(sums, back, out, pieces, k):
        width = sums.shape[2] // pieces
        for i in range(S):
            if i:
                recv(back.at[i - 1], (k, "s", i))
            q = sec(S - i) if i else s
            value = (back[i - 1] if i else sums[s]).astype(f32)
            for piece in range(pieces):
                at = pl.ds(pl.multiple_of(piece * S * width + q * width, width), width)
                out[:, at] = value[:, piece * width : (piece + 1) * width]

    row_result(r.wout, r.zdn, r.gdn_out, "gdn", shd, grads_near_recv)
    give("gdn_out")
    column_send(r.win, r.zup, r.ups, r.upr, "gup", grads_near_recv)
    column_send(r.gqk, r.zqk, r.qks, r.qkr, "gqk", grads_near_recv)
    row_result(r.gwo, r.zwo, r.gwo_out, "gwo", sh, grads_near_recv)
    give("gwo_out")
    finish_out(0)
    finish_out(1)
    give("out")
    total = r.vsum[...]
    for j in range(1, G):
        recv(r.vsr.at[j - 1], ("vs", j))
        total += r.vsr[j - 1]
    shard = jnp.zeros((8, sh), f32)
    for j in range(G):
        shard += jnp.where(d == j, 1.0, 0.0) * total[:, j * sh : (j + 1) * sh]
    r.vgo[...] = jnp.zeros_like(r.vgo)
    r.vgo[:, 0:sh] = shard
    give("vgo")
    column_result(r.ups, r.upr, r.gup_out, 1, "gup")
    give("gup_out")
    column_result(r.qks, r.qkr, r.gqk_out, 3, "gqk")
    give("gqk_out")
    def drain():
        for write in writes[-2:] + results:
            write.wait()
        for last in pending.values():
            last.wait_send()

    drain()
    assert len(places) == KEYS, len(places)


def hand_over(*refs):
    (out, dx, vgo, gqk, gwo, gup, gdn, evo, gin, gout) = refs[:10]
    results = refs[10:]
    results[8][...] = gin[...].astype(f32)
    results[9][...] = gout[...].astype(f32)

    @pl.when(pl.program_id(0) == 0)
    def _():
        for src, dst in zip((out, dx, gqk, gwo, gup, gdn), results[:2] + results[4:8]):
            dst[...] = src[...]
        for i, dst in enumerate(results[2:4] + results[10:12]):
            dst[...] = vgo[i : i + 1, 0 : dst.shape[1]]
        for i, dst in enumerate(results[12:]):
            dst[...] = evo[i : i + 1, :]


def with_kernel(
    hidden_in,
    cotangent,
    bucket_len,
    live_mask,
    routes,
    ln1_gain,
    ln1_bias,
    w_qkv,
    w_attn_out,
    ln2_gain,
    ln2_bias,
    w_up,
    w_down,
    expert_in,
    expert_out,
    expert_gain,
    expert_bias,
    centroids,
):
    S = lax.axis_size("section")
    G = lax.axis_size("dp")
    M, T, D = hidden_in.shape
    Q = D // S
    FQ = w_up.shape[1] // S
    C = 3 * T // (2 * G)
    sh, shd = w_up.shape[0], w_down.shape[0]
    dims = (S, G, M, T, D, Q, FQ, C, sh, shd)
    scratch = layout(dims)
    names = INPUTS + OUTPUTS + list(scratch) + ["ssem", "rsem", "lsem"]
    vmem = pl.BlockSpec(memory_space=pltpu.VMEM)
    smem = pl.BlockSpec(memory_space=pltpu.SMEM)
    anywhere = pl.BlockSpec(memory_space=pl.ANY)
    shapes = (
        ((M, T, Q), bf16),
        ((M, T, Q), f32),
        ((8, 128), f32),
        ((sh, 3 * D), f32),
        ((sh, D), f32),
        ((sh, S * FQ), f32),
        ((shd, D), f32),
        ((8, Q), f32),
        ((D, FQ), bf16),
        ((FQ, D), bf16),
    )
    outs = pl.pallas_call(
        functools.partial(block_kernel, dims, names),
        name="block",
        out_shape=[jax.ShapeDtypeStruct(*shape) for shape in shapes],
        in_specs=[vmem, vmem, smem] + [vmem] * 13 + [anywhere] * 2,
        out_specs=[anywhere] * len(shapes),
        scratch_shapes=[pltpu.VMEM(*shape) for shape in scratch.values()]
        + [pltpu.SemaphoreType.DMA((KEYS,))] * 2
        + [pltpu.SemaphoreType.DMA((4 + len(RESULTS),))],
        compiler_params=pltpu.CompilerParams(
            collective_id=0, has_side_effects=True, vmem_limit_bytes=63 << 20
        ),
    )(
        hidden_in,
        cotangent,
        bucket_len,
        live_mask,
        jnp.swapaxes(routes, 1, 2),
        ln1_gain.reshape(1, sh),
        ln1_bias.reshape(1, sh),
        ln2_gain.reshape(1, sh),
        ln2_bias.reshape(1, sh),
        expert_gain,
        expert_bias,
        centroids,
        w_qkv,
        w_attn_out,
        w_up,
        w_down,
        expert_in.reshape(S, G // 2, 2, sh, FQ),
        expert_out.reshape(G // 2, 2, shd, D),
    )

    def spec(shape):
        if shape in ((D, FQ), (FQ, D)):
            return pl.BlockSpec((256, shape[1]), lambda i: (i, 0))
        return pl.BlockSpec(shape, lambda i, n=len(shape): (0,) * n)

    finals = (
        shapes[:2]
        + (((1, sh), f32),) * 2
        + shapes[3:7]
        + (((D, FQ), f32), ((FQ, D), f32))
        + (((1, sh), f32),) * 2
        + (((1, Q), f32),) * 3
    )
    outs = pl.pallas_call(
        hand_over,
        name="hand_over",
        grid=(D // 256,),
        out_shape=[jax.ShapeDtypeStruct(*shape) for shape in finals],
        in_specs=[spec(shape) for shape, _ in shapes],
        out_specs=[spec(shape) for shape, _ in finals],
        compiler_params=pltpu.CompilerParams(vmem_limit_bytes=63 << 20),
    )(*outs)
    out, dx, gain1, bias1, gqkv, gwo, gup, gdn, gin, gout, gain2, bias2, eg, eb, ec = outs
    return (
        out,
        dx,
        gain1.reshape(sh),
        bias1.reshape(sh),
        gqkv,
        gwo,
        gain2.reshape(sh),
        bias2.reshape(sh),
        gup,
        gdn,
        gin[None],
        gout[None],
        eg,
        eb,
        ec,
    )


def on_device(*args):
    groups = lax.axis_size("dp")
    rows, shard = args[0].shape[1], args[11].shape[0]
    capacity = 3 * rows // (2 * groups)
    if capacity % 16 or shard % 16 or groups != 8:
        return with_collectives(*args)
    return with_kernel(*args)


def solution(mesh):
    everywhere = ("section", "dp")
    tokens = P(None, "dp", None)
    outs = P(None, "dp", "section")
    per_expert = P("dp", "section")
    return jax.shard_map(
        on_device,
        mesh=mesh,
        in_specs=(
            tokens,
            tokens,
            tokens,
            P(None, "dp"),
            tokens,
            P(everywhere),
            P(everywhere),
            P(everywhere, None),
            P(everywhere, None),
            P(everywhere),
            P(everywhere),
            P(everywhere, None),
            P(everywhere, None),
            P("dp", None, "section"),
            P("dp", "section", None),
            per_expert,
            per_expert,
            per_expert,
        ),
        out_specs=(
            outs,
            outs,
            P(everywhere),
            P(everywhere),
            P(everywhere, None),
            P(everywhere, None),
            P(everywhere),
            P(everywhere),
            P(everywhere, None),
            P(everywhere, None),
            P("dp", None, "section"),
            P("dp", "section", None),
            per_expert,
            per_expert,
            per_expert,
        ),
        check_vma=False,
    )
```

```python
import functools
import math
import types

import jax
import jax.numpy as jnp
from jax import lax
from jax.experimental import pallas as pl
from jax.experimental.pallas import tpu as pltpu
from jax.sharding import PartitionSpec as P

HEADS = 16
SECTION = "section"
DP = "dp"
epsilon = 1e-05
masked_value = -1e30
f32 = jnp.float32
bf16 = jnp.bfloat16


def norm_parts(values):
    center = values - jnp.mean(values, axis=-1, keepdims=True)
    spread = jnp.mean(center * center, axis=-1, keepdims=True)
    rs = lax.rsqrt(spread + epsilon)
    return center * rs, rs


def gelu_back(pre, grad):
    outputs, pullback = jax.vjp(jax.nn.gelu, pre)
    return pullback(grad)[0]


def dot(a, b):
    return jnp.dot(a, b, preferred_element_type=f32)


def dot_tn(a, b):
    return jnp.einsum("rd,re->de", a, b, preferred_element_type=f32)


def dot_nt(a, b):
    return jnp.einsum("re,de->rd", a, b, preferred_element_type=f32)


def sum_scatter(part):
    return lax.psum_scatter(
        part.astype(bf16), SECTION, scatter_dimension=part.ndim - 1, tiled=True
    ).astype(f32)


def gather_features(part):
    return lax.all_gather(part, SECTION, axis=part.ndim - 1, tiled=True)


def with_collectives(
    hidden_in,
    cotangent,
    bucket_len,
    live_mask,
    routes,
    ln1_gain,
    ln1_bias,
    w_qkv,
    w_attn_out,
    ln2_gain,
    ln2_bias,
    w_up,
    w_down,
    expert_in,
    expert_out,
    expert_gain,
    expert_bias,
    centroids,
):
    sections = lax.axis_size(SECTION)
    groups = lax.axis_size(DP)
    section = lax.axis_index(SECTION)
    micro, rows, width = hidden_in.shape
    quarter = width // sections
    heads = HEADS // sections
    size = width // HEADS
    ff = w_up.shape[1] // sections
    capacity = 3 * rows // (2 * groups)
    shard = w_up.shape[0]
    own_cols = section * quarter

    def mine(values):
        return lax.dynamic_slice_in_dim(values, own_cols, quarter, values.ndim - 1)

    def column_group(weight, pieces):
        cols = weight.shape[1] // (pieces * sections)
        parts = weight.reshape(shard, pieces, sections, cols).transpose(2, 0, 1, 3)
        parts = parts.reshape(sections, shard, pieces * cols)
        parts = lax.all_to_all(parts, SECTION, split_axis=0, concat_axis=0, tiled=True)
        full = lax.all_gather(parts, DP, axis=1, tiled=True)
        return full.reshape(width, pieces * cols)

    def column_group_back(grad, pieces):
        cols = grad.shape[1] // pieces
        parts = grad.astype(bf16).reshape(sections, groups * shard, pieces * cols)
        parts = lax.psum_scatter(parts, DP, scatter_dimension=1, tiled=True)
        parts = lax.all_to_all(parts, SECTION, split_axis=0, concat_axis=0, tiled=True)
        parts = parts.reshape(sections, shard, pieces, cols).transpose(1, 2, 0, 3)
        return parts.reshape(shard, pieces * sections * cols).astype(f32)

    def row_group_back(grad):
        return lax.psum_scatter(
            grad.astype(bf16), DP, scatter_dimension=0, tiled=True
        ).astype(f32)

    vectors = lax.all_gather(
        jnp.stack([ln1_gain, ln1_bias, ln2_gain, ln2_bias]), (SECTION, DP), axis=1, tiled=True
    ).astype(f32)
    gain_one, bias_one, gain_two, bias_two = vectors
    expert_vectors = lax.all_gather(
        jnp.concatenate([expert_gain, expert_bias, centroids]), SECTION, axis=1, tiled=True
    ).astype(f32)
    expert_g, expert_b, centroid = expert_vectors
    wqkv = column_group(w_qkv, 3)
    wo = lax.all_gather(w_attn_out, DP, axis=0, tiled=True)
    wup = column_group(w_up, 1)
    wdown = lax.all_gather(w_down, DP, axis=0, tiled=True)
    win = expert_in[0]
    wout = expert_out[0]

    ends = jnp.cumsum(bucket_len[:, 0, :], axis=-1)
    slot_ids = jnp.arange(rows, dtype=jnp.int32)
    segments = jnp.sum((slot_ids[None, :, None] >= ends[:, None, :]).astype(jnp.int32), axis=-1)
    same = segments[:, :, None] == segments[:, None, :]
    causal = slot_ids[None, None, :] <= slot_ids[None, :, None]
    opened = (live_mask[:, None, :] == 1) | (slot_ids[None, None, :] == slot_ids[None, :, None])
    allowed = (same & causal & opened)[:, None]
    chosen = routes[:, :, 0]
    picks = (chosen[:, :, None] == jnp.arange(groups, dtype=jnp.int32)).astype(jnp.int32)
    ranks = jnp.sum((jnp.cumsum(picks, axis=1) - picks) * picks, axis=2)
    places = chosen * capacity + ranks
    place_ids = jnp.arange(groups * capacity, dtype=jnp.int32)
    picked = (places[:, None, :] == place_ids[None, :, None]).astype(bf16)

    def dispatch(values):
        out = jnp.einsum("mpt,mtf->pmf", picked, values, preferred_element_type=f32).astype(bf16)
        out = out.reshape(groups, capacity * micro, quarter)
        return lax.all_to_all(out, DP, split_axis=0, concat_axis=0, tiled=True)

    def give_back(values):
        out = lax.all_to_all(values, DP, split_axis=0, concat_axis=0, tiled=True)
        out = out.reshape(groups * capacity, micro, quarter)
        return jnp.einsum("mpt,pmf->mtf", picked, out, preferred_element_type=f32)

    dge = gather_features(dispatch(mine(cotangent))).reshape(-1, width).astype(f32)

    x = hidden_in.reshape(micro * rows, width).astype(f32)
    n1, rs1 = norm_parts(x)
    a1 = (n1 * gain_one + bias_one).astype(bf16)
    qkv = dot(a1, wqkv).astype(bf16)
    q, k, v = (
        qkv[:, i * quarter : (i + 1) * quarter].reshape(micro, rows, heads, size) for i in range(3)
    )
    scale = size ** (-0.5)
    raw = jnp.einsum("mqhd,mkhd->mhqk", q, k, preferred_element_type=f32) * scale
    scores = jnp.where(allowed, raw, masked_value)
    weights = jnp.exp(scores - jnp.max(scores, axis=-1, keepdims=True))
    probs = weights / jnp.sum(weights, axis=-1, keepdims=True)
    probs_low = probs.astype(bf16)
    mixed = jnp.einsum("mhqk,mkhd->mqhd", probs_low, v, preferred_element_type=f32)
    o = mixed.reshape(micro * rows, quarter).astype(bf16)
    y1q = (mine(x) + sum_scatter(dot(o, wo))).astype(bf16)
    y1 = gather_features(y1q).astype(f32)
    n2, rs2 = norm_parts(y1)
    a2 = (n2 * gain_two + bias_two).astype(bf16)
    h = dot(a2, wup)
    u = jax.nn.gelu(h).astype(bf16)
    y2q = (y1q.astype(f32) + sum_scatter(dot(u, wdown))).astype(bf16)

    xe = gather_features(dispatch(y2q.reshape(micro, rows, quarter))).reshape(-1, width)
    xe = xe.astype(f32)
    ne, rse = norm_parts(xe)
    en = (ne * expert_g + expert_b).astype(bf16)
    he = dot(en, win)
    ue = jax.nn.gelu(he).astype(bf16)
    fe_part = dot(ue, wout)
    alpha = jax.nn.sigmoid(jnp.sum(xe * centroid, axis=-1, keepdims=True))
    fe = sum_scatter(fe_part)
    ge = (alpha * fe).astype(bf16).reshape(groups, capacity * micro, quarter)
    block_out = (
        y2q.reshape(micro, rows, quarter).astype(f32) + give_back(ge)
    ).astype(bf16)

    dfe = (alpha * dge).astype(bf16)
    due = dot_nt(dfe, wout)
    grad_out = dot_tn(ue, dfe)
    dhe = gelu_back(he, due).astype(bf16)
    grad_in = dot_tn(en, dhe)
    den_part = dot_nt(dhe, win)
    gden = den_part * expert_g
    stats = lax.psum(
        jnp.stack(
            [
                jnp.mean(gden, axis=-1),
                jnp.mean(gden * ne, axis=-1),
                jnp.sum(dge * fe_part, axis=-1),
            ]
        ),
        SECTION,
    )[..., None]
    den = sum_scatter(den_part)
    neq = mine(ne)
    dlogit = stats[2] * alpha * (1.0 - alpha)
    dxe_ln = rse * (mine(expert_g) * den - stats[0] - neq * stats[1])
    dxe = (dxe_ln + dlogit * mine(centroid)).astype(bf16)
    grad_expert_gain = jnp.sum(den * neq, axis=0)
    grad_expert_bias = jnp.sum(den, axis=0)
    grad_centroid = jnp.sum(dlogit * mine(xe), axis=0)
    back = give_back(dxe.reshape(groups, capacity * micro, quarter))
    dy2q = (mine(cotangent).astype(f32) + back).astype(bf16).reshape(micro * rows, quarter)

    dy2 = gather_features(dy2q)
    grad_down = dot_tn(u, dy2)
    dh = gelu_back(h, dot_nt(dy2, wdown)).astype(bf16)
    grad_up = dot_tn(a2, dh)
    da2_part = dot_nt(dh, wup)
    gda2 = da2_part * gain_two
    stats = lax.psum(
        jnp.stack([jnp.mean(gda2, axis=-1), jnp.mean(gda2 * n2, axis=-1)]), SECTION
    )[..., None]
    da2 = sum_scatter(da2_part)
    n2q = mine(n2)
    dy1q = dy2q.astype(f32) + rs2 * (mine(gain_two) * da2 - stats[0] - n2q * stats[1])
    dy1q = dy1q.astype(bf16)
    dy1 = gather_features(dy1q)
    grad_wo = dot_tn(o, dy1)
    do = dot_nt(dy1, wo).astype(bf16).reshape(micro, rows, heads, size)
    dp = jnp.einsum("mqhd,mkhd->mhqk", do, v, preferred_element_type=f32)
    dv = jnp.einsum("mhqk,mqhd->mkhd", probs_low, do, preferred_element_type=f32)
    delta = jnp.sum(probs * dp, axis=-1, keepdims=True)
    ds = (probs * (dp - delta)).astype(bf16)
    dq = jnp.einsum("mhqk,mkhd->mqhd", ds, k, preferred_element_type=f32) * scale
    dk = jnp.einsum("mhqk,mqhd->mkhd", ds, q, preferred_element_type=f32) * scale
    dqkv = jnp.concatenate(
        [part.reshape(micro * rows, quarter) for part in (dq, dk, dv)], axis=1
    ).astype(bf16)
    grad_qkv = dot_tn(a1, dqkv)
    da1_part = dot_nt(dqkv, wqkv)
    gda1 = da1_part * gain_one
    stats = lax.psum(
        jnp.stack([jnp.mean(gda1, axis=-1), jnp.mean(gda1 * n1, axis=-1)]), SECTION
    )[..., None]
    da1 = sum_scatter(da1_part)
    n1q = mine(n1)
    dx = dy1q.astype(f32) + rs1 * (mine(gain_one) * da1 - stats[0] - n1q * stats[1])

    vector_grads = lax.psum_scatter(
        jnp.stack(
            [
                jnp.sum(da1 * n1q, axis=0),
                jnp.sum(da1, axis=0),
                jnp.sum(da2 * n2q, axis=0),
                jnp.sum(da2, axis=0),
            ]
        ),
        DP,
        scatter_dimension=1,
        tiled=True,
    )
    return (
        block_out,
        dx.reshape(micro, rows, quarter),
        vector_grads[0],
        vector_grads[1],
        column_group_back(grad_qkv, 3),
        row_group_back(grad_wo),
        vector_grads[2],
        vector_grads[3],
        column_group_back(grad_up, 1),
        row_group_back(grad_down),
        grad_in[None],
        grad_out[None],
        grad_expert_gain[None],
        grad_expert_bias[None],
        grad_centroid[None],
    )


MESH = pl.DeviceIdType.MESH
KEYS = 101
CHAIN = {
    "y1": 0,
    "y1g": 1,
    "y2": 0,
    "xe": 1,
    "den": 0,
    "dy2": 1,
    "da2": 0,
    "dy1": 1,
    "da1": 0,
}
SHARED = {
    "geb": "y2d",
    "dxb": "cot",
    "fe": "dge",
    "est": "stats",
    "tst": "stats",
    "vs": "v2",
    "gdn": "wdn",
    "gup": "wup",
    "gwo": "wo",
    "gqk": "wqkv",
    "p": "c",
    "n": "near",
    "nf": "near far",
    "f": "far",
}


LEGS = {
    "xe": ("x", "y", "xy", "yx"),
    "den": ("x0", "x2", "y1", "y2", "xy", "yx"),
}


def semaphore_of(k):
    if k[0] in LEGS:
        leg = LEGS[k[0]].index(k[2])
        return ("chain", CHAIN[k[0]], k[1], leg + 1) if leg < 3 else ("leg", k[0], k[1], leg)
    if k[0] in CHAIN:
        return ("chain", CHAIN[k[0]]) + k[1:]
    if k[0] == "q1":
        return ("stats", k[1], k[2]) if k[1] < 2 else ("chain", 1, 0, k[2])
    if k[0] == "v1":
        return "chain", 1, 1, k[1]
    if k[1] == "s":
        return "u1" if k[0] == "gup" else "e1", k[2]
    if k[0] == "tst":
        return ("stats",) + k[2:]
    return tuple(SHARED.get(part, part) for part in k)
CHUNK = 128


def tn(a, b):
    return lax.dot_general(a, b, (((0,), (0,)), ((), ())), preferred_element_type=f32)


def nt(a, b):
    return lax.dot_general(a, b, (((1,), (1,)), ((), ())), preferred_element_type=f32)


def tanh_parts(v):
    root = 0.7978845608028654
    t = jnp.tanh(root * (v + 0.044715 * (v * v * v)))
    return t, root


def gelu_both(v):
    t, root = tanh_parts(v)
    half = 0.5 * (1.0 + t)
    return v * half, half + 0.5 * v * (1.0 - t * t) * root * (1.0 + 0.134145 * (v * v))


def to_rows(columns):
    lane = lax.broadcasted_iota(jnp.int32, (columns[0].shape[0], 128), 1)
    wide = jnp.zeros(lane.shape, f32)
    for i, column in enumerate(columns):
        wide = jnp.where(lane == i, column, wide)
    return wide.T[:8]


def to_columns(rows):
    return jnp.concatenate([rows, jnp.zeros((120, rows.shape[1]), f32)], axis=0).T


def layout(dims):
    S, G, M, T, D, Q, FQ, C, sh, shd = dims
    nz = G // 2
    R = G * C
    heads = HEADS // S
    return dict(
        wqkv=((S, nz, 2, sh, 3 * Q), bf16),
        wo=((nz, 2, sh, D), bf16),
        wup=((S, nz, 2, sh, FQ), bf16),
        wdn=((nz, 2, shd, D), bf16),
        win=((S, nz, 2, sh, FQ), bf16),
        wout=((nz, 2, shd, D), bf16),
        vin=((8, 128), f32),
        ein=((8, Q), f32),
        vg=((S, G, 8, 128), f32),
        vecs=((8, D), f32),
        evec=((8, D), f32),
        mask=((M, T, T), f32),
        perm=((M, R, T), bf16),
        cots=((M, R, Q), bf16),
        y2s=((M, R, Q), bf16),
        ges=((M, R, Q), bf16),
        dxs=((M, R, Q), bf16),
        ger=((M, R, Q), bf16),
        dxr=((M, R, Q), bf16),
        tst=((M, T, 128), f32),
        est=((M, R, 128), f32),
        a1=((M, T, D), bf16),
        a2=((M, T, D), bf16),
        qkv=((M, T, 3 * Q), bf16),
        probs=((M, heads, T, T), f32),
        o=((M, T, Q), bf16),
        y1=((M, T, D), bf16),
        h=((M, T, FQ), f32),
        u=((M, T, FQ), bf16),
        y2q=((M, T, Q), bf16),
        xe=((M, R, D), bf16),
        dge=((M, R, D), bf16),
        en=((M, R, D), bf16),
        ue=((M, R, FQ), bf16),
        dhe=((M, R, FQ), bf16),
        dfe=((M, R, D), bf16),
        slope=((R, FQ), f32),
        fes=((M, S - 1, R, Q), bf16),
        fer=((M, S - 1, R, Q), bf16),
        feo=((M, R, Q), f32),
        dns=((M, S - 1, R, Q), bf16),
        dnr=((M, S - 1, R, Q), bf16),
        dno=((M, R, Q), f32),
        ess=((M, 8, R), f32),
        esr=((M, S - 1, 8, R), f32),
        ts=((M, S - 1, T, Q), bf16),
        r1=((M, S - 1, T, Q), bf16),
        r2=((M, S - 1, T, Q), bf16),
        own=((M, T, Q), f32),
        tss=((2, M, 8, T), f32),
        tsr=((2, M, S - 1, 8, T), f32),
        dy2=((M, T, D), bf16),
        dh=((M, T, FQ), bf16),
        dqkv=((M, T, 3 * Q), bf16),
        gwo=((nz, 2, sh, D), bf16),
        gqk=((S, nz, 2, sh, 3 * Q), bf16),
        bdn=((nz, shd, D), bf16),
        bup=((S, nz, sh, FQ), bf16),
        bwo=((nz, sh, D), bf16),
        bqk=((S, nz, sh, 3 * Q), bf16),
        zdn=((nz - 1, shd, D), bf16),
        zup=((nz - 1, S, sh, FQ), bf16),
        zwo=((nz - 1, sh, D), bf16),
        zqk=((nz - 1, S, sh, 3 * Q), bf16),
        ups=((S, sh, FQ), bf16),
        upr=((S - 1, sh, FQ), bf16),
        qks=((S, sh, 3 * Q), bf16),
        qkr=((S - 1, sh, 3 * Q), bf16),
        stage=((2, 256, D), bf16),
        out=((M, T, Q), bf16),
        dx=((M, T, Q), f32),
        vgo=((8, 128), f32),
        gqk_out=((sh, 3 * D), f32),
        gwo_out=((sh, D), f32),
        gup_out=((sh, S * FQ), f32),
        gdn_out=((shd, D), f32),
        evo=((8, Q), f32),
        vsum=((8, Q), f32),
        vsr=((G - 1, 8, Q), f32),
    )


INPUTS = [
    "hidden",
    "cot",
    "bucket",
    "live",
    "routes",
    "gain_one",
    "bias_one",
    "gain_two",
    "bias_two",
    "gain_e",
    "bias_e",
    "centroid",
    "wqkv_in",
    "wo_in",
    "wup_in",
    "wdn_in",
    "win_in",
    "wout_in",
]
RESULTS = [
    "out",
    "dx",
    "vgo",
    "gqk_out",
    "gwo_out",
    "gup_out",
    "gdn_out",
    "evo",
]
OUTPUTS = ["to_" + name for name in RESULTS] + ["gin_out", "gout_out"]


def block_kernel(dims, names, *args):
    r = types.SimpleNamespace(**dict(zip(names, args)))
    S, G, M, T, D, Q, FQ, C, sh, shd = dims
    nz = G // 2
    R = G * C
    heads = HEADS // S
    size = D // HEADS
    scale = size ** (-0.5)
    s = lax.axis_index(SECTION)
    d = lax.axis_index(DP)
    z = lax.div(d, 2)
    c = lax.rem(d, 2)
    beside = (s, d + 1 - 2 * c)
    near = z + 1 - 2 * lax.rem(z, 2)
    far = lax.rem(z + 2, nz)
    near_far = lax.rem(near + 2, nz)
    beside_x = s + 1 - 2 * lax.rem(s, 2)
    beside_y = lax.rem(s + 2, S)
    across = lax.rem(beside_x + 2, S)

    def sec(i):
        return lax.rem(s + i, S)

    def dpi(j):
        return lax.rem(d + j, G)

    def zi(j):
        return lax.rem(z + j, nz)

    def to_sec(i):
        return (sec(i), d)

    def to_dp(j):
        return (s, dpi(j))

    def to_z(j):
        return (s, zi(j) * 2 + c)

    def col(q, n=Q):
        return pl.ds(pl.multiple_of(q * n, n), n)

    def seats(e):
        return pl.ds(pl.multiple_of(e * C, C), C)

    mine = col(s)
    places = {}
    pending = {}

    def copy(src, dst, k, device):
        i = places.setdefault(semaphore_of(k), len(places))
        return pltpu.make_async_remote_copy(
            src_ref=src,
            dst_ref=dst,
            send_sem=r.ssem.at[i],
            recv_sem=r.rsem.at[i],
            device_id=device,
            device_id_type=MESH,
        )

    def send(src, dst, k, device):
        sent(k)
        pending[semaphore_of(k)] = copy(src, dst, k, device)
        pending[semaphore_of(k)].start()

    def sent(k):
        last = pending.pop(semaphore_of(k), None)
        if last is not None:
            last.wait_send()

    def recv(dst, k):
        copy(dst, dst, k, beside).wait_recv()

    def each(rows, body):
        step = math.gcd(rows, CHUNK)

        @pl.loop(0, rows // step)
        def _(i):
            body(pl.ds(pl.multiple_of(i * step, step), step))

    others = range(1, S)

    def gather_send(ref, m, k):
        for i in others:
            send(ref.at[m, :, mine], ref.at[m, :, mine], (k, m, i), to_sec(i))

    def gather_recv(ref, m, k, then=None):
        for i in others:
            recv(ref.at[m, :, col(sec(S - i))], (k, m, i))
            if then is not None and i == S - 2:
                then()

    def sum_send(tile, out, arrive, own, m, k, before=None, hold=False):
        for i in others:
            if before is not None:
                sent((before, m, i))
            out[m, i - 1] = tile(sec(i)).astype(bf16)
        own[m] = tile(s)
        if not hold:
            sum_start(out, arrive, m, k)

    def sum_start(out, arrive, m, k):
        for i in others:
            send(out.at[m, i - 1], arrive.at[m, i - 1], (k, m, i), to_sec(i))

    def sum_recv(arrive, m, k, then=None):
        for i in others:
            recv(arrive.at[m, i - 1], (k, m, i))
            if then is not None and i == S - 2:
                then()

    def summed(own, arrive, m, rows):
        total = own[m, rows]
        for i in others:
            total += arrive[m, i - 1, rows].astype(f32)
        return total

    top, low = slice(0, R // 2), slice(R // 2, R)

    def legs_send(ref, m, k):
        send(ref.at[m, :, mine], ref.at[m, :, mine], (k, m, "x"), (beside_x, d))
        send(ref.at[m, :, mine], ref.at[m, :, mine], (k, m, "y"), (beside_y, d))

    def legs_pass(ref, m, k):
        recv(ref.at[m, :, col(beside_x)], (k, m, "x"))
        block = ref.at[m, top, col(beside_x)]
        send(block, block, (k, m, "xy"), (beside_y, d))
        recv(ref.at[m, :, col(beside_y)], (k, m, "y"))
        block = ref.at[m, low, col(beside_y)]
        send(block, block, (k, m, "yx"), (beside_x, d))

    def legs_recv(ref, m, k):
        recv(ref.at[m, top, col(across)], (k, m, "xy"))
        recv(ref.at[m, low, col(across)], (k, m, "yx"))

    quarters = (beside_x, beside_y, across)

    def legs_sum_send(tile, out, arrive, own, m, k):
        for i, q in enumerate(quarters):
            out[m, i] = tile(q).astype(bf16)
        own[m] = tile(s)
        for i in (2, 0):
            send(out.at[m, i, top], arrive.at[m, i, top], (k, m, "x" + str(i)), (beside_x, d))
        for i in (2, 1):
            send(out.at[m, i, low], arrive.at[m, i, low], (k, m, "y" + str(i)), (beside_y, d))

    def legs_sum_pass(out, arrive, m, k):
        recv(arrive.at[m, 2, top], (k, m, "x2"))
        both = out[m, 1, top].astype(f32) + arrive[m, 2, top].astype(f32)
        out[m, 1, top] = both.astype(bf16)
        send(out.at[m, 1, top], arrive.at[m, 1, top], (k, m, "xy"), (beside_y, d))
        recv(arrive.at[m, 2, low], (k, m, "y2"))
        both = out[m, 0, low].astype(f32) + arrive[m, 2, low].astype(f32)
        out[m, 0, low] = both.astype(bf16)
        send(out.at[m, 0, low], arrive.at[m, 0, low], (k, m, "yx"), (beside_x, d))

    def legs_sum_recv(arrive, m, k):
        recv(arrive.at[m, 0, top], (k, m, "x0"))
        recv(arrive.at[m, 1, low], (k, m, "y1"))
        recv(arrive.at[m, 1, top], (k, m, "xy"))
        recv(arrive.at[m, 0, low], (k, m, "yx"))

    def dispatch_send(src, dst, m, k):
        dst[m, seats(d), mine] = src[m, seats(d)]
        for j in range(1, G):
            send(src.at[m, seats(dpi(j))], dst.at[m, seats(d), mine], (k, m, j), to_dp(j))

    def dispatch_recv(dst, m, k):
        for j in range(1, G):
            recv(dst.at[m, seats(dpi(G - j)), mine], (k, m, j))

    def return_send(src, dst, m, k):
        dst[m, seats(d)] = src[m, seats(d)]
        for j in range(1, G):
            send(src.at[m, seats(dpi(j))], dst.at[m, seats(d)], (k, m, j), to_dp(j))

    def return_recv(dst, m, k):
        for j in range(1, G):
            recv(dst.at[m, seats(dpi(G - j))], (k, m, j))

    def part(ref, zz, cc):
        return ref.at[:, zz, cc] if len(ref.shape) == 5 else ref.at[zz, cc]

    def weight_start(ref, k):
        send(part(ref, z, c), part(ref, z, c), (k, "far"), (s, far * 2 + c))
        send(part(ref, z, c), part(ref, z, c), (k, "c", 0), beside)

    def weight_next(ref, k):
        send(part(ref, z, c), part(ref, z, c), (k, "near"), (s, near * 2 + c))

    def weight_far(ref, k):
        recv(part(ref, far, c), (k, "far"))
        send(part(ref, far, c), part(ref, far, c), (k, "near far"), (s, near * 2 + c))
        send(part(ref, far, c), part(ref, far, c), (k, "c", 1), beside)

    def weight_near(ref, k):
        recv(part(ref, near, c), (k, "near"))
        send(part(ref, near, c), part(ref, near, c), (k, "c", 2), beside)
        recv(part(ref, near_far, c), (k, "near far"))
        send(part(ref, near_far, c), part(ref, near_far, c), (k, "c", 3), beside)

    def weight_wait(ref, k):
        for i, zz in enumerate((z, far, near, near_far)):
            recv(part(ref, zz, 1 - c), (k, "c", i))

    load_in = pltpu.make_async_copy(r.win_in, r.win, r.lsem.at[0])
    load_out = pltpu.make_async_copy(r.wout_in, r.wout, r.lsem.at[1])

    early = lax.broadcasted_iota(jnp.int32, (T, T), 0)
    late = lax.broadcasted_iota(jnp.int32, (T, T), 1)

    def seat_tokens(m):
        route = r.routes[m]
        expert_ids = lax.broadcasted_iota(jnp.int32, (G, T), 0)
        picks = jnp.where(expert_ids == route, 1.0, 0.0)
        before = jnp.where(early < late, 1.0, 0.0).astype(bf16)
        counts = jnp.dot(picks.astype(bf16), before, preferred_element_type=f32)
        rank = jnp.sum(counts * picks, axis=0, keepdims=True)
        place = route.astype(f32) * float(C) + rank
        seat_ids = lax.broadcasted_iota(jnp.int32, (R, T), 0).astype(f32)
        r.perm[m] = jnp.where(seat_ids == place, 1.0, 0.0).astype(bf16)
        r.cots[m] = jnp.dot(r.perm[m], r.cot[m, :, mine], preferred_element_type=f32).astype(bf16)

    def entry():
        barrier = pltpu.get_barrier_semaphore()
        for i in others:
            pl.semaphore_signal(barrier, inc=1, device_id=to_sec(i), device_id_type=MESH)
        for j in range(1, G):
            pl.semaphore_signal(barrier, inc=1, device_id=to_dp(j), device_id_type=MESH)
        r.vin[...] = jnp.zeros_like(r.vin)
        for i, ref in enumerate((r.gain_one, r.bias_one, r.gain_two, r.bias_two)):
            r.vin[i : i + 1, 0:sh] = ref[...].astype(f32)
        r.ein[...] = jnp.zeros_like(r.ein)
        for i, ref in enumerate((r.gain_e, r.bias_e, r.centroid)):
            r.ein[i : i + 1, :] = ref[...].astype(f32)
        r.vg[s, d] = r.vin[...]
        r.evec[:, mine] = r.ein[...]
        for piece in range(3):
            r.wqkv[s, z, c, :, piece * Q : (piece + 1) * Q] = r.wqkv_in[
                :, pl.ds(pl.multiple_of(piece * D + s * Q, Q), Q)
            ]
        r.wo[z, c] = r.wo_in[...]
        seat_tokens(0)
        seat_tokens(1)
        pl.semaphore_wait(barrier, S + G - 2)
        for i in others:
            send(r.vin, r.vg.at[s, d], ("v1", i), to_sec(i))
        for i in others:
            for piece in range(3):
                src = r.wqkv_in.at[:, pl.ds(pl.multiple_of(piece * D + sec(i) * Q, Q), Q)]
                dst = r.wqkv.at[s, z, c, :, piece * Q : (piece + 1) * Q]
                send(src, dst, ("q1", piece, i), to_sec(i))
        dispatch_send(r.cots, r.dge, 0, "cot")
        dispatch_send(r.cots, r.dge, 1, "cot")
        for i in others:
            recv(r.vg.at[sec(S - i), d], ("v1", i))
        for j in range(1, G):
            send(r.vg.at[:, d], r.vg.at[:, d], ("v2", j), to_dp(j))
        for i in others:
            for piece in range(3):
                recv(r.wqkv.at[sec(S - i), z, c, :, piece * Q : (piece + 1) * Q], ("q1", piece, i))
        weight_start(r.wqkv, "wqkv")
        weight_next(r.wqkv, "wqkv")
        for i in others:
            send(r.wup_in.at[:, col(sec(i), FQ)], r.wup.at[s, z, c], ("u1", i), to_sec(i))
            send(r.ein, r.evec.at[:, mine], ("e1", i), to_sec(i))
        load_in.start()
        load_out.start()

    def mask_tokens(m):
        end = r.bucket[m, 0, 0]
        seg_q = (early >= end).astype(jnp.int32)
        seg_k = (late >= end).astype(jnp.int32)
        for b in range(1, r.bucket.shape[2]):
            end = end + r.bucket[m, 0, b]
            seg_q += (early >= end).astype(jnp.int32)
            seg_k += (late >= end).astype(jnp.int32)
        live = jnp.broadcast_to(r.live[m : m + 1, :], (T, T))
        allowed = (seg_q == seg_k) & (late <= early) & ((live == 1) | (late == early))
        r.mask[m] = jnp.where(allowed, 1.0, 0.0)

    def spread_vectors():
        for j in range(1, G):
            recv(r.vg.at[:, dpi(G - j)], ("v2", j))
        spread_row = lax.broadcasted_iota(jnp.int32, (128, D), 0)
        spread_lane = lax.broadcasted_iota(jnp.int32, (128, D), 1)
        spread = jnp.where(lax.rem(spread_lane, sh) == spread_row, 1.0, 0.0).astype(bf16)
        stacked = r.vg[...].reshape(S * G * 8, 128).astype(bf16)
        wide = jnp.dot(stacked, spread, preferred_element_type=f32)
        row_id = lax.broadcasted_iota(jnp.int32, (S * G * 8, D), 0)
        lane_id = lax.broadcasted_iota(jnp.int32, (S * G * 8, D), 1)
        low = lax.shift_right_logical(row_id, 3) * sh
        wide = jnp.where((lane_id >= low) & (lane_id < low + sh), wide, 0.0)
        r.vecs[...] = jnp.sum(wide.reshape(S * G, 8, D), axis=0)

    def normed(values):
        mean = jnp.mean(values, axis=1, keepdims=True)
        center = values - mean
        rs = lax.rsqrt(jnp.mean(center * center, axis=1, keepdims=True) + epsilon)
        return center * rs, mean, rs

    def norm_tokens(src, dst, m, at):
        gain = r.vecs[2 * at : 2 * at + 1, :]
        bias = r.vecs[2 * at + 1 : 2 * at + 2, :]

        def body(rows):
            n, mean, rs = normed(src[m, rows].astype(f32))
            r.tst[m, rows, 2 * at : 2 * at + 1] = mean
            r.tst[m, rows, 2 * at + 1 : 2 * at + 2] = rs
            dst[m, rows] = (n * gain + bias).astype(bf16)

        each(T, body)

    entry()
    r.wup[s, z, c] = r.wup_in[:, col(s, FQ)]
    r.wdn[z, c] = r.wdn_in[...]
    mask_tokens(0)
    mask_tokens(1)
    for m in range(M):
        dispatch_recv(r.dge, m, "cot")
        gather_send(r.dge, m, "dge")
    weight_far(r.wqkv, "wqkv")
    weight_start(r.wo, "wo")
    weight_next(r.wo, "wo")
    for i in others:
        recv(r.evec.at[:, col(sec(S - i))], ("e1", i))
        recv(r.wup.at[sec(S - i), z, c], ("u1", i))
    weight_start(r.wup, "wup")
    spread_vectors()
    norm_tokens(r.hidden, r.a1, 0, 0)
    norm_tokens(r.hidden, r.a1, 1, 0)
    weight_near(r.wqkv, "wqkv")
    weight_far(r.wo, "wo")
    weight_next(r.wup, "wup")
    weight_wait(r.wqkv, "wqkv")

    def attend(m):
        @pl.loop(0, 3, unroll=True)
        def _(t):
            w = r.wqkv[:, :, :, :, col(t)].reshape(D, Q)
            r.qkv[m, :, col(t)] = jnp.dot(r.a1[m], w, preferred_element_type=f32).astype(bf16)

        for hh in range(heads):
            at = hh * size
            q = r.qkv[m, :, at : at + size]
            k = r.qkv[m, :, Q + at : Q + at + size]
            v = r.qkv[m, :, 2 * Q + at : 2 * Q + at + size]
            scores = jnp.where(r.mask[m] > 0.0, nt(q, k) * scale, masked_value)
            weights = jnp.exp(scores - jnp.max(scores, axis=1, keepdims=True))
            p = weights / jnp.sum(weights, axis=1, keepdims=True)
            r.probs[m, hh] = p
            mixed = jnp.dot(p.astype(bf16), v, preferred_element_type=f32)
            r.o[m, :, at : at + size] = mixed.astype(bf16)

    def y1_tile(m):
        return lambda q: jnp.dot(
            r.o[m], r.wo[:, :, :, col(q)].reshape(Q, Q), preferred_element_type=f32
        )

    def finish_y1(m):
        sum_recv(r.r1, m, "y1")

        def body(rows):
            total = r.hidden[m, rows, mine].astype(f32) + summed(r.own, r.r1, m, rows)
            r.y1[m, rows, mine] = total.astype(bf16)

        each(T, body)
        gather_send(r.y1, m, "y1g")

    attend(0)
    weight_near(r.wo, "wo")
    weight_wait(r.wo, "wo")
    sum_send(y1_tile(0), r.ts, r.r1, r.own, 0, "y1")
    attend(1)
    sum_send(y1_tile(1), r.ts, r.r1, r.own, 1, "y1")
    weight_far(r.wup, "wup")
    weight_start(r.wdn, "wdn")
    weight_next(r.wdn, "wdn")
    finish_y1(0)
    finish_y1(1)
    weight_near(r.wup, "wup")
    weight_wait(r.wup, "wup")

    def up(m):
        gather_recv(r.y1, m, "y1g")
        norm_tokens(r.y1, r.a2, m, 1)

        @pl.loop(0, FQ // Q, unroll=True)
        def _(t):
            w = r.wup[:, :, :, :, col(t)].reshape(D, Q)
            pre = jnp.dot(r.a2[m], w, preferred_element_type=f32)
            value, slope = gelu_both(pre)
            r.u[m, :, col(t)] = value.astype(bf16)
            r.h[m, :, col(t)] = slope

    def y2_tile(m):
        return lambda q: jnp.dot(
            r.u[m], r.wdn[:, :, :, col(q)].reshape(FQ, Q), preferred_element_type=f32
        )

    weight_far(r.wdn, "wdn")
    up(0)
    up(1)
    weight_near(r.wdn, "wdn")
    weight_wait(r.wdn, "wdn")
    sum_send(y2_tile(0), r.ts, r.r2, r.own, 0, "y2", "y1")
    sum_send(y2_tile(1), r.ts, r.r2, r.own, 1, "y2", "y1", hold=True)

    def finish_y2(m):
        sum_recv(r.r2, m, "y2", None if m else lambda: sum_start(r.ts, r.r2, 1, "y2"))

        def body(rows):
            total = r.y1[m, rows, mine].astype(f32) + summed(r.own, r.r2, m, rows)
            r.y2q[m, rows] = total.astype(bf16)

        each(T, body)
        r.y2s[m] = jnp.dot(r.perm[m], r.y2q[m], preferred_element_type=f32).astype(bf16)
        dispatch_send(r.y2s, r.xe, m, "y2d")

    finish_y2(0)
    dispatch_recv(r.xe, 0, "y2d")
    legs_send(r.xe, 0, "xe")
    finish_y2(1)
    legs_pass(r.xe, 0, "xe")
    dispatch_recv(r.xe, 1, "y2d")
    legs_send(r.xe, 1, "xe")
    load_in.wait()
    load_out.wait()

    def expert(m):
        gather_recv(r.dge, m, "dge")
        legs_recv(r.xe, m, "xe")
        gain, bias, centroid = r.evec[0:1, :], r.evec[1:2, :], r.evec[2:3, :]

        def body(rows):
            v = r.xe[m, rows].astype(f32)
            n, mean, rs = normed(v)
            alpha = jax.nn.sigmoid(jnp.sum(v * centroid, axis=1, keepdims=True))
            r.est[m, rows, 0:1] = mean
            r.est[m, rows, 1:2] = rs
            r.est[m, rows, 2:3] = alpha
            r.en[m, rows] = (n * gain + bias).astype(bf16)
            r.dfe[m, rows] = (alpha * r.dge[m, rows].astype(f32)).astype(bf16)

        each(R, body)

        @pl.loop(0, FQ // Q, unroll=True)
        def _(t):
            w = r.win[:, :, :, :, col(t)].reshape(D, Q)
            pre = jnp.dot(r.en[m], w, preferred_element_type=f32)
            value, slope = gelu_both(pre)
            r.ue[m, :, col(t)] = value.astype(bf16)
            r.slope[:, col(t)] = slope

        if m == 0:
            legs_pass(r.xe, 1, "xe")
        else:
            legs_sum_pass(r.dns, r.dnr, 0, "den")
        stats = [jnp.zeros((R, 1), f32) for _ in range(3)]

        def fe_tile(q):
            tile = jnp.dot(
                r.ue[m], r.wout[:, :, :, col(q)].reshape(FQ, Q), preferred_element_type=f32
            )
            stats[2] += jnp.sum(tile * r.dge[m, :, col(q)].astype(f32), axis=1, keepdims=True)
            return tile

        def den_tile(q):
            return nt(r.dhe[m], r.win[q].reshape(Q, FQ))

        @pl.loop(0, FQ // Q, unroll=True)
        def _(t):
            due = nt(r.dfe[m], r.wout[t].reshape(Q, D))
            r.dhe[m, :, col(t)] = (due * r.slope[:, col(t)]).astype(bf16)

        legs_sum_send(den_tile, r.dns, r.dnr, r.dno, m, "den")
        sum_send(fe_tile, r.fes, r.fer, r.feo, m, "fe", hold=True)
        for i, q in enumerate(quarters + (s,)):
            tile = r.dns[m, i].astype(f32) if i < S - 1 else r.dno[m]
            scaled = tile * r.evec[0:1, col(q)]
            n = (r.xe[m, :, col(q)].astype(f32) - r.est[m, :, 0:1]) * r.est[m, :, 1:2]
            stats[0] += jnp.sum(scaled, axis=1, keepdims=True)
            stats[1] += jnp.sum(scaled * n, axis=1, keepdims=True)
        r.ess[m] = to_rows(stats)
        for i in others:
            send(r.ess.at[m], r.esr.at[m, i - 1], ("est", m, i), to_sec(i))

    expert(0)
    expert(1)

    def finish_den(m):
        legs_sum_recv(r.dnr, m, "den")
        total = r.ess[m]
        for i in others:
            recv(r.esr.at[m, i - 1], ("est", m, i))
            total += r.esr[m, i - 1]
        r.est[m, :, 8:16] = to_columns(total)[:, 0:8]
        gain, centroid = r.evec[0:1, mine], r.evec[2:3, mine]
        if m == 0:
            r.evo[...] = jnp.zeros_like(r.evo)

        def body(rows):
            den = r.dno[m, rows] + r.dnr[m, 0, rows].astype(f32) + r.dnr[m, 1, rows].astype(f32)
            xq = r.xe[m, rows, mine].astype(f32)
            rs, alpha = r.est[m, rows, 1:2], r.est[m, rows, 2:3]
            n = (xq - r.est[m, rows, 0:1]) * rs
            m1, m2 = r.est[m, rows, 8:9] * (1.0 / D), r.est[m, rows, 9:10] * (1.0 / D)
            dlogit = r.est[m, rows, 10:11] * alpha * (1.0 - alpha)
            grad = rs * (gain * den - m1 - n * m2) + dlogit * centroid
            r.dxs[m, rows] = grad.astype(bf16)
            r.evo[0:1, :] += jnp.sum(den * n, axis=0, keepdims=True)
            r.evo[1:2, :] += jnp.sum(den, axis=0, keepdims=True)
            r.evo[2:3, :] += jnp.sum(dlogit * xq, axis=0, keepdims=True)

        each(R, body)
        return_send(r.dxs, r.dxr, m, "dxb")

    def finish_fe(m):
        sum_recv(r.fer, m, "fe")

        def body(rows):
            fe = summed(r.feo, r.fer, m, rows)
            r.ges[m, rows] = (r.est[m, rows, 2:3] * fe).astype(bf16)

        each(R, body)
        return_send(r.ges, r.ger, m, "geb")

    def finish_dxe(m):
        return_recv(r.dxr, m, "dxb")
        back = tn(r.perm[m], r.dxr[m])
        r.dy2[m, :, mine] = (r.cot[m, :, mine].astype(f32) + back).astype(bf16)
        gather_send(r.dy2, m, "dy2")

    finish_den(0)
    legs_sum_pass(r.dns, r.dnr, 1, "den")
    finish_dxe(0)
    finish_den(1)

    writes = []
    results = []

    def give(name):
        i = RESULTS.index(name)
        one = pltpu.make_async_copy(getattr(r, name), getattr(r, "to_" + name), r.lsem.at[4 + i])
        one.start()
        results.append(one)

    def expert_weights(left, right, out):
        for t in range(D // 256):
            slot = len(writes) % 2
            if len(writes) >= 2:
                writes[-2].wait()
            rows = slice(t * 256, (t + 1) * 256)
            lhs = left[:, :, rows].reshape(M * R, 256)
            r.stage[slot] = tn(lhs, right[...].reshape(M * R, D)).astype(bf16)
            writes.append(pltpu.make_async_copy(r.stage.at[slot], out.at[rows], r.lsem.at[2 + slot]))
            writes[-1].start()

    give("evo")

    finish_dxe(1)

    def token_stats(m, at, src):
        stats = [jnp.zeros((T, 1), f32) for _ in range(2)]
        mean, rs = r.tst[m, :, 2 * at : 2 * at + 1], r.tst[m, :, 2 * at + 1 : 2 * at + 2]
        for i in range(S):
            q = sec(i)
            tile = r.ts[m, i - 1].astype(f32) if i else r.own[m]
            scaled = tile * r.vecs[2 * at : 2 * at + 1, col(q)]
            n = (src[m, :, col(q)].astype(f32) - mean) * rs
            stats[0] += jnp.sum(scaled, axis=1, keepdims=True)
            stats[1] += jnp.sum(scaled * n, axis=1, keepdims=True)
        return stats

    def stats_send(m, at, stats):
        r.tss[at, m] = to_rows(stats)
        for i in others:
            send(r.tss.at[at, m], r.tsr.at[at, m, i - 1], ("tst", at, m, i), to_sec(i))

    def stats_recv(m, at):
        total = r.tss[at, m]
        for i in others:
            recv(r.tsr.at[at, m, i - 1], ("tst", at, m, i))
            total += r.tsr[at, m, i - 1]
        r.tst[m, :, 8:16] = to_columns(total)[:, 0:8]

    def dense_back(m):
        if m == 0:
            gather_recv(r.dy2, m, "dy2")

        @pl.loop(0, FQ // Q, unroll=True)
        def _(t):
            du = nt(r.dy2[m], r.wdn[t].reshape(Q, D))
            r.dh[m, :, col(t)] = (du * r.h[m, :, col(t)]).astype(bf16)

        sum_send(
            lambda q: nt(r.dh[m], r.wup[q].reshape(Q, FQ)),
            r.ts,
            r.r1,
            r.own,
            m,
            "da2",
            "y2",
            hold=m == 0,
        )
        stats_send(m, 1, token_stats(m, 1, r.y1))

    def norm_back(m, at, src, grad_in, own, arrive, emit):
        gain = r.vecs[2 * at : 2 * at + 1, mine]

        def body(rows):
            grad = summed(own, arrive, m, rows)
            mean, rs = r.tst[m, rows, 2 * at : 2 * at + 1], r.tst[m, rows, 2 * at + 1 : 2 * at + 2]
            n = (src[m, rows, mine].astype(f32) - mean) * rs
            m1, m2 = r.tst[m, rows, 8:9] * (1.0 / D), r.tst[m, rows, 9:10] * (1.0 / D)
            emit(rows, grad_in[m, rows, mine].astype(f32) + rs * (gain * grad - m1 - n * m2))
            r.vsum[2 * at : 2 * at + 1, :] += jnp.sum(grad * n, axis=0, keepdims=True)
            r.vsum[2 * at + 1 : 2 * at + 2, :] += jnp.sum(grad, axis=0, keepdims=True)

        each(T, body)

    def finish_da2(m):
        sum_recv(r.r1, m, "da2")
        stats_recv(m, 1)
        for i in others:
            sent(("y1g", m, i))

        def emit(rows, value):
            r.y1[m, rows, mine] = value.astype(bf16)

        norm_back(m, 1, r.y1, r.dy2, r.own, r.r1, emit)
        gather_send(r.y1, m, "dy1")

    blocks = (near_far, near, far, z)

    def grads_pair(g, b, k):
        for i, zz in enumerate(blocks):
            src = g.at[:, zz, 1 - c] if len(g.shape) == 5 else g.at[zz, 1 - c]
            dst = b.at[:, zz] if len(g.shape) == 5 else b.at[zz]
            send(src, dst, (k, "p", i), beside)

    def grads_add(g, zz, arrive):
        if len(g.shape) == 5:

            @pl.loop(0, S)
            def _(q):
                g[q, zz, c] = (g[q, zz, c].astype(f32) + arrive[q].astype(f32)).astype(bf16)
        else:
            g[zz, c] = (g[zz, c].astype(f32) + arrive[...].astype(f32)).astype(bf16)

    def grads_paired(g, b, k, i):
        zz = blocks[i]
        piece = b.at[:, zz] if len(g.shape) == 5 else b.at[zz]
        recv(piece, (k, "p", i))
        grads_add(g, zz, piece)

    def grads_near(g, b, arrive, k):
        grads_paired(g, b, k, 0)
        send(part(g, near_far, c), arrive.at[1], (k, "nf"), (s, near * 2 + c))
        for i in range(1, nz):
            grads_paired(g, b, k, i)

    def grads_far(g, arrive, k):
        recv(arrive.at[1], (k, "nf"))
        grads_add(g, far, arrive.at[1])
        send(part(g, far, c), arrive.at[2], (k, "f"), (s, far * 2 + c))
        send(part(g, near, c), arrive.at[0], (k, "n"), (s, near * 2 + c))

    def grads_near_recv(arrive, k):
        recv(arrive.at[0], (k, "n"))
        recv(arrive.at[2], (k, "f"))
        return 0, 2

    def down_weights():
        for i, t in enumerate(blocks):
            lhs = r.u[:, :, col(t)].reshape(M * T, Q)
            grad = tn(lhs, r.dy2[...].reshape(M * T, D))
            r.wout[t] = grad.astype(bf16).reshape(2, shd, D)
            send(r.wout.at[t, 1 - c], r.bdn.at[t], ("gdn", "p", i), beside)

    def up_weights():
        @pl.loop(0, S, unroll=True)
        def _(t):
            lhs = r.a2[:, :, col(t)].reshape(M * T, Q)
            grad = tn(lhs, r.dh[...].reshape(M * T, FQ))
            r.win[t] = grad.astype(bf16).reshape(nz, 2, sh, FQ)

        grads_pair(r.win, r.bup, "gup")

    def qkv_weights():
        @pl.loop(0, S, unroll=True)
        def _(t):
            lhs = r.a1[:, :, col(t)].reshape(M * T, Q)
            grad = tn(lhs, r.dqkv[...].reshape(M * T, 3 * Q))
            r.gqk[t] = grad.astype(bf16).reshape(nz, 2, sh, 3 * Q)

        grads_pair(r.gqk, r.bqk, "gqk")

    def out_weights():
        grad = tn(r.o[...].reshape(M * T, Q), r.y1[...].reshape(M * T, D))
        r.gwo[...] = grad.astype(bf16).reshape(nz, 2, sh, D)
        grads_pair(r.gwo, r.bwo, "gwo")

    r.vsum[...] = jnp.zeros_like(r.vsum)
    dense_back(0)
    gather_recv(r.dy2, 1, "dy2", lambda: sum_start(r.ts, r.r1, 0, "da2"))
    down_weights()
    grads_near(r.wout, r.bdn, r.zdn, "gdn")
    dense_back(1)
    finish_da2(0)
    up_weights()
    grads_far(r.wout, r.zdn, "gdn")
    finish_da2(1)
    grads_near(r.win, r.bup, r.zup, "gup")

    def attend_back(m):
        if m == 0:
            gather_recv(r.y1, m, "dy1")
        out_grad = nt(r.y1[m], r.wo[...].reshape(Q, D)).astype(bf16)
        for hh in range(heads):
            at = hh * size
            q = r.qkv[m, :, at : at + size]
            k = r.qkv[m, :, Q + at : Q + at + size]
            v = r.qkv[m, :, 2 * Q + at : 2 * Q + at + size]
            go = out_grad[:, at : at + size]
            p = r.probs[m, hh]
            dp = nt(go, v)
            dv = tn(p.astype(bf16), go)
            ds = (p * (dp - jnp.sum(p * dp, axis=1, keepdims=True))).astype(bf16)
            dq = jnp.dot(ds, k, preferred_element_type=f32) * scale
            dk = tn(ds, q) * scale
            r.dqkv[m, :, at : at + size] = dq.astype(bf16)
            r.dqkv[m, :, Q + at : Q + at + size] = dk.astype(bf16)
            r.dqkv[m, :, 2 * Q + at : 2 * Q + at + size] = dv.astype(bf16)
        sum_send(
            lambda q: nt(r.dqkv[m], r.wqkv[q].reshape(Q, 3 * Q)),
            r.ts,
            r.r2,
            r.own,
            m,
            "da1",
            "da2",
            hold=True,
        )
        stats_send(m, 0, token_stats(m, 0, r.hidden))

    def finish_da1(m):
        sum_recv(r.r2, m, "da1")
        stats_recv(m, 0)

        def emit(rows, value):
            r.dx[m, rows] = value

        norm_back(m, 0, r.hidden, r.y1, r.own, r.r2, emit)

    attend_back(0)
    gather_recv(r.y1, 1, "dy1")
    sum_start(r.fes, r.fer, 0, "fe")
    sum_start(r.fes, r.fer, 1, "fe")
    attend_back(1)
    grads_far(r.win, r.zup, "gup")
    qkv_weights()
    grads_near(r.gqk, r.bqk, r.zqk, "gqk")
    out_weights()
    grads_near(r.gwo, r.bwo, r.zwo, "gwo")
    expert_weights(r.en, r.dhe, r.gin_out)
    finish_fe(0)
    sum_start(r.ts, r.r2, 0, "da1")
    sum_start(r.ts, r.r2, 1, "da1")
    grads_far(r.gqk, r.zqk, "gqk")
    grads_far(r.gwo, r.zwo, "gwo")
    finish_fe(1)
    expert_weights(r.ue, r.dfe, r.gout_out)

    def finish_out(m):
        return_recv(r.ger, m, "geb")
        back = tn(r.perm[m], r.ger[m])
        r.out[m] = (r.y2q[m].astype(f32) + back).astype(bf16)


    def row_result(g, arrive, out, k, rows, wait):
        slots = wait(arrive, k)
        mine_part = part(g, z, c)

        def body(at):
            total = mine_part[at].astype(f32)
            for slot in slots:
                total += arrive[slot, at].astype(f32)
            out[at] = total

        each(rows, body)

    def column_send(g, arrive, out, back, k, wait):
        slots = wait(arrive, k)

        @pl.loop(0, S)
        def _(q):
            total = g[q, z, c].astype(f32)
            for slot in slots:
                total += arrive[slot, q].astype(f32)
            out[q] = total.astype(bf16)

        for i in others:
            send(out.at[sec(i)], back.at[i - 1], (k, "s", i), to_sec(i))

    def column_result(sums, back, out, pieces, k):
        width = sums.shape[2] // pieces
        for i in range(S):
            if i:
                recv(back.at[i - 1], (k, "s", i))
            q = sec(S - i) if i else s
            value = (back[i - 1] if i else sums[s]).astype(f32)
            for piece in range(pieces):
                at = pl.ds(pl.multiple_of(piece * S * width + q * width, width), width)
                out[:, at] = value[:, piece * width : (piece + 1) * width]

    row_result(r.wout, r.zdn, r.gdn_out, "gdn", shd, grads_near_recv)
    give("gdn_out")
    column_send(r.win, r.zup, r.ups, r.upr, "gup", grads_near_recv)
    finish_da1(0)
    finish_da1(1)
    give("dx")
    for j in range(1, G):
        send(r.vsum, r.vsr.at[j - 1], ("vs", j), to_dp(j))
    column_send(r.gqk, r.zqk, r.qks, r.qkr, "gqk", grads_near_recv)
    row_result(r.gwo, r.zwo, r.gwo_out, "gwo", sh, grads_near_recv)
    give("gwo_out")
    column_result(r.ups, r.upr, r.gup_out, 1, "gup")
    give("gup_out")
    finish_out(0)
    finish_out(1)
    give("out")
    total = r.vsum[...]
    for j in range(1, G):
        recv(r.vsr.at[j - 1], ("vs", j))
        total += r.vsr[j - 1]
    shard = jnp.zeros((8, sh), f32)
    for j in range(G):
        shard += jnp.where(d == j, 1.0, 0.0) * total[:, j * sh : (j + 1) * sh]
    r.vgo[...] = jnp.zeros_like(r.vgo)
    r.vgo[:, 0:sh] = shard
    give("vgo")
    column_result(r.qks, r.qkr, r.gqk_out, 3, "gqk")
    give("gqk_out")

    def drain():
        for write in writes[-2:] + results:
            write.wait()
        for last in pending.values():
            last.wait_send()

    drain()
    assert len(places) == KEYS, len(places)


def hand_over(*refs):
    (out, dx, vgo, gqk, gwo, gup, gdn, evo, gin, gout) = refs[:10]
    results = refs[10:]
    results[8][...] = gin[...].astype(f32)
    results[9][...] = gout[...].astype(f32)

    @pl.when(pl.program_id(0) == 0)
    def _():
        for src, dst in zip((out, dx, gqk, gwo, gup, gdn), results[:2] + results[4:8]):
            dst[...] = src[...]
        for i, dst in enumerate(results[2:4] + results[10:12]):
            dst[...] = vgo[i : i + 1, 0 : dst.shape[1]]
        for i, dst in enumerate(results[12:]):
            dst[...] = evo[i : i + 1, :]


def with_kernel(
    hidden_in,
    cotangent,
    bucket_len,
    live_mask,
    routes,
    ln1_gain,
    ln1_bias,
    w_qkv,
    w_attn_out,
    ln2_gain,
    ln2_bias,
    w_up,
    w_down,
    expert_in,
    expert_out,
    expert_gain,
    expert_bias,
    centroids,
):
    S = lax.axis_size(SECTION)
    G = lax.axis_size(DP)
    M, T, D = hidden_in.shape
    Q = D // S
    FQ = w_up.shape[1] // S
    C = 3 * T // (2 * G)
    sh, shd = w_up.shape[0], w_down.shape[0]
    dims = (S, G, M, T, D, Q, FQ, C, sh, shd)
    scratch = layout(dims)
    names = INPUTS + OUTPUTS + list(scratch) + ["ssem", "rsem", "lsem"]
    vmem = pl.BlockSpec(memory_space=pltpu.VMEM)
    smem = pl.BlockSpec(memory_space=pltpu.SMEM)
    anywhere = pl.BlockSpec(memory_space=pl.ANY)
    shapes = (
        ((M, T, Q), bf16),
        ((M, T, Q), f32),
        ((8, 128), f32),
        ((sh, 3 * D), f32),
        ((sh, D), f32),
        ((sh, S * FQ), f32),
        ((shd, D), f32),
        ((8, Q), f32),
        ((D, FQ), bf16),
        ((FQ, D), bf16),
    )
    outs = pl.pallas_call(
        functools.partial(block_kernel, dims, names),
        name="block",
        out_shape=[jax.ShapeDtypeStruct(*shape) for shape in shapes],
        in_specs=[vmem, vmem, smem] + [vmem] * 13 + [anywhere] * 2,
        out_specs=[anywhere] * len(shapes),
        scratch_shapes=[pltpu.VMEM(*shape) for shape in scratch.values()]
        + [pltpu.SemaphoreType.DMA((KEYS,))] * 2
        + [pltpu.SemaphoreType.DMA((4 + len(RESULTS),))],
        compiler_params=pltpu.CompilerParams(
            collective_id=0, has_side_effects=True, vmem_limit_bytes=63 << 20
        ),
    )(
        hidden_in,
        cotangent,
        bucket_len,
        live_mask,
        jnp.swapaxes(routes, 1, 2),
        ln1_gain.reshape(1, sh),
        ln1_bias.reshape(1, sh),
        ln2_gain.reshape(1, sh),
        ln2_bias.reshape(1, sh),
        expert_gain,
        expert_bias,
        centroids,
        w_qkv,
        w_attn_out,
        w_up,
        w_down,
        expert_in.reshape(S, G // 2, 2, sh, FQ),
        expert_out.reshape(G // 2, 2, shd, D),
    )

    def spec(shape):
        if shape in ((D, FQ), (FQ, D)):
            return pl.BlockSpec((512, shape[1]), lambda i: (i, 0))
        return pl.BlockSpec(shape, lambda i, n=len(shape): (0,) * n)

    finals = (
        shapes[:2]
        + (((1, sh), f32),) * 2
        + shapes[3:7]
        + (((D, FQ), f32), ((FQ, D), f32))
        + (((1, sh), f32),) * 2
        + (((1, Q), f32),) * 3
    )
    outs = pl.pallas_call(
        hand_over,
        name="hand_over",
        grid=(D // 512,),
        out_shape=[jax.ShapeDtypeStruct(*shape) for shape in finals],
        in_specs=[spec(shape) for shape, _ in shapes],
        out_specs=[spec(shape) for shape, _ in finals],
        compiler_params=pltpu.CompilerParams(vmem_limit_bytes=63 << 20),
    )(*outs)
    out, dx, gain1, bias1, gqkv, gwo, gup, gdn, gin, gout, gain2, bias2, eg, eb, ec = outs
    return (
        out,
        dx,
        gain1.reshape(sh),
        bias1.reshape(sh),
        gqkv,
        gwo,
        gain2.reshape(sh),
        bias2.reshape(sh),
        gup,
        gdn,
        gin[None],
        gout[None],
        eg,
        eb,
        ec,
    )


def on_device(*args):
    groups = lax.axis_size(DP)
    rows, shard = args[0].shape[1], args[11].shape[0]
    capacity = 3 * rows // (2 * groups)
    if capacity % 16 or shard % 16 or groups != 8:
        return with_collectives(*args)
    return with_kernel(*args)


def solution(mesh):
    everywhere = (SECTION, DP)
    tokens = P(None, DP, None)
    outs = P(None, DP, SECTION)
    per_expert = P(DP, SECTION)
    return jax.shard_map(
        on_device,
        mesh=mesh,
        in_specs=(
            tokens,
            tokens,
            tokens,
            P(None, DP),
            tokens,
            P(everywhere),
            P(everywhere),
            P(everywhere, None),
            P(everywhere, None),
            P(everywhere),
            P(everywhere),
            P(everywhere, None),
            P(everywhere, None),
            P(DP, None, SECTION),
            P(DP, SECTION, None),
            per_expert,
            per_expert,
            per_expert,
        ),
        out_specs=(
            outs,
            outs,
            P(everywhere),
            P(everywhere),
            P(everywhere, None),
            P(everywhere, None),
            P(everywhere),
            P(everywhere),
            P(everywhere, None),
            P(everywhere, None),
            P(DP, None, SECTION),
            P(DP, SECTION, None),
            per_expert,
            per_expert,
            per_expert,
        ),
        check_vma=False,
    )
```

```python
import functools
import math
import types

import jax
import jax.numpy as jnp
from jax import lax
from jax.experimental import pallas as pl
from jax.experimental.pallas import tpu as pltpu
from jax.sharding import PartitionSpec as P

HEADS = 16
SECTION = "section"
DP = "dp"
epsilon = 1e-05
masked_value = -1e30
f32 = jnp.float32
bf16 = jnp.bfloat16


def norm_parts(values):
    center = values - jnp.mean(values, axis=-1, keepdims=True)
    spread = jnp.mean(center * center, axis=-1, keepdims=True)
    rs = lax.rsqrt(spread + epsilon)
    return center * rs, rs


def gelu_back(pre, grad):
    outputs, pullback = jax.vjp(jax.nn.gelu, pre)
    return pullback(grad)[0]


def dot(a, b):
    return jnp.dot(a, b, preferred_element_type=f32)


def dot_tn(a, b):
    return jnp.einsum("rd,re->de", a, b, preferred_element_type=f32)


def dot_nt(a, b):
    return jnp.einsum("re,de->rd", a, b, preferred_element_type=f32)


def sum_scatter(part):
    return lax.psum_scatter(
        part.astype(bf16), SECTION, scatter_dimension=part.ndim - 1, tiled=True
    ).astype(f32)


def gather_features(part):
    return lax.all_gather(part, SECTION, axis=part.ndim - 1, tiled=True)


def with_collectives(
    hidden_in,
    cotangent,
    bucket_len,
    live_mask,
    routes,
    ln1_gain,
    ln1_bias,
    w_qkv,
    w_attn_out,
    ln2_gain,
    ln2_bias,
    w_up,
    w_down,
    expert_in,
    expert_out,
    expert_gain,
    expert_bias,
    centroids,
):
    sections = lax.axis_size(SECTION)
    groups = lax.axis_size(DP)
    section = lax.axis_index(SECTION)
    micro, rows, width = hidden_in.shape
    quarter = width // sections
    heads = HEADS // sections
    size = width // HEADS
    ff = w_up.shape[1] // sections
    capacity = 3 * rows // (2 * groups)
    shard = w_up.shape[0]
    own_cols = section * quarter

    def mine(values):
        return lax.dynamic_slice_in_dim(values, own_cols, quarter, values.ndim - 1)

    def column_group(weight, pieces):
        cols = weight.shape[1] // (pieces * sections)
        parts = weight.reshape(shard, pieces, sections, cols).transpose(2, 0, 1, 3)
        parts = parts.reshape(sections, shard, pieces * cols)
        parts = lax.all_to_all(parts, SECTION, split_axis=0, concat_axis=0, tiled=True)
        full = lax.all_gather(parts, DP, axis=1, tiled=True)
        return full.reshape(width, pieces * cols)

    def column_group_back(grad, pieces):
        cols = grad.shape[1] // pieces
        parts = grad.astype(bf16).reshape(sections, groups * shard, pieces * cols)
        parts = lax.psum_scatter(parts, DP, scatter_dimension=1, tiled=True)
        parts = lax.all_to_all(parts, SECTION, split_axis=0, concat_axis=0, tiled=True)
        parts = parts.reshape(sections, shard, pieces, cols).transpose(1, 2, 0, 3)
        return parts.reshape(shard, pieces * sections * cols).astype(f32)

    def row_group_back(grad):
        return lax.psum_scatter(
            grad.astype(bf16), DP, scatter_dimension=0, tiled=True
        ).astype(f32)

    vectors = lax.all_gather(
        jnp.stack([ln1_gain, ln1_bias, ln2_gain, ln2_bias]), (SECTION, DP), axis=1, tiled=True
    ).astype(f32)
    gain_one, bias_one, gain_two, bias_two = vectors
    expert_vectors = lax.all_gather(
        jnp.concatenate([expert_gain, expert_bias, centroids]), SECTION, axis=1, tiled=True
    ).astype(f32)
    expert_g, expert_b, centroid = expert_vectors
    wqkv = column_group(w_qkv, 3)
    wo = lax.all_gather(w_attn_out, DP, axis=0, tiled=True)
    wup = column_group(w_up, 1)
    wdown = lax.all_gather(w_down, DP, axis=0, tiled=True)
    win = expert_in[0]
    wout = expert_out[0]

    ends = jnp.cumsum(bucket_len[:, 0, :], axis=-1)
    slot_ids = jnp.arange(rows, dtype=jnp.int32)
    segments = jnp.sum((slot_ids[None, :, None] >= ends[:, None, :]).astype(jnp.int32), axis=-1)
    same = segments[:, :, None] == segments[:, None, :]
    causal = slot_ids[None, None, :] <= slot_ids[None, :, None]
    opened = (live_mask[:, None, :] == 1) | (slot_ids[None, None, :] == slot_ids[None, :, None])
    allowed = (same & causal & opened)[:, None]
    chosen = routes[:, :, 0]
    picks = (chosen[:, :, None] == jnp.arange(groups, dtype=jnp.int32)).astype(jnp.int32)
    ranks = jnp.sum((jnp.cumsum(picks, axis=1) - picks) * picks, axis=2)
    places = chosen * capacity + ranks
    place_ids = jnp.arange(groups * capacity, dtype=jnp.int32)
    picked = (places[:, None, :] == place_ids[None, :, None]).astype(bf16)

    def dispatch(values):
        out = jnp.einsum("mpt,mtf->pmf", picked, values, preferred_element_type=f32).astype(bf16)
        out = out.reshape(groups, capacity * micro, quarter)
        return lax.all_to_all(out, DP, split_axis=0, concat_axis=0, tiled=True)

    def give_back(values):
        out = lax.all_to_all(values, DP, split_axis=0, concat_axis=0, tiled=True)
        out = out.reshape(groups * capacity, micro, quarter)
        return jnp.einsum("mpt,pmf->mtf", picked, out, preferred_element_type=f32)

    dge = gather_features(dispatch(mine(cotangent))).reshape(-1, width).astype(f32)

    x = hidden_in.reshape(micro * rows, width).astype(f32)
    n1, rs1 = norm_parts(x)
    a1 = (n1 * gain_one + bias_one).astype(bf16)
    qkv = dot(a1, wqkv).astype(bf16)
    q, k, v = (
        qkv[:, i * quarter : (i + 1) * quarter].reshape(micro, rows, heads, size) for i in range(3)
    )
    scale = size ** (-0.5)
    raw = jnp.einsum("mqhd,mkhd->mhqk", q, k, preferred_element_type=f32) * scale
    scores = jnp.where(allowed, raw, masked_value)
    weights = jnp.exp(scores - jnp.max(scores, axis=-1, keepdims=True))
    probs = weights / jnp.sum(weights, axis=-1, keepdims=True)
    probs_low = probs.astype(bf16)
    mixed = jnp.einsum("mhqk,mkhd->mqhd", probs_low, v, preferred_element_type=f32)
    o = mixed.reshape(micro * rows, quarter).astype(bf16)
    y1q = (mine(x) + sum_scatter(dot(o, wo))).astype(bf16)
    y1 = gather_features(y1q).astype(f32)
    n2, rs2 = norm_parts(y1)
    a2 = (n2 * gain_two + bias_two).astype(bf16)
    h = dot(a2, wup)
    u = jax.nn.gelu(h).astype(bf16)
    y2q = (y1q.astype(f32) + sum_scatter(dot(u, wdown))).astype(bf16)

    xe = gather_features(dispatch(y2q.reshape(micro, rows, quarter))).reshape(-1, width)
    xe = xe.astype(f32)
    ne, rse = norm_parts(xe)
    en = (ne * expert_g + expert_b).astype(bf16)
    he = dot(en, win)
    ue = jax.nn.gelu(he).astype(bf16)
    fe_part = dot(ue, wout)
    alpha = jax.nn.sigmoid(jnp.sum(xe * centroid, axis=-1, keepdims=True))
    fe = sum_scatter(fe_part)
    ge = (alpha * fe).astype(bf16).reshape(groups, capacity * micro, quarter)
    block_out = (
        y2q.reshape(micro, rows, quarter).astype(f32) + give_back(ge)
    ).astype(bf16)

    dfe = (alpha * dge).astype(bf16)
    due = dot_nt(dfe, wout)
    grad_out = dot_tn(ue, dfe)
    dhe = gelu_back(he, due).astype(bf16)
    grad_in = dot_tn(en, dhe)
    den_part = dot_nt(dhe, win)
    gden = den_part * expert_g
    stats = lax.psum(
        jnp.stack(
            [
                jnp.mean(gden, axis=-1),
                jnp.mean(gden * ne, axis=-1),
                jnp.sum(dge * fe_part, axis=-1),
            ]
        ),
        SECTION,
    )[..., None]
    den = sum_scatter(den_part)
    neq = mine(ne)
    dlogit = stats[2] * alpha * (1.0 - alpha)
    dxe_ln = rse * (mine(expert_g) * den - stats[0] - neq * stats[1])
    dxe = (dxe_ln + dlogit * mine(centroid)).astype(bf16)
    grad_expert_gain = jnp.sum(den * neq, axis=0)
    grad_expert_bias = jnp.sum(den, axis=0)
    grad_centroid = jnp.sum(dlogit * mine(xe), axis=0)
    back = give_back(dxe.reshape(groups, capacity * micro, quarter))
    dy2q = (mine(cotangent).astype(f32) + back).astype(bf16).reshape(micro * rows, quarter)

    dy2 = gather_features(dy2q)
    grad_down = dot_tn(u, dy2)
    dh = gelu_back(h, dot_nt(dy2, wdown)).astype(bf16)
    grad_up = dot_tn(a2, dh)
    da2_part = dot_nt(dh, wup)
    gda2 = da2_part * gain_two
    stats = lax.psum(
        jnp.stack([jnp.mean(gda2, axis=-1), jnp.mean(gda2 * n2, axis=-1)]), SECTION
    )[..., None]
    da2 = sum_scatter(da2_part)
    n2q = mine(n2)
    dy1q = dy2q.astype(f32) + rs2 * (mine(gain_two) * da2 - stats[0] - n2q * stats[1])
    dy1q = dy1q.astype(bf16)
    dy1 = gather_features(dy1q)
    grad_wo = dot_tn(o, dy1)
    do = dot_nt(dy1, wo).astype(bf16).reshape(micro, rows, heads, size)
    dp = jnp.einsum("mqhd,mkhd->mhqk", do, v, preferred_element_type=f32)
    dv = jnp.einsum("mhqk,mqhd->mkhd", probs_low, do, preferred_element_type=f32)
    delta = jnp.sum(probs * dp, axis=-1, keepdims=True)
    ds = (probs * (dp - delta)).astype(bf16)
    dq = jnp.einsum("mhqk,mkhd->mqhd", ds, k, preferred_element_type=f32) * scale
    dk = jnp.einsum("mhqk,mqhd->mkhd", ds, q, preferred_element_type=f32) * scale
    dqkv = jnp.concatenate(
        [part.reshape(micro * rows, quarter) for part in (dq, dk, dv)], axis=1
    ).astype(bf16)
    grad_qkv = dot_tn(a1, dqkv)
    da1_part = dot_nt(dqkv, wqkv)
    gda1 = da1_part * gain_one
    stats = lax.psum(
        jnp.stack([jnp.mean(gda1, axis=-1), jnp.mean(gda1 * n1, axis=-1)]), SECTION
    )[..., None]
    da1 = sum_scatter(da1_part)
    n1q = mine(n1)
    dx = dy1q.astype(f32) + rs1 * (mine(gain_one) * da1 - stats[0] - n1q * stats[1])

    vector_grads = lax.psum_scatter(
        jnp.stack(
            [
                jnp.sum(da1 * n1q, axis=0),
                jnp.sum(da1, axis=0),
                jnp.sum(da2 * n2q, axis=0),
                jnp.sum(da2, axis=0),
            ]
        ),
        DP,
        scatter_dimension=1,
        tiled=True,
    )
    return (
        block_out,
        dx.reshape(micro, rows, quarter),
        vector_grads[0],
        vector_grads[1],
        column_group_back(grad_qkv, 3),
        row_group_back(grad_wo),
        vector_grads[2],
        vector_grads[3],
        column_group_back(grad_up, 1),
        row_group_back(grad_down),
        grad_in[None],
        grad_out[None],
        grad_expert_gain[None],
        grad_expert_bias[None],
        grad_centroid[None],
    )


MESH = pl.DeviceIdType.MESH
KEYS = 101
CHAIN = {
    "y1": 0,
    "y1g": 1,
    "y2": 0,
    "xe": 1,
    "den": 0,
    "dy2": 1,
    "da2": 0,
    "dy1": 1,
    "da1": 0,
}
SHARED = {
    "geb": "y2d",
    "dxb": "cot",
    "fe": "dge",
    "est": "stats",
    "tst": "stats",
    "vs": "v2",
    "gdn": "wdn",
    "gup": "wup",
    "gwo": "wo",
    "gqk": "wqkv",
    "p": "c",
    "n": "near",
    "nf": "near far",
    "f": "far",
}


LEGS = {
    "xe": ("x", "y", "xy", "yx"),
    "den": ("x0", "x2", "y1", "y2", "xy", "yx"),
}


def semaphore_of(k):
    if k[0] in LEGS:
        leg = LEGS[k[0]].index(k[2])
        return ("chain", CHAIN[k[0]], k[1], leg + 1) if leg < 3 else ("leg", k[0], k[1], leg)
    if k[0] in CHAIN:
        return ("chain", CHAIN[k[0]]) + k[1:]
    if k[0] == "q1":
        return ("stats", k[1], k[2]) if k[1] < 2 else ("chain", 1, 0, k[2])
    if k[0] == "v1":
        return "chain", 1, 1, k[1]
    if k[1] == "s":
        return "u1" if k[0] == "gup" else "e1", k[2]
    if k[0] == "tst":
        return ("stats",) + k[2:]
    return tuple(SHARED.get(part, part) for part in k)
CHUNK = 128


def tn(a, b):
    return lax.dot_general(a, b, (((0,), (0,)), ((), ())), preferred_element_type=f32)


def nt(a, b):
    return lax.dot_general(a, b, (((1,), (1,)), ((), ())), preferred_element_type=f32)


def tanh_parts(v):
    root = 0.7978845608028654
    t = jnp.tanh(root * (v + 0.044715 * (v * v * v)))
    return t, root


def gelu_both(v):
    t, root = tanh_parts(v)
    half = 0.5 * (1.0 + t)
    return v * half, half + 0.5 * v * (1.0 - t * t) * root * (1.0 + 0.134145 * (v * v))


def to_rows(columns):
    lane = lax.broadcasted_iota(jnp.int32, (columns[0].shape[0], 128), 1)
    wide = jnp.zeros(lane.shape, f32)
    for i, column in enumerate(columns):
        wide = jnp.where(lane == i, column, wide)
    return wide.T[:8]


def to_columns(rows):
    return jnp.concatenate([rows, jnp.zeros((120, rows.shape[1]), f32)], axis=0).T


def layout(dims):
    S, G, M, T, D, Q, FQ, C, sh, shd = dims
    nz = G // 2
    R = G * C
    heads = HEADS // S
    return dict(
        wqkv=((S, nz, 2, sh, 3 * Q), bf16),
        wo=((nz, 2, sh, D), bf16),
        wup=((S, nz, 2, sh, FQ), bf16),
        wdn=((nz, 2, shd, D), bf16),
        win=((S, nz, 2, sh, FQ), bf16),
        wout=((nz, 2, shd, D), bf16),
        vin=((8, 128), f32),
        ein=((8, Q), f32),
        vg=((S, G, 8, 128), f32),
        vecs=((8, D), f32),
        evec=((8, D), f32),
        mask=((M, T, T), f32),
        perm=((M, R, T), bf16),
        cots=((M, R, Q), bf16),
        y2s=((M, R, Q), bf16),
        ges=((M, R, Q), bf16),
        dxs=((M, R, Q), bf16),
        ger=((M, R, Q), bf16),
        dxr=((M, R, Q), bf16),
        tst=((M, T, 128), f32),
        est=((M, R, 128), f32),
        a1=((M, T, D), bf16),
        a2=((M, T, D), bf16),
        qkv=((M, T, 3 * Q), bf16),
        probs=((M, heads, T, T), f32),
        o=((M, T, Q), bf16),
        y1=((M, T, D), bf16),
        h=((M, T, FQ), f32),
        u=((M, T, FQ), bf16),
        y2q=((M, T, Q), bf16),
        xe=((M, R, D), bf16),
        dge=((M, R, D), bf16),
        en=((M, R, D), bf16),
        ue=((M, R, FQ), bf16),
        dhe=((M, R, FQ), bf16),
        dfe=((M, R, D), bf16),
        slope=((R, FQ), f32),
        fes=((M, S - 1, R, Q), bf16),
        fer=((M, S - 1, R, Q), bf16),
        feo=((M, R, Q), f32),
        dns=((M, S - 1, R, Q), bf16),
        dnr=((M, S - 1, R, Q), bf16),
        dno=((M, R, Q), f32),
        ess=((M, 8, R), f32),
        esr=((M, S - 1, 8, R), f32),
        ts=((M, S - 1, T, Q), bf16),
        r1=((M, S - 1, T, Q), bf16),
        r2=((M, S - 1, T, Q), bf16),
        own=((M, T, Q), f32),
        tss=((2, M, 8, T), f32),
        tsr=((2, M, S - 1, 8, T), f32),
        dy2=((M, T, D), bf16),
        dh=((M, T, FQ), bf16),
        dqkv=((M, T, 3 * Q), bf16),
        gwo=((nz, 2, sh, D), bf16),
        gqk=((S, nz, 2, sh, 3 * Q), bf16),
        bdn=((nz, shd, D), bf16),
        bup=((S, nz, sh, FQ), bf16),
        bwo=((nz, sh, D), bf16),
        bqk=((S, nz, sh, 3 * Q), bf16),
        zdn=((nz - 1, shd, D), bf16),
        zup=((nz - 1, S, sh, FQ), bf16),
        zwo=((nz - 1, sh, D), bf16),
        zqk=((nz - 1, S, sh, 3 * Q), bf16),
        ups=((S, sh, FQ), bf16),
        upr=((S - 1, sh, FQ), bf16),
        qks=((S, sh, 3 * Q), bf16),
        qkr=((S - 1, sh, 3 * Q), bf16),
        stage=((2, 256, D), bf16),
        out=((M, T, Q), bf16),
        dx=((M, T, Q), f32),
        vgo=((8, 128), f32),
        gqk_out=((sh, 3 * D), f32),
        gwo_out=((sh, D), f32),
        gup_out=((sh, S * FQ), f32),
        gdn_out=((shd, D), f32),
        evo=((8, Q), f32),
        vsum=((8, Q), f32),
        vsr=((G - 1, 8, Q), f32),
    )


INPUTS = [
    "hidden",
    "cot",
    "bucket",
    "live",
    "routes",
    "gain_one",
    "bias_one",
    "gain_two",
    "bias_two",
    "gain_e",
    "bias_e",
    "centroid",
    "wqkv_in",
    "wo_in",
    "wup_in",
    "wdn_in",
    "win_in",
    "wout_in",
]
RESULTS = [
    "out",
    "dx",
    "vgo",
    "gqk_out",
    "gwo_out",
    "gup_out",
    "gdn_out",
    "evo",
]
OUTPUTS = ["to_" + name for name in RESULTS] + ["gin_out", "gout_out"]


def block_kernel(dims, names, *args):
    r = types.SimpleNamespace(**dict(zip(names, args)))
    S, G, M, T, D, Q, FQ, C, sh, shd = dims
    nz = G // 2
    R = G * C
    heads = HEADS // S
    size = D // HEADS
    scale = size ** (-0.5)
    s = lax.axis_index(SECTION)
    d = lax.axis_index(DP)
    z = lax.div(d, 2)
    c = lax.rem(d, 2)
    beside = (s, d + 1 - 2 * c)
    near = z + 1 - 2 * lax.rem(z, 2)
    far = lax.rem(z + 2, nz)
    near_far = lax.rem(near + 2, nz)
    beside_x = s + 1 - 2 * lax.rem(s, 2)
    beside_y = lax.rem(s + 2, S)
    across = lax.rem(beside_x + 2, S)

    def sec(i):
        return lax.rem(s + i, S)

    def dpi(j):
        return lax.rem(d + j, G)

    def zi(j):
        return lax.rem(z + j, nz)

    def to_sec(i):
        return (sec(i), d)

    def to_dp(j):
        return (s, dpi(j))

    def to_z(j):
        return (s, zi(j) * 2 + c)

    def col(q, n=Q):
        return pl.ds(pl.multiple_of(q * n, n), n)

    def seats(e):
        return pl.ds(pl.multiple_of(e * C, C), C)

    mine = col(s)
    places = {}
    pending = {}

    def copy(src, dst, k, device):
        i = places.setdefault(semaphore_of(k), len(places))
        return pltpu.make_async_remote_copy(
            src_ref=src,
            dst_ref=dst,
            send_sem=r.ssem.at[i],
            recv_sem=r.rsem.at[i],
            device_id=device,
            device_id_type=MESH,
        )

    def send(src, dst, k, device):
        sent(k)
        pending[semaphore_of(k)] = copy(src, dst, k, device)
        pending[semaphore_of(k)].start()

    def sent(k):
        last = pending.pop(semaphore_of(k), None)
        if last is not None:
            last.wait_send()

    def recv(dst, k):
        copy(dst, dst, k, beside).wait_recv()

    def each(rows, body):
        step = math.gcd(rows, CHUNK)

        @pl.loop(0, rows // step)
        def _(i):
            body(pl.ds(pl.multiple_of(i * step, step), step))

    others = range(1, S)

    def gather_send(ref, m, k):
        for i in others:
            send(ref.at[m, :, mine], ref.at[m, :, mine], (k, m, i), to_sec(i))

    def gather_recv(ref, m, k, then=None):
        for i in others:
            recv(ref.at[m, :, col(sec(S - i))], (k, m, i))
            if then is not None and i == S - 2:
                then()

    def sum_send(tile, out, arrive, own, m, k, before=None, hold=False):
        for i in others:
            if before is not None:
                sent((before, m, i))
            out[m, i - 1] = tile(sec(i)).astype(bf16)
        own[m] = tile(s)
        if not hold:
            sum_start(out, arrive, m, k)

    def sum_start(out, arrive, m, k):
        for i in others:
            send(out.at[m, i - 1], arrive.at[m, i - 1], (k, m, i), to_sec(i))

    def sum_recv(arrive, m, k, then=None):
        for i in others:
            recv(arrive.at[m, i - 1], (k, m, i))
            if then is not None and i == S - 2:
                then()

    def summed(own, arrive, m, rows):
        total = own[m, rows]
        for i in others:
            total += arrive[m, i - 1, rows].astype(f32)
        return total

    top, low = slice(0, R // 2), slice(R // 2, R)

    def legs_send(ref, m, k):
        send(ref.at[m, :, mine], ref.at[m, :, mine], (k, m, "x"), (beside_x, d))
        send(ref.at[m, :, mine], ref.at[m, :, mine], (k, m, "y"), (beside_y, d))

    def legs_pass(ref, m, k):
        recv(ref.at[m, :, col(beside_x)], (k, m, "x"))
        block = ref.at[m, top, col(beside_x)]
        send(block, block, (k, m, "xy"), (beside_y, d))
        recv(ref.at[m, :, col(beside_y)], (k, m, "y"))
        block = ref.at[m, low, col(beside_y)]
        send(block, block, (k, m, "yx"), (beside_x, d))

    def legs_recv(ref, m, k):
        recv(ref.at[m, top, col(across)], (k, m, "xy"))
        recv(ref.at[m, low, col(across)], (k, m, "yx"))

    quarters = (beside_x, beside_y, across)

    def legs_sum_send(tile, out, arrive, own, m, k):
        for i, q in enumerate(quarters):
            out[m, i] = tile(q).astype(bf16)
        own[m] = tile(s)
        for i in (2, 0):
            send(out.at[m, i, top], arrive.at[m, i, top], (k, m, "x" + str(i)), (beside_x, d))
        for i in (2, 1):
            send(out.at[m, i, low], arrive.at[m, i, low], (k, m, "y" + str(i)), (beside_y, d))

    def legs_sum_pass(out, arrive, m, k):
        recv(arrive.at[m, 2, top], (k, m, "x2"))
        both = out[m, 1, top].astype(f32) + arrive[m, 2, top].astype(f32)
        out[m, 1, top] = both.astype(bf16)
        send(out.at[m, 1, top], arrive.at[m, 1, top], (k, m, "xy"), (beside_y, d))
        recv(arrive.at[m, 2, low], (k, m, "y2"))
        both = out[m, 0, low].astype(f32) + arrive[m, 2, low].astype(f32)
        out[m, 0, low] = both.astype(bf16)
        send(out.at[m, 0, low], arrive.at[m, 0, low], (k, m, "yx"), (beside_x, d))

    def legs_sum_recv(arrive, m, k):
        recv(arrive.at[m, 0, top], (k, m, "x0"))
        recv(arrive.at[m, 1, low], (k, m, "y1"))
        recv(arrive.at[m, 1, top], (k, m, "xy"))
        recv(arrive.at[m, 0, low], (k, m, "yx"))

    def dispatch_send(src, dst, m, k):
        dst[m, seats(d), mine] = src[m, seats(d)]
        for j in range(1, G):
            send(src.at[m, seats(dpi(j))], dst.at[m, seats(d), mine], (k, m, j), to_dp(j))

    def dispatch_recv(dst, m, k):
        for j in range(1, G):
            recv(dst.at[m, seats(dpi(G - j)), mine], (k, m, j))

    def return_send(src, dst, m, k):
        dst[m, seats(d)] = src[m, seats(d)]
        for j in range(1, G):
            send(src.at[m, seats(dpi(j))], dst.at[m, seats(d)], (k, m, j), to_dp(j))

    def return_recv(dst, m, k):
        for j in range(1, G):
            recv(dst.at[m, seats(dpi(G - j))], (k, m, j))

    def part(ref, zz, cc):
        return ref.at[:, zz, cc] if len(ref.shape) == 5 else ref.at[zz, cc]

    def weight_start(ref, k):
        send(part(ref, z, c), part(ref, z, c), (k, "far"), (s, far * 2 + c))
        send(part(ref, z, c), part(ref, z, c), (k, "c", 0), beside)

    def weight_next(ref, k):
        send(part(ref, z, c), part(ref, z, c), (k, "near"), (s, near * 2 + c))

    def weight_far(ref, k):
        recv(part(ref, far, c), (k, "far"))
        send(part(ref, far, c), part(ref, far, c), (k, "near far"), (s, near * 2 + c))
        send(part(ref, far, c), part(ref, far, c), (k, "c", 1), beside)

    def weight_near(ref, k):
        recv(part(ref, near, c), (k, "near"))
        send(part(ref, near, c), part(ref, near, c), (k, "c", 2), beside)
        recv(part(ref, near_far, c), (k, "near far"))
        send(part(ref, near_far, c), part(ref, near_far, c), (k, "c", 3), beside)

    def weight_wait(ref, k):
        for i, zz in enumerate((z, far, near, near_far)):
            recv(part(ref, zz, 1 - c), (k, "c", i))

    load_in = pltpu.make_async_copy(r.win_in, r.win, r.lsem.at[0])
    load_out = pltpu.make_async_copy(r.wout_in, r.wout, r.lsem.at[1])

    early = lax.broadcasted_iota(jnp.int32, (T, T), 0)
    late = lax.broadcasted_iota(jnp.int32, (T, T), 1)

    def seat_tokens(m):
        route = r.routes[m]
        expert_ids = lax.broadcasted_iota(jnp.int32, (G, T), 0)
        picks = jnp.where(expert_ids == route, 1.0, 0.0)
        before = jnp.where(early < late, 1.0, 0.0).astype(bf16)
        counts = jnp.dot(picks.astype(bf16), before, preferred_element_type=f32)
        rank = jnp.sum(counts * picks, axis=0, keepdims=True)
        place = route.astype(f32) * float(C) + rank
        seat_ids = lax.broadcasted_iota(jnp.int32, (R, T), 0).astype(f32)
        r.perm[m] = jnp.where(seat_ids == place, 1.0, 0.0).astype(bf16)
        r.cots[m] = jnp.dot(r.perm[m], r.cot[m, :, mine], preferred_element_type=f32).astype(bf16)

    def entry():
        barrier = pltpu.get_barrier_semaphore()
        for i in others:
            pl.semaphore_signal(barrier, inc=1, device_id=to_sec(i), device_id_type=MESH)
        for j in range(1, G):
            pl.semaphore_signal(barrier, inc=1, device_id=to_dp(j), device_id_type=MESH)
        r.vin[...] = jnp.zeros_like(r.vin)
        for i, ref in enumerate((r.gain_one, r.bias_one, r.gain_two, r.bias_two)):
            r.vin[i : i + 1, 0:sh] = ref[...].astype(f32)
        r.ein[...] = jnp.zeros_like(r.ein)
        for i, ref in enumerate((r.gain_e, r.bias_e, r.centroid)):
            r.ein[i : i + 1, :] = ref[...].astype(f32)
        r.vg[s, d] = r.vin[...]
        r.evec[:, mine] = r.ein[...]
        for piece in range(3):
            r.wqkv[s, z, c, :, piece * Q : (piece + 1) * Q] = r.wqkv_in[
                :, pl.ds(pl.multiple_of(piece * D + s * Q, Q), Q)
            ]
        r.wo[z, c] = r.wo_in[...]
        seat_tokens(0)
        seat_tokens(1)
        pl.semaphore_wait(barrier, S + G - 2)
        for i in others:
            send(r.vin, r.vg.at[s, d], ("v1", i), to_sec(i))
        for i in others:
            for piece in range(3):
                src = r.wqkv_in.at[:, pl.ds(pl.multiple_of(piece * D + sec(i) * Q, Q), Q)]
                dst = r.wqkv.at[s, z, c, :, piece * Q : (piece + 1) * Q]
                send(src, dst, ("q1", piece, i), to_sec(i))
        dispatch_send(r.cots, r.dge, 0, "cot")
        dispatch_send(r.cots, r.dge, 1, "cot")
        for i in others:
            recv(r.vg.at[sec(S - i), d], ("v1", i))
        for j in range(1, G):
            send(r.vg.at[:, d], r.vg.at[:, d], ("v2", j), to_dp(j))
        for i in others:
            for piece in range(3):
                recv(r.wqkv.at[sec(S - i), z, c, :, piece * Q : (piece + 1) * Q], ("q1", piece, i))
        weight_start(r.wqkv, "wqkv")
        weight_next(r.wqkv, "wqkv")
        for i in others:
            send(r.wup_in.at[:, col(sec(i), FQ)], r.wup.at[s, z, c], ("u1", i), to_sec(i))
            send(r.ein, r.evec.at[:, mine], ("e1", i), to_sec(i))
        load_in.start()
        load_out.start()

    def mask_tokens(m):
        end = r.bucket[m, 0, 0]
        seg_q = (early >= end).astype(jnp.int32)
        seg_k = (late >= end).astype(jnp.int32)
        for b in range(1, r.bucket.shape[2]):
            end = end + r.bucket[m, 0, b]
            seg_q += (early >= end).astype(jnp.int32)
            seg_k += (late >= end).astype(jnp.int32)
        live = jnp.broadcast_to(r.live[m : m + 1, :], (T, T))
        allowed = (seg_q == seg_k) & (late <= early) & ((live == 1) | (late == early))
        r.mask[m] = jnp.where(allowed, 1.0, 0.0)

    def spread_vectors():
        for j in range(1, G):
            recv(r.vg.at[:, dpi(G - j)], ("v2", j))
        spread_row = lax.broadcasted_iota(jnp.int32, (128, D), 0)
        spread_lane = lax.broadcasted_iota(jnp.int32, (128, D), 1)
        spread = jnp.where(lax.rem(spread_lane, sh) == spread_row, 1.0, 0.0).astype(bf16)
        stacked = r.vg[...].reshape(S * G * 8, 128).astype(bf16)
        wide = jnp.dot(stacked, spread, preferred_element_type=f32)
        row_id = lax.broadcasted_iota(jnp.int32, (S * G * 8, D), 0)
        lane_id = lax.broadcasted_iota(jnp.int32, (S * G * 8, D), 1)
        low = lax.shift_right_logical(row_id, 3) * sh
        wide = jnp.where((lane_id >= low) & (lane_id < low + sh), wide, 0.0)
        r.vecs[...] = jnp.sum(wide.reshape(S * G, 8, D), axis=0)

    def normed(values):
        mean = jnp.mean(values, axis=1, keepdims=True)
        center = values - mean
        rs = lax.rsqrt(jnp.mean(center * center, axis=1, keepdims=True) + epsilon)
        return center * rs, mean, rs

    def norm_tokens(src, dst, m, at):
        gain = r.vecs[2 * at : 2 * at + 1, :]
        bias = r.vecs[2 * at + 1 : 2 * at + 2, :]

        def body(rows):
            n, mean, rs = normed(src[m, rows].astype(f32))
            r.tst[m, rows, 2 * at : 2 * at + 1] = mean
            r.tst[m, rows, 2 * at + 1 : 2 * at + 2] = rs
            dst[m, rows] = (n * gain + bias).astype(bf16)

        each(T, body)

    entry()
    r.wup[s, z, c] = r.wup_in[:, col(s, FQ)]
    r.wdn[z, c] = r.wdn_in[...]
    mask_tokens(0)
    mask_tokens(1)
    for m in range(M):
        dispatch_recv(r.dge, m, "cot")
        gather_send(r.dge, m, "dge")
    weight_far(r.wqkv, "wqkv")
    weight_start(r.wo, "wo")
    weight_next(r.wo, "wo")
    for i in others:
        recv(r.evec.at[:, col(sec(S - i))], ("e1", i))
        recv(r.wup.at[sec(S - i), z, c], ("u1", i))
    weight_start(r.wup, "wup")
    spread_vectors()
    norm_tokens(r.hidden, r.a1, 0, 0)
    norm_tokens(r.hidden, r.a1, 1, 0)
    weight_near(r.wqkv, "wqkv")
    weight_far(r.wo, "wo")
    weight_next(r.wup, "wup")
    weight_wait(r.wqkv, "wqkv")

    def attend(m):
        @pl.loop(0, 3, unroll=True)
        def _(t):
            w = r.wqkv[:, :, :, :, col(t)].reshape(D, Q)
            r.qkv[m, :, col(t)] = jnp.dot(r.a1[m], w, preferred_element_type=f32).astype(bf16)

        for hh in range(heads):
            at = hh * size
            q = r.qkv[m, :, at : at + size]
            k = r.qkv[m, :, Q + at : Q + at + size]
            v = r.qkv[m, :, 2 * Q + at : 2 * Q + at + size]
            scores = jnp.where(r.mask[m] > 0.0, nt(q, k) * scale, masked_value)
            weights = jnp.exp(scores - jnp.max(scores, axis=1, keepdims=True))
            p = weights / jnp.sum(weights, axis=1, keepdims=True)
            r.probs[m, hh] = p
            mixed = jnp.dot(p.astype(bf16), v, preferred_element_type=f32)
            r.o[m, :, at : at + size] = mixed.astype(bf16)

    def y1_tile(m):
        return lambda q: jnp.dot(
            r.o[m], r.wo[:, :, :, col(q)].reshape(Q, Q), preferred_element_type=f32
        )

    def finish_y1(m):
        sum_recv(r.r1, m, "y1")

        def body(rows):
            total = r.hidden[m, rows, mine].astype(f32) + summed(r.own, r.r1, m, rows)
            r.y1[m, rows, mine] = total.astype(bf16)

        each(T, body)
        gather_send(r.y1, m, "y1g")

    attend(0)
    weight_near(r.wo, "wo")
    weight_wait(r.wo, "wo")
    sum_send(y1_tile(0), r.ts, r.r1, r.own, 0, "y1")
    attend(1)
    sum_send(y1_tile(1), r.ts, r.r1, r.own, 1, "y1")
    weight_far(r.wup, "wup")
    weight_start(r.wdn, "wdn")
    weight_next(r.wdn, "wdn")
    finish_y1(0)
    finish_y1(1)
    weight_near(r.wup, "wup")
    weight_wait(r.wup, "wup")

    def up(m):
        gather_recv(r.y1, m, "y1g")
        norm_tokens(r.y1, r.a2, m, 1)

        @pl.loop(0, FQ // Q, unroll=True)
        def _(t):
            w = r.wup[:, :, :, :, col(t)].reshape(D, Q)
            pre = jnp.dot(r.a2[m], w, preferred_element_type=f32)
            value, slope = gelu_both(pre)
            r.u[m, :, col(t)] = value.astype(bf16)
            r.h[m, :, col(t)] = slope

    def y2_tile(m):
        return lambda q: jnp.dot(
            r.u[m], r.wdn[:, :, :, col(q)].reshape(FQ, Q), preferred_element_type=f32
        )

    weight_far(r.wdn, "wdn")
    up(0)
    up(1)
    weight_near(r.wdn, "wdn")
    weight_wait(r.wdn, "wdn")
    sum_send(y2_tile(0), r.ts, r.r2, r.own, 0, "y2", "y1")
    sum_send(y2_tile(1), r.ts, r.r2, r.own, 1, "y2", "y1", hold=True)

    def finish_y2(m):
        sum_recv(r.r2, m, "y2", None if m else lambda: sum_start(r.ts, r.r2, 1, "y2"))

        def body(rows):
            total = r.y1[m, rows, mine].astype(f32) + summed(r.own, r.r2, m, rows)
            r.y2q[m, rows] = total.astype(bf16)

        each(T, body)
        r.y2s[m] = jnp.dot(r.perm[m], r.y2q[m], preferred_element_type=f32).astype(bf16)
        dispatch_send(r.y2s, r.xe, m, "y2d")

    finish_y2(0)
    dispatch_recv(r.xe, 0, "y2d")
    legs_send(r.xe, 0, "xe")
    finish_y2(1)
    legs_pass(r.xe, 0, "xe")
    dispatch_recv(r.xe, 1, "y2d")
    legs_send(r.xe, 1, "xe")
    load_in.wait()
    load_out.wait()

    def expert(m):
        gather_recv(r.dge, m, "dge")
        legs_recv(r.xe, m, "xe")
        gain, bias, centroid = r.evec[0:1, :], r.evec[1:2, :], r.evec[2:3, :]

        def body(rows):
            v = r.xe[m, rows].astype(f32)
            n, mean, rs = normed(v)
            alpha = jax.nn.sigmoid(jnp.sum(v * centroid, axis=1, keepdims=True))
            r.est[m, rows, 0:1] = mean
            r.est[m, rows, 1:2] = rs
            r.est[m, rows, 2:3] = alpha
            r.en[m, rows] = (n * gain + bias).astype(bf16)
            r.dfe[m, rows] = (alpha * r.dge[m, rows].astype(f32)).astype(bf16)

        each(R, body)

        @pl.loop(0, FQ // Q, unroll=True)
        def _(t):
            w = r.win[:, :, :, :, col(t)].reshape(D, Q)
            pre = jnp.dot(r.en[m], w, preferred_element_type=f32)
            value, slope = gelu_both(pre)
            r.ue[m, :, col(t)] = value.astype(bf16)
            r.slope[:, col(t)] = slope

        if m == 0:
            legs_pass(r.xe, 1, "xe")
        else:
            legs_sum_pass(r.dns, r.dnr, 0, "den")
        stats = [jnp.zeros((R, 1), f32) for _ in range(3)]

        def fe_tile(q):
            tile = jnp.dot(
                r.ue[m], r.wout[:, :, :, col(q)].reshape(FQ, Q), preferred_element_type=f32
            )
            stats[2] += jnp.sum(tile * r.dge[m, :, col(q)].astype(f32), axis=1, keepdims=True)
            return tile

        def den_tile(q):
            return nt(r.dhe[m], r.win[q].reshape(Q, FQ))

        @pl.loop(0, FQ // Q, unroll=True)
        def _(t):
            due = nt(r.dfe[m], r.wout[t].reshape(Q, D))
            r.dhe[m, :, col(t)] = (due * r.slope[:, col(t)]).astype(bf16)

        legs_sum_send(den_tile, r.dns, r.dnr, r.dno, m, "den")
        sum_send(fe_tile, r.fes, r.fer, r.feo, m, "fe", hold=True)
        for i, q in enumerate(quarters + (s,)):
            tile = r.dns[m, i].astype(f32) if i < S - 1 else r.dno[m]
            scaled = tile * r.evec[0:1, col(q)]
            n = (r.xe[m, :, col(q)].astype(f32) - r.est[m, :, 0:1]) * r.est[m, :, 1:2]
            stats[0] += jnp.sum(scaled, axis=1, keepdims=True)
            stats[1] += jnp.sum(scaled * n, axis=1, keepdims=True)
        r.ess[m] = to_rows(stats)
        for i in others:
            send(r.ess.at[m], r.esr.at[m, i - 1], ("est", m, i), to_sec(i))

    expert(0)
    expert(1)

    def finish_den(m):
        legs_sum_recv(r.dnr, m, "den")
        total = r.ess[m]
        for i in others:
            recv(r.esr.at[m, i - 1], ("est", m, i))
            total += r.esr[m, i - 1]
        r.est[m, :, 8:16] = to_columns(total)[:, 0:8]
        gain, centroid = r.evec[0:1, mine], r.evec[2:3, mine]
        if m == 0:
            r.evo[...] = jnp.zeros_like(r.evo)

        def body(rows):
            den = r.dno[m, rows] + r.dnr[m, 0, rows].astype(f32) + r.dnr[m, 1, rows].astype(f32)
            xq = r.xe[m, rows, mine].astype(f32)
            rs, alpha = r.est[m, rows, 1:2], r.est[m, rows, 2:3]
            n = (xq - r.est[m, rows, 0:1]) * rs
            m1, m2 = r.est[m, rows, 8:9] * (1.0 / D), r.est[m, rows, 9:10] * (1.0 / D)
            dlogit = r.est[m, rows, 10:11] * alpha * (1.0 - alpha)
            grad = rs * (gain * den - m1 - n * m2) + dlogit * centroid
            r.dxs[m, rows] = grad.astype(bf16)
            r.evo[0:1, :] += jnp.sum(den * n, axis=0, keepdims=True)
            r.evo[1:2, :] += jnp.sum(den, axis=0, keepdims=True)
            r.evo[2:3, :] += jnp.sum(dlogit * xq, axis=0, keepdims=True)

        each(R, body)
        return_send(r.dxs, r.dxr, m, "dxb")

    def finish_fe(m):
        sum_recv(r.fer, m, "fe")

        def body(rows):
            fe = summed(r.feo, r.fer, m, rows)
            r.ges[m, rows] = (r.est[m, rows, 2:3] * fe).astype(bf16)

        each(R, body)
        return_send(r.ges, r.ger, m, "geb")

    def finish_dxe(m):
        return_recv(r.dxr, m, "dxb")
        back = tn(r.perm[m], r.dxr[m])
        r.dy2[m, :, mine] = (r.cot[m, :, mine].astype(f32) + back).astype(bf16)
        gather_send(r.dy2, m, "dy2")

    finish_den(0)
    legs_sum_pass(r.dns, r.dnr, 1, "den")
    finish_dxe(0)
    finish_den(1)

    writes = []
    results = []

    def give(name):
        i = RESULTS.index(name)
        one = pltpu.make_async_copy(getattr(r, name), getattr(r, "to_" + name), r.lsem.at[4 + i])
        one.start()
        results.append(one)

    def expert_weights(left, right, out):
        for t in range(D // 256):
            slot = len(writes) % 2
            if len(writes) >= 2:
                writes[-2].wait()
            rows = slice(t * 256, (t + 1) * 256)
            lhs = left[:, :, rows].reshape(M * R, 256)
            r.stage[slot] = tn(lhs, right[...].reshape(M * R, D)).astype(bf16)
            writes.append(pltpu.make_async_copy(r.stage.at[slot], out.at[rows], r.lsem.at[2 + slot]))
            writes[-1].start()

    give("evo")

    finish_dxe(1)

    def token_stats(m, at, src):
        stats = [jnp.zeros((T, 1), f32) for _ in range(2)]
        mean, rs = r.tst[m, :, 2 * at : 2 * at + 1], r.tst[m, :, 2 * at + 1 : 2 * at + 2]
        for i in range(S):
            q = sec(i)
            tile = r.ts[m, i - 1].astype(f32) if i else r.own[m]
            scaled = tile * r.vecs[2 * at : 2 * at + 1, col(q)]
            n = (src[m, :, col(q)].astype(f32) - mean) * rs
            stats[0] += jnp.sum(scaled, axis=1, keepdims=True)
            stats[1] += jnp.sum(scaled * n, axis=1, keepdims=True)
        return stats

    def stats_send(m, at, stats):
        r.tss[at, m] = to_rows(stats)
        for i in others:
            send(r.tss.at[at, m], r.tsr.at[at, m, i - 1], ("tst", at, m, i), to_sec(i))

    def stats_recv(m, at):
        total = r.tss[at, m]
        for i in others:
            recv(r.tsr.at[at, m, i - 1], ("tst", at, m, i))
            total += r.tsr[at, m, i - 1]
        r.tst[m, :, 8:16] = to_columns(total)[:, 0:8]

    def dense_back(m):
        if m == 0:
            gather_recv(r.dy2, m, "dy2")

        @pl.loop(0, FQ // Q, unroll=True)
        def _(t):
            du = nt(r.dy2[m], r.wdn[t].reshape(Q, D))
            r.dh[m, :, col(t)] = (du * r.h[m, :, col(t)]).astype(bf16)

        sum_send(
            lambda q: nt(r.dh[m], r.wup[q].reshape(Q, FQ)),
            r.ts,
            r.r1,
            r.own,
            m,
            "da2",
            "y2",
            hold=m == 0,
        )
        stats_send(m, 1, token_stats(m, 1, r.y1))

    def norm_back(m, at, src, grad_in, own, arrive, emit):
        gain = r.vecs[2 * at : 2 * at + 1, mine]

        def body(rows):
            grad = summed(own, arrive, m, rows)
            mean, rs = r.tst[m, rows, 2 * at : 2 * at + 1], r.tst[m, rows, 2 * at + 1 : 2 * at + 2]
            n = (src[m, rows, mine].astype(f32) - mean) * rs
            m1, m2 = r.tst[m, rows, 8:9] * (1.0 / D), r.tst[m, rows, 9:10] * (1.0 / D)
            emit(rows, grad_in[m, rows, mine].astype(f32) + rs * (gain * grad - m1 - n * m2))
            r.vsum[2 * at : 2 * at + 1, :] += jnp.sum(grad * n, axis=0, keepdims=True)
            r.vsum[2 * at + 1 : 2 * at + 2, :] += jnp.sum(grad, axis=0, keepdims=True)

        each(T, body)

    def finish_da2(m):
        sum_recv(r.r1, m, "da2")
        stats_recv(m, 1)
        for i in others:
            sent(("y1g", m, i))

        def emit(rows, value):
            r.y1[m, rows, mine] = value.astype(bf16)

        norm_back(m, 1, r.y1, r.dy2, r.own, r.r1, emit)
        gather_send(r.y1, m, "dy1")

    blocks = (near_far, near, far, z)

    def grads_pair(g, b, k):
        for i, zz in enumerate(blocks):
            src = g.at[:, zz, 1 - c] if len(g.shape) == 5 else g.at[zz, 1 - c]
            dst = b.at[:, zz] if len(g.shape) == 5 else b.at[zz]
            send(src, dst, (k, "p", i), beside)

    def grads_add(g, zz, arrive):
        if len(g.shape) == 5:

            @pl.loop(0, S)
            def _(q):
                g[q, zz, c] = (g[q, zz, c].astype(f32) + arrive[q].astype(f32)).astype(bf16)
        else:
            g[zz, c] = (g[zz, c].astype(f32) + arrive[...].astype(f32)).astype(bf16)

    def grads_paired(g, b, k, i):
        zz = blocks[i]
        piece = b.at[:, zz] if len(g.shape) == 5 else b.at[zz]
        recv(piece, (k, "p", i))
        grads_add(g, zz, piece)

    def grads_near(g, b, arrive, k):
        grads_paired(g, b, k, 0)
        send(part(g, near_far, c), arrive.at[1], (k, "nf"), (s, near * 2 + c))
        grads_paired(g, b, k, 1)
        send(part(g, near, c), arrive.at[0], (k, "n"), (s, near * 2 + c))
        for i in range(2, nz):
            grads_paired(g, b, k, i)

    def grads_far(g, arrive, k):
        recv(arrive.at[1], (k, "nf"))
        grads_add(g, far, arrive.at[1])
        send(part(g, far, c), arrive.at[2], (k, "f"), (s, far * 2 + c))

    def grads_near_recv(arrive, k):
        recv(arrive.at[0], (k, "n"))
        recv(arrive.at[2], (k, "f"))
        return 0, 2

    def down_weights():
        for i, t in enumerate(blocks):
            lhs = r.u[:, :, col(t)].reshape(M * T, Q)
            grad = tn(lhs, r.dy2[...].reshape(M * T, D))
            r.wout[t] = grad.astype(bf16).reshape(2, shd, D)
            send(r.wout.at[t, 1 - c], r.bdn.at[t], ("gdn", "p", i), beside)

    def up_weights():
        @pl.loop(0, S, unroll=True)
        def _(t):
            lhs = r.a2[:, :, col(t)].reshape(M * T, Q)
            grad = tn(lhs, r.dh[...].reshape(M * T, FQ))
            r.win[t] = grad.astype(bf16).reshape(nz, 2, sh, FQ)

        grads_pair(r.win, r.bup, "gup")

    def qkv_weights():
        @pl.loop(0, S, unroll=True)
        def _(t):
            lhs = r.a1[:, :, col(t)].reshape(M * T, Q)
            grad = tn(lhs, r.dqkv[...].reshape(M * T, 3 * Q))
            r.gqk[t] = grad.astype(bf16).reshape(nz, 2, sh, 3 * Q)

        grads_pair(r.gqk, r.bqk, "gqk")

    def out_weights():
        grad = tn(r.o[...].reshape(M * T, Q), r.y1[...].reshape(M * T, D))
        r.gwo[...] = grad.astype(bf16).reshape(nz, 2, sh, D)
        grads_pair(r.gwo, r.bwo, "gwo")

    r.vsum[...] = jnp.zeros_like(r.vsum)
    dense_back(0)
    gather_recv(r.dy2, 1, "dy2", lambda: sum_start(r.ts, r.r1, 0, "da2"))
    down_weights()
    grads_near(r.wout, r.bdn, r.zdn, "gdn")
    dense_back(1)
    finish_da2(0)
    up_weights()
    grads_far(r.wout, r.zdn, "gdn")
    finish_da2(1)
    grads_near(r.win, r.bup, r.zup, "gup")

    def attend_back(m):
        if m == 0:
            gather_recv(r.y1, m, "dy1")
        out_grad = nt(r.y1[m], r.wo[...].reshape(Q, D)).astype(bf16)
        for hh in range(heads):
            at = hh * size
            q = r.qkv[m, :, at : at + size]
            k = r.qkv[m, :, Q + at : Q + at + size]
            v = r.qkv[m, :, 2 * Q + at : 2 * Q + at + size]
            go = out_grad[:, at : at + size]
            p = r.probs[m, hh]
            dp = nt(go, v)
            dv = tn(p.astype(bf16), go)
            ds = (p * (dp - jnp.sum(p * dp, axis=1, keepdims=True))).astype(bf16)
            dq = jnp.dot(ds, k, preferred_element_type=f32) * scale
            dk = tn(ds, q) * scale
            r.dqkv[m, :, at : at + size] = dq.astype(bf16)
            r.dqkv[m, :, Q + at : Q + at + size] = dk.astype(bf16)
            r.dqkv[m, :, 2 * Q + at : 2 * Q + at + size] = dv.astype(bf16)
        sum_send(
            lambda q: nt(r.dqkv[m], r.wqkv[q].reshape(Q, 3 * Q)),
            r.ts,
            r.r2,
            r.own,
            m,
            "da1",
            "da2",
            hold=True,
        )
        stats_send(m, 0, token_stats(m, 0, r.hidden))

    def finish_da1(m):
        sum_recv(r.r2, m, "da1")
        stats_recv(m, 0)

        def emit(rows, value):
            r.dx[m, rows] = value

        norm_back(m, 0, r.hidden, r.y1, r.own, r.r2, emit)

    attend_back(0)
    gather_recv(r.y1, 1, "dy1")
    sum_start(r.fes, r.fer, 0, "fe")
    sum_start(r.fes, r.fer, 1, "fe")
    attend_back(1)
    grads_far(r.win, r.zup, "gup")
    qkv_weights()
    grads_near(r.gqk, r.bqk, r.zqk, "gqk")
    out_weights()
    grads_near(r.gwo, r.bwo, r.zwo, "gwo")
    expert_weights(r.en, r.dhe, r.gin_out)
    finish_fe(0)
    sum_start(r.ts, r.r2, 0, "da1")
    sum_start(r.ts, r.r2, 1, "da1")
    grads_far(r.gqk, r.zqk, "gqk")
    grads_far(r.gwo, r.zwo, "gwo")
    finish_fe(1)
    expert_weights(r.ue, r.dfe, r.gout_out)

    def finish_out(m):
        return_recv(r.ger, m, "geb")
        back = tn(r.perm[m], r.ger[m])
        r.out[m] = (r.y2q[m].astype(f32) + back).astype(bf16)


    def row_result(g, arrive, out, k, rows, wait):
        slots = wait(arrive, k)
        mine_part = part(g, z, c)

        def body(at):
            total = mine_part[at].astype(f32)
            for slot in slots:
                total += arrive[slot, at].astype(f32)
            out[at] = total

        each(rows, body)

    def column_send(g, arrive, out, back, k, wait):
        slots = wait(arrive, k)

        @pl.loop(0, S)
        def _(q):
            total = g[q, z, c].astype(f32)
            for slot in slots:
                total += arrive[slot, q].astype(f32)
            out[q] = total.astype(bf16)

        for i in others:
            send(out.at[sec(i)], back.at[i - 1], (k, "s", i), to_sec(i))

    def column_result(sums, back, out, pieces, k):
        width = sums.shape[2] // pieces
        for i in range(S):
            if i:
                recv(back.at[i - 1], (k, "s", i))
            q = sec(S - i) if i else s
            value = (back[i - 1] if i else sums[s]).astype(f32)
            for piece in range(pieces):
                at = pl.ds(pl.multiple_of(piece * S * width + q * width, width), width)
                out[:, at] = value[:, piece * width : (piece + 1) * width]

    row_result(r.wout, r.zdn, r.gdn_out, "gdn", shd, grads_near_recv)
    give("gdn_out")
    column_send(r.win, r.zup, r.ups, r.upr, "gup", grads_near_recv)
    finish_da1(0)
    finish_da1(1)
    give("dx")
    for j in range(1, G):
        send(r.vsum, r.vsr.at[j - 1], ("vs", j), to_dp(j))
    column_send(r.gqk, r.zqk, r.qks, r.qkr, "gqk", grads_near_recv)
    row_result(r.gwo, r.zwo, r.gwo_out, "gwo", sh, grads_near_recv)
    give("gwo_out")
    column_result(r.ups, r.upr, r.gup_out, 1, "gup")
    give("gup_out")
    finish_out(0)
    finish_out(1)
    give("out")
    total = r.vsum[...]
    for j in range(1, G):
        recv(r.vsr.at[j - 1], ("vs", j))
        total += r.vsr[j - 1]
    shard = jnp.zeros((8, sh), f32)
    for j in range(G):
        shard += jnp.where(d == j, 1.0, 0.0) * total[:, j * sh : (j + 1) * sh]
    r.vgo[...] = jnp.zeros_like(r.vgo)
    r.vgo[:, 0:sh] = shard
    give("vgo")
    column_result(r.qks, r.qkr, r.gqk_out, 3, "gqk")
    give("gqk_out")

    def drain():
        for write in writes[-2:] + results:
            write.wait()
        for last in pending.values():
            last.wait_send()

    drain()
    assert len(places) == KEYS, len(places)


def hand_over(*refs):
    (out, dx, vgo, gqk, gwo, gup, gdn, evo, gin, gout) = refs[:10]
    results = refs[10:]
    results[8][...] = gin[...].astype(f32)
    results[9][...] = gout[...].astype(f32)

    @pl.when(pl.program_id(0) == 0)
    def _():
        for src, dst in zip((out, dx, gqk, gwo, gup, gdn), results[:2] + results[4:8]):
            dst[...] = src[...]
        for i, dst in enumerate(results[2:4] + results[10:12]):
            dst[...] = vgo[i : i + 1, 0 : dst.shape[1]]
        for i, dst in enumerate(results[12:]):
            dst[...] = evo[i : i + 1, :]


def with_kernel(
    hidden_in,
    cotangent,
    bucket_len,
    live_mask,
    routes,
    ln1_gain,
    ln1_bias,
    w_qkv,
    w_attn_out,
    ln2_gain,
    ln2_bias,
    w_up,
    w_down,
    expert_in,
    expert_out,
    expert_gain,
    expert_bias,
    centroids,
):
    S = lax.axis_size(SECTION)
    G = lax.axis_size(DP)
    M, T, D = hidden_in.shape
    Q = D // S
    FQ = w_up.shape[1] // S
    C = 3 * T // (2 * G)
    sh, shd = w_up.shape[0], w_down.shape[0]
    dims = (S, G, M, T, D, Q, FQ, C, sh, shd)
    scratch = layout(dims)
    names = INPUTS + OUTPUTS + list(scratch) + ["ssem", "rsem", "lsem"]
    vmem = pl.BlockSpec(memory_space=pltpu.VMEM)
    smem = pl.BlockSpec(memory_space=pltpu.SMEM)
    anywhere = pl.BlockSpec(memory_space=pl.ANY)
    shapes = (
        ((M, T, Q), bf16),
        ((M, T, Q), f32),
        ((8, 128), f32),
        ((sh, 3 * D), f32),
        ((sh, D), f32),
        ((sh, S * FQ), f32),
        ((shd, D), f32),
        ((8, Q), f32),
        ((D, FQ), bf16),
        ((FQ, D), bf16),
    )
    outs = pl.pallas_call(
        functools.partial(block_kernel, dims, names),
        name="block",
        out_shape=[jax.ShapeDtypeStruct(*shape) for shape in shapes],
        in_specs=[vmem, vmem, smem] + [vmem] * 13 + [anywhere] * 2,
        out_specs=[anywhere] * len(shapes),
        scratch_shapes=[pltpu.VMEM(*shape) for shape in scratch.values()]
        + [pltpu.SemaphoreType.DMA((KEYS,))] * 2
        + [pltpu.SemaphoreType.DMA((4 + len(RESULTS),))],
        compiler_params=pltpu.CompilerParams(
            collective_id=0, has_side_effects=True, vmem_limit_bytes=63 << 20
        ),
    )(
        hidden_in,
        cotangent,
        bucket_len,
        live_mask,
        jnp.swapaxes(routes, 1, 2),
        ln1_gain.reshape(1, sh),
        ln1_bias.reshape(1, sh),
        ln2_gain.reshape(1, sh),
        ln2_bias.reshape(1, sh),
        expert_gain,
        expert_bias,
        centroids,
        w_qkv,
        w_attn_out,
        w_up,
        w_down,
        expert_in.reshape(S, G // 2, 2, sh, FQ),
        expert_out.reshape(G // 2, 2, shd, D),
    )

    def spec(shape):
        if shape in ((D, FQ), (FQ, D)):
            return pl.BlockSpec((512, shape[1]), lambda i: (i, 0))
        return pl.BlockSpec(shape, lambda i, n=len(shape): (0,) * n)

    finals = (
        shapes[:2]
        + (((1, sh), f32),) * 2
        + shapes[3:7]
        + (((D, FQ), f32), ((FQ, D), f32))
        + (((1, sh), f32),) * 2
        + (((1, Q), f32),) * 3
    )
    outs = pl.pallas_call(
        hand_over,
        name="hand_over",
        grid=(D // 512,),
        out_shape=[jax.ShapeDtypeStruct(*shape) for shape in finals],
        in_specs=[spec(shape) for shape, _ in shapes],
        out_specs=[spec(shape) for shape, _ in finals],
        compiler_params=pltpu.CompilerParams(vmem_limit_bytes=63 << 20),
    )(*outs)
    out, dx, gain1, bias1, gqkv, gwo, gup, gdn, gin, gout, gain2, bias2, eg, eb, ec = outs
    return (
        out,
        dx,
        gain1.reshape(sh),
        bias1.reshape(sh),
        gqkv,
        gwo,
        gain2.reshape(sh),
        bias2.reshape(sh),
        gup,
        gdn,
        gin[None],
        gout[None],
        eg,
        eb,
        ec,
    )


def on_device(*args):
    groups = lax.axis_size(DP)
    rows, shard = args[0].shape[1], args[11].shape[0]
    capacity = 3 * rows // (2 * groups)
    if capacity % 16 or shard % 16 or groups != 8:
        return with_collectives(*args)
    return with_kernel(*args)


def solution(mesh):
    everywhere = (SECTION, DP)
    tokens = P(None, DP, None)
    outs = P(None, DP, SECTION)
    per_expert = P(DP, SECTION)
    return jax.shard_map(
        on_device,
        mesh=mesh,
        in_specs=(
            tokens,
            tokens,
            tokens,
            P(None, DP),
            tokens,
            P(everywhere),
            P(everywhere),
            P(everywhere, None),
            P(everywhere, None),
            P(everywhere),
            P(everywhere),
            P(everywhere, None),
            P(everywhere, None),
            P(DP, None, SECTION),
            P(DP, SECTION, None),
            per_expert,
            per_expert,
            per_expert,
        ),
        out_specs=(
            outs,
            outs,
            P(everywhere),
            P(everywhere),
            P(everywhere, None),
            P(everywhere, None),
            P(everywhere),
            P(everywhere),
            P(everywhere, None),
            P(everywhere, None),
            P(DP, None, SECTION),
            P(DP, SECTION, None),
            per_expert,
            per_expert,
            per_expert,
        ),
        check_vma=False,
    )
```

```python
import functools
import math
import types

import jax
import jax.numpy as jnp
from jax import lax
from jax.experimental import pallas as pl
from jax.experimental.pallas import tpu as pltpu
from jax.sharding import PartitionSpec as P

HEADS = 16
SECTION = "section"
DP = "dp"
epsilon = 1e-05
masked_value = -1e30
f32 = jnp.float32
bf16 = jnp.bfloat16


def norm_parts(values):
    center = values - jnp.mean(values, axis=-1, keepdims=True)
    spread = jnp.mean(center * center, axis=-1, keepdims=True)
    rs = lax.rsqrt(spread + epsilon)
    return center * rs, rs


def gelu_back(pre, grad):
    outputs, pullback = jax.vjp(jax.nn.gelu, pre)
    return pullback(grad)[0]


def dot(a, b):
    return jnp.dot(a, b, preferred_element_type=f32)


def dot_tn(a, b):
    return jnp.einsum("rd,re->de", a, b, preferred_element_type=f32)


def dot_nt(a, b):
    return jnp.einsum("re,de->rd", a, b, preferred_element_type=f32)


def sum_scatter(part):
    return lax.psum_scatter(
        part.astype(bf16), SECTION, scatter_dimension=part.ndim - 1, tiled=True
    ).astype(f32)


def gather_features(part):
    return lax.all_gather(part, SECTION, axis=part.ndim - 1, tiled=True)


def with_collectives(
    hidden_in,
    cotangent,
    bucket_len,
    live_mask,
    routes,
    ln1_gain,
    ln1_bias,
    w_qkv,
    w_attn_out,
    ln2_gain,
    ln2_bias,
    w_up,
    w_down,
    expert_in,
    expert_out,
    expert_gain,
    expert_bias,
    centroids,
):
    sections = lax.axis_size(SECTION)
    groups = lax.axis_size(DP)
    section = lax.axis_index(SECTION)
    micro, rows, width = hidden_in.shape
    quarter = width // sections
    heads = HEADS // sections
    size = width // HEADS
    ff = w_up.shape[1] // sections
    capacity = 3 * rows // (2 * groups)
    shard = w_up.shape[0]
    own_cols = section * quarter

    def mine(values):
        return lax.dynamic_slice_in_dim(values, own_cols, quarter, values.ndim - 1)

    def column_group(weight, pieces):
        cols = weight.shape[1] // (pieces * sections)
        parts = weight.reshape(shard, pieces, sections, cols).transpose(2, 0, 1, 3)
        parts = parts.reshape(sections, shard, pieces * cols)
        parts = lax.all_to_all(parts, SECTION, split_axis=0, concat_axis=0, tiled=True)
        full = lax.all_gather(parts, DP, axis=1, tiled=True)
        return full.reshape(width, pieces * cols)

    def column_group_back(grad, pieces):
        cols = grad.shape[1] // pieces
        parts = grad.astype(bf16).reshape(sections, groups * shard, pieces * cols)
        parts = lax.psum_scatter(parts, DP, scatter_dimension=1, tiled=True)
        parts = lax.all_to_all(parts, SECTION, split_axis=0, concat_axis=0, tiled=True)
        parts = parts.reshape(sections, shard, pieces, cols).transpose(1, 2, 0, 3)
        return parts.reshape(shard, pieces * sections * cols).astype(f32)

    def row_group_back(grad):
        return lax.psum_scatter(
            grad.astype(bf16), DP, scatter_dimension=0, tiled=True
        ).astype(f32)

    vectors = lax.all_gather(
        jnp.stack([ln1_gain, ln1_bias, ln2_gain, ln2_bias]), (SECTION, DP), axis=1, tiled=True
    ).astype(f32)
    gain_one, bias_one, gain_two, bias_two = vectors
    expert_vectors = lax.all_gather(
        jnp.concatenate([expert_gain, expert_bias, centroids]), SECTION, axis=1, tiled=True
    ).astype(f32)
    expert_g, expert_b, centroid = expert_vectors
    wqkv = column_group(w_qkv, 3)
    wo = lax.all_gather(w_attn_out, DP, axis=0, tiled=True)
    wup = column_group(w_up, 1)
    wdown = lax.all_gather(w_down, DP, axis=0, tiled=True)
    win = expert_in[0]
    wout = expert_out[0]

    ends = jnp.cumsum(bucket_len[:, 0, :], axis=-1)
    slot_ids = jnp.arange(rows, dtype=jnp.int32)
    segments = jnp.sum((slot_ids[None, :, None] >= ends[:, None, :]).astype(jnp.int32), axis=-1)
    same = segments[:, :, None] == segments[:, None, :]
    causal = slot_ids[None, None, :] <= slot_ids[None, :, None]
    opened = (live_mask[:, None, :] == 1) | (slot_ids[None, None, :] == slot_ids[None, :, None])
    allowed = (same & causal & opened)[:, None]
    chosen = routes[:, :, 0]
    picks = (chosen[:, :, None] == jnp.arange(groups, dtype=jnp.int32)).astype(jnp.int32)
    ranks = jnp.sum((jnp.cumsum(picks, axis=1) - picks) * picks, axis=2)
    places = chosen * capacity + ranks
    place_ids = jnp.arange(groups * capacity, dtype=jnp.int32)
    picked = (places[:, None, :] == place_ids[None, :, None]).astype(bf16)

    def dispatch(values):
        out = jnp.einsum("mpt,mtf->pmf", picked, values, preferred_element_type=f32).astype(bf16)
        out = out.reshape(groups, capacity * micro, quarter)
        return lax.all_to_all(out, DP, split_axis=0, concat_axis=0, tiled=True)

    def give_back(values):
        out = lax.all_to_all(values, DP, split_axis=0, concat_axis=0, tiled=True)
        out = out.reshape(groups * capacity, micro, quarter)
        return jnp.einsum("mpt,pmf->mtf", picked, out, preferred_element_type=f32)

    dge = gather_features(dispatch(mine(cotangent))).reshape(-1, width).astype(f32)

    x = hidden_in.reshape(micro * rows, width).astype(f32)
    n1, rs1 = norm_parts(x)
    a1 = (n1 * gain_one + bias_one).astype(bf16)
    qkv = dot(a1, wqkv).astype(bf16)
    q, k, v = (
        qkv[:, i * quarter : (i + 1) * quarter].reshape(micro, rows, heads, size) for i in range(3)
    )
    scale = size ** (-0.5)
    raw = jnp.einsum("mqhd,mkhd->mhqk", q, k, preferred_element_type=f32) * scale
    scores = jnp.where(allowed, raw, masked_value)
    weights = jnp.exp(scores - jnp.max(scores, axis=-1, keepdims=True))
    probs = weights / jnp.sum(weights, axis=-1, keepdims=True)
    probs_low = probs.astype(bf16)
    mixed = jnp.einsum("mhqk,mkhd->mqhd", probs_low, v, preferred_element_type=f32)
    o = mixed.reshape(micro * rows, quarter).astype(bf16)
    y1q = (mine(x) + sum_scatter(dot(o, wo))).astype(bf16)
    y1 = gather_features(y1q).astype(f32)
    n2, rs2 = norm_parts(y1)
    a2 = (n2 * gain_two + bias_two).astype(bf16)
    h = dot(a2, wup)
    u = jax.nn.gelu(h).astype(bf16)
    y2q = (y1q.astype(f32) + sum_scatter(dot(u, wdown))).astype(bf16)

    xe = gather_features(dispatch(y2q.reshape(micro, rows, quarter))).reshape(-1, width)
    xe = xe.astype(f32)
    ne, rse = norm_parts(xe)
    en = (ne * expert_g + expert_b).astype(bf16)
    he = dot(en, win)
    ue = jax.nn.gelu(he).astype(bf16)
    fe_part = dot(ue, wout)
    alpha = jax.nn.sigmoid(jnp.sum(xe * centroid, axis=-1, keepdims=True))
    fe = sum_scatter(fe_part)
    ge = (alpha * fe).astype(bf16).reshape(groups, capacity * micro, quarter)
    block_out = (
        y2q.reshape(micro, rows, quarter).astype(f32) + give_back(ge)
    ).astype(bf16)

    dfe = (alpha * dge).astype(bf16)
    due = dot_nt(dfe, wout)
    grad_out = dot_tn(ue, dfe)
    dhe = gelu_back(he, due).astype(bf16)
    grad_in = dot_tn(en, dhe)
    den_part = dot_nt(dhe, win)
    gden = den_part * expert_g
    stats = lax.psum(
        jnp.stack(
            [
                jnp.mean(gden, axis=-1),
                jnp.mean(gden * ne, axis=-1),
                jnp.sum(dge * fe_part, axis=-1),
            ]
        ),
        SECTION,
    )[..., None]
    den = sum_scatter(den_part)
    neq = mine(ne)
    dlogit = stats[2] * alpha * (1.0 - alpha)
    dxe_ln = rse * (mine(expert_g) * den - stats[0] - neq * stats[1])
    dxe = (dxe_ln + dlogit * mine(centroid)).astype(bf16)
    grad_expert_gain = jnp.sum(den * neq, axis=0)
    grad_expert_bias = jnp.sum(den, axis=0)
    grad_centroid = jnp.sum(dlogit * mine(xe), axis=0)
    back = give_back(dxe.reshape(groups, capacity * micro, quarter))
    dy2q = (mine(cotangent).astype(f32) + back).astype(bf16).reshape(micro * rows, quarter)

    dy2 = gather_features(dy2q)
    grad_down = dot_tn(u, dy2)
    dh = gelu_back(h, dot_nt(dy2, wdown)).astype(bf16)
    grad_up = dot_tn(a2, dh)
    da2_part = dot_nt(dh, wup)
    gda2 = da2_part * gain_two
    stats = lax.psum(
        jnp.stack([jnp.mean(gda2, axis=-1), jnp.mean(gda2 * n2, axis=-1)]), SECTION
    )[..., None]
    da2 = sum_scatter(da2_part)
    n2q = mine(n2)
    dy1q = dy2q.astype(f32) + rs2 * (mine(gain_two) * da2 - stats[0] - n2q * stats[1])
    dy1q = dy1q.astype(bf16)
    dy1 = gather_features(dy1q)
    grad_wo = dot_tn(o, dy1)
    do = dot_nt(dy1, wo).astype(bf16).reshape(micro, rows, heads, size)
    dp = jnp.einsum("mqhd,mkhd->mhqk", do, v, preferred_element_type=f32)
    dv = jnp.einsum("mhqk,mqhd->mkhd", probs_low, do, preferred_element_type=f32)
    delta = jnp.sum(probs * dp, axis=-1, keepdims=True)
    ds = (probs * (dp - delta)).astype(bf16)
    dq = jnp.einsum("mhqk,mkhd->mqhd", ds, k, preferred_element_type=f32) * scale
    dk = jnp.einsum("mhqk,mqhd->mkhd", ds, q, preferred_element_type=f32) * scale
    dqkv = jnp.concatenate(
        [part.reshape(micro * rows, quarter) for part in (dq, dk, dv)], axis=1
    ).astype(bf16)
    grad_qkv = dot_tn(a1, dqkv)
    da1_part = dot_nt(dqkv, wqkv)
    gda1 = da1_part * gain_one
    stats = lax.psum(
        jnp.stack([jnp.mean(gda1, axis=-1), jnp.mean(gda1 * n1, axis=-1)]), SECTION
    )[..., None]
    da1 = sum_scatter(da1_part)
    n1q = mine(n1)
    dx = dy1q.astype(f32) + rs1 * (mine(gain_one) * da1 - stats[0] - n1q * stats[1])

    vector_grads = lax.psum_scatter(
        jnp.stack(
            [
                jnp.sum(da1 * n1q, axis=0),
                jnp.sum(da1, axis=0),
                jnp.sum(da2 * n2q, axis=0),
                jnp.sum(da2, axis=0),
            ]
        ),
        DP,
        scatter_dimension=1,
        tiled=True,
    )
    return (
        block_out,
        dx.reshape(micro, rows, quarter),
        vector_grads[0],
        vector_grads[1],
        column_group_back(grad_qkv, 3),
        row_group_back(grad_wo),
        vector_grads[2],
        vector_grads[3],
        column_group_back(grad_up, 1),
        row_group_back(grad_down),
        grad_in[None],
        grad_out[None],
        grad_expert_gain[None],
        grad_expert_bias[None],
        grad_centroid[None],
    )


MESH = pl.DeviceIdType.MESH
KEYS = 101
CHAIN = {
    "y1": 0,
    "y1g": 1,
    "y2": 0,
    "xe": 1,
    "den": 0,
    "dy2": 1,
    "da2": 0,
    "dy1": 1,
    "da1": 0,
}
SHARED = {
    "geb": "y2d",
    "dxb": "cot",
    "fe": "dge",
    "est": "stats",
    "tst": "stats",
    "vs": "v2",
    "gdn": "wdn",
    "gup": "wup",
    "gwo": "wo",
    "gqk": "wqkv",
    "p": "c",
    "n": "near",
    "nf": "near far",
    "f": "far",
}


LEGS = {
    "xe": ("x", "y", "xy", "yx"),
    "den": ("x0", "x2", "y1", "y2", "xy", "yx"),
}


def semaphore_of(k):
    if k[0] in LEGS:
        leg = LEGS[k[0]].index(k[2])
        return ("chain", CHAIN[k[0]], k[1], leg + 1) if leg < 3 else ("leg", k[0], k[1], leg)
    if k[0] in CHAIN:
        return ("chain", CHAIN[k[0]]) + k[1:]
    if k[0] == "q1":
        return ("stats", k[1], k[2]) if k[1] < 2 else ("chain", 1, 0, k[2])
    if k[0] == "v1":
        return "chain", 1, 1, k[1]
    if k[1] == "s":
        return "u1" if k[0] == "gup" else "e1", k[2]
    if k[0] == "tst":
        return ("stats",) + k[2:]
    return tuple(SHARED.get(part, part) for part in k)
CHUNK = 128


def tn(a, b):
    return lax.dot_general(a, b, (((0,), (0,)), ((), ())), preferred_element_type=f32)


def nt(a, b):
    return lax.dot_general(a, b, (((1,), (1,)), ((), ())), preferred_element_type=f32)


def tanh_parts(v):
    root = 0.7978845608028654
    t = jnp.tanh(root * (v + 0.044715 * (v * v * v)))
    return t, root


def gelu_both(v):
    t, root = tanh_parts(v)
    half = 0.5 * (1.0 + t)
    return v * half, half + 0.5 * v * (1.0 - t * t) * root * (1.0 + 0.134145 * (v * v))


def to_rows(columns):
    lane = lax.broadcasted_iota(jnp.int32, (columns[0].shape[0], 128), 1)
    wide = jnp.zeros(lane.shape, f32)
    for i, column in enumerate(columns):
        wide = jnp.where(lane == i, column, wide)
    return wide.T[:8]


def to_columns(rows):
    return jnp.concatenate([rows, jnp.zeros((120, rows.shape[1]), f32)], axis=0).T


def layout(dims):
    S, G, M, T, D, Q, FQ, C, sh, shd = dims
    nz = G // 2
    R = G * C
    heads = HEADS // S
    return dict(
        wqkv=((S, nz, 2, sh, 3 * Q), bf16),
        wo=((nz, 2, sh, D), bf16),
        wup=((S, nz, 2, sh, FQ), bf16),
        wdn=((nz, 2, shd, D), bf16),
        win=((S, nz, 2, sh, FQ), bf16),
        wout=((nz, 2, shd, D), bf16),
        vin=((8, 128), f32),
        ein=((8, Q), f32),
        vg=((S, G, 8, 128), f32),
        vecs=((8, D), f32),
        evec=((8, D), f32),
        mask=((M, T, T), f32),
        perm=((M, R, T), bf16),
        cots=((M, R, Q), bf16),
        y2s=((M, R, Q), bf16),
        ges=((M, R, Q), bf16),
        dxs=((M, R, Q), bf16),
        ger=((M, R, Q), bf16),
        dxr=((M, R, Q), bf16),
        tst=((M, T, 128), f32),
        est=((M, R, 128), f32),
        a1=((M, T, D), bf16),
        a2=((M, T, D), bf16),
        qkv=((M, T, 3 * Q), bf16),
        probs=((M, heads, T, T), f32),
        o=((M, T, Q), bf16),
        y1=((M, T, D), bf16),
        h=((M, T, FQ), f32),
        u=((M, T, FQ), bf16),
        y2q=((M, T, Q), bf16),
        xe=((M, R, D), bf16),
        dge=((M, R, D), bf16),
        en=((M, R, D), bf16),
        ue=((M, R, FQ), bf16),
        dhe=((M, R, FQ), bf16),
        dfe=((M, R, D), bf16),
        slope=((R, FQ), f32),
        fes=((M, S - 1, R, Q), bf16),
        fer=((M, S - 1, R, Q), bf16),
        feo=((M, R, Q), f32),
        dns=((M, S - 1, R, Q), bf16),
        dnr=((M, S - 1, R, Q), bf16),
        dno=((M, R, Q), f32),
        ess=((M, 8, R), f32),
        esr=((M, S - 1, 8, R), f32),
        ts=((M, S - 1, T, Q), bf16),
        r1=((M, S - 1, T, Q), bf16),
        r2=((M, S - 1, T, Q), bf16),
        own=((M, T, Q), f32),
        tss=((2, M, 8, T), f32),
        tsr=((2, M, S - 1, 8, T), f32),
        dy2=((M, T, D), bf16),
        dh=((M, T, FQ), bf16),
        dqkv=((M, T, 3 * Q), bf16),
        gwo=((nz, 2, sh, D), bf16),
        gqk=((S, nz, 2, sh, 3 * Q), bf16),
        bdn=((nz, shd, D), bf16),
        bup=((S, nz, sh, FQ), bf16),
        bwo=((nz, sh, D), bf16),
        bqk=((S, nz, sh, 3 * Q), bf16),
        zdn=((nz - 1, shd, D), bf16),
        zup=((nz - 1, S, sh, FQ), bf16),
        zwo=((nz - 1, sh, D), bf16),
        zqk=((nz - 1, S, sh, 3 * Q), bf16),
        ups=((S, sh, FQ), bf16),
        upr=((S - 1, sh, FQ), bf16),
        qks=((S, sh, 3 * Q), bf16),
        qkr=((S - 1, sh, 3 * Q), bf16),
        stage=((2, 256, D), bf16),
        out=((M, T, Q), bf16),
        dx=((M, T, Q), f32),
        vgo=((8, 128), f32),
        gqk_out=((sh, 3 * D), f32),
        gwo_out=((sh, D), f32),
        gup_out=((sh, S * FQ), f32),
        gdn_out=((shd, D), f32),
        evo=((8, Q), f32),
        vsum=((8, Q), f32),
        vsr=((G - 1, 8, Q), f32),
    )


INPUTS = [
    "hidden",
    "cot",
    "bucket",
    "live",
    "routes",
    "gain_one",
    "bias_one",
    "gain_two",
    "bias_two",
    "gain_e",
    "bias_e",
    "centroid",
    "wqkv_in",
    "wo_in",
    "wup_in",
    "wdn_in",
    "win_in",
    "wout_in",
]
RESULTS = [
    "out",
    "dx",
    "vgo",
    "gqk_out",
    "gwo_out",
    "gup_out",
    "gdn_out",
    "evo",
]
OUTPUTS = ["to_" + name for name in RESULTS] + ["gin_out", "gout_out"]


def block_kernel(dims, names, *args):
    r = types.SimpleNamespace(**dict(zip(names, args)))
    S, G, M, T, D, Q, FQ, C, sh, shd = dims
    nz = G // 2
    R = G * C
    heads = HEADS // S
    size = D // HEADS
    scale = size ** (-0.5)
    s = lax.axis_index(SECTION)
    d = lax.axis_index(DP)
    z = lax.div(d, 2)
    c = lax.rem(d, 2)
    beside = (s, d + 1 - 2 * c)
    near = z + 1 - 2 * lax.rem(z, 2)
    far = lax.rem(z + 2, nz)
    near_far = lax.rem(near + 2, nz)
    beside_x = s + 1 - 2 * lax.rem(s, 2)
    beside_y = lax.rem(s + 2, S)
    across = lax.rem(beside_x + 2, S)

    def sec(i):
        return lax.rem(s + i, S)

    def dpi(j):
        return lax.rem(d + j, G)

    def zi(j):
        return lax.rem(z + j, nz)

    def to_sec(i):
        return (sec(i), d)

    def to_dp(j):
        return (s, dpi(j))

    def to_z(j):
        return (s, zi(j) * 2 + c)

    def col(q, n=Q):
        return pl.ds(pl.multiple_of(q * n, n), n)

    def seats(e):
        return pl.ds(pl.multiple_of(e * C, C), C)

    mine = col(s)
    places = {}
    pending = {}

    def copy(src, dst, k, device):
        i = places.setdefault(semaphore_of(k), len(places))
        return pltpu.make_async_remote_copy(
            src_ref=src,
            dst_ref=dst,
            send_sem=r.ssem.at[i],
            recv_sem=r.rsem.at[i],
            device_id=device,
            device_id_type=MESH,
        )

    def send(src, dst, k, device):
        sent(k)
        pending[semaphore_of(k)] = copy(src, dst, k, device)
        pending[semaphore_of(k)].start()

    def sent(k):
        last = pending.pop(semaphore_of(k), None)
        if last is not None:
            last.wait_send()

    def recv(dst, k):
        copy(dst, dst, k, beside).wait_recv()

    def each(rows, body):
        step = math.gcd(rows, CHUNK)

        @pl.loop(0, rows // step)
        def _(i):
            body(pl.ds(pl.multiple_of(i * step, step), step))

    others = range(1, S)

    def gather_send(ref, m, k):
        for i in others:
            send(ref.at[m, :, mine], ref.at[m, :, mine], (k, m, i), to_sec(i))

    def gather_recv(ref, m, k, then=None):
        for i in others:
            recv(ref.at[m, :, col(sec(S - i))], (k, m, i))
            if then is not None and i == S - 2:
                then()

    def sum_send(tile, out, arrive, own, m, k, before=None, hold=False):
        for i in others:
            if before is not None:
                sent((before, m, i))
            out[m, i - 1] = tile(sec(i)).astype(bf16)
        own[m] = tile(s)
        if not hold:
            sum_start(out, arrive, m, k)

    def sum_start(out, arrive, m, k):
        for i in others:
            send(out.at[m, i - 1], arrive.at[m, i - 1], (k, m, i), to_sec(i))

    def sum_recv(arrive, m, k, then=None):
        for i in others:
            recv(arrive.at[m, i - 1], (k, m, i))
            if then is not None and i == S - 2:
                then()

    def summed(own, arrive, m, rows):
        total = own[m, rows]
        for i in others:
            total += arrive[m, i - 1, rows].astype(f32)
        return total

    top, low = slice(0, R // 2), slice(R // 2, R)

    def legs_send(ref, m, k):
        send(ref.at[m, :, mine], ref.at[m, :, mine], (k, m, "x"), (beside_x, d))
        send(ref.at[m, :, mine], ref.at[m, :, mine], (k, m, "y"), (beside_y, d))

    def legs_pass(ref, m, k):
        recv(ref.at[m, :, col(beside_x)], (k, m, "x"))
        block = ref.at[m, top, col(beside_x)]
        send(block, block, (k, m, "xy"), (beside_y, d))
        recv(ref.at[m, :, col(beside_y)], (k, m, "y"))
        block = ref.at[m, low, col(beside_y)]
        send(block, block, (k, m, "yx"), (beside_x, d))

    def legs_recv(ref, m, k):
        recv(ref.at[m, top, col(across)], (k, m, "xy"))
        recv(ref.at[m, low, col(across)], (k, m, "yx"))

    quarters = (beside_x, beside_y, across)

    def legs_sum_send(tile, out, arrive, own, m, k):
        for i, q in enumerate(quarters):
            out[m, i] = tile(q).astype(bf16)
        own[m] = tile(s)
        for i in (2, 0):
            send(out.at[m, i, top], arrive.at[m, i, top], (k, m, "x" + str(i)), (beside_x, d))
        for i in (2, 1):
            send(out.at[m, i, low], arrive.at[m, i, low], (k, m, "y" + str(i)), (beside_y, d))

    def legs_sum_pass(out, arrive, m, k):
        recv(arrive.at[m, 2, top], (k, m, "x2"))
        both = out[m, 1, top].astype(f32) + arrive[m, 2, top].astype(f32)
        out[m, 1, top] = both.astype(bf16)
        send(out.at[m, 1, top], arrive.at[m, 1, top], (k, m, "xy"), (beside_y, d))
        recv(arrive.at[m, 2, low], (k, m, "y2"))
        both = out[m, 0, low].astype(f32) + arrive[m, 2, low].astype(f32)
        out[m, 0, low] = both.astype(bf16)
        send(out.at[m, 0, low], arrive.at[m, 0, low], (k, m, "yx"), (beside_x, d))

    def legs_sum_recv(arrive, m, k):
        recv(arrive.at[m, 0, top], (k, m, "x0"))
        recv(arrive.at[m, 1, low], (k, m, "y1"))
        recv(arrive.at[m, 1, top], (k, m, "xy"))
        recv(arrive.at[m, 0, low], (k, m, "yx"))

    def dispatch_send(src, dst, m, k):
        dst[m, seats(d), mine] = src[m, seats(d)]
        for j in range(1, G):
            send(src.at[m, seats(dpi(j))], dst.at[m, seats(d), mine], (k, m, j), to_dp(j))

    def dispatch_recv(dst, m, k):
        for j in range(1, G):
            recv(dst.at[m, seats(dpi(G - j)), mine], (k, m, j))

    def return_send(src, dst, m, k):
        dst[m, seats(d)] = src[m, seats(d)]
        for j in range(1, G):
            send(src.at[m, seats(dpi(j))], dst.at[m, seats(d)], (k, m, j), to_dp(j))

    def return_recv(dst, m, k):
        for j in range(1, G):
            recv(dst.at[m, seats(dpi(G - j))], (k, m, j))

    def part(ref, zz, cc):
        return ref.at[:, zz, cc] if len(ref.shape) == 5 else ref.at[zz, cc]

    def weight_start(ref, k):
        send(part(ref, z, c), part(ref, z, c), (k, "far"), (s, far * 2 + c))
        send(part(ref, z, c), part(ref, z, c), (k, "c", 0), beside)

    def weight_next(ref, k):
        send(part(ref, z, c), part(ref, z, c), (k, "near"), (s, near * 2 + c))

    def weight_far(ref, k):
        recv(part(ref, far, c), (k, "far"))
        send(part(ref, far, c), part(ref, far, c), (k, "near far"), (s, near * 2 + c))
        send(part(ref, far, c), part(ref, far, c), (k, "c", 1), beside)

    def weight_near(ref, k):
        recv(part(ref, near, c), (k, "near"))
        send(part(ref, near, c), part(ref, near, c), (k, "c", 2), beside)
        recv(part(ref, near_far, c), (k, "near far"))
        send(part(ref, near_far, c), part(ref, near_far, c), (k, "c", 3), beside)

    def weight_wait(ref, k):
        for i, zz in enumerate((z, far, near, near_far)):
            recv(part(ref, zz, 1 - c), (k, "c", i))

    load_in = pltpu.make_async_copy(r.win_in, r.win, r.lsem.at[0])
    load_out = pltpu.make_async_copy(r.wout_in, r.wout, r.lsem.at[1])

    early = lax.broadcasted_iota(jnp.int32, (T, T), 0)
    late = lax.broadcasted_iota(jnp.int32, (T, T), 1)

    def seat_tokens(m):
        route = r.routes[m]
        expert_ids = lax.broadcasted_iota(jnp.int32, (G, T), 0)
        picks = jnp.where(expert_ids == route, 1.0, 0.0)
        before = jnp.where(early < late, 1.0, 0.0).astype(bf16)
        counts = jnp.dot(picks.astype(bf16), before, preferred_element_type=f32)
        rank = jnp.sum(counts * picks, axis=0, keepdims=True)
        place = route.astype(f32) * float(C) + rank
        seat_ids = lax.broadcasted_iota(jnp.int32, (R, T), 0).astype(f32)
        r.perm[m] = jnp.where(seat_ids == place, 1.0, 0.0).astype(bf16)
        r.cots[m] = jnp.dot(r.perm[m], r.cot[m, :, mine], preferred_element_type=f32).astype(bf16)

    def entry():
        barrier = pltpu.get_barrier_semaphore()
        for i in others:
            pl.semaphore_signal(barrier, inc=1, device_id=to_sec(i), device_id_type=MESH)
        for j in range(1, G):
            pl.semaphore_signal(barrier, inc=1, device_id=to_dp(j), device_id_type=MESH)
        r.vin[...] = jnp.zeros_like(r.vin)
        for i, ref in enumerate((r.gain_one, r.bias_one, r.gain_two, r.bias_two)):
            r.vin[i : i + 1, 0:sh] = ref[...].astype(f32)
        r.ein[...] = jnp.zeros_like(r.ein)
        for i, ref in enumerate((r.gain_e, r.bias_e, r.centroid)):
            r.ein[i : i + 1, :] = ref[...].astype(f32)
        r.vg[s, d] = r.vin[...]
        r.evec[:, mine] = r.ein[...]
        for piece in range(3):
            r.wqkv[s, z, c, :, piece * Q : (piece + 1) * Q] = r.wqkv_in[
                :, pl.ds(pl.multiple_of(piece * D + s * Q, Q), Q)
            ]
        r.wo[z, c] = r.wo_in[...]
        seat_tokens(0)
        seat_tokens(1)
        pl.semaphore_wait(barrier, S + G - 2)
        for i in others:
            send(r.vin, r.vg.at[s, d], ("v1", i), to_sec(i))
        for i in others:
            for piece in range(3):
                src = r.wqkv_in.at[:, pl.ds(pl.multiple_of(piece * D + sec(i) * Q, Q), Q)]
                dst = r.wqkv.at[s, z, c, :, piece * Q : (piece + 1) * Q]
                send(src, dst, ("q1", piece, i), to_sec(i))
        dispatch_send(r.cots, r.dge, 0, "cot")
        dispatch_send(r.cots, r.dge, 1, "cot")
        for i in others:
            recv(r.vg.at[sec(S - i), d], ("v1", i))
        for j in range(1, G):
            send(r.vg.at[:, d], r.vg.at[:, d], ("v2", j), to_dp(j))
        for i in others:
            for piece in range(3):
                recv(r.wqkv.at[sec(S - i), z, c, :, piece * Q : (piece + 1) * Q], ("q1", piece, i))
        weight_start(r.wqkv, "wqkv")
        weight_next(r.wqkv, "wqkv")
        for i in others:
            send(r.wup_in.at[:, col(sec(i), FQ)], r.wup.at[s, z, c], ("u1", i), to_sec(i))
            send(r.ein, r.evec.at[:, mine], ("e1", i), to_sec(i))
        load_in.start()
        load_out.start()

    def mask_tokens(m):
        end = r.bucket[m, 0, 0]
        seg_q = (early >= end).astype(jnp.int32)
        seg_k = (late >= end).astype(jnp.int32)
        for b in range(1, r.bucket.shape[2]):
            end = end + r.bucket[m, 0, b]
            seg_q += (early >= end).astype(jnp.int32)
            seg_k += (late >= end).astype(jnp.int32)
        live = jnp.broadcast_to(r.live[m : m + 1, :], (T, T))
        allowed = (seg_q == seg_k) & (late <= early) & ((live == 1) | (late == early))
        r.mask[m] = jnp.where(allowed, 1.0, 0.0)

    def spread_vectors():
        for j in range(1, G):
            recv(r.vg.at[:, dpi(G - j)], ("v2", j))
        spread_row = lax.broadcasted_iota(jnp.int32, (128, D), 0)
        spread_lane = lax.broadcasted_iota(jnp.int32, (128, D), 1)
        spread = jnp.where(lax.rem(spread_lane, sh) == spread_row, 1.0, 0.0).astype(bf16)
        stacked = r.vg[...].reshape(S * G * 8, 128).astype(bf16)
        wide = jnp.dot(stacked, spread, preferred_element_type=f32)
        row_id = lax.broadcasted_iota(jnp.int32, (S * G * 8, D), 0)
        lane_id = lax.broadcasted_iota(jnp.int32, (S * G * 8, D), 1)
        low = lax.shift_right_logical(row_id, 3) * sh
        wide = jnp.where((lane_id >= low) & (lane_id < low + sh), wide, 0.0)
        r.vecs[...] = jnp.sum(wide.reshape(S * G, 8, D), axis=0)

    def normed(values):
        mean = jnp.mean(values, axis=1, keepdims=True)
        center = values - mean
        rs = lax.rsqrt(jnp.mean(center * center, axis=1, keepdims=True) + epsilon)
        return center * rs, mean, rs

    def norm_tokens(src, dst, m, at):
        gain = r.vecs[2 * at : 2 * at + 1, :]
        bias = r.vecs[2 * at + 1 : 2 * at + 2, :]

        def body(rows):
            n, mean, rs = normed(src[m, rows].astype(f32))
            r.tst[m, rows, 2 * at : 2 * at + 1] = mean
            r.tst[m, rows, 2 * at + 1 : 2 * at + 2] = rs
            dst[m, rows] = (n * gain + bias).astype(bf16)

        each(T, body)

    entry()
    r.wup[s, z, c] = r.wup_in[:, col(s, FQ)]
    r.wdn[z, c] = r.wdn_in[...]
    mask_tokens(0)
    mask_tokens(1)
    for m in range(M):
        dispatch_recv(r.dge, m, "cot")
        gather_send(r.dge, m, "dge")
    weight_far(r.wqkv, "wqkv")
    weight_start(r.wo, "wo")
    weight_next(r.wo, "wo")
    for i in others:
        recv(r.evec.at[:, col(sec(S - i))], ("e1", i))
        recv(r.wup.at[sec(S - i), z, c], ("u1", i))
    weight_start(r.wup, "wup")
    spread_vectors()
    norm_tokens(r.hidden, r.a1, 0, 0)
    norm_tokens(r.hidden, r.a1, 1, 0)
    weight_near(r.wqkv, "wqkv")
    weight_far(r.wo, "wo")
    weight_next(r.wup, "wup")
    weight_wait(r.wqkv, "wqkv")

    def attend(m):
        @pl.loop(0, 3)
        def _(t):
            w = r.wqkv[:, :, :, :, col(t)].reshape(D, Q)
            r.qkv[m, :, col(t)] = jnp.dot(r.a1[m], w, preferred_element_type=f32).astype(bf16)

        for hh in range(heads):
            at = hh * size
            q = r.qkv[m, :, at : at + size]
            k = r.qkv[m, :, Q + at : Q + at + size]
            v = r.qkv[m, :, 2 * Q + at : 2 * Q + at + size]
            scores = jnp.where(r.mask[m] > 0.0, nt(q, k) * scale, masked_value)
            weights = jnp.exp(scores - jnp.max(scores, axis=1, keepdims=True))
            p = weights / jnp.sum(weights, axis=1, keepdims=True)
            r.probs[m, hh] = p
            mixed = jnp.dot(p.astype(bf16), v, preferred_element_type=f32)
            r.o[m, :, at : at + size] = mixed.astype(bf16)

    def y1_tile(m):
        return lambda q: jnp.dot(
            r.o[m], r.wo[:, :, :, col(q)].reshape(Q, Q), preferred_element_type=f32
        )

    def finish_y1(m):
        sum_recv(r.r1, m, "y1")

        def body(rows):
            total = r.hidden[m, rows, mine].astype(f32) + summed(r.own, r.r1, m, rows)
            r.y1[m, rows, mine] = total.astype(bf16)

        each(T, body)
        gather_send(r.y1, m, "y1g")

    attend(0)
    weight_near(r.wo, "wo")
    weight_wait(r.wo, "wo")
    sum_send(y1_tile(0), r.ts, r.r1, r.own, 0, "y1")
    attend(1)
    sum_send(y1_tile(1), r.ts, r.r1, r.own, 1, "y1")
    weight_far(r.wup, "wup")
    weight_start(r.wdn, "wdn")
    weight_next(r.wdn, "wdn")
    finish_y1(0)
    finish_y1(1)
    weight_near(r.wup, "wup")
    weight_wait(r.wup, "wup")

    def up(m):
        gather_recv(r.y1, m, "y1g")
        norm_tokens(r.y1, r.a2, m, 1)

        @pl.loop(0, FQ // Q)
        def _(t):
            w = r.wup[:, :, :, :, col(t)].reshape(D, Q)
            pre = jnp.dot(r.a2[m], w, preferred_element_type=f32)
            value, slope = gelu_both(pre)
            r.u[m, :, col(t)] = value.astype(bf16)
            r.h[m, :, col(t)] = slope

    def y2_tile(m):
        return lambda q: jnp.dot(
            r.u[m], r.wdn[:, :, :, col(q)].reshape(FQ, Q), preferred_element_type=f32
        )

    weight_far(r.wdn, "wdn")
    up(0)
    up(1)
    weight_near(r.wdn, "wdn")
    weight_wait(r.wdn, "wdn")
    sum_send(y2_tile(0), r.ts, r.r2, r.own, 0, "y2", "y1")
    sum_send(y2_tile(1), r.ts, r.r2, r.own, 1, "y2", "y1", hold=True)

    def finish_y2(m):
        sum_recv(r.r2, m, "y2", None if m else lambda: sum_start(r.ts, r.r2, 1, "y2"))

        def body(rows):
            total = r.y1[m, rows, mine].astype(f32) + summed(r.own, r.r2, m, rows)
            r.y2q[m, rows] = total.astype(bf16)

        each(T, body)
        r.y2s[m] = jnp.dot(r.perm[m], r.y2q[m], preferred_element_type=f32).astype(bf16)
        dispatch_send(r.y2s, r.xe, m, "y2d")

    finish_y2(0)
    dispatch_recv(r.xe, 0, "y2d")
    legs_send(r.xe, 0, "xe")
    finish_y2(1)
    legs_pass(r.xe, 0, "xe")
    dispatch_recv(r.xe, 1, "y2d")
    legs_send(r.xe, 1, "xe")
    load_in.wait()
    load_out.wait()

    def expert(m):
        gather_recv(r.dge, m, "dge")
        legs_recv(r.xe, m, "xe")
        gain, bias, centroid = r.evec[0:1, :], r.evec[1:2, :], r.evec[2:3, :]

        def body(rows):
            v = r.xe[m, rows].astype(f32)
            n, mean, rs = normed(v)
            alpha = jax.nn.sigmoid(jnp.sum(v * centroid, axis=1, keepdims=True))
            r.est[m, rows, 0:1] = mean
            r.est[m, rows, 1:2] = rs
            r.est[m, rows, 2:3] = alpha
            r.en[m, rows] = (n * gain + bias).astype(bf16)
            r.dfe[m, rows] = (alpha * r.dge[m, rows].astype(f32)).astype(bf16)

        each(R, body)

        @pl.loop(0, FQ // Q)
        def _(t):
            w = r.win[:, :, :, :, col(t)].reshape(D, Q)
            pre = jnp.dot(r.en[m], w, preferred_element_type=f32)
            value, slope = gelu_both(pre)
            r.ue[m, :, col(t)] = value.astype(bf16)
            r.slope[:, col(t)] = slope

        if m == 0:
            legs_pass(r.xe, 1, "xe")
        else:
            legs_sum_pass(r.dns, r.dnr, 0, "den")
        stats = [jnp.zeros((R, 1), f32) for _ in range(3)]

        def fe_tile(q):
            tile = jnp.dot(
                r.ue[m], r.wout[:, :, :, col(q)].reshape(FQ, Q), preferred_element_type=f32
            )
            stats[2] += jnp.sum(tile * r.dge[m, :, col(q)].astype(f32), axis=1, keepdims=True)
            return tile

        def den_tile(q):
            return nt(r.dhe[m], r.win[q].reshape(Q, FQ))

        @pl.loop(0, FQ // Q)
        def _(t):
            due = nt(r.dfe[m], r.wout[t].reshape(Q, D))
            r.dhe[m, :, col(t)] = (due * r.slope[:, col(t)]).astype(bf16)

        legs_sum_send(den_tile, r.dns, r.dnr, r.dno, m, "den")
        sum_send(fe_tile, r.fes, r.fer, r.feo, m, "fe", hold=True)
        for i, q in enumerate(quarters + (s,)):
            tile = r.dns[m, i].astype(f32) if i < S - 1 else r.dno[m]
            scaled = tile * r.evec[0:1, col(q)]
            n = (r.xe[m, :, col(q)].astype(f32) - r.est[m, :, 0:1]) * r.est[m, :, 1:2]
            stats[0] += jnp.sum(scaled, axis=1, keepdims=True)
            stats[1] += jnp.sum(scaled * n, axis=1, keepdims=True)
        r.ess[m] = to_rows(stats)
        for i in others:
            send(r.ess.at[m], r.esr.at[m, i - 1], ("est", m, i), to_sec(i))

    expert(0)
    expert(1)

    def finish_den(m):
        legs_sum_recv(r.dnr, m, "den")
        total = r.ess[m]
        for i in others:
            recv(r.esr.at[m, i - 1], ("est", m, i))
            total += r.esr[m, i - 1]
        r.est[m, :, 8:16] = to_columns(total)[:, 0:8]
        gain, centroid = r.evec[0:1, mine], r.evec[2:3, mine]
        if m == 0:
            r.evo[...] = jnp.zeros_like(r.evo)

        def body(rows):
            den = r.dno[m, rows] + r.dnr[m, 0, rows].astype(f32) + r.dnr[m, 1, rows].astype(f32)
            xq = r.xe[m, rows, mine].astype(f32)
            rs, alpha = r.est[m, rows, 1:2], r.est[m, rows, 2:3]
            n = (xq - r.est[m, rows, 0:1]) * rs
            m1, m2 = r.est[m, rows, 8:9] * (1.0 / D), r.est[m, rows, 9:10] * (1.0 / D)
            dlogit = r.est[m, rows, 10:11] * alpha * (1.0 - alpha)
            grad = rs * (gain * den - m1 - n * m2) + dlogit * centroid
            r.dxs[m, rows] = grad.astype(bf16)
            r.evo[0:1, :] += jnp.sum(den * n, axis=0, keepdims=True)
            r.evo[1:2, :] += jnp.sum(den, axis=0, keepdims=True)
            r.evo[2:3, :] += jnp.sum(dlogit * xq, axis=0, keepdims=True)

        each(R, body)
        return_send(r.dxs, r.dxr, m, "dxb")

    def finish_fe(m):
        sum_recv(r.fer, m, "fe")

        def body(rows):
            fe = summed(r.feo, r.fer, m, rows)
            r.ges[m, rows] = (r.est[m, rows, 2:3] * fe).astype(bf16)

        each(R, body)
        return_send(r.ges, r.ger, m, "geb")

    def finish_dxe(m):
        return_recv(r.dxr, m, "dxb")
        back = tn(r.perm[m], r.dxr[m])
        r.dy2[m, :, mine] = (r.cot[m, :, mine].astype(f32) + back).astype(bf16)
        gather_send(r.dy2, m, "dy2")

    finish_den(0)
    legs_sum_pass(r.dns, r.dnr, 1, "den")
    finish_dxe(0)
    finish_den(1)

    writes = []
    results = []

    def give(name):
        i = RESULTS.index(name)
        one = pltpu.make_async_copy(getattr(r, name), getattr(r, "to_" + name), r.lsem.at[4 + i])
        one.start()
        results.append(one)

    def expert_weights(left, right, out):
        for t in range(D // 256):
            slot = len(writes) % 2
            if len(writes) >= 2:
                writes[-2].wait()
            rows = slice(t * 256, (t + 1) * 256)
            lhs = left[:, :, rows].reshape(M * R, 256)
            r.stage[slot] = tn(lhs, right[...].reshape(M * R, D)).astype(bf16)
            writes.append(pltpu.make_async_copy(r.stage.at[slot], out.at[rows], r.lsem.at[2 + slot]))
            writes[-1].start()

    give("evo")

    finish_dxe(1)

    def token_stats(m, at, src):
        stats = [jnp.zeros((T, 1), f32) for _ in range(2)]
        mean, rs = r.tst[m, :, 2 * at : 2 * at + 1], r.tst[m, :, 2 * at + 1 : 2 * at + 2]
        for i in range(S):
            q = sec(i)
            tile = r.ts[m, i - 1].astype(f32) if i else r.own[m]
            scaled = tile * r.vecs[2 * at : 2 * at + 1, col(q)]
            n = (src[m, :, col(q)].astype(f32) - mean) * rs
            stats[0] += jnp.sum(scaled, axis=1, keepdims=True)
            stats[1] += jnp.sum(scaled * n, axis=1, keepdims=True)
        return stats

    def stats_send(m, at, stats):
        r.tss[at, m] = to_rows(stats)
        for i in others:
            send(r.tss.at[at, m], r.tsr.at[at, m, i - 1], ("tst", at, m, i), to_sec(i))

    def stats_recv(m, at):
        total = r.tss[at, m]
        for i in others:
            recv(r.tsr.at[at, m, i - 1], ("tst", at, m, i))
            total += r.tsr[at, m, i - 1]
        r.tst[m, :, 8:16] = to_columns(total)[:, 0:8]

    def dense_back(m):
        if m == 0:
            gather_recv(r.dy2, m, "dy2")

        @pl.loop(0, FQ // Q)
        def _(t):
            du = nt(r.dy2[m], r.wdn[t].reshape(Q, D))
            r.dh[m, :, col(t)] = (du * r.h[m, :, col(t)]).astype(bf16)

        sum_send(
            lambda q: nt(r.dh[m], r.wup[q].reshape(Q, FQ)),
            r.ts,
            r.r1,
            r.own,
            m,
            "da2",
            "y2",
            hold=m == 0,
        )
        stats_send(m, 1, token_stats(m, 1, r.y1))

    def norm_back(m, at, src, grad_in, own, arrive, emit):
        gain = r.vecs[2 * at : 2 * at + 1, mine]

        def body(rows):
            grad = summed(own, arrive, m, rows)
            mean, rs = r.tst[m, rows, 2 * at : 2 * at + 1], r.tst[m, rows, 2 * at + 1 : 2 * at + 2]
            n = (src[m, rows, mine].astype(f32) - mean) * rs
            m1, m2 = r.tst[m, rows, 8:9] * (1.0 / D), r.tst[m, rows, 9:10] * (1.0 / D)
            emit(rows, grad_in[m, rows, mine].astype(f32) + rs * (gain * grad - m1 - n * m2))
            r.vsum[2 * at : 2 * at + 1, :] += jnp.sum(grad * n, axis=0, keepdims=True)
            r.vsum[2 * at + 1 : 2 * at + 2, :] += jnp.sum(grad, axis=0, keepdims=True)

        each(T, body)

    def finish_da2(m):
        sum_recv(r.r1, m, "da2")
        stats_recv(m, 1)
        for i in others:
            sent(("y1g", m, i))

        def emit(rows, value):
            r.y1[m, rows, mine] = value.astype(bf16)

        norm_back(m, 1, r.y1, r.dy2, r.own, r.r1, emit)
        gather_send(r.y1, m, "dy1")

    blocks = (near_far, near, far, z)

    def grads_pair(g, b, k):
        for i, zz in enumerate(blocks):
            src = g.at[:, zz, 1 - c] if len(g.shape) == 5 else g.at[zz, 1 - c]
            dst = b.at[:, zz] if len(g.shape) == 5 else b.at[zz]
            send(src, dst, (k, "p", i), beside)

    def grads_add(g, zz, arrive):
        if len(g.shape) == 5:

            @pl.loop(0, S)
            def _(q):
                g[q, zz, c] = (g[q, zz, c].astype(f32) + arrive[q].astype(f32)).astype(bf16)
        else:
            g[zz, c] = (g[zz, c].astype(f32) + arrive[...].astype(f32)).astype(bf16)

    def grads_paired(g, b, k, i):
        zz = blocks[i]
        piece = b.at[:, zz] if len(g.shape) == 5 else b.at[zz]
        recv(piece, (k, "p", i))
        grads_add(g, zz, piece)

    def grads_near(g, b, arrive, k):
        grads_paired(g, b, k, 0)
        send(part(g, near_far, c), arrive.at[1], (k, "nf"), (s, near * 2 + c))
        grads_paired(g, b, k, 1)
        send(part(g, near, c), arrive.at[0], (k, "n"), (s, near * 2 + c))
        for i in range(2, nz):
            grads_paired(g, b, k, i)

    def grads_far(g, arrive, k):
        recv(arrive.at[1], (k, "nf"))
        grads_add(g, far, arrive.at[1])
        send(part(g, far, c), arrive.at[2], (k, "f"), (s, far * 2 + c))

    def grads_near_recv(arrive, k):
        recv(arrive.at[0], (k, "n"))
        recv(arrive.at[2], (k, "f"))
        return 0, 2

    def down_weights():
        for i, t in enumerate(blocks):
            lhs = r.u[:, :, col(t)].reshape(M * T, Q)
            grad = tn(lhs, r.dy2[...].reshape(M * T, D))
            r.wout[t] = grad.astype(bf16).reshape(2, shd, D)
            send(r.wout.at[t, 1 - c], r.bdn.at[t], ("gdn", "p", i), beside)

    def up_weights():
        @pl.loop(0, S)
        def _(t):
            lhs = r.a2[:, :, col(t)].reshape(M * T, Q)
            grad = tn(lhs, r.dh[...].reshape(M * T, FQ))
            r.win[t] = grad.astype(bf16).reshape(nz, 2, sh, FQ)

        grads_pair(r.win, r.bup, "gup")

    def qkv_weights():
        @pl.loop(0, S)
        def _(t):
            lhs = r.a1[:, :, col(t)].reshape(M * T, Q)
            grad = tn(lhs, r.dqkv[...].reshape(M * T, 3 * Q))
            r.gqk[t] = grad.astype(bf16).reshape(nz, 2, sh, 3 * Q)

        grads_pair(r.gqk, r.bqk, "gqk")

    def out_weights():
        grad = tn(r.o[...].reshape(M * T, Q), r.y1[...].reshape(M * T, D))
        r.gwo[...] = grad.astype(bf16).reshape(nz, 2, sh, D)
        grads_pair(r.gwo, r.bwo, "gwo")

    r.vsum[...] = jnp.zeros_like(r.vsum)
    dense_back(0)
    gather_recv(r.dy2, 1, "dy2", lambda: sum_start(r.ts, r.r1, 0, "da2"))
    down_weights()
    grads_near(r.wout, r.bdn, r.zdn, "gdn")
    dense_back(1)
    finish_da2(0)
    up_weights()
    grads_far(r.wout, r.zdn, "gdn")
    finish_da2(1)
    grads_near(r.win, r.bup, r.zup, "gup")

    def attend_back(m):
        if m == 0:
            gather_recv(r.y1, m, "dy1")
        out_grad = nt(r.y1[m], r.wo[...].reshape(Q, D)).astype(bf16)
        for hh in range(heads):
            at = hh * size
            q = r.qkv[m, :, at : at + size]
            k = r.qkv[m, :, Q + at : Q + at + size]
            v = r.qkv[m, :, 2 * Q + at : 2 * Q + at + size]
            go = out_grad[:, at : at + size]
            p = r.probs[m, hh]
            dp = nt(go, v)
            dv = tn(p.astype(bf16), go)
            ds = (p * (dp - jnp.sum(p * dp, axis=1, keepdims=True))).astype(bf16)
            dq = jnp.dot(ds, k, preferred_element_type=f32) * scale
            dk = tn(ds, q) * scale
            r.dqkv[m, :, at : at + size] = dq.astype(bf16)
            r.dqkv[m, :, Q + at : Q + at + size] = dk.astype(bf16)
            r.dqkv[m, :, 2 * Q + at : 2 * Q + at + size] = dv.astype(bf16)
        sum_send(
            lambda q: nt(r.dqkv[m], r.wqkv[q].reshape(Q, 3 * Q)),
            r.ts,
            r.r2,
            r.own,
            m,
            "da1",
            "da2",
            hold=True,
        )
        stats_send(m, 0, token_stats(m, 0, r.hidden))

    def finish_da1(m):
        sum_recv(r.r2, m, "da1")
        stats_recv(m, 0)

        def emit(rows, value):
            r.dx[m, rows] = value

        norm_back(m, 0, r.hidden, r.y1, r.own, r.r2, emit)

    attend_back(0)
    gather_recv(r.y1, 1, "dy1")
    sum_start(r.fes, r.fer, 0, "fe")
    sum_start(r.fes, r.fer, 1, "fe")
    attend_back(1)
    grads_far(r.win, r.zup, "gup")
    qkv_weights()
    grads_near(r.gqk, r.bqk, r.zqk, "gqk")
    out_weights()
    grads_near(r.gwo, r.bwo, r.zwo, "gwo")
    expert_weights(r.en, r.dhe, r.gin_out)
    finish_fe(0)
    sum_start(r.ts, r.r2, 0, "da1")
    sum_start(r.ts, r.r2, 1, "da1")
    grads_far(r.gqk, r.zqk, "gqk")
    grads_far(r.gwo, r.zwo, "gwo")
    finish_fe(1)
    expert_weights(r.ue, r.dfe, r.gout_out)

    def finish_out(m):
        return_recv(r.ger, m, "geb")
        back = tn(r.perm[m], r.ger[m])
        r.out[m] = (r.y2q[m].astype(f32) + back).astype(bf16)


    def row_result(g, arrive, out, k, rows, wait):
        slots = wait(arrive, k)
        mine_part = part(g, z, c)

        def body(at):
            total = mine_part[at].astype(f32)
            for slot in slots:
                total += arrive[slot, at].astype(f32)
            out[at] = total

        each(rows, body)

    def column_send(g, arrive, out, back, k, wait):
        slots = wait(arrive, k)

        @pl.loop(0, S)
        def _(q):
            total = g[q, z, c].astype(f32)
            for slot in slots:
                total += arrive[slot, q].astype(f32)
            out[q] = total.astype(bf16)

        for i in others:
            send(out.at[sec(i)], back.at[i - 1], (k, "s", i), to_sec(i))

    def column_result(sums, back, out, pieces, k):
        width = sums.shape[2] // pieces
        for i in range(S):
            if i:
                recv(back.at[i - 1], (k, "s", i))
            q = sec(S - i) if i else s
            value = (back[i - 1] if i else sums[s]).astype(f32)
            for piece in range(pieces):
                at = pl.ds(pl.multiple_of(piece * S * width + q * width, width), width)
                out[:, at] = value[:, piece * width : (piece + 1) * width]

    row_result(r.wout, r.zdn, r.gdn_out, "gdn", shd, grads_near_recv)
    give("gdn_out")
    column_send(r.win, r.zup, r.ups, r.upr, "gup", grads_near_recv)
    finish_da1(0)
    finish_da1(1)
    give("dx")
    for j in range(1, G):
        send(r.vsum, r.vsr.at[j - 1], ("vs", j), to_dp(j))
    column_send(r.gqk, r.zqk, r.qks, r.qkr, "gqk", grads_near_recv)
    row_result(r.gwo, r.zwo, r.gwo_out, "gwo", sh, grads_near_recv)
    give("gwo_out")
    column_result(r.ups, r.upr, r.gup_out, 1, "gup")
    give("gup_out")
    finish_out(0)
    finish_out(1)
    give("out")
    total = r.vsum[...]
    for j in range(1, G):
        recv(r.vsr.at[j - 1], ("vs", j))
        total += r.vsr[j - 1]
    shard = jnp.zeros((8, sh), f32)
    for j in range(G):
        shard += jnp.where(d == j, 1.0, 0.0) * total[:, j * sh : (j + 1) * sh]
    r.vgo[...] = jnp.zeros_like(r.vgo)
    r.vgo[:, 0:sh] = shard
    give("vgo")
    column_result(r.qks, r.qkr, r.gqk_out, 3, "gqk")
    give("gqk_out")

    def drain():
        for write in writes[-2:] + results:
            write.wait()
        for last in pending.values():
            last.wait_send()

    drain()
    assert len(places) == KEYS, len(places)


def hand_over(*refs):
    (out, dx, vgo, gqk, gwo, gup, gdn, evo, gin, gout) = refs[:10]
    results = refs[10:]
    results[8][...] = gin[...].astype(f32)
    results[9][...] = gout[...].astype(f32)

    @pl.when(pl.program_id(0) == 0)
    def _():
        for src, dst in zip((out, dx, gqk, gwo, gup, gdn), results[:2] + results[4:8]):
            dst[...] = src[...]
        for i, dst in enumerate(results[2:4] + results[10:12]):
            dst[...] = vgo[i : i + 1, 0 : dst.shape[1]]
        for i, dst in enumerate(results[12:]):
            dst[...] = evo[i : i + 1, :]


def with_kernel(
    hidden_in,
    cotangent,
    bucket_len,
    live_mask,
    routes,
    ln1_gain,
    ln1_bias,
    w_qkv,
    w_attn_out,
    ln2_gain,
    ln2_bias,
    w_up,
    w_down,
    expert_in,
    expert_out,
    expert_gain,
    expert_bias,
    centroids,
):
    S = lax.axis_size(SECTION)
    G = lax.axis_size(DP)
    M, T, D = hidden_in.shape
    Q = D // S
    FQ = w_up.shape[1] // S
    C = 3 * T // (2 * G)
    sh, shd = w_up.shape[0], w_down.shape[0]
    dims = (S, G, M, T, D, Q, FQ, C, sh, shd)
    scratch = layout(dims)
    names = INPUTS + OUTPUTS + list(scratch) + ["ssem", "rsem", "lsem"]
    vmem = pl.BlockSpec(memory_space=pltpu.VMEM)
    smem = pl.BlockSpec(memory_space=pltpu.SMEM)
    anywhere = pl.BlockSpec(memory_space=pl.ANY)
    shapes = (
        ((M, T, Q), bf16),
        ((M, T, Q), f32),
        ((8, 128), f32),
        ((sh, 3 * D), f32),
        ((sh, D), f32),
        ((sh, S * FQ), f32),
        ((shd, D), f32),
        ((8, Q), f32),
        ((D, FQ), bf16),
        ((FQ, D), bf16),
    )
    outs = pl.pallas_call(
        functools.partial(block_kernel, dims, names),
        name="block",
        out_shape=[jax.ShapeDtypeStruct(*shape) for shape in shapes],
        in_specs=[vmem, vmem, smem] + [vmem] * 13 + [anywhere] * 2,
        out_specs=[anywhere] * len(shapes),
        scratch_shapes=[pltpu.VMEM(*shape) for shape in scratch.values()]
        + [pltpu.SemaphoreType.DMA((KEYS,))] * 2
        + [pltpu.SemaphoreType.DMA((4 + len(RESULTS),))],
        compiler_params=pltpu.CompilerParams(
            collective_id=0, has_side_effects=True, vmem_limit_bytes=63 << 20
        ),
    )(
        hidden_in,
        cotangent,
        bucket_len,
        live_mask,
        jnp.swapaxes(routes, 1, 2),
        ln1_gain.reshape(1, sh),
        ln1_bias.reshape(1, sh),
        ln2_gain.reshape(1, sh),
        ln2_bias.reshape(1, sh),
        expert_gain,
        expert_bias,
        centroids,
        w_qkv,
        w_attn_out,
        w_up,
        w_down,
        expert_in.reshape(S, G // 2, 2, sh, FQ),
        expert_out.reshape(G // 2, 2, shd, D),
    )

    def spec(shape):
        if shape in ((D, FQ), (FQ, D)):
            return pl.BlockSpec((256, shape[1]), lambda i: (i, 0))
        return pl.BlockSpec(shape, lambda i, n=len(shape): (0,) * n)

    finals = (
        shapes[:2]
        + (((1, sh), f32),) * 2
        + shapes[3:7]
        + (((D, FQ), f32), ((FQ, D), f32))
        + (((1, sh), f32),) * 2
        + (((1, Q), f32),) * 3
    )
    outs = pl.pallas_call(
        hand_over,
        name="hand_over",
        grid=(D // 256,),
        out_shape=[jax.ShapeDtypeStruct(*shape) for shape in finals],
        in_specs=[spec(shape) for shape, _ in shapes],
        out_specs=[spec(shape) for shape, _ in finals],
        compiler_params=pltpu.CompilerParams(vmem_limit_bytes=63 << 20),
    )(*outs)
    out, dx, gain1, bias1, gqkv, gwo, gup, gdn, gin, gout, gain2, bias2, eg, eb, ec = outs
    return (
        out,
        dx,
        gain1.reshape(sh),
        bias1.reshape(sh),
        gqkv,
        gwo,
        gain2.reshape(sh),
        bias2.reshape(sh),
        gup,
        gdn,
        gin[None],
        gout[None],
        eg,
        eb,
        ec,
    )


def on_device(*args):
    groups = lax.axis_size(DP)
    rows, shard = args[0].shape[1], args[11].shape[0]
    capacity = 3 * rows // (2 * groups)
    if capacity % 16 or shard % 16 or groups != 8:
        return with_collectives(*args)
    return with_kernel(*args)


def solution(mesh):
    everywhere = (SECTION, DP)
    tokens = P(None, DP, None)
    outs = P(None, DP, SECTION)
    per_expert = P(DP, SECTION)
    return jax.shard_map(
        on_device,
        mesh=mesh,
        in_specs=(
            tokens,
            tokens,
            tokens,
            P(None, DP),
            tokens,
            P(everywhere),
            P(everywhere),
            P(everywhere, None),
            P(everywhere, None),
            P(everywhere),
            P(everywhere),
            P(everywhere, None),
            P(everywhere, None),
            P(DP, None, SECTION),
            P(DP, SECTION, None),
            per_expert,
            per_expert,
            per_expert,
        ),
        out_specs=(
            outs,
            outs,
            P(everywhere),
            P(everywhere),
            P(everywhere, None),
            P(everywhere, None),
            P(everywhere),
            P(everywhere),
            P(everywhere, None),
            P(everywhere, None),
            P(DP, None, SECTION),
            P(DP, SECTION, None),
            per_expert,
            per_expert,
            per_expert,
        ),
        check_vma=False,
    )
```

```python
import functools
import math
import types

import jax
import jax.numpy as jnp
from jax import lax
from jax.experimental import pallas as pl
from jax.experimental.pallas import tpu as pltpu
from jax.sharding import PartitionSpec as P

HEADS = 16
SECTION = "section"
DP = "dp"
epsilon = 1e-05
masked_value = -1e30
f32 = jnp.float32
bf16 = jnp.bfloat16


def norm_parts(values):
    center = values - jnp.mean(values, axis=-1, keepdims=True)
    spread = jnp.mean(center * center, axis=-1, keepdims=True)
    rs = lax.rsqrt(spread + epsilon)
    return center * rs, rs


def gelu_back(pre, grad):
    outputs, pullback = jax.vjp(jax.nn.gelu, pre)
    return pullback(grad)[0]


def dot(a, b):
    return jnp.dot(a, b, preferred_element_type=f32)


def dot_tn(a, b):
    return jnp.einsum("rd,re->de", a, b, preferred_element_type=f32)


def dot_nt(a, b):
    return jnp.einsum("re,de->rd", a, b, preferred_element_type=f32)


def sum_scatter(part):
    return lax.psum_scatter(
        part.astype(bf16), SECTION, scatter_dimension=part.ndim - 1, tiled=True
    ).astype(f32)


def gather_features(part):
    return lax.all_gather(part, SECTION, axis=part.ndim - 1, tiled=True)


def with_collectives(
    hidden_in,
    cotangent,
    bucket_len,
    live_mask,
    routes,
    ln1_gain,
    ln1_bias,
    w_qkv,
    w_attn_out,
    ln2_gain,
    ln2_bias,
    w_up,
    w_down,
    expert_in,
    expert_out,
    expert_gain,
    expert_bias,
    centroids,
):
    sections = lax.axis_size(SECTION)
    groups = lax.axis_size(DP)
    section = lax.axis_index(SECTION)
    micro, rows, width = hidden_in.shape
    quarter = width // sections
    heads = HEADS // sections
    size = width // HEADS
    ff = w_up.shape[1] // sections
    capacity = 3 * rows // (2 * groups)
    shard = w_up.shape[0]
    own_cols = section * quarter

    def mine(values):
        return lax.dynamic_slice_in_dim(values, own_cols, quarter, values.ndim - 1)

    def column_group(weight, pieces):
        cols = weight.shape[1] // (pieces * sections)
        parts = weight.reshape(shard, pieces, sections, cols).transpose(2, 0, 1, 3)
        parts = parts.reshape(sections, shard, pieces * cols)
        parts = lax.all_to_all(parts, SECTION, split_axis=0, concat_axis=0, tiled=True)
        full = lax.all_gather(parts, DP, axis=1, tiled=True)
        return full.reshape(width, pieces * cols)

    def column_group_back(grad, pieces):
        cols = grad.shape[1] // pieces
        parts = grad.astype(bf16).reshape(sections, groups * shard, pieces * cols)
        parts = lax.psum_scatter(parts, DP, scatter_dimension=1, tiled=True)
        parts = lax.all_to_all(parts, SECTION, split_axis=0, concat_axis=0, tiled=True)
        parts = parts.reshape(sections, shard, pieces, cols).transpose(1, 2, 0, 3)
        return parts.reshape(shard, pieces * sections * cols).astype(f32)

    def row_group_back(grad):
        return lax.psum_scatter(
            grad.astype(bf16), DP, scatter_dimension=0, tiled=True
        ).astype(f32)

    vectors = lax.all_gather(
        jnp.stack([ln1_gain, ln1_bias, ln2_gain, ln2_bias]), (SECTION, DP), axis=1, tiled=True
    ).astype(f32)
    gain_one, bias_one, gain_two, bias_two = vectors
    expert_vectors = lax.all_gather(
        jnp.concatenate([expert_gain, expert_bias, centroids]), SECTION, axis=1, tiled=True
    ).astype(f32)
    expert_g, expert_b, centroid = expert_vectors
    wqkv = column_group(w_qkv, 3)
    wo = lax.all_gather(w_attn_out, DP, axis=0, tiled=True)
    wup = column_group(w_up, 1)
    wdown = lax.all_gather(w_down, DP, axis=0, tiled=True)
    win = expert_in[0]
    wout = expert_out[0]

    ends = jnp.cumsum(bucket_len[:, 0, :], axis=-1)
    slot_ids = jnp.arange(rows, dtype=jnp.int32)
    segments = jnp.sum((slot_ids[None, :, None] >= ends[:, None, :]).astype(jnp.int32), axis=-1)
    same = segments[:, :, None] == segments[:, None, :]
    causal = slot_ids[None, None, :] <= slot_ids[None, :, None]
    opened = (live_mask[:, None, :] == 1) | (slot_ids[None, None, :] == slot_ids[None, :, None])
    allowed = (same & causal & opened)[:, None]
    chosen = routes[:, :, 0]
    picks = (chosen[:, :, None] == jnp.arange(groups, dtype=jnp.int32)).astype(jnp.int32)
    ranks = jnp.sum((jnp.cumsum(picks, axis=1) - picks) * picks, axis=2)
    places = chosen * capacity + ranks
    place_ids = jnp.arange(groups * capacity, dtype=jnp.int32)
    picked = (places[:, None, :] == place_ids[None, :, None]).astype(bf16)

    def dispatch(values):
        out = jnp.einsum("mpt,mtf->pmf", picked, values, preferred_element_type=f32).astype(bf16)
        out = out.reshape(groups, capacity * micro, quarter)
        return lax.all_to_all(out, DP, split_axis=0, concat_axis=0, tiled=True)

    def give_back(values):
        out = lax.all_to_all(values, DP, split_axis=0, concat_axis=0, tiled=True)
        out = out.reshape(groups * capacity, micro, quarter)
        return jnp.einsum("mpt,pmf->mtf", picked, out, preferred_element_type=f32)

    dge = gather_features(dispatch(mine(cotangent))).reshape(-1, width).astype(f32)

    x = hidden_in.reshape(micro * rows, width).astype(f32)
    n1, rs1 = norm_parts(x)
    a1 = (n1 * gain_one + bias_one).astype(bf16)
    qkv = dot(a1, wqkv).astype(bf16)
    q, k, v = (
        qkv[:, i * quarter : (i + 1) * quarter].reshape(micro, rows, heads, size) for i in range(3)
    )
    scale = size ** (-0.5)
    raw = jnp.einsum("mqhd,mkhd->mhqk", q, k, preferred_element_type=f32) * scale
    scores = jnp.where(allowed, raw, masked_value)
    weights = jnp.exp(scores - jnp.max(scores, axis=-1, keepdims=True))
    probs = weights / jnp.sum(weights, axis=-1, keepdims=True)
    probs_low = probs.astype(bf16)
    mixed = jnp.einsum("mhqk,mkhd->mqhd", probs_low, v, preferred_element_type=f32)
    o = mixed.reshape(micro * rows, quarter).astype(bf16)
    y1q = (mine(x) + sum_scatter(dot(o, wo))).astype(bf16)
    y1 = gather_features(y1q).astype(f32)
    n2, rs2 = norm_parts(y1)
    a2 = (n2 * gain_two + bias_two).astype(bf16)
    h = dot(a2, wup)
    u = jax.nn.gelu(h).astype(bf16)
    y2q = (y1q.astype(f32) + sum_scatter(dot(u, wdown))).astype(bf16)

    xe = gather_features(dispatch(y2q.reshape(micro, rows, quarter))).reshape(-1, width)
    xe = xe.astype(f32)
    ne, rse = norm_parts(xe)
    en = (ne * expert_g + expert_b).astype(bf16)
    he = dot(en, win)
    ue = jax.nn.gelu(he).astype(bf16)
    fe_part = dot(ue, wout)
    alpha = jax.nn.sigmoid(jnp.sum(xe * centroid, axis=-1, keepdims=True))
    fe = sum_scatter(fe_part)
    ge = (alpha * fe).astype(bf16).reshape(groups, capacity * micro, quarter)
    block_out = (
        y2q.reshape(micro, rows, quarter).astype(f32) + give_back(ge)
    ).astype(bf16)

    dfe = (alpha * dge).astype(bf16)
    due = dot_nt(dfe, wout)
    grad_out = dot_tn(ue, dfe)
    dhe = gelu_back(he, due).astype(bf16)
    grad_in = dot_tn(en, dhe)
    den_part = dot_nt(dhe, win)
    gden = den_part * expert_g
    stats = lax.psum(
        jnp.stack(
            [
                jnp.mean(gden, axis=-1),
                jnp.mean(gden * ne, axis=-1),
                jnp.sum(dge * fe_part, axis=-1),
            ]
        ),
        SECTION,
    )[..., None]
    den = sum_scatter(den_part)
    neq = mine(ne)
    dlogit = stats[2] * alpha * (1.0 - alpha)
    dxe_ln = rse * (mine(expert_g) * den - stats[0] - neq * stats[1])
    dxe = (dxe_ln + dlogit * mine(centroid)).astype(bf16)
    grad_expert_gain = jnp.sum(den * neq, axis=0)
    grad_expert_bias = jnp.sum(den, axis=0)
    grad_centroid = jnp.sum(dlogit * mine(xe), axis=0)
    back = give_back(dxe.reshape(groups, capacity * micro, quarter))
    dy2q = (mine(cotangent).astype(f32) + back).astype(bf16).reshape(micro * rows, quarter)

    dy2 = gather_features(dy2q)
    grad_down = dot_tn(u, dy2)
    dh = gelu_back(h, dot_nt(dy2, wdown)).astype(bf16)
    grad_up = dot_tn(a2, dh)
    da2_part = dot_nt(dh, wup)
    gda2 = da2_part * gain_two
    stats = lax.psum(
        jnp.stack([jnp.mean(gda2, axis=-1), jnp.mean(gda2 * n2, axis=-1)]), SECTION
    )[..., None]
    da2 = sum_scatter(da2_part)
    n2q = mine(n2)
    dy1q = dy2q.astype(f32) + rs2 * (mine(gain_two) * da2 - stats[0] - n2q * stats[1])
    dy1q = dy1q.astype(bf16)
    dy1 = gather_features(dy1q)
    grad_wo = dot_tn(o, dy1)
    do = dot_nt(dy1, wo).astype(bf16).reshape(micro, rows, heads, size)
    dp = jnp.einsum("mqhd,mkhd->mhqk", do, v, preferred_element_type=f32)
    dv = jnp.einsum("mhqk,mqhd->mkhd", probs_low, do, preferred_element_type=f32)
    delta = jnp.sum(probs * dp, axis=-1, keepdims=True)
    ds = (probs * (dp - delta)).astype(bf16)
    dq = jnp.einsum("mhqk,mkhd->mqhd", ds, k, preferred_element_type=f32) * scale
    dk = jnp.einsum("mhqk,mqhd->mkhd", ds, q, preferred_element_type=f32) * scale
    dqkv = jnp.concatenate(
        [part.reshape(micro * rows, quarter) for part in (dq, dk, dv)], axis=1
    ).astype(bf16)
    grad_qkv = dot_tn(a1, dqkv)
    da1_part = dot_nt(dqkv, wqkv)
    gda1 = da1_part * gain_one
    stats = lax.psum(
        jnp.stack([jnp.mean(gda1, axis=-1), jnp.mean(gda1 * n1, axis=-1)]), SECTION
    )[..., None]
    da1 = sum_scatter(da1_part)
    n1q = mine(n1)
    dx = dy1q.astype(f32) + rs1 * (mine(gain_one) * da1 - stats[0] - n1q * stats[1])

    vector_grads = lax.psum_scatter(
        jnp.stack(
            [
                jnp.sum(da1 * n1q, axis=0),
                jnp.sum(da1, axis=0),
                jnp.sum(da2 * n2q, axis=0),
                jnp.sum(da2, axis=0),
            ]
        ),
        DP,
        scatter_dimension=1,
        tiled=True,
    )
    return (
        block_out,
        dx.reshape(micro, rows, quarter),
        vector_grads[0],
        vector_grads[1],
        column_group_back(grad_qkv, 3),
        row_group_back(grad_wo),
        vector_grads[2],
        vector_grads[3],
        column_group_back(grad_up, 1),
        row_group_back(grad_down),
        grad_in[None],
        grad_out[None],
        grad_expert_gain[None],
        grad_expert_bias[None],
        grad_centroid[None],
    )


MESH = pl.DeviceIdType.MESH
KEYS = 101
CHAIN = {
    "y1": 0,
    "y1g": 1,
    "y2": 0,
    "xe": 1,
    "den": 0,
    "dy2": 1,
    "da2": 0,
    "dy1": 1,
    "da1": 0,
}
SHARED = {
    "geb": "y2d",
    "dxb": "cot",
    "fe": "dge",
    "est": "stats",
    "tst": "stats",
    "vs": "v2",
    "gdn": "wdn",
    "gup": "wup",
    "gwo": "wo",
    "gqk": "wqkv",
    "p": "c",
    "n": "near",
    "nf": "near far",
    "f": "far",
}


LEGS = {
    "xe": ("x", "y", "xy", "yx"),
    "den": ("x0", "x2", "y1", "y2", "xy", "yx"),
}


def semaphore_of(k):
    if k[0] in LEGS:
        leg = LEGS[k[0]].index(k[2])
        return ("chain", CHAIN[k[0]], k[1], leg + 1) if leg < 3 else ("leg", k[0], k[1], leg)
    if k[0] in CHAIN:
        return ("chain", CHAIN[k[0]]) + k[1:]
    if k[0] == "q1":
        return ("stats", k[1], k[2]) if k[1] < 2 else ("chain", 1, 0, k[2])
    if k[0] == "v1":
        return "chain", 1, 1, k[1]
    if k[1] == "s":
        return "u1" if k[0] == "gup" else "e1", k[2]
    if k[0] == "tst":
        return ("stats",) + k[2:]
    return tuple(SHARED.get(part, part) for part in k)
CHUNK = 128


def tn(a, b):
    return lax.dot_general(a, b, (((0,), (0,)), ((), ())), preferred_element_type=f32)


def nt(a, b):
    return lax.dot_general(a, b, (((1,), (1,)), ((), ())), preferred_element_type=f32)


def tanh_parts(v):
    root = 0.7978845608028654
    t = jnp.tanh(root * (v + 0.044715 * (v * v * v)))
    return t, root


def gelu_both(v):
    t, root = tanh_parts(v)
    half = 0.5 * (1.0 + t)
    return v * half, half + 0.5 * v * (1.0 - t * t) * root * (1.0 + 0.134145 * (v * v))


def to_rows(columns):
    lane = lax.broadcasted_iota(jnp.int32, (columns[0].shape[0], 128), 1)
    wide = jnp.zeros(lane.shape, f32)
    for i, column in enumerate(columns):
        wide = jnp.where(lane == i, column, wide)
    return wide.T[:8]


def to_columns(rows):
    return jnp.concatenate([rows, jnp.zeros((120, rows.shape[1]), f32)], axis=0).T


def layout(dims):
    S, G, M, T, D, Q, FQ, C, sh, shd = dims
    nz = G // 2
    R = G * C
    heads = HEADS // S
    return dict(
        wqkv=((S, nz, 2, sh, 3 * Q), bf16),
        wo=((nz, 2, sh, D), bf16),
        wup=((S, nz, 2, sh, FQ), bf16),
        wdn=((nz, 2, shd, D), bf16),
        win=((S, nz, 2, sh, FQ), bf16),
        wout=((nz, 2, shd, D), bf16),
        vin=((8, 128), f32),
        ein=((8, Q), f32),
        vg=((S, G, 8, 128), f32),
        vecs=((8, D), f32),
        evec=((8, D), f32),
        mask=((M, T, T), f32),
        perm=((M, R, T), bf16),
        cots=((M, R, Q), bf16),
        y2s=((M, R, Q), bf16),
        ges=((M, R, Q), bf16),
        dxs=((M, R, Q), bf16),
        ger=((M, R, Q), bf16),
        dxr=((M, R, Q), bf16),
        tst=((M, T, 128), f32),
        est=((M, R, 128), f32),
        a1=((M, T, D), bf16),
        a2=((M, T, D), bf16),
        qkv=((M, T, 3 * Q), bf16),
        probs=((M, heads, T, T), f32),
        o=((M, T, Q), bf16),
        y1=((M, T, D), bf16),
        h=((M, T, FQ), f32),
        u=((M, T, FQ), bf16),
        y2q=((M, T, Q), bf16),
        xe=((M, R, D), bf16),
        dge=((M, R, D), bf16),
        en=((M, R, D), bf16),
        ue=((M, R, FQ), bf16),
        dhe=((M, R, FQ), bf16),
        dfe=((M, R, D), bf16),
        slope=((R, FQ), f32),
        fes=((M, S - 1, R, Q), bf16),
        fer=((M, S - 1, R, Q), bf16),
        feo=((M, R, Q), f32),
        dns=((M, S - 1, R, Q), bf16),
        dnr=((M, S - 1, R, Q), bf16),
        dno=((M, R, Q), f32),
        ess=((M, 8, R), f32),
        esr=((M, S - 1, 8, R), f32),
        ts=((M, S - 1, T, Q), bf16),
        r1=((M, S - 1, T, Q), bf16),
        r2=((M, S - 1, T, Q), bf16),
        own=((M, T, Q), f32),
        tss=((2, M, 8, T), f32),
        tsr=((2, M, S - 1, 8, T), f32),
        dy2=((M, T, D), bf16),
        dh=((M, T, FQ), bf16),
        dqkv=((M, T, 3 * Q), bf16),
        gwo=((nz, 2, sh, D), bf16),
        gqk=((S, nz, 2, sh, 3 * Q), bf16),
        bdn=((nz, shd, D), bf16),
        bup=((S, nz, sh, FQ), bf16),
        bwo=((nz, sh, D), bf16),
        bqk=((S, nz, sh, 3 * Q), bf16),
        zdn=((nz - 1, shd, D), bf16),
        zup=((nz - 1, S, sh, FQ), bf16),
        zwo=((nz - 1, sh, D), bf16),
        zqk=((nz - 1, S, sh, 3 * Q), bf16),
        ups=((S, sh, FQ), bf16),
        upr=((S - 1, sh, FQ), bf16),
        qks=((S, sh, 3 * Q), bf16),
        qkr=((S - 1, sh, 3 * Q), bf16),
        stage=((2, 256, D), bf16),
        out=((M, T, Q), bf16),
        dx=((M, T, Q), f32),
        vgo=((8, 128), f32),
        gqk_out=((sh, 3 * D), f32),
        gwo_out=((sh, D), f32),
        gup_out=((sh, S * FQ), f32),
        gdn_out=((shd, D), f32),
        evo=((8, Q), f32),
        vsum=((8, Q), f32),
        vsr=((G - 1, 8, Q), f32),
    )


INPUTS = [
    "hidden",
    "cot",
    "bucket",
    "live",
    "routes",
    "gain_one",
    "bias_one",
    "gain_two",
    "bias_two",
    "gain_e",
    "bias_e",
    "centroid",
    "wqkv_in",
    "wo_in",
    "wup_in",
    "wdn_in",
    "win_in",
    "wout_in",
]
RESULTS = [
    "out",
    "dx",
    "vgo",
    "gqk_out",
    "gwo_out",
    "gup_out",
    "gdn_out",
    "evo",
]
OUTPUTS = ["to_" + name for name in RESULTS] + ["gin_out", "gout_out"]


def block_kernel(dims, names, *args):
    r = types.SimpleNamespace(**dict(zip(names, args)))
    S, G, M, T, D, Q, FQ, C, sh, shd = dims
    nz = G // 2
    R = G * C
    heads = HEADS // S
    size = D // HEADS
    scale = size ** (-0.5)
    s = lax.axis_index(SECTION)
    d = lax.axis_index(DP)
    z = lax.div(d, 2)
    c = lax.rem(d, 2)
    beside = (s, d + 1 - 2 * c)
    near = z + 1 - 2 * lax.rem(z, 2)
    far = lax.rem(z + 2, nz)
    near_far = lax.rem(near + 2, nz)
    beside_x = s + 1 - 2 * lax.rem(s, 2)
    beside_y = lax.rem(s + 2, S)
    across = lax.rem(beside_x + 2, S)

    def sec(i):
        return lax.rem(s + i, S)

    def dpi(j):
        return lax.rem(d + j, G)

    def zi(j):
        return lax.rem(z + j, nz)

    def to_sec(i):
        return (sec(i), d)

    def to_dp(j):
        return (s, dpi(j))

    def to_z(j):
        return (s, zi(j) * 2 + c)

    def col(q, n=Q):
        return pl.ds(pl.multiple_of(q * n, n), n)

    def seats(e):
        return pl.ds(pl.multiple_of(e * C, C), C)

    mine = col(s)
    places = {}
    pending = {}

    def copy(src, dst, k, device):
        i = places.setdefault(semaphore_of(k), len(places))
        return pltpu.make_async_remote_copy(
            src_ref=src,
            dst_ref=dst,
            send_sem=r.ssem.at[i],
            recv_sem=r.rsem.at[i],
            device_id=device,
            device_id_type=MESH,
        )

    def send(src, dst, k, device):
        sent(k)
        pending[semaphore_of(k)] = copy(src, dst, k, device)
        pending[semaphore_of(k)].start()

    def sent(k):
        last = pending.pop(semaphore_of(k), None)
        if last is not None:
            last.wait_send()

    def recv(dst, k):
        copy(dst, dst, k, beside).wait_recv()

    def each(rows, body):
        step = math.gcd(rows, CHUNK)

        @pl.loop(0, rows // step)
        def _(i):
            body(pl.ds(pl.multiple_of(i * step, step), step))

    others = range(1, S)

    def gather_send(ref, m, k):
        for i in others:
            send(ref.at[m, :, mine], ref.at[m, :, mine], (k, m, i), to_sec(i))

    def gather_recv(ref, m, k, then=None):
        for i in others:
            recv(ref.at[m, :, col(sec(S - i))], (k, m, i))
            if then is not None and i == S - 2:
                then()

    def sum_send(tile, out, arrive, own, m, k, before=None, hold=False):
        for i in others:
            if before is not None:
                sent((before, m, i))
            out[m, i - 1] = tile(sec(i)).astype(bf16)
        own[m] = tile(s)
        if not hold:
            sum_start(out, arrive, m, k)

    def sum_start(out, arrive, m, k):
        for i in others:
            send(out.at[m, i - 1], arrive.at[m, i - 1], (k, m, i), to_sec(i))

    def sum_recv(arrive, m, k, then=None):
        for i in others:
            recv(arrive.at[m, i - 1], (k, m, i))
            if then is not None and i == S - 2:
                then()

    def summed(own, arrive, m, rows):
        total = own[m, rows]
        for i in others:
            total += arrive[m, i - 1, rows].astype(f32)
        return total

    top, low = slice(0, R // 2), slice(R // 2, R)

    def legs_send(ref, m, k):
        send(ref.at[m, :, mine], ref.at[m, :, mine], (k, m, "x"), (beside_x, d))
        send(ref.at[m, :, mine], ref.at[m, :, mine], (k, m, "y"), (beside_y, d))

    def legs_pass(ref, m, k):
        recv(ref.at[m, :, col(beside_x)], (k, m, "x"))
        block = ref.at[m, top, col(beside_x)]
        send(block, block, (k, m, "xy"), (beside_y, d))
        recv(ref.at[m, :, col(beside_y)], (k, m, "y"))
        block = ref.at[m, low, col(beside_y)]
        send(block, block, (k, m, "yx"), (beside_x, d))

    def legs_recv(ref, m, k):
        recv(ref.at[m, top, col(across)], (k, m, "xy"))
        recv(ref.at[m, low, col(across)], (k, m, "yx"))

    quarters = (beside_x, beside_y, across)

    def legs_sum_send(tile, out, arrive, own, m, k):
        for i, q in enumerate(quarters):
            out[m, i] = tile(q).astype(bf16)
        own[m] = tile(s)
        for i in (2, 0):
            send(out.at[m, i, top], arrive.at[m, i, top], (k, m, "x" + str(i)), (beside_x, d))
        for i in (2, 1):
            send(out.at[m, i, low], arrive.at[m, i, low], (k, m, "y" + str(i)), (beside_y, d))

    def legs_sum_pass(out, arrive, m, k):
        recv(arrive.at[m, 2, top], (k, m, "x2"))
        both = out[m, 1, top].astype(f32) + arrive[m, 2, top].astype(f32)
        out[m, 1, top] = both.astype(bf16)
        send(out.at[m, 1, top], arrive.at[m, 1, top], (k, m, "xy"), (beside_y, d))
        recv(arrive.at[m, 2, low], (k, m, "y2"))
        both = out[m, 0, low].astype(f32) + arrive[m, 2, low].astype(f32)
        out[m, 0, low] = both.astype(bf16)
        send(out.at[m, 0, low], arrive.at[m, 0, low], (k, m, "yx"), (beside_x, d))

    def legs_sum_recv(arrive, m, k):
        recv(arrive.at[m, 0, top], (k, m, "x0"))
        recv(arrive.at[m, 1, low], (k, m, "y1"))
        recv(arrive.at[m, 1, top], (k, m, "xy"))
        recv(arrive.at[m, 0, low], (k, m, "yx"))

    def dispatch_send(src, dst, m, k):
        dst[m, seats(d), mine] = src[m, seats(d)]
        for j in range(1, G):
            send(src.at[m, seats(dpi(j))], dst.at[m, seats(d), mine], (k, m, j), to_dp(j))

    def dispatch_recv(dst, m, k):
        for j in range(1, G):
            recv(dst.at[m, seats(dpi(G - j)), mine], (k, m, j))

    def return_send(src, dst, m, k):
        dst[m, seats(d)] = src[m, seats(d)]
        for j in range(1, G):
            send(src.at[m, seats(dpi(j))], dst.at[m, seats(d)], (k, m, j), to_dp(j))

    def return_recv(dst, m, k):
        for j in range(1, G):
            recv(dst.at[m, seats(dpi(G - j))], (k, m, j))

    def part(ref, zz, cc):
        return ref.at[:, zz, cc] if len(ref.shape) == 5 else ref.at[zz, cc]

    def weight_start(ref, k):
        send(part(ref, z, c), part(ref, z, c), (k, "far"), (s, far * 2 + c))
        send(part(ref, z, c), part(ref, z, c), (k, "c", 0), beside)

    def weight_next(ref, k):
        send(part(ref, z, c), part(ref, z, c), (k, "near"), (s, near * 2 + c))

    def weight_far(ref, k):
        recv(part(ref, far, c), (k, "far"))
        send(part(ref, far, c), part(ref, far, c), (k, "near far"), (s, near * 2 + c))
        send(part(ref, far, c), part(ref, far, c), (k, "c", 1), beside)

    def weight_near(ref, k):
        recv(part(ref, near, c), (k, "near"))
        send(part(ref, near, c), part(ref, near, c), (k, "c", 2), beside)
        recv(part(ref, near_far, c), (k, "near far"))
        send(part(ref, near_far, c), part(ref, near_far, c), (k, "c", 3), beside)

    def weight_wait(ref, k):
        for i, zz in enumerate((z, far, near, near_far)):
            recv(part(ref, zz, 1 - c), (k, "c", i))

    load_in = pltpu.make_async_copy(r.win_in, r.win, r.lsem.at[0])
    load_out = pltpu.make_async_copy(r.wout_in, r.wout, r.lsem.at[1])

    early = lax.broadcasted_iota(jnp.int32, (T, T), 0)
    late = lax.broadcasted_iota(jnp.int32, (T, T), 1)

    def seat_tokens(m):
        route = r.routes[m]
        expert_ids = lax.broadcasted_iota(jnp.int32, (G, T), 0)
        picks = jnp.where(expert_ids == route, 1.0, 0.0)
        before = jnp.where(early < late, 1.0, 0.0).astype(bf16)
        counts = jnp.dot(picks.astype(bf16), before, preferred_element_type=f32)
        rank = jnp.sum(counts * picks, axis=0, keepdims=True)
        place = route.astype(f32) * float(C) + rank
        seat_ids = lax.broadcasted_iota(jnp.int32, (R, T), 0).astype(f32)
        r.perm[m] = jnp.where(seat_ids == place, 1.0, 0.0).astype(bf16)
        r.cots[m] = jnp.dot(r.perm[m], r.cot[m, :, mine], preferred_element_type=f32).astype(bf16)

    def entry():
        barrier = pltpu.get_barrier_semaphore()
        for i in others:
            pl.semaphore_signal(barrier, inc=1, device_id=to_sec(i), device_id_type=MESH)
        for j in range(1, G):
            pl.semaphore_signal(barrier, inc=1, device_id=to_dp(j), device_id_type=MESH)
        r.vin[...] = jnp.zeros_like(r.vin)
        for i, ref in enumerate((r.gain_one, r.bias_one, r.gain_two, r.bias_two)):
            r.vin[i : i + 1, 0:sh] = ref[...].astype(f32)
        r.ein[...] = jnp.zeros_like(r.ein)
        for i, ref in enumerate((r.gain_e, r.bias_e, r.centroid)):
            r.ein[i : i + 1, :] = ref[...].astype(f32)
        r.vg[s, d] = r.vin[...]
        r.evec[:, mine] = r.ein[...]
        for piece in range(3):
            r.wqkv[s, z, c, :, piece * Q : (piece + 1) * Q] = r.wqkv_in[
                :, pl.ds(pl.multiple_of(piece * D + s * Q, Q), Q)
            ]
        r.wo[z, c] = r.wo_in[...]
        seat_tokens(0)
        seat_tokens(1)
        pl.semaphore_wait(barrier, S + G - 2)
        for i in others:
            send(r.vin, r.vg.at[s, d], ("v1", i), to_sec(i))
        for i in others:
            for piece in range(3):
                src = r.wqkv_in.at[:, pl.ds(pl.multiple_of(piece * D + sec(i) * Q, Q), Q)]
                dst = r.wqkv.at[s, z, c, :, piece * Q : (piece + 1) * Q]
                send(src, dst, ("q1", piece, i), to_sec(i))
        dispatch_send(r.cots, r.dge, 0, "cot")
        for i in others:
            recv(r.vg.at[sec(S - i), d], ("v1", i))
        for j in range(1, G):
            send(r.vg.at[:, d], r.vg.at[:, d], ("v2", j), to_dp(j))
        for i in others:
            for piece in range(3):
                recv(r.wqkv.at[sec(S - i), z, c, :, piece * Q : (piece + 1) * Q], ("q1", piece, i))
        weight_start(r.wqkv, "wqkv")
        weight_next(r.wqkv, "wqkv")
        dispatch_send(r.cots, r.dge, 1, "cot")
        for i in others:
            send(r.wup_in.at[:, col(sec(i), FQ)], r.wup.at[s, z, c], ("u1", i), to_sec(i))
            send(r.ein, r.evec.at[:, mine], ("e1", i), to_sec(i))
        load_in.start()
        load_out.start()

    def mask_tokens(m):
        end = r.bucket[m, 0, 0]
        seg_q = (early >= end).astype(jnp.int32)
        seg_k = (late >= end).astype(jnp.int32)
        for b in range(1, r.bucket.shape[2]):
            end = end + r.bucket[m, 0, b]
            seg_q += (early >= end).astype(jnp.int32)
            seg_k += (late >= end).astype(jnp.int32)
        live = jnp.broadcast_to(r.live[m : m + 1, :], (T, T))
        allowed = (seg_q == seg_k) & (late <= early) & ((live == 1) | (late == early))
        r.mask[m] = jnp.where(allowed, 1.0, 0.0)

    def spread_vectors():
        for j in range(1, G):
            recv(r.vg.at[:, dpi(G - j)], ("v2", j))
        spread_row = lax.broadcasted_iota(jnp.int32, (128, D), 0)
        spread_lane = lax.broadcasted_iota(jnp.int32, (128, D), 1)
        spread = jnp.where(lax.rem(spread_lane, sh) == spread_row, 1.0, 0.0).astype(bf16)
        stacked = r.vg[...].reshape(S * G * 8, 128).astype(bf16)
        wide = jnp.dot(stacked, spread, preferred_element_type=f32)
        row_id = lax.broadcasted_iota(jnp.int32, (S * G * 8, D), 0)
        lane_id = lax.broadcasted_iota(jnp.int32, (S * G * 8, D), 1)
        low = lax.shift_right_logical(row_id, 3) * sh
        wide = jnp.where((lane_id >= low) & (lane_id < low + sh), wide, 0.0)
        r.vecs[...] = jnp.sum(wide.reshape(S * G, 8, D), axis=0)

    def normed(values):
        mean = jnp.mean(values, axis=1, keepdims=True)
        center = values - mean
        rs = lax.rsqrt(jnp.mean(center * center, axis=1, keepdims=True) + epsilon)
        return center * rs, mean, rs

    def norm_tokens(src, dst, m, at):
        gain = r.vecs[2 * at : 2 * at + 1, :]
        bias = r.vecs[2 * at + 1 : 2 * at + 2, :]

        def body(rows):
            n, mean, rs = normed(src[m, rows].astype(f32))
            r.tst[m, rows, 2 * at : 2 * at + 1] = mean
            r.tst[m, rows, 2 * at + 1 : 2 * at + 2] = rs
            dst[m, rows] = (n * gain + bias).astype(bf16)

        each(T, body)

    entry()
    r.wup[s, z, c] = r.wup_in[:, col(s, FQ)]
    r.wdn[z, c] = r.wdn_in[...]
    mask_tokens(0)
    mask_tokens(1)
    for m in range(M):
        dispatch_recv(r.dge, m, "cot")
        gather_send(r.dge, m, "dge")
    weight_far(r.wqkv, "wqkv")
    weight_start(r.wo, "wo")
    weight_next(r.wo, "wo")
    for i in others:
        recv(r.evec.at[:, col(sec(S - i))], ("e1", i))
        recv(r.wup.at[sec(S - i), z, c], ("u1", i))
    weight_start(r.wup, "wup")
    spread_vectors()
    norm_tokens(r.hidden, r.a1, 0, 0)
    norm_tokens(r.hidden, r.a1, 1, 0)
    weight_near(r.wqkv, "wqkv")
    weight_far(r.wo, "wo")
    weight_next(r.wup, "wup")
    weight_wait(r.wqkv, "wqkv")

    def attend(m):
        @pl.loop(0, 3)
        def _(t):
            w = r.wqkv[:, :, :, :, col(t)].reshape(D, Q)
            r.qkv[m, :, col(t)] = jnp.dot(r.a1[m], w, preferred_element_type=f32).astype(bf16)

        for hh in range(heads):
            at = hh * size
            q = r.qkv[m, :, at : at + size]
            k = r.qkv[m, :, Q + at : Q + at + size]
            v = r.qkv[m, :, 2 * Q + at : 2 * Q + at + size]
            scores = jnp.where(r.mask[m] > 0.0, nt(q, k) * scale, masked_value)
            weights = jnp.exp(scores - jnp.max(scores, axis=1, keepdims=True))
            p = weights / jnp.sum(weights, axis=1, keepdims=True)
            r.probs[m, hh] = p
            mixed = jnp.dot(p.astype(bf16), v, preferred_element_type=f32)
            r.o[m, :, at : at + size] = mixed.astype(bf16)

    def y1_tile(m):
        return lambda q: jnp.dot(
            r.o[m], r.wo[:, :, :, col(q)].reshape(Q, Q), preferred_element_type=f32
        )

    def finish_y1(m):
        sum_recv(r.r1, m, "y1")

        def body(rows):
            total = r.hidden[m, rows, mine].astype(f32) + summed(r.own, r.r1, m, rows)
            r.y1[m, rows, mine] = total.astype(bf16)

        each(T, body)
        gather_send(r.y1, m, "y1g")

    attend(0)
    weight_near(r.wo, "wo")
    weight_wait(r.wo, "wo")
    sum_send(y1_tile(0), r.ts, r.r1, r.own, 0, "y1")
    attend(1)
    sum_send(y1_tile(1), r.ts, r.r1, r.own, 1, "y1")
    weight_far(r.wup, "wup")
    weight_start(r.wdn, "wdn")
    weight_next(r.wdn, "wdn")
    finish_y1(0)
    finish_y1(1)
    weight_near(r.wup, "wup")
    weight_wait(r.wup, "wup")

    def up(m):
        gather_recv(r.y1, m, "y1g")
        norm_tokens(r.y1, r.a2, m, 1)

        @pl.loop(0, FQ // Q)
        def _(t):
            w = r.wup[:, :, :, :, col(t)].reshape(D, Q)
            pre = jnp.dot(r.a2[m], w, preferred_element_type=f32)
            value, slope = gelu_both(pre)
            r.u[m, :, col(t)] = value.astype(bf16)
            r.h[m, :, col(t)] = slope

    def y2_tile(m):
        return lambda q: jnp.dot(
            r.u[m], r.wdn[:, :, :, col(q)].reshape(FQ, Q), preferred_element_type=f32
        )

    weight_far(r.wdn, "wdn")
    up(0)
    up(1)
    weight_near(r.wdn, "wdn")
    weight_wait(r.wdn, "wdn")
    sum_send(y2_tile(0), r.ts, r.r2, r.own, 0, "y2", "y1")
    sum_send(y2_tile(1), r.ts, r.r2, r.own, 1, "y2", "y1", hold=True)

    def finish_y2(m):
        sum_recv(r.r2, m, "y2", None if m else lambda: sum_start(r.ts, r.r2, 1, "y2"))

        def body(rows):
            total = r.y1[m, rows, mine].astype(f32) + summed(r.own, r.r2, m, rows)
            r.y2q[m, rows] = total.astype(bf16)

        each(T, body)
        r.y2s[m] = jnp.dot(r.perm[m], r.y2q[m], preferred_element_type=f32).astype(bf16)
        dispatch_send(r.y2s, r.xe, m, "y2d")

    finish_y2(0)
    dispatch_recv(r.xe, 0, "y2d")
    legs_send(r.xe, 0, "xe")
    finish_y2(1)
    legs_pass(r.xe, 0, "xe")
    dispatch_recv(r.xe, 1, "y2d")
    legs_send(r.xe, 1, "xe")
    load_in.wait()
    load_out.wait()

    def expert(m):
        gather_recv(r.dge, m, "dge")
        legs_recv(r.xe, m, "xe")
        gain, bias, centroid = r.evec[0:1, :], r.evec[1:2, :], r.evec[2:3, :]

        def body(rows):
            v = r.xe[m, rows].astype(f32)
            n, mean, rs = normed(v)
            alpha = jax.nn.sigmoid(jnp.sum(v * centroid, axis=1, keepdims=True))
            r.est[m, rows, 0:1] = mean
            r.est[m, rows, 1:2] = rs
            r.est[m, rows, 2:3] = alpha
            r.en[m, rows] = (n * gain + bias).astype(bf16)
            r.dfe[m, rows] = (alpha * r.dge[m, rows].astype(f32)).astype(bf16)

        each(R, body)

        @pl.loop(0, FQ // Q)
        def _(t):
            w = r.win[:, :, :, :, col(t)].reshape(D, Q)
            pre = jnp.dot(r.en[m], w, preferred_element_type=f32)
            value, slope = gelu_both(pre)
            r.ue[m, :, col(t)] = value.astype(bf16)
            r.slope[:, col(t)] = slope

        if m == 0:
            legs_pass(r.xe, 1, "xe")
        else:
            legs_sum_pass(r.dns, r.dnr, 0, "den")
        stats = [jnp.zeros((R, 1), f32) for _ in range(3)]

        def fe_tile(q):
            tile = jnp.dot(
                r.ue[m], r.wout[:, :, :, col(q)].reshape(FQ, Q), preferred_element_type=f32
            )
            stats[2] += jnp.sum(tile * r.dge[m, :, col(q)].astype(f32), axis=1, keepdims=True)
            return tile

        def den_tile(q):
            return nt(r.dhe[m], r.win[q].reshape(Q, FQ))

        @pl.loop(0, FQ // Q)
        def _(t):
            due = nt(r.dfe[m], r.wout[t].reshape(Q, D))
            r.dhe[m, :, col(t)] = (due * r.slope[:, col(t)]).astype(bf16)

        legs_sum_send(den_tile, r.dns, r.dnr, r.dno, m, "den")
        sum_send(fe_tile, r.fes, r.fer, r.feo, m, "fe", hold=True)
        for i, q in enumerate(quarters + (s,)):
            tile = r.dns[m, i].astype(f32) if i < S - 1 else r.dno[m]
            scaled = tile * r.evec[0:1, col(q)]
            n = (r.xe[m, :, col(q)].astype(f32) - r.est[m, :, 0:1]) * r.est[m, :, 1:2]
            stats[0] += jnp.sum(scaled, axis=1, keepdims=True)
            stats[1] += jnp.sum(scaled * n, axis=1, keepdims=True)
        r.ess[m] = to_rows(stats)
        for i in others:
            send(r.ess.at[m], r.esr.at[m, i - 1], ("est", m, i), to_sec(i))

    expert(0)
    expert(1)

    def finish_den(m):
        legs_sum_recv(r.dnr, m, "den")
        total = r.ess[m]
        for i in others:
            recv(r.esr.at[m, i - 1], ("est", m, i))
            total += r.esr[m, i - 1]
        r.est[m, :, 8:16] = to_columns(total)[:, 0:8]
        gain, centroid = r.evec[0:1, mine], r.evec[2:3, mine]
        if m == 0:
            r.evo[...] = jnp.zeros_like(r.evo)

        def body(rows):
            den = r.dno[m, rows] + r.dnr[m, 0, rows].astype(f32) + r.dnr[m, 1, rows].astype(f32)
            xq = r.xe[m, rows, mine].astype(f32)
            rs, alpha = r.est[m, rows, 1:2], r.est[m, rows, 2:3]
            n = (xq - r.est[m, rows, 0:1]) * rs
            m1, m2 = r.est[m, rows, 8:9] * (1.0 / D), r.est[m, rows, 9:10] * (1.0 / D)
            dlogit = r.est[m, rows, 10:11] * alpha * (1.0 - alpha)
            grad = rs * (gain * den - m1 - n * m2) + dlogit * centroid
            r.dxs[m, rows] = grad.astype(bf16)
            r.evo[0:1, :] += jnp.sum(den * n, axis=0, keepdims=True)
            r.evo[1:2, :] += jnp.sum(den, axis=0, keepdims=True)
            r.evo[2:3, :] += jnp.sum(dlogit * xq, axis=0, keepdims=True)

        each(R, body)
        return_send(r.dxs, r.dxr, m, "dxb")

    def finish_fe(m):
        sum_recv(r.fer, m, "fe")

        def body(rows):
            fe = summed(r.feo, r.fer, m, rows)
            r.ges[m, rows] = (r.est[m, rows, 2:3] * fe).astype(bf16)

        each(R, body)
        return_send(r.ges, r.ger, m, "geb")

    def finish_dxe(m):
        return_recv(r.dxr, m, "dxb")
        back = tn(r.perm[m], r.dxr[m])
        r.dy2[m, :, mine] = (r.cot[m, :, mine].astype(f32) + back).astype(bf16)
        gather_send(r.dy2, m, "dy2")

    finish_den(0)
    legs_sum_pass(r.dns, r.dnr, 1, "den")
    finish_dxe(0)
    finish_den(1)

    writes = []
    results = []

    def give(name):
        i = RESULTS.index(name)
        one = pltpu.make_async_copy(getattr(r, name), getattr(r, "to_" + name), r.lsem.at[4 + i])
        one.start()
        results.append(one)

    def expert_weights(left, right, out):
        for t in range(D // 256):
            slot = len(writes) % 2
            if len(writes) >= 2:
                writes[-2].wait()
            rows = slice(t * 256, (t + 1) * 256)
            lhs = left[:, :, rows].reshape(M * R, 256)
            r.stage[slot] = tn(lhs, right[...].reshape(M * R, D)).astype(bf16)
            writes.append(pltpu.make_async_copy(r.stage.at[slot], out.at[rows], r.lsem.at[2 + slot]))
            writes[-1].start()

    give("evo")

    finish_dxe(1)

    def token_stats(m, at, src):
        stats = [jnp.zeros((T, 1), f32) for _ in range(2)]
        mean, rs = r.tst[m, :, 2 * at : 2 * at + 1], r.tst[m, :, 2 * at + 1 : 2 * at + 2]
        for i in range(S):
            q = sec(i)
            tile = r.ts[m, i - 1].astype(f32) if i else r.own[m]
            scaled = tile * r.vecs[2 * at : 2 * at + 1, col(q)]
            n = (src[m, :, col(q)].astype(f32) - mean) * rs
            stats[0] += jnp.sum(scaled, axis=1, keepdims=True)
            stats[1] += jnp.sum(scaled * n, axis=1, keepdims=True)
        return stats

    def stats_send(m, at, stats):
        r.tss[at, m] = to_rows(stats)
        for i in others:
            send(r.tss.at[at, m], r.tsr.at[at, m, i - 1], ("tst", at, m, i), to_sec(i))

    def stats_recv(m, at):
        total = r.tss[at, m]
        for i in others:
            recv(r.tsr.at[at, m, i - 1], ("tst", at, m, i))
            total += r.tsr[at, m, i - 1]
        r.tst[m, :, 8:16] = to_columns(total)[:, 0:8]

    def dense_back(m):
        if m == 0:
            gather_recv(r.dy2, m, "dy2")

        @pl.loop(0, FQ // Q)
        def _(t):
            du = nt(r.dy2[m], r.wdn[t].reshape(Q, D))
            r.dh[m, :, col(t)] = (du * r.h[m, :, col(t)]).astype(bf16)

        sum_send(
            lambda q: nt(r.dh[m], r.wup[q].reshape(Q, FQ)),
            r.ts,
            r.r1,
            r.own,
            m,
            "da2",
            "y2",
            hold=m == 0,
        )
        stats_send(m, 1, token_stats(m, 1, r.y1))

    def norm_back(m, at, src, grad_in, own, arrive, emit):
        gain = r.vecs[2 * at : 2 * at + 1, mine]

        def body(rows):
            grad = summed(own, arrive, m, rows)
            mean, rs = r.tst[m, rows, 2 * at : 2 * at + 1], r.tst[m, rows, 2 * at + 1 : 2 * at + 2]
            n = (src[m, rows, mine].astype(f32) - mean) * rs
            m1, m2 = r.tst[m, rows, 8:9] * (1.0 / D), r.tst[m, rows, 9:10] * (1.0 / D)
            emit(rows, grad_in[m, rows, mine].astype(f32) + rs * (gain * grad - m1 - n * m2))
            r.vsum[2 * at : 2 * at + 1, :] += jnp.sum(grad * n, axis=0, keepdims=True)
            r.vsum[2 * at + 1 : 2 * at + 2, :] += jnp.sum(grad, axis=0, keepdims=True)

        each(T, body)

    def finish_da2(m):
        sum_recv(r.r1, m, "da2")
        stats_recv(m, 1)
        for i in others:
            sent(("y1g", m, i))

        def emit(rows, value):
            r.y1[m, rows, mine] = value.astype(bf16)

        norm_back(m, 1, r.y1, r.dy2, r.own, r.r1, emit)
        gather_send(r.y1, m, "dy1")

    blocks = (near_far, near, far, z)

    def grads_pair(g, b, k):
        for i, zz in enumerate(blocks):
            src = g.at[:, zz, 1 - c] if len(g.shape) == 5 else g.at[zz, 1 - c]
            dst = b.at[:, zz] if len(g.shape) == 5 else b.at[zz]
            send(src, dst, (k, "p", i), beside)

    def grads_add(g, zz, arrive):
        if len(g.shape) == 5:

            @pl.loop(0, S)
            def _(q):
                g[q, zz, c] = (g[q, zz, c].astype(f32) + arrive[q].astype(f32)).astype(bf16)
        else:
            g[zz, c] = (g[zz, c].astype(f32) + arrive[...].astype(f32)).astype(bf16)

    def grads_paired(g, b, k, i):
        zz = blocks[i]
        piece = b.at[:, zz] if len(g.shape) == 5 else b.at[zz]
        recv(piece, (k, "p", i))
        grads_add(g, zz, piece)

    def grads_near(g, b, arrive, k):
        grads_paired(g, b, k, 0)
        send(part(g, near_far, c), arrive.at[1], (k, "nf"), (s, near * 2 + c))
        grads_paired(g, b, k, 1)
        send(part(g, near, c), arrive.at[0], (k, "n"), (s, near * 2 + c))
        for i in range(2, nz):
            grads_paired(g, b, k, i)

    def grads_far(g, arrive, k):
        recv(arrive.at[1], (k, "nf"))
        grads_add(g, far, arrive.at[1])
        send(part(g, far, c), arrive.at[2], (k, "f"), (s, far * 2 + c))

    def grads_near_recv(arrive, k):
        recv(arrive.at[0], (k, "n"))
        recv(arrive.at[2], (k, "f"))
        return 0, 2

    def down_weights():
        for i, t in enumerate(blocks):
            lhs = r.u[:, :, col(t)].reshape(M * T, Q)
            grad = tn(lhs, r.dy2[...].reshape(M * T, D))
            r.wout[t] = grad.astype(bf16).reshape(2, shd, D)
            send(r.wout.at[t, 1 - c], r.bdn.at[t], ("gdn", "p", i), beside)

    def up_weights():
        @pl.loop(0, S)
        def _(t):
            lhs = r.a2[:, :, col(t)].reshape(M * T, Q)
            grad = tn(lhs, r.dh[...].reshape(M * T, FQ))
            r.win[t] = grad.astype(bf16).reshape(nz, 2, sh, FQ)

        grads_pair(r.win, r.bup, "gup")

    def qkv_weights():
        @pl.loop(0, S)
        def _(t):
            lhs = r.a1[:, :, col(t)].reshape(M * T, Q)
            grad = tn(lhs, r.dqkv[...].reshape(M * T, 3 * Q))
            r.gqk[t] = grad.astype(bf16).reshape(nz, 2, sh, 3 * Q)

        grads_pair(r.gqk, r.bqk, "gqk")

    def out_weights():
        grad = tn(r.o[...].reshape(M * T, Q), r.y1[...].reshape(M * T, D))
        r.gwo[...] = grad.astype(bf16).reshape(nz, 2, sh, D)
        grads_pair(r.gwo, r.bwo, "gwo")

    r.vsum[...] = jnp.zeros_like(r.vsum)
    dense_back(0)
    gather_recv(r.dy2, 1, "dy2", lambda: sum_start(r.ts, r.r1, 0, "da2"))
    down_weights()
    grads_near(r.wout, r.bdn, r.zdn, "gdn")
    dense_back(1)
    finish_da2(0)
    up_weights()
    grads_far(r.wout, r.zdn, "gdn")
    finish_da2(1)
    grads_near(r.win, r.bup, r.zup, "gup")

    def attend_back(m):
        if m == 0:
            gather_recv(r.y1, m, "dy1")
        out_grad = nt(r.y1[m], r.wo[...].reshape(Q, D)).astype(bf16)
        for hh in range(heads):
            at = hh * size
            q = r.qkv[m, :, at : at + size]
            k = r.qkv[m, :, Q + at : Q + at + size]
            v = r.qkv[m, :, 2 * Q + at : 2 * Q + at + size]
            go = out_grad[:, at : at + size]
            p = r.probs[m, hh]
            dp = nt(go, v)
            dv = tn(p.astype(bf16), go)
            ds = (p * (dp - jnp.sum(p * dp, axis=1, keepdims=True))).astype(bf16)
            dq = jnp.dot(ds, k, preferred_element_type=f32) * scale
            dk = tn(ds, q) * scale
            r.dqkv[m, :, at : at + size] = dq.astype(bf16)
            r.dqkv[m, :, Q + at : Q + at + size] = dk.astype(bf16)
            r.dqkv[m, :, 2 * Q + at : 2 * Q + at + size] = dv.astype(bf16)
        sum_send(
            lambda q: nt(r.dqkv[m], r.wqkv[q].reshape(Q, 3 * Q)),
            r.ts,
            r.r2,
            r.own,
            m,
            "da1",
            "da2",
            hold=True,
        )
        stats_send(m, 0, token_stats(m, 0, r.hidden))

    def finish_da1(m):
        sum_recv(r.r2, m, "da1")
        stats_recv(m, 0)

        def emit(rows, value):
            r.dx[m, rows] = value

        norm_back(m, 0, r.hidden, r.y1, r.own, r.r2, emit)

    attend_back(0)
    gather_recv(r.y1, 1, "dy1")
    sum_start(r.fes, r.fer, 0, "fe")
    sum_start(r.fes, r.fer, 1, "fe")
    attend_back(1)
    grads_far(r.win, r.zup, "gup")
    qkv_weights()
    grads_near(r.gqk, r.bqk, r.zqk, "gqk")
    out_weights()
    grads_near(r.gwo, r.bwo, r.zwo, "gwo")
    expert_weights(r.en, r.dhe, r.gin_out)
    finish_fe(0)
    sum_start(r.ts, r.r2, 0, "da1")
    sum_start(r.ts, r.r2, 1, "da1")
    grads_far(r.gqk, r.zqk, "gqk")
    grads_far(r.gwo, r.zwo, "gwo")
    finish_fe(1)
    expert_weights(r.ue, r.dfe, r.gout_out)

    def finish_out(m):
        return_recv(r.ger, m, "geb")
        back = tn(r.perm[m], r.ger[m])
        r.out[m] = (r.y2q[m].astype(f32) + back).astype(bf16)


    def row_result(g, arrive, out, k, rows, wait):
        slots = wait(arrive, k)
        mine_part = part(g, z, c)

        def body(at):
            total = mine_part[at].astype(f32)
            for slot in slots:
                total += arrive[slot, at].astype(f32)
            out[at] = total

        each(rows, body)

    def column_send(g, arrive, out, back, k, wait):
        slots = wait(arrive, k)

        @pl.loop(0, S)
        def _(q):
            total = g[q, z, c].astype(f32)
            for slot in slots:
                total += arrive[slot, q].astype(f32)
            out[q] = total.astype(bf16)

        for i in others:
            send(out.at[sec(i)], back.at[i - 1], (k, "s", i), to_sec(i))

    def column_result(sums, back, out, pieces, k):
        width = sums.shape[2] // pieces
        for i in range(S):
            if i:
                recv(back.at[i - 1], (k, "s", i))
            q = sec(S - i) if i else s
            value = (back[i - 1] if i else sums[s]).astype(f32)
            for piece in range(pieces):
                at = pl.ds(pl.multiple_of(piece * S * width + q * width, width), width)
                out[:, at] = value[:, piece * width : (piece + 1) * width]

    row_result(r.wout, r.zdn, r.gdn_out, "gdn", shd, grads_near_recv)
    give("gdn_out")
    column_send(r.win, r.zup, r.ups, r.upr, "gup", grads_near_recv)
    finish_da1(0)
    finish_da1(1)
    give("dx")
    for j in range(1, G):
        send(r.vsum, r.vsr.at[j - 1], ("vs", j), to_dp(j))
    column_send(r.gqk, r.zqk, r.qks, r.qkr, "gqk", grads_near_recv)
    row_result(r.gwo, r.zwo, r.gwo_out, "gwo", sh, grads_near_recv)
    give("gwo_out")
    column_result(r.ups, r.upr, r.gup_out, 1, "gup")
    give("gup_out")
    finish_out(0)
    finish_out(1)
    give("out")
    total = r.vsum[...]
    for j in range(1, G):
        recv(r.vsr.at[j - 1], ("vs", j))
        total += r.vsr[j - 1]
    shard = jnp.zeros((8, sh), f32)
    for j in range(G):
        shard += jnp.where(d == j, 1.0, 0.0) * total[:, j * sh : (j + 1) * sh]
    r.vgo[...] = jnp.zeros_like(r.vgo)
    r.vgo[:, 0:sh] = shard
    give("vgo")
    column_result(r.qks, r.qkr, r.gqk_out, 3, "gqk")
    give("gqk_out")

    def drain():
        for write in writes[-2:] + results:
            write.wait()
        for last in pending.values():
            last.wait_send()

    drain()
    assert len(places) == KEYS, len(places)


def hand_over(*refs):
    (out, dx, vgo, gqk, gwo, gup, gdn, evo, gin, gout) = refs[:10]
    results = refs[10:]
    results[8][...] = gin[...].astype(f32)
    results[9][...] = gout[...].astype(f32)

    @pl.when(pl.program_id(0) == 0)
    def _():
        for src, dst in zip((out, dx, gqk, gwo, gup, gdn), results[:2] + results[4:8]):
            dst[...] = src[...]
        for i, dst in enumerate(results[2:4] + results[10:12]):
            dst[...] = vgo[i : i + 1, 0 : dst.shape[1]]
        for i, dst in enumerate(results[12:]):
            dst[...] = evo[i : i + 1, :]


def with_kernel(
    hidden_in,
    cotangent,
    bucket_len,
    live_mask,
    routes,
    ln1_gain,
    ln1_bias,
    w_qkv,
    w_attn_out,
    ln2_gain,
    ln2_bias,
    w_up,
    w_down,
    expert_in,
    expert_out,
    expert_gain,
    expert_bias,
    centroids,
):
    S = lax.axis_size(SECTION)
    G = lax.axis_size(DP)
    M, T, D = hidden_in.shape
    Q = D // S
    FQ = w_up.shape[1] // S
    C = 3 * T // (2 * G)
    sh, shd = w_up.shape[0], w_down.shape[0]
    dims = (S, G, M, T, D, Q, FQ, C, sh, shd)
    scratch = layout(dims)
    names = INPUTS + OUTPUTS + list(scratch) + ["ssem", "rsem", "lsem"]
    vmem = pl.BlockSpec(memory_space=pltpu.VMEM)
    smem = pl.BlockSpec(memory_space=pltpu.SMEM)
    anywhere = pl.BlockSpec(memory_space=pl.ANY)
    shapes = (
        ((M, T, Q), bf16),
        ((M, T, Q), f32),
        ((8, 128), f32),
        ((sh, 3 * D), f32),
        ((sh, D), f32),
        ((sh, S * FQ), f32),
        ((shd, D), f32),
        ((8, Q), f32),
        ((D, FQ), bf16),
        ((FQ, D), bf16),
    )
    outs = pl.pallas_call(
        functools.partial(block_kernel, dims, names),
        name="block",
        out_shape=[jax.ShapeDtypeStruct(*shape) for shape in shapes],
        in_specs=[vmem, vmem, smem] + [vmem] * 13 + [anywhere] * 2,
        out_specs=[anywhere] * len(shapes),
        scratch_shapes=[pltpu.VMEM(*shape) for shape in scratch.values()]
        + [pltpu.SemaphoreType.DMA((KEYS,))] * 2
        + [pltpu.SemaphoreType.DMA((4 + len(RESULTS),))],
        compiler_params=pltpu.CompilerParams(
            collective_id=0, has_side_effects=True, vmem_limit_bytes=63 << 20
        ),
    )(
        hidden_in,
        cotangent,
        bucket_len,
        live_mask,
        jnp.swapaxes(routes, 1, 2),
        ln1_gain.reshape(1, sh),
        ln1_bias.reshape(1, sh),
        ln2_gain.reshape(1, sh),
        ln2_bias.reshape(1, sh),
        expert_gain,
        expert_bias,
        centroids,
        w_qkv,
        w_attn_out,
        w_up,
        w_down,
        expert_in.reshape(S, G // 2, 2, sh, FQ),
        expert_out.reshape(G // 2, 2, shd, D),
    )

    def spec(shape):
        if shape in ((D, FQ), (FQ, D)):
            return pl.BlockSpec((512, shape[1]), lambda i: (i, 0))
        return pl.BlockSpec(shape, lambda i, n=len(shape): (0,) * n)

    finals = (
        shapes[:2]
        + (((1, sh), f32),) * 2
        + shapes[3:7]
        + (((D, FQ), f32), ((FQ, D), f32))
        + (((1, sh), f32),) * 2
        + (((1, Q), f32),) * 3
    )
    outs = pl.pallas_call(
        hand_over,
        name="hand_over",
        grid=(D // 512,),
        out_shape=[jax.ShapeDtypeStruct(*shape) for shape in finals],
        in_specs=[spec(shape) for shape, _ in shapes],
        out_specs=[spec(shape) for shape, _ in finals],
        compiler_params=pltpu.CompilerParams(vmem_limit_bytes=63 << 20),
    )(*outs)
    out, dx, gain1, bias1, gqkv, gwo, gup, gdn, gin, gout, gain2, bias2, eg, eb, ec = outs
    return (
        out,
        dx,
        gain1.reshape(sh),
        bias1.reshape(sh),
        gqkv,
        gwo,
        gain2.reshape(sh),
        bias2.reshape(sh),
        gup,
        gdn,
        gin[None],
        gout[None],
        eg,
        eb,
        ec,
    )


def on_device(*args):
    groups = lax.axis_size(DP)
    rows, shard = args[0].shape[1], args[11].shape[0]
    capacity = 3 * rows // (2 * groups)
    if capacity % 16 or shard % 16 or groups != 8:
        return with_collectives(*args)
    return with_kernel(*args)


def solution(mesh):
    everywhere = (SECTION, DP)
    tokens = P(None, DP, None)
    outs = P(None, DP, SECTION)
    per_expert = P(DP, SECTION)
    return jax.shard_map(
        on_device,
        mesh=mesh,
        in_specs=(
            tokens,
            tokens,
            tokens,
            P(None, DP),
            tokens,
            P(everywhere),
            P(everywhere),
            P(everywhere, None),
            P(everywhere, None),
            P(everywhere),
            P(everywhere),
            P(everywhere, None),
            P(everywhere, None),
            P(DP, None, SECTION),
            P(DP, SECTION, None),
            per_expert,
            per_expert,
            per_expert,
        ),
        out_specs=(
            outs,
            outs,
            P(everywhere),
            P(everywhere),
            P(everywhere, None),
            P(everywhere, None),
            P(everywhere),
            P(everywhere),
            P(everywhere, None),
            P(everywhere, None),
            P(DP, None, SECTION),
            P(DP, SECTION, None),
            per_expert,
            per_expert,
            per_expert,
        ),
        check_vma=False,
    )
```
